32 devices in a mesh: dp: 16 (over z, y, x), blk: 2 (over core).
Axes of the slice: x: 2, y: 2, z: 4, core: 2. Of those that a mesh axis runs over, the one named last changes fastest.
Arguments:
- patches: bfloat16 [24576, 768], P(('dp', 'blk')), may hold values from -6 to 6
- visible: int32 [24576], P(('dp', 'blk')), may hold values 0 or 1
- padding: int32 [24576], P(('dp', 'blk')), may hold values from 0 to 1, as said below
- field_ids: int32 [24576], P(('dp', 'blk')), may hold values from 0 to 1, as said below
- enc_gain_a: bfloat16 [768], replicated, may hold values from 0.25 to 1.75
- enc_shift_a: bfloat16 [768], replicated, may hold values from -1.5 to 1.5
- enc_qkv: bfloat16 [768, 2304], replicated, may hold values from -0.21875 to 0.21875
- enc_out: bfloat16 [768, 768], replicated, may hold values from -0.875 to 0.875
- enc_out_bias: bfloat16 [768], replicated, may hold values from -1.5 to 1.5
- enc_gain_b: bfloat16 [768], replicated, may hold values from 0.25 to 1.75
- enc_shift_b: bfloat16 [768], replicated, may hold values from -1.5 to 1.5
- enc_up: bfloat16 [768, 3072], replicated, may hold values from -0.21875 to 0.21875
- enc_up_bias: bfloat16 [3072], replicated, may hold values from -1.5 to 1.5
- enc_down: bfloat16 [3072, 768], replicated, may hold values from -0.109375 to 0.109375
- enc_down_bias: bfloat16 [768], replicated, may hold values from -1.5 to 1.5
- embed_map: bfloat16 [768, 512], replicated, may hold values from -0.21875 to 0.21875
- embed_bias: bfloat16 [512], replicated, may hold values from -1.5 to 1.5
- mask_token: bfloat16 [512], replicated, may hold values from -4 to 4
- dec_gain_a: bfloat16 [512], replicated, may hold values from 0.25 to 1.75
- dec_shift_a: bfloat16 [512], replicated, may hold values from -1.5 to 1.5
- dec_qkv: bfloat16 [512, 1536], replicated, may hold values from -0.25 to 0.25
- dec_out: bfloat16 [512, 512], replicated, may hold values from -1.5 to 1.5
- dec_out_bias: bfloat16 [512], replicated, may hold values from -1.5 to 1.5
- dec_gain_b: bfloat16 [512], replicated, may hold values from 0.25 to 1.75
- dec_shift_b: bfloat16 [512], replicated, may hold values from -1.5 to 1.5
- dec_up: bfloat16 [512, 2048], replicated, may hold values from -0.25 to 0.25
- dec_up_bias: bfloat16 [2048], replicated, may hold values from -1.5 to 1.5
- dec_down: bfloat16 [2048, 512], replicated, may hold values from -0.125 to 0.125
- dec_down_bias: bfloat16 [512], replicated, may hold values from -1.5 to 1.5
- cotangent: bfloat16 [24576, 512], P(('dp', 'blk')), may hold values from -6 to 6
Outputs:
- decoded: bfloat16 [24576, 512], P(('dp', 'blk'))
- patches_grad: bfloat16 [24576, 768], P(('dp', 'blk'))
- grad_enc_gain_a: float32 [768], replicated
- grad_enc_shift_a: float32 [768], replicated
- grad_enc_qkv: float32 [768, 2304], replicated
- grad_enc_out: float32 [768, 768], replicated
- grad_enc_out_bias: float32 [768], replicated
- grad_enc_gain_b: float32 [768], replicated
- grad_enc_shift_b: float32 [768], replicated
- grad_enc_up: float32 [768, 3072], replicated
- grad_enc_up_bias: float32 [3072], replicated
- grad_enc_down: float32 [3072, 768], replicated
- grad_enc_down_bias: float32 [768], replicated
- grad_embed_map: float32 [768, 512], replicated
- grad_embed_bias: float32 [512], replicated
- grad_mask_token: float32 [512], replicated
- grad_dec_gain_a: float32 [512], replicated
- grad_dec_shift_a: float32 [512], replicated
- grad_dec_qkv: float32 [512, 1536], replicated
- grad_dec_out: float32 [512, 512], replicated
- grad_dec_out_bias: float32 [512], replicated
- grad_dec_gain_b: float32 [512], replicated
- grad_dec_shift_b: float32 [512], replicated
- grad_dec_up: float32 [512, 2048], replicated
- grad_dec_up_bias: float32 [2048], replicated
- grad_dec_down: float32 [2048, 512], replicated
- grad_dec_down_bias: float32 [512], replicated
The draws below stay inside these ranges and needn't reach their ends.
Inputs may be any that keep to these rules, and one draw needn't show every extreme that they name: In each group of 1536 consecutive rows the padding rows, if any, form a trailing run of at most 383 rows; some group has exactly that many. `field_ids`: in each group of 1536 consecutive rows field 0 is a leading run shorter than half the group and field 1 is all the rest.
All inputs are finite; a program needn't handle non-finite values. No bound on the sum of `visible` on one device may be relied on, other than what follows from the above.
Results may differ from the reference program's by a relative error of at most 0.019.
Values may be sent and summed in bfloat16 or wider, within the bound.
No kernel may reach another device: no remote copies, remote signals or barrier semaphores. Data moves between devices by JAX's collectives and lax.ppermute only.
A program may use at most 320 MiB of HBM per device.

```python
import jax
import jax.numpy as jnp
from jax import lax

DE = 768
HE = 12
FE = 3072
DD = 512
HD = 16
FD = 2048
GROUP = 1536
TOKENS = 24576


def group_layout(key):
    groups = TOKENS // GROUP
    cut_key, pad_key, full_key = jax.random.split(key, 3)
    cut_points = jax.random.randint(cut_key, (groups, 1), GROUP // 8, 3 * GROUP // 8)
    pad_counts = jax.random.randint(pad_key, (groups, 1), 0, GROUP // 4)
    full_group = jax.random.randint(full_key, (), 0, groups)
    pad_counts = jnp.where(jnp.arange(groups)[:, None] == full_group, GROUP // 4 - 1, pad_counts)
    position = jnp.arange(GROUP)[None, :]
    labels = (position >= cut_points).astype(jnp.int32).reshape(TOKENS)
    padded = (position >= GROUP - pad_counts).astype(jnp.int32).reshape(TOKENS)
    return (labels, padded)


def draw_padding(key, part):
    layout = group_layout(key)
    return layout[1]


def draw_field_ids(key, part):
    layout = group_layout(key)
    return layout[0]


def set_ends(entries, key, low, largest):
    index_at = [jax.random.randint(jax.random.fold_in(key, axis), (), 0, length) for axis, length in enumerate(entries.shape)]
    longest = entries.shape.index(max(entries.shape))
    next_to = index_at[:longest] + [(index_at[longest] + 1) % entries.shape[longest]] + index_at[longest + 1:]
    return entries.at[tuple(index_at)].set(low).at[tuple(next_to)].set(largest)


def spiked(values, own_key, source, target, parts, factor):
    owner, partner = [(jnp.arange(values.shape[axis_at]) // (values.shape[axis_at] // parts)).reshape([-1 if axis == axis_at else 1 for axis in range(values.ndim)]) for axis_at in (source, target)]
    chosen = jax.random.permutation(own_key, parts)[partner]
    strong = (owner == chosen) | (owner == (partner + parts // 2) % parts)
    return jnp.where(strong, factor * values, values)


def shard_levels(stream_key, dims, cuts, smallest, largest):
    def one(dim, blocks):
        heights = jax.random.uniform(jax.random.fold_in(jax.random.fold_in(stream_key, 6), dim), (blocks,), jnp.float32, smallest / len(cuts), largest / len(cuts))
        return jnp.repeat(jnp.exp(heights), dims[dim] // blocks).reshape((-1,) + (1,) * (len(dims) - dim - 1))

    level = one(*cuts[0])
    for cut in cuts[1:]:
        level = level * one(*cut)
    return level


def scatter_about(rng, extent, width, most, cuts=(), dtype=jnp.bfloat16):
    entries = jax.random.normal(rng, extent, jnp.float32) * width
    if len(cuts) > 0:
        entries = shard_levels(rng, extent, cuts, -0.22, 0.18) * entries
    return jnp.clip(entries, min=-most, max=most).astype(dtype)


def noise_with(own_key, dims, scale, most, cuts, heavy, held_as=jnp.bfloat16):
    array = scale * jax.random.normal(own_key, dims, jnp.float32)
    if cuts:
        array = array * shard_levels(own_key, dims, cuts, -0.22, 0.18)
    return jnp.clip(spiked(array, jax.random.fold_in(own_key, 3), *heavy), -most, most).astype(held_as)


def setup_inputs(seed: int = 0) -> dict:
    key_of = jax.random.split(jax.random.key(seed), 31)
    return {
        "patches": scatter_about(key_of[0], (TOKENS, DE), 1.0, 6.0, ((0, 32),)),
        "visible": set_ends((jax.random.randint(key_of[1], (TOKENS,), 0, 4) < 1).astype(jnp.int32), jax.random.fold_in(key_of[1], 1), 0, 1),
        "padding": draw_padding(jax.random.fold_in(key_of[30], 71), 0),
        "field_ids": draw_field_ids(jax.random.fold_in(key_of[30], 71), 0),
        "enc_gain_a": jnp.clip(1.0 + 0.15 * jax.random.normal(key_of[4], (DE,), jnp.float32), 0.25, 1.75).astype(jnp.bfloat16),
        "enc_shift_a": scatter_about(key_of[5], (DE,), 0.3, 1.5),
        "enc_qkv": scatter_about(key_of[6], (DE, 3 * DE), DE ** -0.5, 0.21875),
        "enc_out": scatter_about(key_of[7], (DE, DE), (DE // 16) ** -0.5, 0.875),
        "enc_out_bias": scatter_about(key_of[8], (DE,), 0.3, 1.5),
        "enc_gain_b": jnp.clip(1.0 + 0.15 * jax.random.normal(key_of[9], (DE,), jnp.float32), 0.25, 1.75).astype(jnp.bfloat16),
        "enc_shift_b": scatter_about(key_of[10], (DE,), 0.3, 1.5),
        "enc_up": scatter_about(key_of[11], (DE, FE), DE ** -0.5, 0.21875),
        "enc_up_bias": scatter_about(key_of[12], (FE,), 0.3, 1.5),
        "enc_down": scatter_about(key_of[13], (FE, DE), FE ** -0.5, 0.109375),
        "enc_down_bias": scatter_about(key_of[14], (DE,), 0.3, 1.5),
        "embed_map": scatter_about(key_of[15], (DE, DD), DE ** -0.5, 0.21875),
        "embed_bias": scatter_about(key_of[16], (DD,), 0.3, 1.5),
        "mask_token": scatter_about(key_of[17], (DD,), 1.0, 4.0),
        "dec_gain_a": jnp.clip(1.0 + 0.15 * jax.random.normal(key_of[18], (DD,), jnp.float32), 0.25, 1.75).astype(jnp.bfloat16),
        "dec_shift_a": scatter_about(key_of[19], (DD,), 0.3, 1.5),
        "dec_qkv": scatter_about(key_of[20], (DD, 3 * DD), DD ** -0.5, 0.25),
        "dec_out": scatter_about(key_of[21], (DD, DD), (DD // 32) ** -0.5, 1.5),
        "dec_out_bias": scatter_about(key_of[22], (DD,), 0.3, 1.5),
        "dec_gain_b": jnp.clip(1.0 + 0.15 * jax.random.normal(key_of[23], (DD,), jnp.float32), 0.25, 1.75).astype(jnp.bfloat16),
        "dec_shift_b": scatter_about(key_of[24], (DD,), 0.3, 1.5),
        "dec_up": scatter_about(key_of[25], (DD, FD), DD ** -0.5, 0.25),
        "dec_up_bias": scatter_about(key_of[26], (FD,), 0.3, 1.5),
        "dec_down": scatter_about(key_of[27], (FD, DD), FD ** -0.5, 0.125),
        "dec_down_bias": scatter_about(key_of[28], (DD,), 0.3, 1.5),
        "cotangent": noise_with(key_of[29], (TOKENS, DD), 1.0, 6.0, ((0, 32),), (0, 1, 32, 2.75)),
    }


@jax.custom_vjp
def low(v):
    return lax.optimization_barrier(v.astype(jnp.bfloat16)).astype(jnp.float32)

@jax.custom_vjp
def low_back(v):
    return v

def low_keep(v):
    return (low(v), None)

def low_pass(kept, grad):
    return (grad,)

def back_keep(v):
    return (v, None)

def back_low(kept, grad):
    return (low(grad),)
low.defvjp(low_keep, low_pass)
low_back.defvjp(back_keep, back_low)
precise = lax.Precision.HIGHEST
epsilon = 1e-06

def layer_norm(stream, gain_term, bias_term):
    row_mean = lax.optimization_barrier(jnp.mean(stream, axis=-1, keepdims=True))
    centred = stream - row_mean
    spread = lax.optimization_barrier(jnp.mean(centred * centred, axis=-1, keepdims=True))
    return centred * lax.rsqrt(spread + epsilon) * gain_term + bias_term

def group_attention(queries, key_rows, value_rows, key_ok, labels, head_count):
    row_count, columns = queries.shape
    head_size = columns // head_count
    query_heads = queries.reshape(row_count, head_count, head_size)
    key_heads = key_rows.reshape(row_count, head_count, head_size)
    value_heads = value_rows.reshape(row_count, head_count, head_size)
    raw_scores = jnp.einsum('qhd,khd->hqk', query_heads, key_heads, precision=precise) * head_size ** (-0.5)
    scores = low_back(raw_scores)
    position = jnp.arange(row_count)
    allowed = (labels[:, None] == labels[None, :]) & (key_ok[None, :] > 0) | (position[:, None] == position[None, :])
    scores = jnp.where(allowed[None], scores, -1e+30)
    weight_tensors = low(jax.nn.softmax(scores, axis=-1))
    blended = jnp.einsum('hqk,khd->qhd', weight_tensors, value_heads, precision=precise)
    return low(low_back(blended.reshape(row_count, columns)))

def block(stream, params, key_ok, labels, head_count):
    gain_a, shift_a, qkv_weight, out_weight, out_bias, gain_b, shift_b, up_weight, up_bias, down_weight, down_bias = params
    columns = stream.shape[1]
    groups = stream.shape[0] // GROUP
    normed = low(layer_norm(stream, gain_a, shift_a))
    projected = low(low_back(jnp.dot(normed, qkv_weight, precision=precise)))
    queries = projected[:, :columns].reshape(groups, GROUP, columns)
    key_rows = projected[:, columns:2 * columns].reshape(groups, GROUP, columns)
    value_rows = projected[:, 2 * columns:].reshape(groups, GROUP, columns)

    def one_group(pieces):
        return group_attention(pieces[0], pieces[1], pieces[2], pieces[3], pieces[4], head_count)
    attended = lax.map(jax.checkpoint(one_group), (queries, key_rows, value_rows, key_ok.reshape(groups, GROUP), labels.reshape(groups, GROUP)))
    middle = stream + low_back(jnp.dot(attended.reshape(-1, columns), out_weight, precision=precise) + out_bias)
    normed_b = low(layer_norm(middle, gain_b, shift_b))
    pre_act = low_back(jnp.dot(normed_b, up_weight, precision=precise) + up_bias)
    activated = low(jax.nn.gelu(pre_act, approximate=False))
    return middle + low_back(jnp.dot(activated, down_weight, precision=precise) + down_bias)

def forward(patches, weight_tensors, visible, padding, field_ids):
    seen_ok = visible * (1 - padding)
    kept_ok = 1 - padding
    encoded = block(patches, weight_tensors[:11], seen_ok, field_ids, HE)
    lifted = low_back(jnp.dot(low(encoded), weight_tensors[11], precision=precise) + weight_tensors[12])
    start = jnp.where(visible[:, None] > 0, lifted, weight_tensors[13][None, :])
    return block(start, weight_tensors[14:], kept_ok, field_ids, HD)

def reference(patches, visible, padding, field_ids, enc_gain_a, enc_shift_a, enc_qkv, enc_out, enc_out_bias, enc_gain_b, enc_shift_b, enc_up, enc_up_bias, enc_down, enc_down_bias, embed_map, embed_bias, mask_token, dec_gain_a, dec_shift_a, dec_qkv, dec_out, dec_out_bias, dec_gain_b, dec_shift_b, dec_up, dec_up_bias, dec_down, dec_down_bias, cotangent):
    weight_tensors = tuple((tensor.astype(jnp.float32) for tensor in (enc_gain_a, enc_shift_a, enc_qkv, enc_out, enc_out_bias, enc_gain_b, enc_shift_b, enc_up, enc_up_bias, enc_down, enc_down_bias, embed_map, embed_bias, mask_token, dec_gain_a, dec_shift_a, dec_qkv, dec_out, dec_out_bias, dec_gain_b, dec_shift_b, dec_up, dec_up_bias, dec_down, dec_down_bias)))

    def whole_pass(inputs, *params):
        return forward(inputs, params, visible, padding, field_ids)
    decoded, pullback = jax.vjp(whole_pass, patches.astype(jnp.float32), *weight_tensors)
    gradients = pullback(cotangent.astype(jnp.float32))
    return (decoded.astype(jnp.bfloat16), gradients[0].astype(jnp.bfloat16), gradients[1], gradients[2], gradients[3], gradients[4], gradients[5], gradients[6], gradients[7], gradients[8], gradients[9], gradients[10], gradients[11], gradients[12], gradients[13], gradients[14], gradients[15], gradients[16], gradients[17], gradients[18], gradients[19], gradients[20], gradients[21], gradients[22], gradients[23], gradients[24], gradients[25])
```

```python
import math

import jax
import jax.numpy as jnp
from jax import lax
from jax.experimental import pallas as pl
from jax.experimental.pallas import tpu as pltpu
from jax.sharding import PartitionSpec as P

HE = 12
HD = 16


epsilon = 1e-06
TILE = 256
VMEM_LIMIT = 56 * 1024 * 1024


def passed_along(value, axis, steps):
    count = lax.axis_size(axis)
    pairs = [(source, (source + steps) % count) for source in range(count)]
    return lax.ppermute(value, axis, pairs)


def layer_norm(stream, gain_term, bias_term):
    row_mean = jnp.mean(stream, axis=-1, keepdims=True)
    centred = stream - row_mean
    spread = jnp.mean(centred * centred, axis=-1, keepdims=True)
    return centred * lax.rsqrt(spread + epsilon) * gain_term + bias_term


def gelu_exact(pre_act):
    return jax.nn.gelu(pre_act, approximate=False)


def matmul(left_side, right_side):
    return jnp.dot(left_side, right_side, preferred_element_type=jnp.float32)


def matmul_tn(left_side, right_side):
    return lax.dot_general(
        left_side, right_side, (((0,), (0,)), ((), ())), preferred_element_type=jnp.float32
    )


def matmul_nt(left_side, right_side):
    return lax.dot_general(
        left_side, right_side, (((1,), (1,)), ((), ())), preferred_element_type=jnp.float32
    )


def column_sum(gradient):
    return jnp.sum(gradient, axis=0, dtype=jnp.float32)


def norm_forward(stream, gain_term, bias_term):
    normed, pullback = jax.vjp(
        layer_norm, stream, gain_term.astype(jnp.float32), bias_term.astype(jnp.float32)
    )
    return (normed.astype(jnp.bfloat16), pullback)


def heads_per_group():
    return 4


def split_heads(matrix, offset, group_span, group_heads):
    sliced = lax.dynamic_slice_in_dim(matrix, offset, group_span, 1)
    return sliced.reshape(matrix.shape[0], group_heads, group_span // group_heads)


def allowed_keys(label_value, near_code, far_code):
    position = jnp.arange(label_value.shape[0])
    diagonal = position[:, None] == position[None, :]
    near_ok = (label_value[:, None] == near_code.astype(jnp.float32)[None, :]) | diagonal
    far_ok = label_value[:, None] == far_code.astype(jnp.float32)[None, :]
    return jnp.concatenate([near_ok, far_ok], axis=1)


def attend_forward(queries, key_rows, values, allowed, head_count):
    row_count, columns = queries.shape
    head_size = columns // head_count
    group_heads = heads_per_group()
    group_span = group_heads * head_size
    scaling = head_size ** (-0.5)

    def one_group(group_index, state_carry):
        blended, totals = state_carry
        offset = group_index * group_span
        partial_query = split_heads(queries, offset, group_span, group_heads)
        partial_key = split_heads(key_rows, offset, group_span, group_heads)
        partial_value = split_heads(values, offset, group_span, group_heads)
        scores = (
            jnp.einsum(
                "xhr,phr->hxp", partial_query, partial_key, preferred_element_type=jnp.float32
            )
            * scaling
        )
        scores = jnp.where(allowed[None], scores, -1e30)
        row_max = jnp.max(scores, axis=-1, keepdims=True)
        exponent = jnp.exp(scores - row_max)
        row_sum = jnp.sum(exponent, axis=-1, keepdims=True)
        weight_tensors = (exponent / row_sum).astype(jnp.bfloat16)
        block_output = jnp.einsum(
            "pnz,zpc->npc", weight_tensors, partial_value, preferred_element_type=jnp.float32
        )
        blended = lax.dynamic_update_slice_in_dim(
            blended, block_output.reshape(row_count, group_span).astype(jnp.bfloat16), offset, 1
        )
        totals = lax.dynamic_update_slice_in_dim(
            totals, (row_max + jnp.log(row_sum))[:, :, 0], group_index * group_heads, 0
        )
        return (blended, totals)

    initial = (
        jnp.zeros((row_count, columns), jnp.bfloat16),
        jnp.zeros((head_count, row_count), jnp.float32),
    )
    return lax.fori_loop(0, head_count // group_heads, one_group, initial)


def attend_backward(queries, key_rows, values, allowed, totals, grad_out, head_count):
    row_count, columns = queries.shape
    key_count = key_rows.shape[0]
    head_size = columns // head_count
    group_heads = heads_per_group()
    group_span = group_heads * head_size
    scaling = head_size ** (-0.5)

    def one_group(group_index, state_carry):
        grad_query, grad_keys, grad_values = state_carry
        offset = group_index * group_span
        partial_query = split_heads(queries, offset, group_span, group_heads)
        partial_key = split_heads(key_rows, offset, group_span, group_heads)
        partial_value = split_heads(values, offset, group_span, group_heads)
        partial_gradient = split_heads(grad_out, offset, group_span, group_heads)
        scores = (
            jnp.einsum(
                "xhr,phr->hxp", partial_query, partial_key, preferred_element_type=jnp.float32
            )
            * scaling
        )
        scores = jnp.where(allowed[None], scores, -1e30)
        log_totals = lax.dynamic_slice_in_dim(totals, group_index * group_heads, group_heads, 0)
        probs = jnp.exp(scores - log_totals[:, :, None])
        grad_probs = jnp.einsum(
            "xhr,phr->hxp", partial_gradient, partial_value, preferred_element_type=jnp.float32
        )
        row_inner = jnp.sum(probs * grad_probs, axis=-1, keepdims=True)
        score_gradient = (probs * (grad_probs - row_inner)).astype(jnp.bfloat16)
        query_grad = (
            jnp.einsum(
                "pnz,zpc->npc", score_gradient, partial_key, preferred_element_type=jnp.float32
            )
            * scaling
        )
        key_grad = (
            jnp.einsum(
                "zft,fzi->tzi", score_gradient, partial_query, preferred_element_type=jnp.float32
            )
            * scaling
        )
        value_grad = jnp.einsum(
            "zft,fzi->tzi",
            probs.astype(jnp.bfloat16),
            partial_gradient,
            preferred_element_type=jnp.float32,
        )
        grad_query = lax.dynamic_update_slice_in_dim(
            grad_query, query_grad.reshape(row_count, group_span), offset, 1
        )
        grad_keys = lax.dynamic_update_slice_in_dim(
            grad_keys, key_grad.reshape(key_count, group_span), offset, 1
        )
        grad_values = lax.dynamic_update_slice_in_dim(
            grad_values, value_grad.reshape(key_count, group_span), offset, 1
        )
        return (grad_query, grad_keys, grad_values)

    initial = (
        jnp.zeros((row_count, columns), jnp.float32),
        jnp.zeros((key_count, columns), jnp.float32),
        jnp.zeros((key_count, columns), jnp.float32),
    )
    return lax.fori_loop(0, head_count // group_heads, one_group, initial)


def attention_inputs(stream, gain_term, bias_term, qkv_weight):
    normed_low, pullback = norm_forward(stream, gain_term, bias_term)
    projected = matmul(normed_low, qkv_weight).astype(jnp.bfloat16)
    columns = stream.shape[1]
    return (
        normed_low,
        pullback,
        projected[:, :columns],
        projected[:, columns : 2 * columns],
        projected[:, 2 * columns :],
    )


def block_rest(
    stream,
    attended,
    out_weight,
    out_bias,
    gain_b,
    shift_b,
    up_weight,
    up_bias,
    down_weight,
    down_bias,
):
    middle = stream + matmul(attended, out_weight) + out_bias.astype(jnp.float32)
    normed_low, pullback = norm_forward(middle, gain_b, shift_b)
    pre_act = matmul(normed_low, up_weight) + up_bias.astype(jnp.float32)
    activated, gelu_pull = jax.vjp(gelu_exact, pre_act)
    active_low = activated.astype(jnp.bfloat16)
    result = middle + matmul(active_low, down_weight) + down_bias.astype(jnp.float32)
    return (result, (normed_low, pullback, gelu_pull, active_low))


def rest_backward(grad_top, stored, attended, out_weight, up_weight, down_weight):
    normed_low, pullback, gelu_pull, active_low = stored
    grad_branch = grad_top.astype(jnp.bfloat16)
    down_grad = (active_low, grad_branch)
    down_bias_grad = column_sum(grad_branch)
    (pre_grad,) = gelu_pull(matmul_nt(grad_branch, down_weight))
    pre_low = pre_grad.astype(jnp.bfloat16)
    up_grad = (normed_low, pre_low)
    up_bias_grad = column_sum(pre_low)
    middle_grad, gain_b_grad, shift_b_grad = pullback(matmul_nt(pre_low, up_weight))
    middle_grad = middle_grad + grad_top
    attn_branch = middle_grad.astype(jnp.bfloat16)
    out_grad = (attended, attn_branch)
    out_bias_grad = column_sum(attn_branch)
    attended_grad = matmul_nt(attn_branch, out_weight).astype(jnp.bfloat16)
    return (
        middle_grad,
        attended_grad,
        (
            out_grad,
            out_bias_grad,
            gain_b_grad,
            shift_b_grad,
            up_grad,
            up_bias_grad,
            down_grad,
            down_bias_grad,
        ),
    )


def head_backward(
    middle_grad, normed_low, pullback, qkv_weight, query_grad, near_key_grad, near_value_grad
):
    grad_qkv = jnp.concatenate([query_grad, near_key_grad, near_value_grad], axis=1).astype(
        jnp.bfloat16
    )
    qkv_grad = (normed_low, grad_qkv)
    stream_grad, gain_a_grad, shift_a_grad = pullback(matmul_nt(grad_qkv, qkv_weight))
    return (middle_grad + stream_grad, (gain_a_grad, shift_a_grad, qkv_grad))


def bits_of(count):
    return count.bit_length() - 1


class Entry:
    def __init__(self, kind, lhs, rhs, r, n):
        self.kind, self.lhs, self.rhs, self.r, self.n = kind, lhs, rhs, r, n


def weight_grads(entries, width, shards, place, half, tiles, tile_rows):
    first, base, starts, bases = 0, 0, [], []
    for entry in entries:
        starts.append(first)
        bases.append(base)
        first += entry.n
        base += entry.n * entry.r
    steps, rows = first, base
    token_rows = entries[0].lhs.shape[0]
    tallest = max(shards * entry.r for entry in entries)

    def kernel(meta, *refs):
        out_ref, total = refs[-2], refs[-1]
        step = pl.program_id(0)
        spot, count = meta[0], meta[2]
        for index, entry in enumerate(entries):
            lhs_ref, rhs_ref = refs[2 * index], refs[2 * index + 1]
            start, offset, r, n = starts[index], bases[index], entry.r, entry.n
            height = shards * r

            @pl.when((step >= start) & (step < start + n))
            def _(lhs_ref=lhs_ref, rhs_ref=rhs_ref, start=start, offset=offset, r=r, n=n, height=height, kind=entry.kind):
                total[:height, :] = jnp.zeros((height, width), jnp.float32)

                def add(tile, carry):
                    at = pl.ds(pl.multiple_of(tile * tile_rows, tile_rows), tile_rows)
                    total[:height, :] += matmul_tn(lhs_ref[at, :], rhs_ref[at, :])
                    return carry

                lax.fori_loop(0, count, add, 0)
                unit = step - start
                if kind == "wide":
                    at = pl.ds(pl.multiple_of(offset + unit * r, 16), r)
                    for shard in range(shards):
                        piece = total[shard * r : (shard + 1) * r, :]
                        out_ref[lax.bitwise_xor(jnp.int32(shard), spot), at, :] = piece.astype(jnp.bfloat16)
                else:
                    each = shards // n
                    for inner in range(each):
                        piece = total[inner * n * r : (inner + 1) * n * r, :]
                        shard = lax.bitwise_xor(unit * each + inner, spot)
                        out_ref[shard, offset : offset + n * r, :] = piece.astype(jnp.bfloat16)

    in_specs, operands = [], []
    for index, entry in enumerate(entries):
        start, n, height = starts[index], entry.n, shards * entry.r

        def unit_of(step, start=start, n=n):
            return jnp.clip(step - start, 0, n - 1)

        if entry.kind == "wide":
            in_specs.append(pl.BlockSpec((token_rows, height), lambda step, meta: (0, 0)))
            in_specs.append(
                pl.BlockSpec((token_rows, width), lambda step, meta, n=n, unit_of=unit_of: (0, meta[1] * n + unit_of(step)))
            )
        else:
            in_specs.append(pl.BlockSpec((token_rows, height), lambda step, meta, unit_of=unit_of: (0, unit_of(step))))
            in_specs.append(pl.BlockSpec((token_rows, width), lambda step, meta: (0, meta[1])))
        operands += [entry.lhs, entry.rhs]
    flops = sum(2 * token_rows * shards * entry.r * width * entry.n for entry in entries)
    return pl.pallas_call(
        kernel,
        out_shape=jax.ShapeDtypeStruct((shards, rows, width), jnp.bfloat16),
        grid_spec=pltpu.PrefetchScalarGridSpec(
            num_scalar_prefetch=1,
            grid=(steps,),
            in_specs=in_specs,
            out_specs=pl.BlockSpec((shards, rows, width), lambda step, meta: (0, 0, 0)),
            scratch_shapes=[pltpu.VMEM((tallest, width), jnp.float32)],
        ),
        compiler_params=pltpu.CompilerParams(vmem_limit_bytes=VMEM_LIMIT),
        cost_estimate=pl.CostEstimate(flops=flops, bytes_accessed=flops // 500, transcendentals=0),
        name="weight_grads",
    )(jnp.stack([place, half, tiles]).astype(jnp.int32), *operands)


def across(value, axis, bit):
    count = lax.axis_size(axis)
    return lax.ppermute(value, axis, [(i, i ^ (1 << bit)) for i in range(count)])


def added(*terms):
    return sum(term.astype(jnp.float32) for term in terms).astype(jnp.bfloat16)


def sum_shards(kept, got, parts, orders):
    shards, rows, width = kept.shape
    bits = bits_of(shards)
    extra = range(bits, bits_of(lax.axis_size("dp")))
    results = []
    for (low, high), order in zip(parts, orders):
        terms = [value[:, low:high].reshape((2,) * bits + (high - low, width)) for value in (kept, got)]
        left = list(range(bits - 1, -1, -1))
        for bit in order:
            axis = left.index(bit)
            left.remove(bit)
            sent = added(*[lax.index_in_dim(term, 1, axis, keepdims=False) for term in terms])
            arrived = across(sent, "dp", bit)
            stay = added(*[lax.index_in_dim(term, 0, axis, keepdims=False) for term in terms])
            terms = [stay, arrived]
        own = added(*terms)
        for bit in extra:
            own = added(own, across(own, "dp", bit))
        own = own[None]
        for bit in reversed(order[1:]):
            own = jnp.concatenate([own, across(own, "dp", bit)], axis=0)
        results.append((own, across(own, "dp", order[0])))
    return results


def place_shards(entries, shapes, width, shards, place, half, parts, orders, results, others):
    bits = bits_of(shards)
    bases, base = [], 0
    for entry in entries:
        bases.append(base)
        base += entry.n * entry.r

    def kernel(meta, *refs):
        shard = pl.program_id(0)
        spot = lax.bitwise_xor(shard, meta[0])
        mine, other = [], []
        for index, order in enumerate(orders):
            upper = (lax.shift_right_logical(spot, order[0]) & 1) == 1
            mine.append((refs[4 * index], refs[4 * index + 1], upper))
            other.append((refs[4 * index + 2], refs[4 * index + 3], upper))
        outs = refs[4 * len(orders) :]

        def unit_value(source, row, r):
            for (low, high), (low_ref, high_ref, upper) in zip(parts, source):
                if low <= row and row + r <= high:
                    at = slice(row - low, row - low + r)
                    return jnp.where(upper, high_ref[0, at, :], low_ref[0, at, :]).astype(jnp.float32)

        for side in range(2):

            @pl.when(meta[1] == side)
            def _(side=side):
                for entry, offset, out_ref in zip(entries, bases, outs):
                    for unit in range(entry.n):
                        row = offset + unit * entry.r
                        for which, source in ((side, mine), (1 - side, other)):
                            value = unit_value(source, row, entry.r)
                            if entry.kind == "wide":
                                at = (which * entry.n + unit) * width
                                out_ref[:, at : at + width] = value
                            else:
                                out_ref[unit * entry.r : (unit + 1) * entry.r, which * width : (which + 1) * width] = value

    def spot_map(order):
        def index_map(shard, meta):
            spot = lax.bitwise_xor(shard, meta[0])
            at = jnp.int32(0)
            for bit in order[1:]:
                at = at * 2 + (lax.shift_right_logical(spot, bit) & 1)
            return (at, 0, 0)

        return index_map

    in_specs, operands = [], []
    for (low, high), order, result, other in zip(parts, orders, results, others):
        for value in (*result, *other):
            in_specs.append(pl.BlockSpec((1, high - low, width), spot_map(order)))
            operands.append(value)
    out_specs, out_shape = [], []
    for entry, shape in zip(entries, shapes):
        height = entry.r if entry.kind == "wide" else entry.n * entry.r
        out_specs.append(pl.BlockSpec((height, shape[1]), lambda shard, meta: (shard, 0)))
        out_shape.append(jax.ShapeDtypeStruct(shape, jnp.float32))
    return pl.pallas_call(
        kernel,
        out_shape=out_shape,
        grid_spec=pltpu.PrefetchScalarGridSpec(
            num_scalar_prefetch=1, grid=(shards,), in_specs=in_specs, out_specs=out_specs
        ),
        compiler_params=pltpu.CompilerParams(vmem_limit_bytes=VMEM_LIMIT),
        cost_estimate=pl.CostEstimate(
            flops=0, bytes_accessed=sum(8 * shape[0] * shape[1] for shape in shapes), transcendentals=0
        ),
        name="place_shards",
    )(jnp.stack([place, half]).astype(jnp.int32), *operands)


def rotated(shards, by):
    bits = bits_of(shards)
    return tuple((by + i) % bits for i in range(bits))


def split_rows(entries, count):
    edges, base = [0], 0
    for entry in entries:
        for _ in range(entry.n):
            base += entry.r
            edges.append(base)
    cuts = [min(edges, key=lambda edge: abs(edge - base * i / count)) for i in range(count + 1)]
    return list(zip(cuts[:-1], cuts[1:]))


def shard_count():
    return min(16, lax.axis_size("dp"))


def summed_grads(entries, shapes, width, tiles, tile_rows, part_count, first_bit):
    shards = shard_count()
    place = lax.axis_index("dp") & (shards - 1)
    half = lax.axis_index("blk")
    sent = weight_grads(entries, width, shards, place, 1 - half, tiles, tile_rows)
    got = across(sent, "blk", 0)
    kept = weight_grads(entries, width, shards, place, half, tiles, tile_rows)
    parts = split_rows(entries, part_count)
    orders = [rotated(shards, first_bit + i) for i in range(part_count)]
    results = sum_shards(kept, got, parts, orders)
    others = [tuple(across(value, "blk", 0) for value in result) for result in results]
    return place_shards(entries, shapes, width, shards, place, half, parts, orders, results, others)


def sum_small(values):
    flat = jnp.concatenate([value.reshape(-1) for value in values])
    flat = lax.psum(flat, ("dp", "blk"))
    results, offset = [], 0
    for value in values:
        results.append(flat[offset : offset + value.size].reshape(value.shape))
        offset += value.size
    return results


def local(
    patches,
    visible,
    padding,
    field_ids,
    enc_gain_a,
    enc_shift_a,
    enc_qkv,
    enc_out,
    enc_out_bias,
    enc_gain_b,
    enc_shift_b,
    enc_up,
    enc_up_bias,
    enc_down,
    enc_down_bias,
    embed_map,
    embed_bias,
    mask_token,
    dec_gain_a,
    dec_shift_a,
    dec_qkv,
    dec_out,
    dec_out_bias,
    dec_gain_b,
    dec_shift_b,
    dec_up,
    dec_up_bias,
    dec_down,
    dec_down_bias,
    cotangent,
):
    row_count = patches.shape[0]
    seen_rows = visible > 0
    padded_rows = padding > 0
    label_value = field_ids.astype(jnp.float32)
    enc_code = jnp.where(seen_rows & ~padded_rows, label_value, -1.0).astype(jnp.bfloat16)
    dec_code = jnp.where(padded_rows, -1.0, label_value).astype(jnp.bfloat16)
    stream = patches.astype(jnp.float32)
    enc_normed, enc_pull, enc_query, enc_key, enc_value = attention_inputs(
        stream, enc_gain_a, enc_shift_a, enc_qkv
    )
    far_key, far_value, far_enc, far_dec = passed_along(
        (enc_key, enc_value, enc_code, dec_code), "blk", 1
    )
    enc_allowed = allowed_keys(label_value, enc_code, far_enc)
    enc_key_all = jnp.concatenate([enc_key, far_key], axis=0)
    enc_value_all = jnp.concatenate([enc_value, far_value], axis=0)
    enc_attended, enc_totals = attend_forward(
        enc_query, enc_key_all, enc_value_all, enc_allowed, HE
    )
    encoded, enc_stored = block_rest(
        stream,
        enc_attended,
        enc_out,
        enc_out_bias,
        enc_gain_b,
        enc_shift_b,
        enc_up,
        enc_up_bias,
        enc_down,
        enc_down_bias,
    )
    encoded_low = encoded.astype(jnp.bfloat16)
    lifted = matmul(encoded_low, embed_map) + embed_bias.astype(jnp.float32)
    start = jnp.where(seen_rows[:, None], lifted, mask_token.astype(jnp.float32)[None, :])
    dec_normed, dec_pull, dec_query, dec_key, dec_value = attention_inputs(
        start, dec_gain_a, dec_shift_a, dec_qkv
    )
    far_dec_key, far_dec_value = passed_along((dec_key, dec_value), "blk", 1)
    dec_allowed = allowed_keys(label_value, dec_code, far_dec)
    dec_key_all = jnp.concatenate([dec_key, far_dec_key], axis=0)
    dec_value_all = jnp.concatenate([dec_value, far_dec_value], axis=0)
    dec_attended, dec_totals = attend_forward(
        dec_query, dec_key_all, dec_value_all, dec_allowed, HD
    )
    decoded, dec_stored = block_rest(
        start,
        dec_attended,
        dec_out,
        dec_out_bias,
        dec_gain_b,
        dec_shift_b,
        dec_up,
        dec_up_bias,
        dec_down,
        dec_down_bias,
    )
    dec_middle_grad, dec_attended_grad, dec_rest_grads = rest_backward(
        cotangent.astype(jnp.float32), dec_stored, dec_attended, dec_out, dec_up, dec_down
    )
    dec_query_grad, dec_key_grad, dec_value_grad = attend_backward(
        dec_query, dec_key_all, dec_value_all, dec_allowed, dec_totals, dec_attended_grad, HD
    )
    back_dec_key, back_dec_value = (
        passed_along(dec_key_grad[row_count:].astype(jnp.bfloat16), "blk", 1).astype(jnp.float32),
        passed_along(dec_value_grad[row_count:].astype(jnp.bfloat16), "blk", 1).astype(jnp.float32),
    )
    start_grad, dec_head_grads = head_backward(
        dec_middle_grad,
        dec_normed,
        dec_pull,
        dec_qkv,
        dec_query_grad,
        dec_key_grad[:row_count] + back_dec_key,
        dec_value_grad[:row_count] + back_dec_value,
    )
    mask_grad = jnp.sum(jnp.where(seen_rows[:, None], 0.0, start_grad), axis=0)
    lift_low = jnp.where(seen_rows[:, None], start_grad, 0.0).astype(jnp.bfloat16)
    embed_pair, embed_bias_grad = (encoded_low, lift_low), column_sum(lift_low)
    encoded_grad = matmul_nt(lift_low, embed_map)
    enc_middle_grad, enc_attended_grad, enc_rest_grads = rest_backward(
        encoded_grad, enc_stored, enc_attended, enc_out, enc_up, enc_down
    )
    enc_query_grad, enc_key_grad, enc_value_grad = attend_backward(
        enc_query, enc_key_all, enc_value_all, enc_allowed, enc_totals, enc_attended_grad, HE
    )
    back_enc_key, back_enc_value = (
        passed_along(enc_key_grad[row_count:].astype(jnp.bfloat16), "blk", 1).astype(jnp.float32),
        passed_along(enc_value_grad[row_count:].astype(jnp.bfloat16), "blk", 1).astype(jnp.float32),
    )
    patches_grad, enc_head_grads = head_backward(
        enc_middle_grad,
        enc_normed,
        enc_pull,
        enc_qkv,
        enc_query_grad,
        enc_key_grad[:row_count] + back_enc_key,
        enc_value_grad[:row_count] + back_enc_value,
    )
    shards = shard_count()
    de, dd = enc_qkv.shape[0], dec_qkv.shape[0]
    tiles = jnp.int32(row_count // TILE)
    d_out, d_out_b, d_gain_b, d_shift_b, d_up, d_up_b, d_down, d_down_b = dec_rest_grads
    d_gain_a, d_shift_a, d_qkv = dec_head_grads
    e_out, e_out_b, e_gain_b, e_shift_b, e_up, e_up_b, e_down, e_down_b = enc_rest_grads
    e_gain_a, e_shift_a, e_qkv = enc_head_grads
    rd, re = dd // shards, de // shards
    first = [Entry("wide", *d_up, rd, 4), Entry("tall", *d_down, rd, 4), Entry("wide", *d_out, rd, 1)]
    g_dec_up, g_dec_down, g_dec_out = summed_grads(
        first, (dec_up.shape, dec_down.shape, dec_out.shape), dd // 2, tiles, TILE, 2, 0
    )
    second = [Entry("wide", *d_qkv, rd, 3), Entry("wide", *embed_pair, re, 1)]
    g_dec_qkv, g_embed = summed_grads(second, (dec_qkv.shape, embed_map.shape), dd // 2, tiles, TILE, 1, 0)
    third = [Entry("wide", *e_up, re, 4), Entry("tall", *e_down, re, 4), Entry("wide", *e_out, re, 1)]
    g_enc_up, g_enc_down, g_enc_out = summed_grads(
        third, (enc_up.shape, enc_down.shape, enc_out.shape), de // 2, tiles, TILE, 3, 0
    )
    fourth = [Entry("wide", *e_qkv, re, 3)]
    (g_enc_qkv,) = summed_grads(fourth, (enc_qkv.shape,), de // 2, tiles, TILE, 3, 0)
    small = sum_small(
        [e_gain_a, e_shift_a, e_out_b, e_gain_b, e_shift_b, e_up_b, e_down_b, embed_bias_grad, mask_grad]
        + [d_gain_a, d_shift_a, d_out_b, d_gain_b, d_shift_b, d_up_b, d_down_b]
    )
    return (
        (decoded.astype(jnp.bfloat16), patches_grad.astype(jnp.bfloat16))
        + (small[0], small[1], g_enc_qkv, g_enc_out, small[2], small[3], small[4])
        + (g_enc_up, small[5], g_enc_down, small[6], g_embed, small[7], small[8])
        + (small[9], small[10], g_dec_qkv, g_dec_out, small[11], small[12], small[13])
        + (g_dec_up, small[14], g_dec_down, small[15])
    )


def solution(mesh):
    return jax.shard_map(
        local,
        mesh=mesh,
        in_specs=(
            P(("dp", "blk"), None),
            P(("dp", "blk")),
            P(("dp", "blk")),
            P(("dp", "blk")),
            P(),
            P(),
            P(),
            P(),
            P(),
            P(),
            P(),
            P(),
            P(),
            P(),
            P(),
            P(),
            P(),
            P(),
            P(),
            P(),
            P(),
            P(),
            P(),
            P(),
            P(),
            P(),
            P(),
            P(),
            P(),
            P(("dp", "blk"), None),
        ),
        out_specs=(
            P(("dp", "blk"), None),
            P(("dp", "blk"), None),
            P(),
            P(),
            P(),
            P(),
            P(),
            P(),
            P(),
            P(),
            P(),
            P(),
            P(),
            P(),
            P(),
            P(),
            P(),
            P(),
            P(),
            P(),
            P(),
            P(),
            P(),
            P(),
            P(),
            P(),
            P(),
        ),
        check_vma=False,
    )
```

```python
import math

import jax
import jax.numpy as jnp
from jax import lax
from jax.experimental import pallas as pl
from jax.experimental.pallas import tpu as pltpu
from jax.sharding import PartitionSpec as P

HE = 12
HD = 16
TILE = 256
VMEM_LIMIT = 60 * 1024 * 1024


epsilon = 1e-06


def matmul(left_side, right_side):
    return jnp.dot(left_side, right_side, preferred_element_type=jnp.float32)


def matmul_tn(left_side, right_side):
    return lax.dot_general(
        left_side, right_side, (((0,), (0,)), ((), ())), preferred_element_type=jnp.float32
    )


def matmul_nt(left_side, right_side):
    return lax.dot_general(
        left_side, right_side, (((1,), (1,)), ((), ())), preferred_element_type=jnp.float32
    )


def bits_of(count):
    return count.bit_length() - 1


class Entry:
    def __init__(self, kind, lhs, rhs, r, n):
        self.kind, self.lhs, self.rhs, self.r, self.n = kind, lhs, rhs, r, n


def weight_grads(entries, width, shards, place, half, tiles, tile_rows):
    first, base, starts, bases = 0, 0, [], []
    for entry in entries:
        starts.append(first)
        bases.append(base)
        first += entry.n
        base += entry.n * entry.r
    steps, rows = first, base
    token_rows = entries[0].lhs.shape[0]
    tallest = max(shards * entry.r for entry in entries)

    def kernel(meta, *refs):
        out_ref, total = refs[-2], refs[-1]
        step = pl.program_id(0)
        spot, count = meta[0], meta[2]
        for index, entry in enumerate(entries):
            lhs_ref, rhs_ref = refs[2 * index], refs[2 * index + 1]
            start, offset, r, n = starts[index], bases[index], entry.r, entry.n
            height = shards * r

            @pl.when((step >= start) & (step < start + n))
            def _(lhs_ref=lhs_ref, rhs_ref=rhs_ref, start=start, offset=offset, r=r, n=n, height=height, kind=entry.kind):
                total[:height, :] = jnp.zeros((height, width), jnp.float32)

                def add(tile, carry):
                    at = pl.ds(pl.multiple_of(tile * tile_rows, tile_rows), tile_rows)
                    total[:height, :] += matmul_tn(lhs_ref[at, :], rhs_ref[at, :])
                    return carry

                lax.fori_loop(0, count, add, 0)
                unit = step - start
                if kind == "wide":
                    at = pl.ds(pl.multiple_of(offset + unit * r, 16), r)
                    for shard in range(shards):
                        piece = total[shard * r : (shard + 1) * r, :]
                        out_ref[lax.bitwise_xor(jnp.int32(shard), spot), at, :] = piece.astype(jnp.bfloat16)
                else:
                    each = shards // n
                    for inner in range(each):
                        piece = total[inner * n * r : (inner + 1) * n * r, :]
                        shard = lax.bitwise_xor(unit * each + inner, spot)
                        out_ref[shard, offset : offset + n * r, :] = piece.astype(jnp.bfloat16)

    in_specs, operands = [], []
    for index, entry in enumerate(entries):
        start, n, height = starts[index], entry.n, shards * entry.r

        def unit_of(step, start=start, n=n):
            return jnp.clip(step - start, 0, n - 1)

        if entry.kind == "wide":
            in_specs.append(pl.BlockSpec((token_rows, height), lambda step, meta: (0, 0)))
            in_specs.append(
                pl.BlockSpec((token_rows, width), lambda step, meta, n=n, unit_of=unit_of: (0, meta[1] * n + unit_of(step)))
            )
        else:
            in_specs.append(pl.BlockSpec((token_rows, height), lambda step, meta, unit_of=unit_of: (0, unit_of(step))))
            in_specs.append(pl.BlockSpec((token_rows, width), lambda step, meta: (0, meta[1])))
        operands += [entry.lhs, entry.rhs]
    flops = sum(2 * token_rows * shards * entry.r * width * entry.n for entry in entries)
    return pl.pallas_call(
        kernel,
        out_shape=jax.ShapeDtypeStruct((shards, rows, width), jnp.bfloat16),
        grid_spec=pltpu.PrefetchScalarGridSpec(
            num_scalar_prefetch=1,
            grid=(steps,),
            in_specs=in_specs,
            out_specs=pl.BlockSpec((shards, rows, width), lambda step, meta: (0, 0, 0)),
            scratch_shapes=[pltpu.VMEM((tallest, width), jnp.float32)],
        ),
        compiler_params=pltpu.CompilerParams(vmem_limit_bytes=VMEM_LIMIT),
        cost_estimate=pl.CostEstimate(flops=flops, bytes_accessed=flops // 500, transcendentals=0),
        name="weight_grads",
    )(jnp.stack([place, half, tiles]).astype(jnp.int32), *operands)


def across(value, axis, bit):
    count = lax.axis_size(axis)
    return lax.ppermute(value, axis, [(i, i ^ (1 << bit)) for i in range(count)])


def added(*terms):
    return sum(term.astype(jnp.float32) for term in terms).astype(jnp.bfloat16)


def sum_shards(kept, got, parts, orders):
    shards, rows, width = kept.shape
    bits = bits_of(shards)
    extra = range(bits, bits_of(lax.axis_size("dp")))
    results = []
    for (low, high), order in zip(parts, orders):
        terms = [value[:, low:high].reshape((2,) * bits + (high - low, width)) for value in (kept, got)]
        left = list(range(bits - 1, -1, -1))
        for bit in order:
            axis = left.index(bit)
            left.remove(bit)
            sent = added(*[lax.index_in_dim(term, 1, axis, keepdims=False) for term in terms])
            arrived = across(sent, "dp", bit)
            stay = added(*[lax.index_in_dim(term, 0, axis, keepdims=False) for term in terms])
            terms = [stay, arrived]
        own = added(*terms)
        for bit in extra:
            own = added(own, across(own, "dp", bit))
        own = own[None]
        for bit in reversed(order[1:]):
            own = jnp.concatenate([own, across(own, "dp", bit)], axis=0)
        results.append((own, across(own, "dp", order[0])))
    return results


def place_shards(entries, shapes, width, shards, place, half, parts, orders, results, others):
    bits = bits_of(shards)
    bases, base = [], 0
    for entry in entries:
        bases.append(base)
        base += entry.n * entry.r

    def kernel(meta, *refs):
        shard = pl.program_id(0)
        spot = lax.bitwise_xor(shard, meta[0])
        mine, other = [], []
        for index, order in enumerate(orders):
            upper = (lax.shift_right_logical(spot, order[0]) & 1) == 1
            mine.append((refs[4 * index], refs[4 * index + 1], upper))
            other.append((refs[4 * index + 2], refs[4 * index + 3], upper))
        outs = refs[4 * len(orders) :]

        def unit_value(source, row, r):
            for (low, high), (low_ref, high_ref, upper) in zip(parts, source):
                if low <= row and row + r <= high:
                    at = slice(row - low, row - low + r)
                    return jnp.where(upper, high_ref[0, at, :], low_ref[0, at, :]).astype(jnp.float32)

        for side in range(2):

            @pl.when(meta[1] == side)
            def _(side=side):
                for entry, offset, out_ref in zip(entries, bases, outs):
                    for unit in range(entry.n):
                        row = offset + unit * entry.r
                        for which, source in ((side, mine), (1 - side, other)):
                            value = unit_value(source, row, entry.r)
                            if entry.kind == "wide":
                                at = (which * entry.n + unit) * width
                                out_ref[:, at : at + width] = value
                            else:
                                out_ref[unit * entry.r : (unit + 1) * entry.r, which * width : (which + 1) * width] = value

    def spot_map(order):
        def index_map(shard, meta):
            spot = lax.bitwise_xor(shard, meta[0])
            at = jnp.int32(0)
            for bit in order[1:]:
                at = at * 2 + (lax.shift_right_logical(spot, bit) & 1)
            return (at, 0, 0)

        return index_map

    in_specs, operands = [], []
    for (low, high), order, result, other in zip(parts, orders, results, others):
        for value in (*result, *other):
            in_specs.append(pl.BlockSpec((1, high - low, width), spot_map(order)))
            operands.append(value)
    out_specs, out_shape = [], []
    for entry, shape in zip(entries, shapes):
        height = entry.r if entry.kind == "wide" else entry.n * entry.r
        out_specs.append(pl.BlockSpec((height, shape[1]), lambda shard, meta: (shard, 0)))
        out_shape.append(jax.ShapeDtypeStruct(shape, jnp.float32))
    return pl.pallas_call(
        kernel,
        out_shape=out_shape,
        grid_spec=pltpu.PrefetchScalarGridSpec(
            num_scalar_prefetch=1, grid=(shards,), in_specs=in_specs, out_specs=out_specs
        ),
        compiler_params=pltpu.CompilerParams(vmem_limit_bytes=VMEM_LIMIT),
        cost_estimate=pl.CostEstimate(
            flops=0, bytes_accessed=sum(8 * shape[0] * shape[1] for shape in shapes), transcendentals=0
        ),
        name="place_shards",
    )(jnp.stack([place, half]).astype(jnp.int32), *operands)


def rotated(shards, by):
    bits = bits_of(shards)
    return tuple((by + i) % bits for i in range(bits))


def split_rows(entries, count):
    edges, base = [0], 0
    for entry in entries:
        for _ in range(entry.n):
            base += entry.r
            edges.append(base)
    cuts = [min(edges, key=lambda edge: abs(edge - base * i / count)) for i in range(count + 1)]
    return list(zip(cuts[:-1], cuts[1:]))


def shard_count():
    return min(16, lax.axis_size("dp"))


def summed_grads(entries, shapes, width, tiles, tile_rows, part_count, first_bit):
    shards = shard_count()
    place = lax.axis_index("dp") & (shards - 1)
    half = lax.axis_index("blk")
    sent = weight_grads(entries, width, shards, place, 1 - half, tiles, tile_rows)
    got = across(sent, "blk", 0)
    kept = weight_grads(entries, width, shards, place, half, tiles, tile_rows)
    parts = split_rows(entries, part_count)
    orders = [rotated(shards, first_bit + i) for i in range(part_count)]
    results = sum_shards(kept, got, parts, orders)
    others = [tuple(across(value, "blk", 0) for value in result) for result in results]
    return place_shards(entries, shapes, width, shards, place, half, parts, orders, results, others)


LOG2E = math.log2(math.e)
NEVER = -1e30
LANES = 128
BF16, F32 = jnp.bfloat16, jnp.float32


def colsum(value):
    return jnp.sum(value.astype(F32), axis=0, keepdims=True)


def normed_rows(stream):
    centred = stream - jnp.mean(stream, axis=-1, keepdims=True)
    inverse = lax.rsqrt(jnp.mean(centred * centred, axis=-1, keepdims=True) + epsilon)
    return centred * inverse, inverse


def norm_back(grad, unit, inverse, gain):
    grad = grad * gain
    inner = jnp.mean(grad * unit, axis=-1, keepdims=True)
    return inverse * (grad - jnp.mean(grad, axis=-1, keepdims=True) - unit * inner)


def gelu_pair(u):
    bell = jnp.exp2(u * u * (-0.5 * LOG2E))
    t = 1.0 / (1.0 + (0.3275911 * math.sqrt(0.5)) * jnp.abs(u))
    poly = ((((1.061405429 * t - 1.453152027) * t + 1.421413741) * t - 0.284496736) * t + 0.254829592) * t
    tail = 0.5 * poly * bell
    phi = jnp.where(u < 0, tail, 1.0 - tail)
    return u * phi, phi + u * bell * (1.0 / math.sqrt(2.0 * math.pi))


def iota(shape, axis):
    return lax.broadcasted_iota(jnp.int32, shape, axis)


def fill_groups(target, source):
    for group in range(target.shape[0]):
        target[group] = source[:, group * LANES : (group + 1) * LANES].astype(target.dtype)


def attend_forward(keys, head, q_s, k_s, v_s, mask_ref, o_s, probs=None, inverse_s=None, totals=None):
    groups, rows, _ = q_s.shape
    inside = LANES // head
    factor = head ** (-0.5) * LOG2E
    lanes = iota((rows, LANES), 1)
    which = lax.div(lanes, jnp.int32(head))
    if totals is not None:
        totals[...] = jnp.zeros_like(totals)

    def one_group(group, carry):
        queries = q_s[group]
        key_rows = k_s[group, :keys, :]
        values = v_s[group, :keys, :]
        blended = jnp.zeros((rows, LANES), F32)
        inverses = jnp.zeros((rows, LANES), F32)
        for h in range(inside):
            own = which == h
            query = jnp.where(own, queries, 0.0).astype(BF16)
            scores = matmul_nt(query, key_rows) * factor + mask_ref[:, :keys]
            top = jnp.max(scores, axis=1, keepdims=True)
            prob = jnp.exp2(scores - top).astype(BF16)
            if probs is not None:
                probs[group * inside + h, :, :keys] = prob
            both = matmul(prob, values)
            inverse = 1.0 / both[:, LANES:]
            blended = jnp.where(own, both[:, :LANES] * inverse, blended)
            if inverse_s is not None:
                inverses = jnp.where(own, inverse, inverses)
            if totals is not None:
                at = lanes == group * inside + h
                totals[...] = jnp.where(at, top + jnp.log2(both[:, LANES:]), totals[...])
        o_s[group] = blended
        if inverse_s is not None:
            inverse_s[group] = inverses
        return carry

    lax.fori_loop(0, groups, one_group, 0)


def attend_backward(keys, head, q_s, k_s, v_s, o_s, ob_s, dq_s, dk_s, dv_s, probs=None, mask_ref=None, totals=None):
    groups, rows, _ = q_s.shape
    inside = LANES // head
    factor = head ** (-0.5) * LOG2E
    lanes = iota((rows, LANES), 1)
    which = lax.div(lanes, jnp.int32(head))

    def one_group(group, carry):
        queries, grads = q_s[group], ob_s[group]
        key_rows = k_s[group, :keys, :]
        values = v_s[group, :keys, :LANES]
        product = grads * o_s[group]
        queries_t = queries.T.astype(BF16)
        grads_t = grads.T.astype(BF16)
        query_grad = jnp.zeros((rows, LANES), F32)
        for h in range(inside):
            own = which == h
            at = slice(h * head, (h + 1) * head)
            inner = jnp.sum(jnp.where(own, product, 0.0), axis=1, keepdims=True)
            if probs is not None:
                prob = probs[group * inside + h, :, :keys]
            else:
                query = jnp.where(own, queries, 0.0).astype(BF16)
                total = jnp.sum(jnp.where(lanes == group * inside + h, totals, 0.0), axis=1, keepdims=True)
                prob = jnp.exp2(matmul_nt(query, key_rows) * factor + (mask_ref[:, :keys] - total)).astype(BF16)
            grad_probs = matmul_nt(jnp.where(own, grads, 0.0).astype(BF16), values)
            score_grad = (prob.astype(F32) * (grad_probs - inner)).astype(BF16)
            query_grad = jnp.where(own, matmul(score_grad, key_rows), query_grad)
            dk_s[group, at, :keys] += matmul(queries_t[at], score_grad)
            dv_s[group, at, :keys] += matmul(grads_t[at], prob)
        dq_s[group] = query_grad
        return carry

    lax.fori_loop(0, groups, one_group, 0)


def whole(shape):
    rank = len(shape)
    return pl.BlockSpec(shape, lambda step, meta: (0,) * rank, pipeline_mode=pl.Buffered(1))


def out_whole(shape):
    rank = len(shape)
    return pl.BlockSpec(shape, lambda step, meta: (0,) * rank)


def row_tile(width):
    return pl.BlockSpec((TILE, width), lambda step, meta: (step, 0))


def live_tile(width):
    return pl.BlockSpec((TILE, width), lambda step, meta: (jnp.minimum(step, meta[0] - 1), 0))


def call(kernel, name, meta, in_specs, operands, out_specs, out_shape, scratch, flops, steps):
    return pl.pallas_call(
        kernel,
        out_shape=out_shape,
        grid_spec=pltpu.PrefetchScalarGridSpec(
            num_scalar_prefetch=1, grid=(steps,), in_specs=in_specs, out_specs=out_specs, scratch_shapes=scratch
        ),
        compiler_params=pltpu.CompilerParams(vmem_limit_bytes=VMEM_LIMIT),
        cost_estimate=pl.CostEstimate(flops=flops, bytes_accessed=flops // 500, transcendentals=0),
        name=name,
    )(meta, *operands)


def shaped(rows, width, dtype):
    return jax.ShapeDtypeStruct((rows, width), dtype)


def enc_in(meta, patches, marks, far_marks, params, qkv):
    rows, width = patches.shape
    tall = marks.shape[0]

    def picked(marks_ref, step):
        below = (iota((rows, rows), 0) <= iota((rows, rows), 1)).astype(F32).astype(BF16)
        place = matmul(marks_ref[...].astype(BF16), below)[2:3, :].astype(jnp.int32) - 1
        target = step * TILE + iota((TILE, rows), 0)
        hit = (target == place) & (marks_ref[2:3, :] > 0)
        return jnp.where(hit, 1.0, 0.0).astype(BF16)

    def kernel(meta, patches_ref, marks_ref, far_ref, params_ref, qkv_ref, sel_ref, code_ref, far_code_ref, label_ref, s_ref, n_ref, q_ref, kv_ref):
        step = pl.program_id(0)
        sel = picked(marks_ref, step)
        sel_ref[...] = sel
        own_marks = marks_ref[...].astype(BF16)
        code_ref[...] = matmul_nt(own_marks, sel)
        far_code_ref[...] = matmul_nt(far_ref[...].astype(BF16), picked(far_ref, step))
        label_ref[...] = matmul_nt(sel, own_marks)

        @pl.when(step < meta[0])
        def _():
            stream = matmul(sel, patches_ref[...])
            s_ref[...] = stream.astype(BF16)
            unit, _ = normed_rows(stream)
            normed = (unit * params_ref[:, :width] + params_ref[:, width : 2 * width]).astype(BF16)
            n_ref[...] = normed
            q_ref[...] = matmul(normed, qkv_ref[:, :width]).astype(BF16)
            kv_ref[...] = matmul(normed, qkv_ref[:, width:]).astype(BF16)

    lane_tile = pl.BlockSpec((tall, TILE), lambda step, meta: (0, step))
    return call(
        kernel,
        "enc_in",
        meta,
        [whole(value.shape) for value in (patches, marks, far_marks, params, qkv)],
        (patches, marks, far_marks, params, qkv),
        [row_tile(rows), lane_tile, lane_tile, row_tile(tall)] + [live_tile(w) for w in (width, width, width, 2 * width)],
        [shaped(rows, rows, BF16), shaped(tall, rows, F32), shaped(tall, rows, F32), shaped(rows, tall, F32)]
        + [shaped(rows, w, BF16) for w in (width, width, width, 2 * width)],
        [],
        2 * TILE * width * (3 * width + rows),
        rows // TILE,
    )


def spread_keys(count, tiles, kv_ref, far_ref, far_tiles, k_s, v_s):
    size = count * TILE
    width = kv_ref.shape[1] // 2
    for source, live, base in ((kv_ref, tiles, 0), (far_ref, far_tiles, size)):
        ok = iota((size, LANES), 0) < live * TILE
        for group in range(width // LANES):
            at = slice(group * LANES, (group + 1) * LANES)
            value_at = slice(width + group * LANES, width + (group + 1) * LANES)
            k_s[group, base : base + size, :] = jnp.where(ok, source[:size, at].astype(F32), 0.0).astype(BF16)
            v_s[group, base : base + size, :LANES] = jnp.where(ok, source[:size, value_at].astype(F32), 0.0).astype(BF16)
            if v_s.shape[2] > LANES:
                v_s[group, base : base + size, LANES:] = jnp.ones((size, v_s.shape[2] - LANES), BF16)


def write_mask(mask_ref, label, code, far_code, size, step):
    shape = (label.shape[0], size)
    near = (label == code) | (iota(shape, 1) == step * TILE + iota(shape, 0))
    mask_ref[:, :size] = jnp.where(near, 0.0, NEVER)
    mask_ref[:, size : 2 * size] = jnp.where(label == far_code, 0.0, NEVER)


def enc_main(meta, s, q, kv, far_kv, label, code, far_code, params, out, up, down, embed, heads):
    rows, width = s.shape
    wide, lifted_width = up.shape[1], embed.shape[1]
    groups, head, most = width // LANES, width // heads, rows // TILE
    part = width

    def kernel(meta, s_ref, q_ref, kv_ref, far_ref, label_ref, code_ref, far_code_ref, params_ref, out_w, up_w, down_w, embed_w,
               o_ref, tot_ref, m_ref, n_ref, g_ref, gp_ref, e_ref, hi_ref, lo_ref, q_s, k_s, v_s, mask_s, o_s):
        step = pl.program_id(0)
        tiles, far_tiles = meta[0], meta[1]
        count = jnp.maximum(tiles, far_tiles)

        def param(start, size):
            return params_ref[:, start : start + size]

        @pl.when(step < tiles)
        def _():
            fill_groups(q_s, q_ref)
            for size in range(1, most + 1):

                @pl.when(count == size)
                def _(size=size):
                    @pl.when(step == 0)
                    def _():
                        spread_keys(size, tiles, kv_ref, far_ref, far_tiles, k_s, v_s)

                    span = size * TILE
                    write_mask(mask_s, label_ref[:, 1:2], code_ref[0:1, :span], far_code_ref[0:1, :span], span, step)
                    attend_forward(2 * span, head, q_s, k_s, v_s, mask_s, o_s, totals=tot_ref)

            for group in range(groups):
                o_ref[:, group * LANES : (group + 1) * LANES] = o_s[group].astype(BF16)
            middle = s_ref[...].astype(F32) + matmul(o_ref[...], out_w[...]) + param(2 * width, width)
            m_ref[...] = middle
            unit, _ = normed_rows(middle)
            normed = (unit * param(3 * width, width) + param(4 * width, width)).astype(BF16)
            n_ref[...] = normed
            encoded = middle + param(5 * width + wide, width)
            for j in range(0, wide, part):
                u = matmul(normed, up_w[:, j : j + part]) + param(5 * width + j, part)
                g, slope = gelu_pair(u)
                g = g.astype(BF16)
                g_ref[:, j : j + part] = g
                gp_ref[:, j : j + part] = slope.astype(BF16)
                encoded = encoded + matmul(g, down_w[j : j + part, :])
            low = encoded.astype(BF16)
            e_ref[...] = low
            lifted = matmul(low, embed_w[...]) + param(6 * width + wide, lifted_width)
            high = lifted.astype(BF16)
            hi_ref[...] = high
            lo_ref[...] = (lifted - high.astype(F32)).astype(BF16)

    tall = label.shape[1]
    return call(
        kernel,
        "enc_main",
        meta,
        [live_tile(width), live_tile(width), whole(kv.shape), whole(kv.shape), live_tile(tall), whole(code.shape), whole(code.shape)]
        + [whole(value.shape) for value in (params, out, up, down, embed)],
        (s, q, kv, far_kv, label, code, far_code, params, out, up, down, embed),
        [live_tile(w) for w in (width, LANES, width, width, wide, wide, width, lifted_width, lifted_width)],
        [shaped(rows, width, BF16), shaped(rows, LANES, F32), shaped(rows, width, F32), shaped(rows, width, BF16)]
        + [shaped(rows, wide, BF16)] * 2 + [shaped(rows, width, BF16)] + [shaped(rows, lifted_width, BF16)] * 2,
        [
            pltpu.VMEM((groups, TILE, LANES), F32),
            pltpu.VMEM((groups, 2 * rows, LANES), BF16),
            pltpu.VMEM((groups, 2 * rows, 2 * LANES), BF16),
            pltpu.VMEM((TILE, 2 * rows), F32),
            pltpu.VMEM((groups, TILE, LANES), F32),
        ],
        2 * TILE * width * (2 * wide + 2 * width),
        most,
    )


def dec_in(meta, sel, high, low, columns, params, mask_token, qkv):
    rows, width = high.shape
    tall = columns.shape[1]

    def kernel(meta, sel_ref, hi_ref, lo_ref, col_ref, params_ref, token_ref, qkv_ref, start_ref, n_ref, q_ref, kv_ref, total):
        total[...] = jnp.zeros_like(total)

        def add(tile, carry):
            at = pl.ds(pl.multiple_of(tile * TILE, TILE), TILE)
            total[...] += matmul_tn(sel_ref[at, :], hi_ref[at, :]) + matmul_tn(sel_ref[at, :], lo_ref[at, :])
            return carry

        lax.fori_loop(0, meta[0], add, 0)
        start = jnp.where(col_ref[:, 2:3] > 0, total[...], token_ref[...])
        start_ref[...] = start
        unit, _ = normed_rows(start)
        normed = (unit * params_ref[:, :width] + params_ref[:, width : 2 * width]).astype(BF16)
        n_ref[...] = normed
        q_ref[...] = matmul(normed, qkv_ref[:, :width]).astype(BF16)
        kv_ref[...] = matmul(normed, qkv_ref[:, width:]).astype(BF16)

    return call(
        kernel,
        "dec_in",
        meta,
        [pl.BlockSpec((rows, TILE), lambda step, meta: (0, step)), whole(high.shape), whole(low.shape), row_tile(tall)]
        + [whole(value.shape) for value in (params, mask_token, qkv)],
        (sel, high, low, columns, params, mask_token, qkv),
        [row_tile(w) for w in (width, width, width, 2 * width)],
        [shaped(rows, width, F32)] + [shaped(rows, w, BF16) for w in (width, width, 2 * width)],
        [pltpu.VMEM((TILE, width), F32)],
        2 * rows * width * 3 * width,
        rows // TILE,
    )


def give_key_grads(size, scale, dk_s, dv_s, near_ref, far_ref):
    groups = dk_s.shape[0]
    for index, (source, factor) in enumerate(((dk_s, scale), (dv_s, 1.0))):
        for group in range(groups):
            at = slice((index * groups + group) * LANES, (index * groups + group + 1) * LANES)
            near_ref[:size, at] = source[group, :, :size].T * factor
            far_ref[:size, at] = (source[group, :, size : 2 * size].T * factor).astype(BF16)


def dec_main(meta, start, q, kv, far_kv, columns, marks, far_marks, cotangent, params, out, up, down, heads):
    rows, width = start.shape
    wide = up.shape[1]
    groups, head, steps = width // LANES, width // heads, rows // TILE
    part = width
    tall = columns.shape[1]

    def kernel(meta, start_ref, q_ref, kv_ref, far_ref, col_ref, marks_ref, far_marks_ref, cot_ref, params_ref, out_w, up_w, down_w,
               dec_ref, o_ref, n_ref, g_ref, ub_ref, mb_ref, tm_ref, dq_ref, near_ref, back_ref,
               outb_ref, gainb_ref, shiftb_ref, upb_ref, downb_ref,
               q_s, k_s, v_s, mask_s, probs, o_s, inv_s, ob_s, dq_s, dk_s, dv_s, slope_s):
        step = pl.program_id(0)

        def param(begin, size):
            return params_ref[:, begin : begin + size]

        @pl.when(step == 0)
        def _():
            spread_keys(steps, steps, kv_ref, far_ref, steps, k_s, v_s)
            for ref in (dk_s, dv_s, outb_ref, gainb_ref, shiftb_ref, upb_ref, downb_ref):
                ref[...] = jnp.zeros_like(ref)

        fill_groups(q_s, q_ref)
        write_mask(mask_s, col_ref[:, 1:2], marks_ref[3:4, :], far_marks_ref[3:4, :], rows, step)
        attend_forward(2 * rows, head, q_s, k_s, v_s, mask_s, o_s, probs=probs, inverse_s=inv_s)
        for group in range(groups):
            o_ref[:, group * LANES : (group + 1) * LANES] = o_s[group].astype(BF16)
        middle = start_ref[...] + matmul(o_ref[...], out_w[...]) + param(2 * width, width)
        unit, inverse = normed_rows(middle)
        gain_b = param(3 * width, width)
        normed = (unit * gain_b + param(4 * width, width)).astype(BF16)
        n_ref[...] = normed
        decoded = middle + param(5 * width + wide, width)
        for j in range(0, wide, part):
            g, slope = gelu_pair(matmul(normed, up_w[:, j : j + part]) + param(5 * width + j, part))
            g = g.astype(BF16)
            g_ref[:, j : j + part] = g
            slope_s[:, j : j + part] = slope
            decoded = decoded + matmul(g, down_w[j : j + part, :])
        dec_ref[...] = decoded.astype(BF16)
        top = cot_ref[...]
        normed_grad = jnp.zeros((TILE, width), F32)
        for j in range(0, wide, part):
            low = (slope_s[:, j : j + part] * matmul_nt(top, down_w[j : j + part, :])).astype(BF16)
            ub_ref[:, j : j + part] = low
            upb_ref[:, j : j + part] += colsum(low)
            normed_grad = normed_grad + matmul_nt(low, up_w[:, j : j + part])
        downb_ref[...] += colsum(top)
        gainb_ref[...] += colsum(normed_grad * unit)
        shiftb_ref[...] += colsum(normed_grad)
        middle_grad = top.astype(F32) + norm_back(normed_grad, unit, inverse, gain_b)
        tm_ref[...] = middle_grad
        low = middle_grad.astype(BF16)
        mb_ref[...] = low
        outb_ref[...] += colsum(low)
        attended_grad = matmul_nt(low, out_w[...])
        for group in range(groups):
            scaled = attended_grad[:, group * LANES : (group + 1) * LANES] * inv_s[group]
            ob_s[group] = scaled.astype(BF16).astype(F32)
        attend_backward(2 * rows, head, q_s, k_s, v_s, o_s, ob_s, dq_s, dk_s, dv_s, probs=probs)
        scale = head ** (-0.5)
        for group in range(groups):
            dq_ref[:, group * LANES : (group + 1) * LANES] = (dq_s[group] * scale).astype(BF16)

        @pl.when(step == steps - 1)
        def _():
            give_key_grads(rows, scale, dk_s, dv_s, near_ref, back_ref)

    small = [width, width, width, wide, width]
    return call(
        kernel,
        "dec_main",
        meta,
        [row_tile(width), row_tile(width), whole(kv.shape), whole(kv.shape), row_tile(tall), whole(marks.shape), whole(marks.shape)]
        + [row_tile(width)] + [whole(value.shape) for value in (params, out, up, down)],
        (start, q, kv, far_kv, columns, marks, far_marks, cotangent, params, out, up, down),
        [row_tile(w) for w in (width, width, width, wide, wide, width, width, width)]
        + [out_whole((rows, 2 * width))] * 2 + [out_whole((1, w)) for w in small],
        [shaped(rows, w, BF16) for w in (width, width, width, wide, wide, width)]
        + [shaped(rows, width, F32), shaped(rows, width, BF16), shaped(rows, 2 * width, F32), shaped(rows, 2 * width, BF16)]
        + [shaped(1, w, F32) for w in small],
        [
            pltpu.VMEM((groups, TILE, LANES), F32),
            pltpu.VMEM((groups, 2 * rows, LANES), BF16),
            pltpu.VMEM((groups, 2 * rows, 2 * LANES), BF16),
            pltpu.VMEM((TILE, 2 * rows), F32),
            pltpu.VMEM((heads, TILE, 2 * rows), BF16),
        ]
        + [pltpu.VMEM((groups, TILE, LANES), F32)] * 4
        + [pltpu.VMEM((groups, LANES, 2 * rows), F32)] * 2
        + [pltpu.VMEM((TILE, wide), F32)],
        2 * rows * width * (4 * wide + 2 * width + 30 * 2 * rows),
        steps,
    )


def dec_head(meta, start, dq, near, back, middle_grad, columns, params, qkv):
    rows, width = start.shape
    tall = columns.shape[1]

    def kernel(meta, start_ref, dq_ref, near_ref, back_ref, tm_ref, col_ref, params_ref, qkv_ref,
               dqkv_ref, lb_ref, gain_ref, shift_ref, bias_ref, token_ref):
        step = pl.program_id(0)

        @pl.when(step == 0)
        def _():
            for ref in (gain_ref, shift_ref, bias_ref, token_ref):
                ref[...] = jnp.zeros_like(ref)

        dqkv_ref[:, :width] = dq_ref[...]
        dqkv_ref[:, width:] = (near_ref[...] + back_ref[...].astype(F32)).astype(BF16)
        grad = matmul_nt(dqkv_ref[...], qkv_ref[...])
        unit, inverse = normed_rows(start_ref[...])
        gain_ref[...] += colsum(grad * unit)
        shift_ref[...] += colsum(grad)
        start_grad = tm_ref[...] + norm_back(grad, unit, inverse, params_ref[:, :width])
        seen = col_ref[:, 2:3] > 0
        token_ref[...] += colsum(jnp.where(seen, 0.0, start_grad))
        low = jnp.where(seen, start_grad, 0.0).astype(BF16)
        lb_ref[...] = low
        bias_ref[...] += colsum(low)

    return call(
        kernel,
        "dec_head",
        meta,
        [row_tile(width), row_tile(width), row_tile(2 * width), row_tile(2 * width), row_tile(width), row_tile(tall)]
        + [whole(params.shape), whole(qkv.shape)],
        (start, dq, near, back, middle_grad, columns, params, qkv),
        [row_tile(3 * width), row_tile(width)] + [out_whole((1, width))] * 4,
        [shaped(rows, 3 * width, BF16), shaped(rows, width, BF16)] + [shaped(1, width, F32)] * 4,
        [],
        2 * rows * width * 3 * width,
        rows // TILE,
    )


def enc_back(meta, sel, lb, slope, m, q, kv, far_kv, o, totals, label, code, far_code, params, out, up, down, embed, heads):
    rows, width = m.shape
    wide, lifted_width = up.shape[1], embed.shape[1]
    groups, head, most = width // LANES, width // heads, rows // TILE
    part = width
    tall = label.shape[1]

    def kernel(meta, sel_ref, lb_ref, slope_ref, m_ref, q_ref, kv_ref, far_ref, o_ref, tot_ref, label_ref, code_ref, far_code_ref,
               params_ref, out_w, up_w, down_w, embed_w,
               lbc_ref, tb_ref, ub_ref, mb_ref, tm_ref, dq_ref, near_ref, back_ref,
               outb_ref, gainb_ref, shiftb_ref, upb_ref, downb_ref,
               q_s, k_s, v_s, mask_s, o_s, ob_s, dq_s, dk_s, dv_s):
        step = pl.program_id(0)
        tiles, far_tiles = meta[0], meta[1]
        count = jnp.maximum(tiles, far_tiles)
        scale = head ** (-0.5)

        @pl.when(step == 0)
        def _():
            for ref in (dk_s, dv_s, outb_ref, gainb_ref, shiftb_ref, upb_ref, downb_ref):
                ref[...] = jnp.zeros_like(ref)

        @pl.when(step < tiles)
        def _():
            lb_here = matmul(sel_ref[...], lb_ref[...]).astype(BF16)
            lbc_ref[...] = lb_here
            grad_top = matmul_nt(lb_here, embed_w[...])
            top = grad_top.astype(BF16)
            tb_ref[...] = top
            normed_grad = jnp.zeros((TILE, width), F32)
            for j in range(0, wide, part):
                low = (slope_ref[:, j : j + part].astype(F32) * matmul_nt(top, down_w[j : j + part, :])).astype(BF16)
                ub_ref[:, j : j + part] = low
                upb_ref[:, j : j + part] += colsum(low)
                normed_grad = normed_grad + matmul_nt(low, up_w[:, j : j + part])
            unit, inverse = normed_rows(m_ref[...])
            downb_ref[...] += colsum(top)
            gainb_ref[...] += colsum(normed_grad * unit)
            shiftb_ref[...] += colsum(normed_grad)
            middle_grad = grad_top + norm_back(normed_grad, unit, inverse, params_ref[:, 3 * width : 4 * width])
            tm_ref[...] = middle_grad
            low = middle_grad.astype(BF16)
            mb_ref[...] = low
            outb_ref[...] += colsum(low)
            attended_grad = matmul_nt(low, out_w[...]).astype(BF16)
            fill_groups(ob_s, attended_grad)
            fill_groups(o_s, o_ref)
            fill_groups(q_s, q_ref)
            for size in range(1, most + 1):

                @pl.when(count == size)
                def _(size=size):
                    @pl.when(step == 0)
                    def _():
                        spread_keys(size, tiles, kv_ref, far_ref, far_tiles, k_s, v_s)

                    span = size * TILE
                    write_mask(mask_s, label_ref[:, 1:2], code_ref[0:1, :span], far_code_ref[0:1, :span], span, step)
                    attend_backward(
                        2 * span, head, q_s, k_s, v_s, o_s, ob_s, dq_s, dk_s, dv_s, mask_ref=mask_s, totals=tot_ref[...]
                    )

                    @pl.when(step == tiles - 1)
                    def _():
                        give_key_grads(span, scale, dk_s, dv_s, near_ref, back_ref)

            for group in range(groups):
                dq_ref[:, group * LANES : (group + 1) * LANES] = (dq_s[group] * scale).astype(BF16)

    small = [width, width, width, wide, width]
    return call(
        kernel,
        "enc_back",
        meta,
        [live_tile(rows), whole(lb.shape), live_tile(wide), live_tile(width), live_tile(width), whole(kv.shape), whole(kv.shape)]
        + [live_tile(width), live_tile(LANES), live_tile(tall), whole(code.shape), whole(code.shape)]
        + [whole(value.shape) for value in (params, out, up, down, embed)],
        (sel, lb, slope, m, q, kv, far_kv, o, totals, label, code, far_code, params, out, up, down, embed),
        [live_tile(w) for w in (lifted_width, width, wide, width, width, width)]
        + [whole((rows, 2 * width))] * 2 + [out_whole((1, w)) for w in small],
        [shaped(rows, w, BF16) for w in (lifted_width, width, wide, width)]
        + [shaped(rows, width, F32), shaped(rows, width, BF16), shaped(rows, 2 * width, F32), shaped(rows, 2 * width, BF16)]
        + [shaped(1, w, F32) for w in small],
        [
            pltpu.VMEM((groups, TILE, LANES), F32),
            pltpu.VMEM((groups, 2 * rows, LANES), BF16),
            pltpu.VMEM((groups, 2 * rows, LANES), BF16),
            pltpu.VMEM((TILE, 2 * rows), F32),
        ]
        + [pltpu.VMEM((groups, TILE, LANES), F32)] * 3
        + [pltpu.VMEM((groups, LANES, 2 * rows), F32)] * 2,
        2 * TILE * width * (2 * wide + 4 * width),
        most,
    )


def enc_head(meta, sel, s, dq, near, back, middle_grad, params, qkv):
    rows, width = s.shape
    steps = rows // TILE

    def kernel(meta, sel_ref, s_ref, dq_ref, near_ref, back_ref, tm_ref, params_ref, qkv_ref,
               dqkv_ref, grad_ref, gain_ref, shift_ref, total):
        step = pl.program_id(0)

        @pl.when(step == 0)
        def _():
            for ref in (gain_ref, shift_ref, total):
                ref[...] = jnp.zeros_like(ref)

        @pl.when(step < meta[0])
        def _():
            dqkv_ref[:, :width] = dq_ref[...]
            dqkv_ref[:, width:] = (near_ref[...] + back_ref[...].astype(F32)).astype(BF16)
            grad = matmul_nt(dqkv_ref[...], qkv_ref[...])
            unit, inverse = normed_rows(s_ref[...].astype(F32))
            gain_ref[...] += colsum(grad * unit)
            shift_ref[...] += colsum(grad)
            stream_grad = tm_ref[...] + norm_back(grad, unit, inverse, params_ref[:, :width])
            total[...] += matmul_tn(sel_ref[...], stream_grad.astype(BF16))

        @pl.when(step == steps - 1)
        def _():
            grad_ref[...] = total[...].astype(BF16)

    return call(
        kernel,
        "enc_head",
        meta,
        [live_tile(w) for w in (rows, width, width, 2 * width, 2 * width, width)] + [whole(params.shape), whole(qkv.shape)],
        (sel, s, dq, near, back, middle_grad, params, qkv),
        [live_tile(3 * width), out_whole((rows, width))] + [out_whole((1, width))] * 2,
        [shaped(rows, 3 * width, BF16), shaped(rows, width, BF16)] + [shaped(1, width, F32)] * 2,
        [pltpu.VMEM((rows, width), F32)],
        2 * TILE * width * 4 * width,
        steps,
    )


def sum_small(values):
    flat = jnp.concatenate([value.reshape(-1) for value in values])
    for axis in ("blk", "dp"):
        for bit in range(bits_of(lax.axis_size(axis))):
            flat = flat + across(flat, axis, bit)
    results, offset = [], 0
    for value in values:
        results.append(flat[offset : offset + value.size])
        offset += value.size
    return results


def local(
    patches,
    visible,
    padding,
    field_ids,
    enc_gain_a,
    enc_shift_a,
    enc_qkv,
    enc_out,
    enc_out_bias,
    enc_gain_b,
    enc_shift_b,
    enc_up,
    enc_up_bias,
    enc_down,
    enc_down_bias,
    embed_map,
    embed_bias,
    mask_token,
    dec_gain_a,
    dec_shift_a,
    dec_qkv,
    dec_out,
    dec_out_bias,
    dec_gain_b,
    dec_shift_b,
    dec_up,
    dec_up_bias,
    dec_down,
    dec_down_bias,
    cotangent,
):
    rows = patches.shape[0]
    tiles_most = rows // TILE
    raw = jnp.stack([visible, padding, field_ids])
    far_raw = across(raw, "blk", 0)

    def marks_of(raw):
        seen, kept, label = raw[0], 1 - raw[1], raw[2] + 1
        marks = jnp.stack([seen * kept * label, label, seen, kept * label])
        return jnp.pad(marks.astype(F32), ((0, 12), (0, 0)))

    marks, far_marks = marks_of(raw), marks_of(far_raw)
    columns = marks.T
    counts = jnp.stack([jnp.sum(visible), jnp.sum(far_raw[0])]).astype(jnp.int32)
    meta = jnp.clip((counts + TILE - 1) // TILE, 1, tiles_most)

    def joined(*values):
        return jnp.concatenate(values).astype(F32)[None, :]

    enc_params = joined(
        enc_gain_a, enc_shift_a, enc_out_bias, enc_gain_b, enc_shift_b, enc_up_bias, enc_down_bias, embed_bias
    )
    dec_params = joined(dec_gain_a, dec_shift_a, dec_out_bias, dec_gain_b, dec_shift_b, dec_up_bias, dec_down_bias)
    token = mask_token.astype(F32)[None, :]

    sel, code, far_code, label, s, n1, q, kv = enc_in(meta, patches, marks, far_marks, enc_params, enc_qkv)
    far_kv = across(kv, "blk", 0)
    o, totals, m, n2, g, slope, low, lift_high, lift_low = enc_main(
        meta, s, q, kv, far_kv, label, code, far_code, enc_params, enc_out, enc_up, enc_down, embed_map, HE
    )
    start, dn1, dq_rows, dkv = dec_in(meta, sel, lift_high, lift_low, columns, dec_params, token, dec_qkv)
    far_dkv = across(dkv, "blk", 0)
    (decoded, d_o, d_n2, d_g, d_ub, d_mb, d_tm, d_dq, d_near, d_back, d_outb, d_gainb, d_shiftb, d_upb, d_downb) = dec_main(
        meta, start, dq_rows, dkv, far_dkv, columns, marks, far_marks, cotangent, dec_params, dec_out, dec_up, dec_down, HD
    )
    d_back = across(d_back, "blk", 0)

    shards = shard_count()
    de, dd = enc_qkv.shape[0], dec_qkv.shape[0]
    rd, re = dd // shards, de // shards
    all_tiles = jnp.int32(tiles_most)
    first = [Entry("wide", d_n2, d_ub, rd, 4), Entry("tall", d_g, cotangent, rd, 4), Entry("wide", d_o, d_mb, rd, 1)]
    g_dec_up, g_dec_down, g_dec_out = summed_grads(
        first, (dec_up.shape, dec_down.shape, dec_out.shape), dd // 2, all_tiles, TILE, 2, 0
    )

    d_dqkv, lb, d_gaina, d_shifta, embed_b, token_grad = dec_head(meta, start, d_dq, d_near, d_back, d_tm, columns, dec_params, dec_qkv)
    (lbc, tb, ub, mb, tm, dq, near, back, outb, gainb, shiftb, upb, downb) = enc_back(
        meta, sel, lb, slope, m, q, kv, far_kv, o, totals, label, code, far_code, enc_params, enc_out, enc_up, enc_down, embed_map, HE
    )
    back = across(back, "blk", 0)
    second = [Entry("wide", dn1, d_dqkv, rd, 3)]
    (g_dec_qkv,) = summed_grads(second, (dec_qkv.shape,), dd // 2, all_tiles, TILE, 1, 0)
    third = [Entry("wide", n2, ub, re, 4), Entry("tall", g, tb, re, 4), Entry("wide", o, mb, re, 1)]
    g_enc_up, g_enc_down, g_enc_out = summed_grads(
        third, (enc_up.shape, enc_down.shape, enc_out.shape), de // 2, meta[0], TILE, 3, 0
    )
    embed_entry = [Entry("wide", low, lbc, re, 1)]
    (g_embed,) = summed_grads(embed_entry, (embed_map.shape,), dd // 2, meta[0], TILE, 1, 2)
    dqkv, patches_grad, gaina, shifta = enc_head(meta, sel, s, dq, near, back, tm, enc_params, enc_qkv)
    fourth = [Entry("wide", n1, dqkv, re, 3)]
    (g_enc_qkv,) = summed_grads(fourth, (enc_qkv.shape,), de // 2, meta[0], TILE, 3, 0)
    small = sum_small(
        [gaina, shifta, outb, gainb, shiftb, upb, downb, embed_b, token_grad]
        + [d_gaina, d_shifta, d_outb, d_gainb, d_shiftb, d_upb, d_downb]
    )
    return (
        (decoded, patches_grad)
        + (small[0], small[1], g_enc_qkv, g_enc_out, small[2], small[3], small[4])
        + (g_enc_up, small[5], g_enc_down, small[6], g_embed, small[7], small[8])
        + (small[9], small[10], g_dec_qkv, g_dec_out, small[11], small[12], small[13])
        + (g_dec_up, small[14], g_dec_down, small[15])
    )


def solution(mesh):
    return jax.shard_map(
        local,
        mesh=mesh,
        in_specs=(
            P(("dp", "blk"), None),
            P(("dp", "blk")),
            P(("dp", "blk")),
            P(("dp", "blk")),
            P(),
            P(),
            P(),
            P(),
            P(),
            P(),
            P(),
            P(),
            P(),
            P(),
            P(),
            P(),
            P(),
            P(),
            P(),
            P(),
            P(),
            P(),
            P(),
            P(),
            P(),
            P(),
            P(),
            P(),
            P(),
            P(("dp", "blk"), None),
        ),
        out_specs=(
            P(("dp", "blk"), None),
            P(("dp", "blk"), None),
            P(),
            P(),
            P(),
            P(),
            P(),
            P(),
            P(),
            P(),
            P(),
            P(),
            P(),
            P(),
            P(),
            P(),
            P(),
            P(),
            P(),
            P(),
            P(),
            P(),
            P(),
            P(),
            P(),
            P(),
            P(),
        ),
        check_vma=False,
    )
```

```python
import math

import jax
import jax.numpy as jnp
from jax import lax
from jax.experimental import pallas as pl
from jax.experimental.pallas import tpu as pltpu
from jax.sharding import PartitionSpec as P

HE = 12
HD = 16
TILE = 256
VMEM_LIMIT = 60 * 1024 * 1024
FLOPS_PER_MICRO, BYTES_PER_MICRO = 1.15e9, 3.6e6


epsilon = 1e-06


def matmul(left_side, right_side):
    return jnp.dot(left_side, right_side, preferred_element_type=jnp.float32)


def matmul_tn(left_side, right_side):
    return lax.dot_general(
        left_side, right_side, (((0,), (0,)), ((), ())), preferred_element_type=jnp.float32
    )


def matmul_nt(left_side, right_side):
    return lax.dot_general(
        left_side, right_side, (((1,), (1,)), ((), ())), preferred_element_type=jnp.float32
    )


def bits_of(count):
    return count.bit_length() - 1


def across(value, axis, bit):
    count = lax.axis_size(axis)
    return lax.ppermute(value, axis, [(i, i ^ (1 << bit)) for i in range(count)])


class Order:
    def __init__(self):
        self.token = None

    def run(self, kernel, name, scalars, in_specs, operands, out_specs, out_shape, scratch=(), micros=1.0, steps=1):
        count = len(in_specs)
        if self.token is not None:
            in_specs = [*in_specs, pl.BlockSpec(memory_space=pl.ANY)]
            operands = [*operands, self.token]
        more = len(in_specs) - count

        def body(meta, *refs):
            kernel(meta, *refs[:count], *refs[count + more :])

        results = pl.pallas_call(
            body,
            out_shape=out_shape,
            grid_spec=pltpu.PrefetchScalarGridSpec(
                num_scalar_prefetch=1, grid=(steps,), in_specs=in_specs, out_specs=out_specs, scratch_shapes=list(scratch)
            ),
            compiler_params=pltpu.CompilerParams(vmem_limit_bytes=VMEM_LIMIT),
            cost_estimate=pl.CostEstimate(
                flops=int(micros * FLOPS_PER_MICRO), bytes_accessed=int(micros * BYTES_PER_MICRO), transcendentals=0
            ),
            name=name,
        )(scalars, *operands)
        self.token = results[0]
        return results


class Entry:
    def __init__(self, kind, lhs, rhs, r, n, width, shape, counted):
        self.kind, self.lhs, self.rhs, self.r, self.n = kind, lhs, rhs, r, n
        self.width, self.shape, self.counted = width, shape, counted


class Bundle:
    def __init__(self, order, bits, spots, tiles, entries):
        self.run, self.entries = order.run, entries
        self.shards = min(16, lax.axis_size("dp"))
        self.bits = [bit for bit in bits if bit < bits_of(self.shards)]
        self.spots, self.tiles = spots, tiles
        self.width = max(entry.width for entry in entries)
        self.firsts, self.bases, first, base = [], [], 0, 0
        for entry in entries:
            self.firsts.append(first)
            self.bases.append(base)
            first += entry.n
            base += entry.n * entry.r
        self.steps, self.rows = first, base

    def block(self, index_map):
        return pl.BlockSpec((1, self.rows, self.width), index_map)

    def shaped(self, count):
        return jax.ShapeDtypeStruct((count, self.rows, self.width), jnp.bfloat16)

    def size(self, count):
        return 2 * count * self.rows * self.width

    def weigh(self):
        entries, shards, width = self.entries, self.shards, self.width
        token_rows = entries[0].lhs.shape[0]
        tallest = max(shards * entry.r for entry in entries)

        def unit_work(entry, offset, unit, lhs_ref, keep_ref, send_ref, kept_ref, sent_ref, turned, spot, live):
            r, n, height, span = entry.r, entry.n, shards * entry.r, entry.width

            def rows_of(ref, count):
                value = ref[:count, :]
                if count > TILE and entry.counted:
                    value = jnp.where(iota(value.shape, 0) < live * TILE, value.astype(F32), 0.0).astype(BF16)
                return value

            def work(count):
                def turn():
                    turned[:height, :count] = rows_of(lhs_ref, count).T

                if entry.kind == "wide":
                    pl.when(unit == 0)(turn)
                else:
                    turn()
                for rhs_ref, out_ref in ((send_ref, sent_ref), (keep_ref, kept_ref)):
                    whole_unit = matmul(turned[:height, :count], rows_of(rhs_ref, count)).astype(BF16)
                    if entry.kind == "wide":
                        at = pl.ds(pl.multiple_of(offset + unit * r, 16), r)
                        for shard in range(shards):
                            out_ref[lax.bitwise_xor(jnp.int32(shard), spot), at, :span] = whole_unit[shard * r : (shard + 1) * r]
                            if span < width:
                                out_ref[lax.bitwise_xor(jnp.int32(shard), spot), at, span:] = jnp.zeros((r, width - span), BF16)
                    else:
                        each, tall = shards // n, n * r
                        for inner in range(each):
                            shard = lax.bitwise_xor(unit * each + inner, spot)
                            out_ref[shard, offset : offset + tall, :span] = whole_unit[inner * tall : (inner + 1) * tall]

            if entry.counted:
                pl.when(live == 1)(lambda: work(TILE))
                pl.when(live > 1)(lambda: work(token_rows))
            else:
                work(token_rows)

        def kernel(meta, *refs):
            sent_ref, kept_ref, turned = refs[-3:]
            step = pl.program_id(0)
            for index, entry in enumerate(entries):
                first = self.firsts[index]

                @pl.when((step >= first) & (step < first + entry.n))
                def _(index=index, entry=entry, first=first):
                    ins = refs[3 * index : 3 * index + 3]
                    unit_work(entry, self.bases[index], step - first, *ins, kept_ref, sent_ref, turned, meta[0], meta[2])

        in_specs, operands = [], []
        for first, entry in zip(self.firsts, entries):
            n, height, span = entry.n, shards * entry.r, entry.width

            def unit_of(step, first=first, n=n):
                return jnp.clip(step - first, 0, n - 1)

            if entry.kind == "wide":
                in_specs.append(pl.BlockSpec((token_rows, height), lambda step, meta: (0, 0)))
                for flip in (0, 1):
                    in_specs.append(
                        pl.BlockSpec(
                            (token_rows, span),
                            lambda step, meta, n=n, unit_of=unit_of, flip=flip: (0, (meta[1] ^ flip) * n + unit_of(step)),
                        )
                    )
            else:
                in_specs.append(pl.BlockSpec((token_rows, height), lambda step, meta, unit_of=unit_of: (0, unit_of(step))))
                for flip in (0, 1):
                    in_specs.append(pl.BlockSpec((token_rows, span), lambda step, meta, flip=flip: (0, meta[1] ^ flip)))
            operands += [entry.lhs, entry.rhs, entry.rhs]
        shape = (shards, self.rows, width)
        sent, kept = self.run(
            kernel,
            "weight_grads",
            jnp.concatenate([self.spots, self.tiles[:1]]),
            in_specs,
            operands,
            [pl.BlockSpec(shape, lambda step, meta: (0, 0, 0))] * 2,
            [self.shaped(shards)] * 2,
            [pltpu.VMEM((tallest, token_rows), BF16)],
            micros=5.0,
            steps=self.steps,
        )
        self.terms = (kept, across(sent, "blk", 0))
        self.left = list(range(bits_of(shards) - 1, -1, -1))
        self.due = list(self.bits)

    def halve(self):
        bit = self.due.pop(0)
        axis = self.left.index(bit)
        self.left.remove(bit)
        count = 1 << len(self.left)
        after = 1 << (len(self.left) - axis)

        def at(side):
            return self.block(lambda step, meta: ((lax.div(step, after) * 2 + side) * after + lax.rem(step, after), 0, 0))

        def kernel(meta, a_sent, a_stay, b_sent, b_stay, sent_ref, stay_ref):
            for a, b, target in ((a_sent, b_sent, sent_ref), (a_stay, b_stay, stay_ref)):
                target[...] = (a[...].astype(F32) + b[...].astype(F32)).astype(BF16)

        first, second = self.terms
        here = self.block(lambda step, meta: (step, 0, 0))
        sent, stay = self.run(
            kernel,
            "halve",
            self.spots,
            [at(1), at(0), at(1), at(0)],
            [first, first, second, second],
            [here, here],
            [self.shaped(count)] * 2,
            micros=1.0 + self.size(6 * count) / 3e6,
            steps=count,
        )
        self.terms = (stay, across(sent, "dp", bit))

    def own(self):
        def kernel(meta, a_ref, b_ref, out_ref):
            out_ref[...] = (a_ref[...].astype(F32) + b_ref[...].astype(F32)).astype(BF16)

        here = self.block(lambda step, meta: (step, 0, 0))

        def add(a, b):
            (total,) = self.run(
                kernel, "own", self.spots, [here, here], [a, b], [here], [self.shaped(1)], micros=1.5
            )
            return total

        total = add(*self.terms)
        for bit in range(bits_of(self.shards), bits_of(lax.axis_size("dp"))):
            total = add(total, across(total, "dp", bit))
        self.due = list(reversed(self.bits))
        self.spread(total)

    def spread(self, held):
        bit = self.due.pop(0)
        self.held = (held, across(held, "dp", bit))

    def join(self):
        count = self.held[0].shape[0]

        def kernel(meta, a_ref, b_ref, out_ref):
            step = pl.program_id(0)
            pl.when(step < count)(lambda: out_ref.__setitem__(Ellipsis, a_ref[...]))
            pl.when(step >= count)(lambda: out_ref.__setitem__(Ellipsis, b_ref[...]))

        (held,) = self.run(
            kernel,
            "join",
            self.spots,
            [self.block(lambda step, meta: (jnp.minimum(step, count - 1), 0, 0)), self.block(lambda step, meta: (jnp.maximum(step - count, 0), 0, 0))],
            self.held,
            [self.block(lambda step, meta: (step, 0, 0))],
            [self.shaped(2 * count)],
            micros=1.0 + self.size(4 * count) / 3e6,
            steps=2 * count,
        )
        self.spread(held)

    def finish(self):
        self.other = [across(held, "blk", 0) for held in self.held]

    def place(self):
        entries, shards, bits = self.entries, self.shards, self.bits
        half_count = shards // 2

        def shard_of(step, meta):
            shard = jnp.int32(0)
            for index, bit in enumerate(bits):
                shard = shard | ((lax.shift_right_logical(step, len(bits) - 1 - index) & 1) << bit)
            return lax.bitwise_xor(shard, meta[0])

        def kernel(meta, low, high, other_low, other_high, *outs):
            step = pl.program_id(0)

            def write(mine, other, side):
                for entry, offset, out_ref in zip(entries, self.bases, outs):
                    for unit in range(entry.n):
                        row = offset + unit * entry.r
                        for which, source in ((side, mine), (1 - side, other)):
                            value = source[0, row : row + entry.r, : entry.width].astype(F32)
                            if entry.kind == "wide":
                                at = (which * entry.n + unit) * entry.width
                                out_ref[:, at : at + entry.width] = value
                            else:
                                at = which * entry.width
                                out_ref[unit * entry.r : (unit + 1) * entry.r, at : at + entry.width] = value

            for side in range(2):
                is_side = meta[1] == side
                pl.when(is_side & (step < half_count))(lambda side=side: write(low, other_low, side))
                pl.when(is_side & (step >= half_count))(lambda side=side: write(high, other_high, side))

        low_at = self.block(lambda step, meta: (jnp.minimum(step, half_count - 1), 0, 0))
        high_at = self.block(lambda step, meta: (jnp.maximum(step - half_count, 0), 0, 0))
        out_specs, out_shape = [], []
        for entry in entries:
            height = entry.r if entry.kind == "wide" else entry.n * entry.r
            out_specs.append(pl.BlockSpec((height, entry.shape[1]), lambda step, meta: (shard_of(step, meta), 0)))
            out_shape.append(jax.ShapeDtypeStruct(entry.shape, jnp.float32))
        return self.run(
            kernel,
            "place_shards",
            self.spots,
            [low_at, high_at, low_at, high_at],
            [self.held[0], self.held[1], *self.other],
            out_specs,
            out_shape,
            micros=1.0 + sum(8 * entry.shape[0] * entry.shape[1] for entry in entries) / 3e6,
            steps=shards,
        )


LOG2E = math.log2(math.e)
NEVER = -1e30
LANES = 128
BF16, F32 = jnp.bfloat16, jnp.float32


def colsum(value):
    return jnp.sum(value.astype(F32), axis=0, keepdims=True)


def normed_rows(stream):
    centred = stream - jnp.mean(stream, axis=-1, keepdims=True)
    inverse = lax.rsqrt(jnp.mean(centred * centred, axis=-1, keepdims=True) + epsilon)
    return centred * inverse, inverse


def norm_back(grad, unit, inverse, gain):
    grad = grad * gain
    inner = jnp.mean(grad * unit, axis=-1, keepdims=True)
    return inverse * (grad - jnp.mean(grad, axis=-1, keepdims=True) - unit * inner)


def gelu_pair(u):
    bell = jnp.exp2(u * u * (-0.5 * LOG2E))
    t = 1.0 / (1.0 + (0.3275911 * math.sqrt(0.5)) * jnp.abs(u))
    poly = ((((1.061405429 * t - 1.453152027) * t + 1.421413741) * t - 0.284496736) * t + 0.254829592) * t
    tail = 0.5 * poly * bell
    phi = jnp.where(u < 0, tail, 1.0 - tail)
    return u * phi, phi + u * bell * (1.0 / math.sqrt(2.0 * math.pi))


def iota(shape, axis):
    return lax.broadcasted_iota(jnp.int32, shape, axis)


def fill_groups(target, source):
    for group in range(target.shape[0]):
        target[group] = source[:, group * LANES : (group + 1) * LANES].astype(target.dtype)


def attend_forward(keys, head, q_s, k_s, v_s, mask_ref, o_s, probs=None, inverse_s=None, totals=None):
    groups, rows, _ = q_s.shape
    inside = LANES // head
    factor = head ** (-0.5) * LOG2E
    lanes = iota((rows, LANES), 1)
    which = lax.div(lanes, jnp.int32(head))
    if totals is not None:
        totals[...] = jnp.zeros_like(totals)

    def one_group(group, carry):
        queries = q_s[group]
        key_rows = k_s[group, :keys, :]
        values = v_s[group, :keys, :]
        blended = jnp.zeros((rows, LANES), F32)
        inverses = jnp.zeros((rows, LANES), F32)
        for h in range(inside):
            own = which == h
            query = jnp.where(own, queries, 0.0).astype(BF16)
            scores = matmul_nt(query, key_rows) * factor + mask_ref[:, :keys]
            top = jnp.max(scores, axis=1, keepdims=True)
            prob = jnp.exp2(scores - top).astype(BF16)
            if probs is not None:
                probs[group * inside + h, :, :keys] = prob
            both = matmul(prob, values)
            inverse = 1.0 / both[:, LANES:]
            blended = jnp.where(own, both[:, :LANES] * inverse, blended)
            if inverse_s is not None:
                inverses = jnp.where(own, inverse, inverses)
            if totals is not None:
                at = lanes == group * inside + h
                totals[...] = jnp.where(at, top + jnp.log2(both[:, LANES:]), totals[...])
        o_s[group] = blended
        if inverse_s is not None:
            inverse_s[group] = inverses
        return carry

    lax.fori_loop(0, groups, one_group, 0)


def attend_backward(keys, head, q_s, k_s, v_s, o_s, ob_s, dq_s, dk_s, dv_s, probs=None, mask_ref=None, totals=None):
    groups, rows, _ = q_s.shape
    inside = LANES // head
    factor = head ** (-0.5) * LOG2E
    lanes = iota((rows, LANES), 1)
    which = lax.div(lanes, jnp.int32(head))

    def one_group(group, carry):
        queries, grads = q_s[group], ob_s[group]
        key_rows = k_s[group, :keys, :]
        values = v_s[group, :keys, :LANES]
        product = grads * o_s[group]
        queries_t = queries.T.astype(BF16)
        grads_t = grads.T.astype(BF16)
        query_grad = jnp.zeros((rows, LANES), F32)
        for h in range(inside):
            own = which == h
            at = slice(h * head, (h + 1) * head)
            inner = jnp.sum(jnp.where(own, product, 0.0), axis=1, keepdims=True)
            if probs is not None:
                prob = probs[group * inside + h, :, :keys]
            else:
                query = jnp.where(own, queries, 0.0).astype(BF16)
                total = jnp.sum(jnp.where(lanes == group * inside + h, totals, 0.0), axis=1, keepdims=True)
                prob = jnp.exp2(matmul_nt(query, key_rows) * factor + (mask_ref[:, :keys] - total)).astype(BF16)
            grad_probs = matmul_nt(jnp.where(own, grads, 0.0).astype(BF16), values)
            score_grad = (prob.astype(F32) * (grad_probs - inner)).astype(BF16)
            query_grad = jnp.where(own, matmul(score_grad, key_rows), query_grad)
            dk_s[group, at, :keys] += matmul(queries_t[at], score_grad)
            dv_s[group, at, :keys] += matmul(grads_t[at], prob)
        dq_s[group] = query_grad
        return carry

    lax.fori_loop(0, groups, one_group, 0)


def whole(shape):
    rank = len(shape)
    return pl.BlockSpec(shape, lambda step, meta: (0,) * rank, pipeline_mode=pl.Buffered(1))


def out_whole(shape):
    rank = len(shape)
    return pl.BlockSpec(shape, lambda step, meta: (0,) * rank)


def row_tile(width):
    return pl.BlockSpec((TILE, width), lambda step, meta: (step, 0))


def live_tile(width):
    return pl.BlockSpec((TILE, width), lambda step, meta: (jnp.minimum(step, meta[0] - 1), 0))


def call(order, kernel, name, meta, in_specs, operands, out_specs, out_shape, scratch, micros, steps):
    return order.run(kernel, name, meta, in_specs, operands, out_specs, out_shape, scratch, micros=micros, steps=steps)


def shaped(rows, width, dtype):
    return jax.ShapeDtypeStruct((rows, width), dtype)


MARKS = 16


def enc_in(order, meta, patches, raw, far_raw, params, qkv):
    rows, width = patches.shape

    def marks_of(seen, padded, label):
        seen, kept, label = seen[...].astype(F32), 1.0 - padded[...].astype(F32), label[...].astype(F32) + 1.0
        row, result = iota((MARKS, rows), 0), jnp.zeros((MARKS, rows), F32)
        for index, value in enumerate((seen * kept * label, label, seen, kept * label)):
            result = jnp.where(row == index, value, result)
        return result

    def kernel(meta, patches_ref, *refs):
        raw_refs, far_refs, (params_ref, qkv_ref) = refs[:3], refs[3:6], refs[6:8]
        sel_ref, code_ref, far_code_ref, label_ref, marks_ref, far_marks_ref, columns_ref, s_ref, n_ref, q_ref, kv_ref, place_s = refs[8:]
        step = pl.program_id(0)

        @pl.when(step == 0)
        def _():
            below = (iota((rows, rows), 0) <= iota((rows, rows), 1)).astype(F32).astype(BF16)
            for index, (source, target) in enumerate(((raw_refs, marks_ref), (far_refs, far_marks_ref))):
                marks = marks_of(*source)
                target[...] = marks
                place = matmul(marks.astype(BF16), below)[2:3, :]
                place_s[index : index + 1, :] = jnp.where(marks[2:3, :] > 0, place - 1.0, -1.0)
            columns_ref[...] = marks_ref[...].T

        @pl.when(step < jnp.maximum(meta[0], meta[1]))
        def _():
            target = (step * TILE + iota((TILE, rows), 0)).astype(F32)
            sel = jnp.where(target == place_s[0:1, :], 1.0, 0.0).astype(BF16)
            far_sel = jnp.where(target == place_s[1:2, :], 1.0, 0.0).astype(BF16)
            sel_ref[...] = sel
            own_marks = marks_ref[...].astype(BF16)
            code_ref[...] = matmul_nt(own_marks, sel)
            far_code_ref[...] = matmul_nt(far_marks_ref[...].astype(BF16), far_sel)
            label_ref[...] = matmul_nt(sel, own_marks)

        @pl.when(step < meta[0])
        def _():
            stream = matmul(sel_ref[...], patches_ref[...])
            s_ref[...] = stream.astype(BF16)
            unit, _ = normed_rows(stream)
            normed = (unit * params_ref[:, :width] + params_ref[:, width : 2 * width]).astype(BF16)
            n_ref[...] = normed
            q_ref[...] = matmul(normed, qkv_ref[:, :width]).astype(BF16)
            kv_ref[...] = matmul(normed, qkv_ref[:, width:]).astype(BF16)

    def last_tile(step, meta):
        return jnp.minimum(step, jnp.maximum(meta[0], meta[1]) - 1)

    lane_tile = pl.BlockSpec((MARKS, TILE), lambda step, meta: (0, last_tile(step, meta)))

    def tile(size):
        return pl.BlockSpec((TILE, size), lambda step, meta: (last_tile(step, meta), 0))

    operands = (patches, *raw, *far_raw, params, qkv)
    return call(
        order,
        kernel,
        "enc_in",
        meta,
        [whole(value.shape) for value in operands],
        operands,
        [tile(rows), lane_tile, lane_tile, tile(MARKS), out_whole((MARKS, rows)), out_whole((MARKS, rows)), out_whole((rows, MARKS))]
        + [live_tile(w) for w in (width, width, width, 2 * width)],
        [shaped(rows, rows, BF16), shaped(MARKS, rows, F32), shaped(MARKS, rows, F32), shaped(rows, MARKS, F32)]
        + [shaped(MARKS, rows, F32), shaped(MARKS, rows, F32), shaped(rows, MARKS, F32)]
        + [shaped(rows, w, BF16) for w in (width, width, width, 2 * width)],
        [pltpu.VMEM((8, rows), F32)],
        7.0,
        rows // TILE,
    )


def spread_keys(count, tiles, kv_ref, far_ref, far_tiles, k_s, v_s):
    size = count * TILE
    width = kv_ref.shape[1] // 2
    for source, live, base in ((kv_ref, tiles, 0), (far_ref, far_tiles, size)):
        ok = iota((size, LANES), 0) < live * TILE
        for group in range(width // LANES):
            at = slice(group * LANES, (group + 1) * LANES)
            value_at = slice(width + group * LANES, width + (group + 1) * LANES)
            k_s[group, base : base + size, :] = jnp.where(ok, source[:size, at].astype(F32), 0.0).astype(BF16)
            v_s[group, base : base + size, :LANES] = jnp.where(ok, source[:size, value_at].astype(F32), 0.0).astype(BF16)
            if v_s.shape[2] > LANES:
                v_s[group, base : base + size, LANES:] = jnp.ones((size, v_s.shape[2] - LANES), BF16)


def write_mask(mask_ref, label, code, far_code, size, step):
    shape = (label.shape[0], size)
    near = (label == code) | (iota(shape, 1) == step * TILE + iota(shape, 0))
    mask_ref[:, :size] = jnp.where(near, 0.0, NEVER)
    mask_ref[:, size : 2 * size] = jnp.where(label == far_code, 0.0, NEVER)


def enc_main(order, meta, s, q, kv, far_kv, label, code, far_code, params, out, up, down, embed, heads):
    rows, width = s.shape
    wide, lifted_width = up.shape[1], embed.shape[1]
    groups, head, most = width // LANES, width // heads, rows // TILE
    part = width

    def kernel(meta, s_ref, q_ref, kv_ref, far_ref, label_ref, code_ref, far_code_ref, params_ref, out_w, up_w, down_w, embed_w,
               o_ref, tot_ref, m_ref, n_ref, g_ref, gp_ref, e_ref, hi_ref, lo_ref, q_s, k_s, v_s, mask_s, o_s):
        step = pl.program_id(0)
        tiles, far_tiles = meta[0], meta[1]
        count = jnp.maximum(tiles, far_tiles)

        def param(start, size):
            return params_ref[:, start : start + size]

        @pl.when(step < tiles)
        def _():
            fill_groups(q_s, q_ref)
            for size in range(1, most + 1):

                @pl.when(count == size)
                def _(size=size):
                    @pl.when(step == 0)
                    def _():
                        spread_keys(size, tiles, kv_ref, far_ref, far_tiles, k_s, v_s)

                    span = size * TILE
                    write_mask(mask_s, label_ref[:, 1:2], code_ref[0:1, :span], far_code_ref[0:1, :span], span, step)
                    attend_forward(2 * span, head, q_s, k_s, v_s, mask_s, o_s, totals=tot_ref)

            for group in range(groups):
                o_ref[:, group * LANES : (group + 1) * LANES] = o_s[group].astype(BF16)
            middle = s_ref[...].astype(F32) + matmul(o_ref[...], out_w[...]) + param(2 * width, width)
            m_ref[...] = middle
            unit, _ = normed_rows(middle)
            normed = (unit * param(3 * width, width) + param(4 * width, width)).astype(BF16)
            n_ref[...] = normed
            encoded = middle + param(5 * width + wide, width)
            for j in range(0, wide, part):
                u = matmul(normed, up_w[:, j : j + part]) + param(5 * width + j, part)
                g, slope = gelu_pair(u)
                g = g.astype(BF16)
                g_ref[:, j : j + part] = g
                gp_ref[:, j : j + part] = slope.astype(BF16)
                encoded = encoded + matmul(g, down_w[j : j + part, :])
            low = encoded.astype(BF16)
            e_ref[...] = low
            lifted = matmul(low, embed_w[...]) + param(6 * width + wide, lifted_width)
            high = lifted.astype(BF16)
            hi_ref[...] = high
            lo_ref[...] = (lifted - high.astype(F32)).astype(BF16)

    tall = label.shape[1]
    return call(
        order,
        kernel,
        "enc_main",
        meta,
        [live_tile(width), live_tile(width), whole(kv.shape), whole(kv.shape), live_tile(tall), whole(code.shape), whole(code.shape)]
        + [whole(value.shape) for value in (params, out, up, down, embed)],
        (s, q, kv, far_kv, label, code, far_code, params, out, up, down, embed),
        [live_tile(w) for w in (width, LANES, width, width, wide, wide, width, lifted_width, lifted_width)],
        [shaped(rows, width, BF16), shaped(rows, LANES, F32), shaped(rows, width, F32), shaped(rows, width, BF16)]
        + [shaped(rows, wide, BF16)] * 2 + [shaped(rows, width, BF16)] + [shaped(rows, lifted_width, BF16)] * 2,
        [
            pltpu.VMEM((groups, TILE, LANES), F32),
            pltpu.VMEM((groups, 2 * rows, LANES), BF16),
            pltpu.VMEM((groups, 2 * rows, 2 * LANES), BF16),
            pltpu.VMEM((TILE, 2 * rows), F32),
            pltpu.VMEM((groups, TILE, LANES), F32),
        ],
        20.0,
        most,
    )


def dec_in(order, meta, sel, high, low, columns, params, qkv):
    rows, width = high.shape
    tall = columns.shape[1]

    def kernel(meta, sel_ref, hi_ref, lo_ref, col_ref, params_ref, qkv_ref, start_ref, n_ref, q_ref, kv_ref, total):
        total[...] = jnp.zeros_like(total)

        def add(tile, carry):
            at = pl.ds(pl.multiple_of(tile * TILE, TILE), TILE)
            total[...] += matmul_tn(sel_ref[at, :], hi_ref[at, :]) + matmul_tn(sel_ref[at, :], lo_ref[at, :])
            return carry

        lax.fori_loop(0, meta[0], add, 0)
        start = jnp.where(col_ref[:, 2:3] > 0, total[...], params_ref[:, params.shape[1] - width :])
        start_ref[...] = start
        unit, _ = normed_rows(start)
        normed = (unit * params_ref[:, :width] + params_ref[:, width : 2 * width]).astype(BF16)
        n_ref[...] = normed
        q_ref[...] = matmul(normed, qkv_ref[:, :width]).astype(BF16)
        kv_ref[...] = matmul(normed, qkv_ref[:, width:]).astype(BF16)

    return call(
        order,
        kernel,
        "dec_in",
        meta,
        [pl.BlockSpec((rows, TILE), lambda step, meta: (0, step)), whole(high.shape), whole(low.shape), row_tile(tall)]
        + [whole(value.shape) for value in (params, qkv)],
        (sel, high, low, columns, params, qkv),
        [row_tile(w) for w in (width, width, width, 2 * width)],
        [shaped(rows, width, F32)] + [shaped(rows, w, BF16) for w in (width, width, 2 * width)],
        [pltpu.VMEM((TILE, width), F32)],
        7.0,
        rows // TILE,
    )


def give_key_grads(size, scale, dk_s, dv_s, near_ref, far_ref):
    groups = dk_s.shape[0]
    for index, (source, factor) in enumerate(((dk_s, scale), (dv_s, 1.0))):
        for group in range(groups):
            at = slice((index * groups + group) * LANES, (index * groups + group + 1) * LANES)
            near_ref[:size, at] = source[group, :, :size].T * factor
            far_ref[:size, at] = (source[group, :, size : 2 * size].T * factor).astype(BF16)


def dec_main(order, meta, start, q, kv, far_kv, columns, marks, far_marks, cotangent, params, out, up, down, heads):
    rows, width = start.shape
    wide = up.shape[1]
    groups, head, steps = width // LANES, width // heads, rows // TILE
    part = width
    tall = columns.shape[1]

    def kernel(meta, start_ref, q_ref, kv_ref, far_ref, col_ref, marks_ref, far_marks_ref, cot_ref, params_ref, out_w, up_w, down_w,
               dec_ref, o_ref, n_ref, g_ref, ub_ref, mb_ref, tm_ref, dq_ref, near_ref, back_ref,
               outb_ref, gainb_ref, shiftb_ref, upb_ref, downb_ref,
               q_s, k_s, v_s, mask_s, probs, o_s, inv_s, ob_s, dq_s, dk_s, dv_s, slope_s):
        step = pl.program_id(0)

        def param(begin, size):
            return params_ref[:, begin : begin + size]

        @pl.when(step == 0)
        def _():
            spread_keys(steps, steps, kv_ref, far_ref, steps, k_s, v_s)
            for ref in (dk_s, dv_s, outb_ref, gainb_ref, shiftb_ref, upb_ref, downb_ref):
                ref[...] = jnp.zeros_like(ref)

        fill_groups(q_s, q_ref)
        write_mask(mask_s, col_ref[:, 1:2], marks_ref[3:4, :], far_marks_ref[3:4, :], rows, step)
        attend_forward(2 * rows, head, q_s, k_s, v_s, mask_s, o_s, probs=probs, inverse_s=inv_s)
        for group in range(groups):
            o_ref[:, group * LANES : (group + 1) * LANES] = o_s[group].astype(BF16)
        middle = start_ref[...] + matmul(o_ref[...], out_w[...]) + param(2 * width, width)
        unit, inverse = normed_rows(middle)
        gain_b = param(3 * width, width)
        normed = (unit * gain_b + param(4 * width, width)).astype(BF16)
        n_ref[...] = normed
        decoded = middle + param(5 * width + wide, width)
        for j in range(0, wide, part):
            g, slope = gelu_pair(matmul(normed, up_w[:, j : j + part]) + param(5 * width + j, part))
            g = g.astype(BF16)
            g_ref[:, j : j + part] = g
            slope_s[:, j : j + part] = slope
            decoded = decoded + matmul(g, down_w[j : j + part, :])
        dec_ref[...] = decoded.astype(BF16)
        top = cot_ref[...]
        normed_grad = jnp.zeros((TILE, width), F32)
        for j in range(0, wide, part):
            low = (slope_s[:, j : j + part] * matmul_nt(top, down_w[j : j + part, :])).astype(BF16)
            ub_ref[:, j : j + part] = low
            upb_ref[:, j : j + part] += colsum(low)
            normed_grad = normed_grad + matmul_nt(low, up_w[:, j : j + part])
        downb_ref[...] += colsum(top)
        gainb_ref[...] += colsum(normed_grad * unit)
        shiftb_ref[...] += colsum(normed_grad)
        middle_grad = top.astype(F32) + norm_back(normed_grad, unit, inverse, gain_b)
        tm_ref[...] = middle_grad
        low = middle_grad.astype(BF16)
        mb_ref[...] = low
        outb_ref[...] += colsum(low)
        attended_grad = matmul_nt(low, out_w[...])
        for group in range(groups):
            scaled = attended_grad[:, group * LANES : (group + 1) * LANES] * inv_s[group]
            ob_s[group] = scaled.astype(BF16).astype(F32)
        attend_backward(2 * rows, head, q_s, k_s, v_s, o_s, ob_s, dq_s, dk_s, dv_s, probs=probs)
        scale = head ** (-0.5)
        for group in range(groups):
            dq_ref[:, group * LANES : (group + 1) * LANES] = (dq_s[group] * scale).astype(BF16)

        @pl.when(step == steps - 1)
        def _():
            give_key_grads(rows, scale, dk_s, dv_s, near_ref, back_ref)

    small = [width, width, width, wide, width]
    return call(
        order,
        kernel,
        "dec_main",
        meta,
        [row_tile(width), row_tile(width), whole(kv.shape), whole(kv.shape), row_tile(tall), whole(marks.shape), whole(marks.shape)]
        + [row_tile(width)] + [whole(value.shape) for value in (params, out, up, down)],
        (start, q, kv, far_kv, columns, marks, far_marks, cotangent, params, out, up, down),
        [row_tile(w) for w in (width, width, width, wide, wide, width, width, width)]
        + [out_whole((rows, 2 * width))] * 2 + [out_whole((1, w)) for w in small],
        [shaped(rows, w, BF16) for w in (width, width, width, wide, wide, width)]
        + [shaped(rows, width, F32), shaped(rows, width, BF16), shaped(rows, 2 * width, F32), shaped(rows, 2 * width, BF16)]
        + [shaped(1, w, F32) for w in small],
        [
            pltpu.VMEM((groups, TILE, LANES), F32),
            pltpu.VMEM((groups, 2 * rows, LANES), BF16),
            pltpu.VMEM((groups, 2 * rows, 2 * LANES), BF16),
            pltpu.VMEM((TILE, 2 * rows), F32),
            pltpu.VMEM((heads, TILE, 2 * rows), BF16),
        ]
        + [pltpu.VMEM((groups, TILE, LANES), F32)] * 4
        + [pltpu.VMEM((groups, LANES, 2 * rows), F32)] * 2
        + [pltpu.VMEM((TILE, wide), F32)],
        95.0,
        steps,
    )


def dec_head(order, meta, start, dq, near, back, middle_grad, columns, params, qkv):
    rows, width = start.shape
    tall = columns.shape[1]

    def kernel(meta, start_ref, dq_ref, near_ref, back_ref, tm_ref, col_ref, params_ref, qkv_ref,
               dqkv_ref, lb_ref, gain_ref, shift_ref, bias_ref, token_ref):
        step = pl.program_id(0)

        @pl.when(step == 0)
        def _():
            for ref in (gain_ref, shift_ref, bias_ref, token_ref):
                ref[...] = jnp.zeros_like(ref)

        dqkv_ref[:, :width] = dq_ref[...]
        dqkv_ref[:, width:] = (near_ref[...] + back_ref[...].astype(F32)).astype(BF16)
        grad = matmul_nt(dqkv_ref[...], qkv_ref[...])
        unit, inverse = normed_rows(start_ref[...])
        gain_ref[...] += colsum(grad * unit)
        shift_ref[...] += colsum(grad)
        start_grad = tm_ref[...] + norm_back(grad, unit, inverse, params_ref[:, :width])
        seen = col_ref[:, 2:3] > 0
        token_ref[...] += colsum(jnp.where(seen, 0.0, start_grad))
        low = jnp.where(seen, start_grad, 0.0).astype(BF16)
        lb_ref[...] = low
        bias_ref[...] += colsum(low)

    return call(
        order,
        kernel,
        "dec_head",
        meta,
        [row_tile(width), row_tile(width), row_tile(2 * width), row_tile(2 * width), row_tile(width), row_tile(tall)]
        + [whole(params.shape), whole(qkv.shape)],
        (start, dq, near, back, middle_grad, columns, params, qkv),
        [row_tile(3 * width), row_tile(width)] + [out_whole((1, width))] * 4,
        [shaped(rows, 3 * width, BF16), shaped(rows, width, BF16)] + [shaped(1, width, F32)] * 4,
        [],
        7.0,
        rows // TILE,
    )


def enc_back(order, meta, sel, lb, slope, m, q, kv, far_kv, o, totals, label, code, far_code, params, out, up, down, embed, heads):
    rows, width = m.shape
    wide, lifted_width = up.shape[1], embed.shape[1]
    groups, head, most = width // LANES, width // heads, rows // TILE
    part = width
    tall = label.shape[1]

    def kernel(meta, sel_ref, lb_ref, slope_ref, m_ref, q_ref, kv_ref, far_ref, o_ref, tot_ref, label_ref, code_ref, far_code_ref,
               params_ref, out_w, up_w, down_w, embed_w,
               lbc_ref, tb_ref, ub_ref, mb_ref, tm_ref, dq_ref, near_ref, back_ref,
               outb_ref, gainb_ref, shiftb_ref, upb_ref, downb_ref,
               q_s, k_s, v_s, mask_s, o_s, ob_s, dq_s, dk_s, dv_s):
        step = pl.program_id(0)
        tiles, far_tiles = meta[0], meta[1]
        count = jnp.maximum(tiles, far_tiles)
        scale = head ** (-0.5)

        @pl.when(step == 0)
        def _():
            for ref in (dk_s, dv_s, outb_ref, gainb_ref, shiftb_ref, upb_ref, downb_ref):
                ref[...] = jnp.zeros_like(ref)

        @pl.when(step < tiles)
        def _():
            lb_here = matmul(sel_ref[...], lb_ref[...]).astype(BF16)
            lbc_ref[...] = lb_here
            grad_top = matmul_nt(lb_here, embed_w[...])
            top = grad_top.astype(BF16)
            tb_ref[...] = top
            normed_grad = jnp.zeros((TILE, width), F32)
            for j in range(0, wide, part):
                low = (slope_ref[:, j : j + part].astype(F32) * matmul_nt(top, down_w[j : j + part, :])).astype(BF16)
                ub_ref[:, j : j + part] = low
                upb_ref[:, j : j + part] += colsum(low)
                normed_grad = normed_grad + matmul_nt(low, up_w[:, j : j + part])
            unit, inverse = normed_rows(m_ref[...])
            downb_ref[...] += colsum(top)
            gainb_ref[...] += colsum(normed_grad * unit)
            shiftb_ref[...] += colsum(normed_grad)
            middle_grad = grad_top + norm_back(normed_grad, unit, inverse, params_ref[:, 3 * width : 4 * width])
            tm_ref[...] = middle_grad
            low = middle_grad.astype(BF16)
            mb_ref[...] = low
            outb_ref[...] += colsum(low)
            attended_grad = matmul_nt(low, out_w[...]).astype(BF16)
            fill_groups(ob_s, attended_grad)
            fill_groups(o_s, o_ref)
            fill_groups(q_s, q_ref)
            for size in range(1, most + 1):

                @pl.when(count == size)
                def _(size=size):
                    @pl.when(step == 0)
                    def _():
                        spread_keys(size, tiles, kv_ref, far_ref, far_tiles, k_s, v_s)

                    span = size * TILE
                    write_mask(mask_s, label_ref[:, 1:2], code_ref[0:1, :span], far_code_ref[0:1, :span], span, step)
                    attend_backward(
                        2 * span, head, q_s, k_s, v_s, o_s, ob_s, dq_s, dk_s, dv_s, mask_ref=mask_s, totals=tot_ref[...]
                    )

                    @pl.when(step == tiles - 1)
                    def _():
                        give_key_grads(span, scale, dk_s, dv_s, near_ref, back_ref)

            for group in range(groups):
                dq_ref[:, group * LANES : (group + 1) * LANES] = (dq_s[group] * scale).astype(BF16)

    small = [width, width, width, wide, width]
    return call(
        order,
        kernel,
        "enc_back",
        meta,
        [live_tile(rows), whole(lb.shape), live_tile(wide), live_tile(width), live_tile(width), whole(kv.shape), whole(kv.shape)]
        + [live_tile(width), live_tile(LANES), live_tile(tall), whole(code.shape), whole(code.shape)]
        + [whole(value.shape) for value in (params, out, up, down, embed)],
        (sel, lb, slope, m, q, kv, far_kv, o, totals, label, code, far_code, params, out, up, down, embed),
        [live_tile(w) for w in (lifted_width, width, wide, width, width, width)]
        + [whole((rows, 2 * width))] * 2 + [out_whole((1, w)) for w in small],
        [shaped(rows, w, BF16) for w in (lifted_width, width, wide, width)]
        + [shaped(rows, width, F32), shaped(rows, width, BF16), shaped(rows, 2 * width, F32), shaped(rows, 2 * width, BF16)]
        + [shaped(1, w, F32) for w in small],
        [
            pltpu.VMEM((groups, TILE, LANES), F32),
            pltpu.VMEM((groups, 2 * rows, LANES), BF16),
            pltpu.VMEM((groups, 2 * rows, LANES), BF16),
            pltpu.VMEM((TILE, 2 * rows), F32),
        ]
        + [pltpu.VMEM((groups, TILE, LANES), F32)] * 3
        + [pltpu.VMEM((groups, LANES, 2 * rows), F32)] * 2,
        24.0,
        most,
    )


def enc_head(order, meta, sel, s, dq, near, back, middle_grad, params, qkv):
    rows, width = s.shape
    steps = rows // TILE

    def kernel(meta, sel_ref, s_ref, dq_ref, near_ref, back_ref, tm_ref, params_ref, qkv_ref,
               dqkv_ref, grad_ref, gain_ref, shift_ref, total):
        step = pl.program_id(0)

        @pl.when(step == 0)
        def _():
            for ref in (gain_ref, shift_ref, total):
                ref[...] = jnp.zeros_like(ref)

        @pl.when(step < meta[0])
        def _():
            dqkv_ref[:, :width] = dq_ref[...]
            dqkv_ref[:, width:] = (near_ref[...] + back_ref[...].astype(F32)).astype(BF16)
            grad = matmul_nt(dqkv_ref[...], qkv_ref[...])
            unit, inverse = normed_rows(s_ref[...].astype(F32))
            gain_ref[...] += colsum(grad * unit)
            shift_ref[...] += colsum(grad)
            stream_grad = tm_ref[...] + norm_back(grad, unit, inverse, params_ref[:, :width])
            total[...] += matmul_tn(sel_ref[...], stream_grad.astype(BF16))

        @pl.when(step == steps - 1)
        def _():
            grad_ref[...] = total[...].astype(BF16)

    return call(
        order,
        kernel,
        "enc_head",
        meta,
        [live_tile(w) for w in (rows, width, width, 2 * width, 2 * width, width)] + [whole(params.shape), whole(qkv.shape)],
        (sel, s, dq, near, back, middle_grad, params, qkv),
        [live_tile(3 * width), out_whole((rows, width))] + [out_whole((1, width))] * 2,
        [shaped(rows, 3 * width, BF16), shaped(rows, width, BF16)] + [shaped(1, width, F32)] * 2,
        [pltpu.VMEM((rows, width), F32)],
        8.0,
        steps,
    )


class SmallSum:
    def __init__(self, order, scalars, values):
        self.run, self.scalars, self.sizes = order.run, scalars, [value.size for value in values]
        flat = jnp.concatenate([value.reshape(-1) for value in values]).reshape(-1, LANES)
        self.total = flat
        self.due = [(axis, bit) for axis in ("blk", "dp") for bit in range(bits_of(lax.axis_size(axis)))]
        self.send()

    def send(self):
        self.arrived = across(self.total, *self.due.pop(0))

    def add(self):
        def kernel(meta, a_ref, b_ref, out_ref):
            out_ref[...] = a_ref[...] + b_ref[...]

        shape = self.total.shape
        (self.total,) = self.run(
            kernel, "add_small", self.scalars, [whole(shape)] * 2, [self.total, self.arrived], [out_whole(shape)],
            [shaped(*shape, F32)],
        )
        if self.due:
            self.send()

    def parts(self):
        flat, results, offset = self.total.reshape(-1), [], 0
        for size in self.sizes:
            results.append(flat[offset : offset + size])
            offset += size
        return results


def local(
    patches,
    visible,
    padding,
    field_ids,
    enc_gain_a,
    enc_shift_a,
    enc_qkv,
    enc_out,
    enc_out_bias,
    enc_gain_b,
    enc_shift_b,
    enc_up,
    enc_up_bias,
    enc_down,
    enc_down_bias,
    embed_map,
    embed_bias,
    mask_token,
    dec_gain_a,
    dec_shift_a,
    dec_qkv,
    dec_out,
    dec_out_bias,
    dec_gain_b,
    dec_shift_b,
    dec_up,
    dec_up_bias,
    dec_down,
    dec_down_bias,
    cotangent,
):
    rows = patches.shape[0]
    tiles_most = rows // TILE
    raw = [value.reshape(1, rows) for value in (visible, padding, field_ids)]
    far_raw = [across(value, "blk", 0) for value in raw]
    counts = jnp.stack([jnp.sum(raw[0]), jnp.sum(far_raw[0])]).astype(jnp.int32)
    meta = jnp.clip((counts + TILE - 1) // TILE, 1, tiles_most)

    def joined(*values):
        total, offset = sum(value.size for value in values), 0
        row = jnp.zeros((total,), F32)
        for value in values:
            row = row + jnp.pad(value.astype(F32), (offset, total - offset - value.size))
            offset += value.size
        return row.reshape(1, total)

    enc_params = joined(
        enc_gain_a, enc_shift_a, enc_out_bias, enc_gain_b, enc_shift_b, enc_up_bias, enc_down_bias, embed_bias
    )
    dec_params = joined(
        dec_gain_a, dec_shift_a, dec_out_bias, dec_gain_b, dec_shift_b, dec_up_bias, dec_down_bias, mask_token
    )

    order = Order()
    shards = min(16, lax.axis_size("dp"))
    spots = jnp.stack([lax.axis_index("dp") & (shards - 1), lax.axis_index("blk")]).astype(jnp.int32)
    de, dd = enc_qkv.shape[0], dec_qkv.shape[0]
    rd, re = dd // shards, de // shards

    sel, code, far_code, label, marks, far_marks, columns, s, n1, q, kv = enc_in(order, meta, patches, raw, far_raw, enc_params, enc_qkv)
    far_kv = across(kv, "blk", 0)
    o, totals, m, n2, g, slope, low, lift_high, lift_low = enc_main(
        order, meta, s, q, kv, far_kv, label, code, far_code, enc_params, enc_out, enc_up, enc_down, embed_map, HE
    )
    start, dn1, dq_rows, dkv = dec_in(order, meta, sel, lift_high, lift_low, columns, dec_params, dec_qkv)
    far_dkv = across(dkv, "blk", 0)
    (decoded, d_o, d_n2, d_g, d_ub, d_mb, d_tm, d_dq, d_near, d_back, d_outb, d_gainb, d_shiftb, d_upb, d_downb) = dec_main(
        order, meta, start, dq_rows, dkv, far_dkv, columns, marks, far_marks, cotangent, dec_params, dec_out, dec_up, dec_down, HD
    )
    d_back = across(d_back, "blk", 0)

    def bundle(bits, *entries):
        return Bundle(order, bits, spots, meta, [Entry(*entry) for entry in entries])

    dec = bundle(
        (0, 1, 2, 3),
        ("wide", d_n2, d_ub, rd, 4, dd // 2, dec_up.shape, False),
        ("tall", d_g, cotangent, rd, 4, dd // 2, dec_down.shape, False),
        ("wide", d_o, d_mb, rd, 1, dd // 2, dec_out.shape, False),
    )
    dec.weigh()
    d_dqkv, lb, d_gaina, d_shifta, embed_b, token_grad = dec_head(
        order, meta, start, d_dq, d_near, d_back, d_tm, columns, dec_params, dec_qkv
    )
    dec.halve()
    (lbc, tb, ub, mb, tm, dq, near, back, outb, gainb, shiftb, upb, downb) = enc_back(
        order, meta, sel, lb, slope, m, q, kv, far_kv, o, totals, label, code, far_code,
        enc_params, enc_out, enc_up, enc_down, embed_map, HE,
    )
    back = across(back, "blk", 0)
    dec.halve()
    enc_a = bundle(
        (2, 3, 0, 1),
        ("wide", n2, ub, re, 4, de // 2, enc_up.shape, True),
        ("wide", o, mb, re, 1, de // 2, enc_out.shape, True),
    )
    enc_b = bundle(
        (1, 2, 3, 0),
        ("tall", g, tb, re, 4, de // 2, enc_down.shape, True),
        ("wide", low, lbc, re, 1, dd // 2, embed_map.shape, True),
    )
    enc_a.weigh()
    enc_b.weigh()
    enc_a.halve()
    dqkv, patches_grad, gaina, shifta = enc_head(order, meta, sel, s, dq, near, back, tm, enc_params, enc_qkv)
    enc_b.halve()
    enc_c = bundle(
        (0, 1, 2, 3),
        ("wide", n1, dqkv, re, 3, de // 2, enc_qkv.shape, True),
        ("wide", dn1, d_dqkv, rd, 3 * dd // de, de // 2, dec_qkv.shape, False),
    )
    enc_c.weigh()
    dec.halve()
    small = SmallSum(
        order, spots,
        [gaina, shifta, outb, gainb, shiftb, upb, downb, embed_b, token_grad]
        + [d_gaina, d_shifta, d_outb, d_gainb, d_shiftb, d_upb, d_downb],
    )
    encs = (enc_a, enc_b, enc_c)
    enc_a.halve()
    enc_c.halve()
    enc_b.halve()
    dec.halve()
    small.add()
    enc_a.halve()
    enc_b.halve()
    enc_c.halve()
    dec.own()
    small.add()
    enc_a.halve()
    enc_b.halve()
    enc_c.halve()
    dec.join()
    small.add()
    enc_a.own()
    enc_b.own()
    enc_c.halve()
    dec.join()
    small.add()
    enc_a.join()
    enc_b.join()
    enc_c.own()
    dec.join()
    small.add()
    enc_a.join()
    enc_b.join()
    enc_c.join()
    dec.finish()
    enc_a.join()
    enc_b.join()
    enc_c.join()
    g_dec_up, g_dec_down, g_dec_out = dec.place()
    enc_c.join()
    for each in encs:
        each.finish()
    g_enc_up, g_enc_out = enc_a.place()
    g_enc_down, g_embed = enc_b.place()
    g_enc_qkv, g_dec_qkv = enc_c.place()
    small = small.parts()
    return (
        (decoded, patches_grad)
        + (small[0], small[1], g_enc_qkv, g_enc_out, small[2], small[3], small[4])
        + (g_enc_up, small[5], g_enc_down, small[6], g_embed, small[7], small[8])
        + (small[9], small[10], g_dec_qkv, g_dec_out, small[11], small[12], small[13])
        + (g_dec_up, small[14], g_dec_down, small[15])
    )


def solution(mesh):
    return jax.shard_map(
        local,
        mesh=mesh,
        in_specs=(
            P(("dp", "blk"), None),
            P(("dp", "blk")),
            P(("dp", "blk")),
            P(("dp", "blk")),
            P(),
            P(),
            P(),
            P(),
            P(),
            P(),
            P(),
            P(),
            P(),
            P(),
            P(),
            P(),
            P(),
            P(),
            P(),
            P(),
            P(),
            P(),
            P(),
            P(),
            P(),
            P(),
            P(),
            P(),
            P(),
            P(("dp", "blk"), None),
        ),
        out_specs=(
            P(("dp", "blk"), None),
            P(("dp", "blk"), None),
            P(),
            P(),
            P(),
            P(),
            P(),
            P(),
            P(),
            P(),
            P(),
            P(),
            P(),
            P(),
            P(),
            P(),
            P(),
            P(),
            P(),
            P(),
            P(),
            P(),
            P(),
            P(),
            P(),
            P(),
            P(),
        ),
        check_vma=False,
    )
```

```python
import math

import jax
import jax.numpy as jnp
from jax import lax
from jax.experimental import pallas as pl
from jax.experimental.pallas import tpu as pltpu
from jax.sharding import PartitionSpec as P

HE = 12
HD = 16
TILE = 256
VMEM_LIMIT = 60 * 1024 * 1024
SMALL_LIMIT = 24 * 1024 * 1024
FLOPS_PER_MICRO, BYTES_PER_MICRO = 1.15e9, 3.6e6


epsilon = 1e-06


def matmul(left_side, right_side):
    return jnp.dot(left_side, right_side, preferred_element_type=jnp.float32)


def matmul_tn(left_side, right_side):
    return lax.dot_general(
        left_side, right_side, (((0,), (0,)), ((), ())), preferred_element_type=jnp.float32
    )


def matmul_nt(left_side, right_side):
    return lax.dot_general(
        left_side, right_side, (((1,), (1,)), ((), ())), preferred_element_type=jnp.float32
    )


def bits_of(count):
    return count.bit_length() - 1


def across(value, axis, bit):
    count = lax.axis_size(axis)
    return lax.ppermute(value, axis, [(i, i ^ (1 << bit)) for i in range(count)])


def cost(micros):
    return pl.CostEstimate(
        flops=int(micros * FLOPS_PER_MICRO), bytes_accessed=int(micros * BYTES_PER_MICRO), transcendentals=0
    )


TOKEN = jax.ShapeDtypeStruct((8, 128), jnp.float32)


class Order:
    def __init__(self):
        self.token = None

    def run(self, kernel, name, scalars, in_specs, operands, out_specs, out_shape, scratch=(), micros=1.0, steps=1, limit=VMEM_LIMIT):
        count = len(in_specs)
        if self.token is not None:
            in_specs = [*in_specs, pl.BlockSpec(memory_space=pl.ANY)]
            operands = [*operands, self.token]
        more = len(in_specs) - count

        outs = len(out_specs)

        def body(meta, *refs):
            rest = refs[count + more :]
            kernel(meta, *refs[:count], *rest[:outs], *rest[outs + 1 :])

        out_specs = [*out_specs, pl.BlockSpec(memory_space=pl.ANY)]
        results = pl.pallas_call(
            body,
            out_shape=[*out_shape, TOKEN],
            grid_spec=pltpu.PrefetchScalarGridSpec(
                num_scalar_prefetch=1, grid=(steps,), in_specs=in_specs, out_specs=out_specs, scratch_shapes=list(scratch)
            ),
            compiler_params=pltpu.CompilerParams(vmem_limit_bytes=limit),
            cost_estimate=cost(micros),
            name=name,
        )(scalars, *operands)
        self.token = results[-1]
        return results[:-1]

    def run_small(self, kernel, name, operands, out_shape, micros=12.0, scalars=None, out_specs=None, scratch=()):
        count, outs = len(operands), len(out_shape)
        in_specs = [pl.BlockSpec(memory_space=pltpu.VMEM)] * count
        first = []
        if scalars is not None:
            in_specs, first = [pl.BlockSpec(memory_space=pltpu.SMEM), *in_specs], [scalars]
        if self.token is not None:
            in_specs = [*in_specs, pl.BlockSpec(memory_space=pl.ANY)]
            operands = [*operands, self.token]
        used = count + len(first)

        def body(*refs):
            rest = refs[len(in_specs) :]
            kernel(*refs[:used], *rest[:outs], *rest[outs + 1 :])

        out_specs = out_specs or [pl.BlockSpec(memory_space=pltpu.VMEM)] * outs
        results = pl.pallas_call(
            body,
            out_shape=[*out_shape, TOKEN],
            in_specs=in_specs,
            out_specs=[*out_specs, pl.BlockSpec(memory_space=pl.ANY)],
            scratch_shapes=list(scratch),
            compiler_params=pltpu.CompilerParams(vmem_limit_bytes=SMALL_LIMIT),
            cost_estimate=cost(micros),
            name=name,
        )(*first, *operands)
        self.token = results[-1]
        return results[:-1]


class Entry:
    def __init__(self, kind, lhs, rhs, r, n, width, shape, counted):
        self.kind, self.lhs, self.rhs, self.r, self.n = kind, lhs, rhs, r, n
        self.width, self.shape, self.counted = width, shape, counted


class Bundle:
    def __init__(self, order, bits, spots, tiles, entries):
        self.order, self.run, self.entries = order, order.run, entries
        self.shards = min(16, lax.axis_size("dp"))
        self.bits = [bit for bit in bits if bit < bits_of(self.shards)]
        self.spots, self.tiles = spots, tiles
        self.width = max(entry.width for entry in entries)
        self.firsts, self.bases, first, base = [], [], 0, 0
        for entry in entries:
            self.firsts.append(first)
            self.bases.append(base)
            first += entry.n
            base += entry.n * entry.r
        self.steps, self.rows = first, base

    def block(self, index_map):
        return pl.BlockSpec((1, self.rows, self.width), index_map)

    def shaped(self, count):
        return jax.ShapeDtypeStruct((count, self.rows, self.width), jnp.bfloat16)

    def size(self, count):
        return 2 * count * self.rows * self.width

    def spot_of(self, index):
        spot = jnp.int32(0)
        for at, bit in enumerate(self.bits):
            spot = spot | ((lax.shift_right_logical(index, bit) & 1) << (len(self.bits) - 1 - at))
        return spot

    def weigh(self):
        entries, shards, width = self.entries, self.shards, self.width
        token_rows = entries[0].lhs.shape[0]
        tallest = max(shards * entry.r for entry in entries)

        def unit_work(entry, offset, unit, lhs_ref, keep_ref, send_ref, kept_ref, sent_ref, turned, spot, live):
            r, n, height, span = entry.r, entry.n, shards * entry.r, entry.width

            def rows_of(ref, count):
                value = ref[:count, :]
                if count > TILE and entry.counted:
                    value = jnp.where(iota(value.shape, 0) < live * TILE, value.astype(F32), 0.0).astype(BF16)
                return value

            def work(count):
                def turn():
                    turned[:height, :count] = rows_of(lhs_ref, count).T

                if entry.kind == "wide":
                    pl.when(unit == 0)(turn)
                else:
                    turn()
                for rhs_ref, out_ref in ((send_ref, sent_ref), (keep_ref, kept_ref)):
                    whole_unit = matmul(turned[:height, :count], rows_of(rhs_ref, count)).astype(BF16)
                    if entry.kind == "wide":
                        at = pl.ds(pl.multiple_of(offset + unit * r, 16), r)
                        for shard in range(shards):
                            target = self.spot_of(lax.bitwise_xor(jnp.int32(shard), spot))
                            out_ref[target, at, :span] = whole_unit[shard * r : (shard + 1) * r]
                            if span < width:
                                out_ref[target, at, span:] = jnp.zeros((r, width - span), BF16)
                    else:
                        each, tall = shards // n, n * r
                        for inner in range(each):
                            target = self.spot_of(lax.bitwise_xor(unit * each + inner, spot))
                            out_ref[target, offset : offset + tall, :span] = whole_unit[inner * tall : (inner + 1) * tall]

            if entry.counted:
                pl.when(live == 1)(lambda: work(TILE))
                pl.when(live > 1)(lambda: work(token_rows))
            else:
                work(token_rows)

        def kernel(meta, *refs):
            sent_ref, kept_ref, turned = refs[-3:]
            step = pl.program_id(0)
            for index, entry in enumerate(entries):
                first = self.firsts[index]

                @pl.when((step >= first) & (step < first + entry.n))
                def _(index=index, entry=entry, first=first):
                    ins = refs[3 * index : 3 * index + 3]
                    unit_work(entry, self.bases[index], step - first, *ins, kept_ref, sent_ref, turned, meta[0], meta[2])

        in_specs, operands = [], []
        for first, entry in zip(self.firsts, entries):
            n, height, span = entry.n, shards * entry.r, entry.width

            def unit_of(step, first=first, n=n):
                return jnp.clip(step - first, 0, n - 1)

            if entry.kind == "wide":
                in_specs.append(pl.BlockSpec((token_rows, height), lambda step, meta: (0, 0)))
                for flip in (0, 1):
                    in_specs.append(
                        pl.BlockSpec(
                            (token_rows, span),
                            lambda step, meta, n=n, unit_of=unit_of, flip=flip: (0, (meta[1] ^ flip) * n + unit_of(step)),
                        )
                    )
            else:
                in_specs.append(pl.BlockSpec((token_rows, height), lambda step, meta, unit_of=unit_of: (0, unit_of(step))))
                for flip in (0, 1):
                    in_specs.append(pl.BlockSpec((token_rows, span), lambda step, meta, flip=flip: (0, meta[1] ^ flip)))
            operands += [entry.lhs, entry.rhs, entry.rhs]
        shape = (shards, self.rows, width)
        sent, kept = self.run(
            kernel,
            "weight_grads",
            jnp.concatenate([self.spots, self.tiles[:1]]),
            in_specs,
            operands,
            [pl.BlockSpec(shape, lambda step, meta: (0, 0, 0))] * 2,
            [self.shaped(shards)] * 2,
            [pltpu.VMEM((tallest, token_rows), BF16)],
            micros=5.0,
            steps=self.steps,
        )
        self.terms = (kept, across(sent, "blk", 0))
        self.due = list(self.bits)

    def halve(self):
        bit = self.due.pop(0)
        first, second = self.terms
        count = first.shape[0] // 2

        def kernel(a_ref, b_ref, sent_ref, stay_ref):
            for base, target in ((count, sent_ref), (0, stay_ref)):

                def add(index, carry, base=base, target=target):
                    target[index] = (a_ref[base + index].astype(F32) + b_ref[base + index].astype(F32)).astype(BF16)
                    return carry

                lax.fori_loop(0, count, add, 0)

        sent, stay = self.order.run_small(
            kernel, "halve", [first, second], [self.shaped(count)] * 2
        )
        self.terms = (stay, across(sent, "dp", bit))

    def own(self):
        def kernel(a_ref, b_ref, out_ref):
            out_ref[...] = (a_ref[...].astype(F32) + b_ref[...].astype(F32)).astype(BF16)

        def add(a, b):
            return self.order.run_small(kernel, "own", [a, b], [self.shaped(1)])[0]

        total = add(*self.terms)
        for bit in range(bits_of(self.shards), bits_of(lax.axis_size("dp"))):
            total = add(total, across(total, "dp", bit))
        self.due = list(reversed(self.bits))
        self.spread(total)

    def spread(self, held):
        bit = self.due.pop(0)
        self.held = (held, across(held, "dp", bit))

    def join(self):
        count = self.held[0].shape[0]

        def kernel(a_ref, b_ref, out_ref):
            out_ref[:count] = a_ref[...]
            out_ref[count:] = b_ref[...]

        (held,) = self.order.run_small(
            kernel, "join", list(self.held), [self.shaped(2 * count)]
        )
        self.spread(held)

    def finish(self):
        self.other = [across(held, "blk", 0) for held in self.held]

    def place(self):
        entries, shards, bits, slots = self.entries, self.shards, self.bits, 4
        half_count = shards // 2
        heights = [entry.r if entry.kind == "wide" else entry.n * entry.r for entry in entries]
        count = len(entries)

        def kernel(meta, *refs):
            sources = refs[:4]
            outs, stages, sems = refs[4 : 4 + count], refs[4 + count : 4 + 2 * count], refs[-1]
            side = meta[1]

            def copies(slot, row_block):
                return [
                    pltpu.make_async_copy(
                        stage.at[slot],
                        out_ref.at[pl.ds(pl.multiple_of(row_block * height, 8), height), :],
                        sems.at[index, slot],
                    )
                    for index, (stage, out_ref, height) in enumerate(zip(stages, outs, heights))
                ]

            for upper in range(2):
                mine, other = sources[upper], sources[2 + upper]

                def one(index, carry, upper=upper, mine=mine, other=other):
                    step = upper * half_count + index
                    slot = lax.rem(step, slots)

                    @pl.when(step >= slots)
                    def _():
                        for copy in copies(slot, 0):
                            copy.wait()

                    for entry, offset, stage in zip(entries, self.bases, stages):
                        span = entry.width
                        for which, source in ((side, mine), (1 - side, other)):
                            for unit in range(entry.n):
                                row = offset + unit * entry.r
                                value = source[index, row : row + entry.r, :span].astype(F32)
                                if entry.kind == "wide":
                                    at = pl.ds(pl.multiple_of((which * entry.n + unit) * span, LANES), span)
                                    stage[slot, :, at] = value
                                else:
                                    at = pl.ds(pl.multiple_of(which * span, LANES), span)
                                    stage[slot, unit * entry.r : (unit + 1) * entry.r, at] = value
                    shard = jnp.int32(0)
                    for at, bit in enumerate(bits):
                        shard = shard | ((lax.shift_right_logical(step, len(bits) - 1 - at) & 1) << bit)
                    for copy in copies(slot, lax.bitwise_xor(shard, meta[0])):
                        copy.start()
                    return carry

                lax.fori_loop(0, half_count, one, 0)
            for step in range(max(shards - slots, 0), shards):
                for copy in copies(step % slots, 0):
                    copy.wait()

        return self.order.run_small(
            kernel,
            "place_shards",
            [self.held[0], self.held[1], *self.other],
            [jax.ShapeDtypeStruct(entry.shape, jnp.float32) for entry in entries],
            scalars=self.spots,
            out_specs=[pl.BlockSpec(memory_space=pl.ANY)] * count,
            scratch=[pltpu.VMEM((slots, height, entry.shape[1]), F32) for height, entry in zip(heights, entries)]
            + [pltpu.SemaphoreType.DMA((count, slots))],
        )


LOG2E = math.log2(math.e)
NEVER = -1e30
LANES = 128
BF16, F32 = jnp.bfloat16, jnp.float32


def colsum(value):
    return jnp.sum(value.astype(F32), axis=0, keepdims=True)


def normed_rows(stream):
    centred = stream - jnp.mean(stream, axis=-1, keepdims=True)
    inverse = lax.rsqrt(jnp.mean(centred * centred, axis=-1, keepdims=True) + epsilon)
    return centred * inverse, inverse


def norm_back(grad, unit, inverse, gain):
    grad = grad * gain
    inner = jnp.mean(grad * unit, axis=-1, keepdims=True)
    return inverse * (grad - jnp.mean(grad, axis=-1, keepdims=True) - unit * inner)


def gelu_pair(u):
    bell = jnp.exp2(u * u * (-0.5 * LOG2E))
    t = 1.0 / (1.0 + (0.3275911 * math.sqrt(0.5)) * jnp.abs(u))
    poly = ((((1.061405429 * t - 1.453152027) * t + 1.421413741) * t - 0.284496736) * t + 0.254829592) * t
    tail = 0.5 * poly * bell
    phi = jnp.where(u < 0, tail, 1.0 - tail)
    return u * phi, phi + u * bell * (1.0 / math.sqrt(2.0 * math.pi))


def iota(shape, axis):
    return lax.broadcasted_iota(jnp.int32, shape, axis)


def fill_groups(target, source):
    for group in range(target.shape[0]):
        target[group] = source[:, group * LANES : (group + 1) * LANES].astype(target.dtype)


def attend_forward(keys, head, q_s, k_s, v_s, mask_ref, o_s, probs=None, inverse_s=None, totals=None):
    groups, rows, _ = q_s.shape
    inside = LANES // head
    factor = head ** (-0.5) * LOG2E
    lanes = iota((rows, LANES), 1)
    which = lax.div(lanes, jnp.int32(head))
    if totals is not None:
        totals[...] = jnp.zeros_like(totals)

    def one_group(group, carry):
        queries = q_s[group]
        key_rows = k_s[group, :keys, :]
        values = v_s[group, :keys, :]
        blended = jnp.zeros((rows, LANES), F32)
        inverses = jnp.zeros((rows, LANES), F32)
        for h in range(inside):
            own = which == h
            query = jnp.where(own, queries, 0.0).astype(BF16)
            scores = matmul_nt(query, key_rows) * factor + mask_ref[:, :keys]
            top = jnp.max(scores, axis=1, keepdims=True)
            prob = jnp.exp2(scores - top).astype(BF16)
            if probs is not None:
                probs[group * inside + h, :, :keys] = prob
            both = matmul(prob, values)
            inverse = 1.0 / both[:, LANES:]
            blended = jnp.where(own, both[:, :LANES] * inverse, blended)
            if inverse_s is not None:
                inverses = jnp.where(own, inverse, inverses)
            if totals is not None:
                at = lanes == group * inside + h
                totals[...] = jnp.where(at, top + jnp.log2(both[:, LANES:]), totals[...])
        o_s[group] = blended
        if inverse_s is not None:
            inverse_s[group] = inverses
        return carry

    lax.fori_loop(0, groups, one_group, 0)


def attend_backward(keys, head, q_s, k_s, v_s, o_s, ob_s, dq_s, dk_s, dv_s, probs=None, mask_ref=None, totals=None):
    groups, rows, _ = q_s.shape
    inside = LANES // head
    factor = head ** (-0.5) * LOG2E
    lanes = iota((rows, LANES), 1)
    which = lax.div(lanes, jnp.int32(head))

    def one_group(group, carry):
        queries, grads = q_s[group], ob_s[group]
        key_rows = k_s[group, :keys, :]
        values = v_s[group, :keys, :LANES]
        product = grads * o_s[group]
        queries_t = queries.T.astype(BF16)
        grads_t = grads.T.astype(BF16)
        query_grad = jnp.zeros((rows, LANES), F32)
        for h in range(inside):
            own = which == h
            at = slice(h * head, (h + 1) * head)
            inner = jnp.sum(jnp.where(own, product, 0.0), axis=1, keepdims=True)
            if probs is not None:
                prob = probs[group * inside + h, :, :keys]
            else:
                query = jnp.where(own, queries, 0.0).astype(BF16)
                total = jnp.sum(jnp.where(lanes == group * inside + h, totals, 0.0), axis=1, keepdims=True)
                prob = jnp.exp2(matmul_nt(query, key_rows) * factor + (mask_ref[:, :keys] - total)).astype(BF16)
            grad_probs = matmul_nt(jnp.where(own, grads, 0.0).astype(BF16), values)
            score_grad = (prob.astype(F32) * (grad_probs - inner)).astype(BF16)
            query_grad = jnp.where(own, matmul(score_grad, key_rows), query_grad)
            dk_s[group, at, :keys] += matmul(queries_t[at], score_grad)
            dv_s[group, at, :keys] += matmul(grads_t[at], prob)
        dq_s[group] = query_grad
        return carry

    lax.fori_loop(0, groups, one_group, 0)


def whole(shape):
    rank = len(shape)
    return pl.BlockSpec(shape, lambda step, meta: (0,) * rank, pipeline_mode=pl.Buffered(1))


def out_whole(shape):
    rank = len(shape)
    return pl.BlockSpec(shape, lambda step, meta: (0,) * rank)


def row_tile(width):
    return pl.BlockSpec((TILE, width), lambda step, meta: (step, 0))


def live_tile(width):
    return pl.BlockSpec((TILE, width), lambda step, meta: (jnp.minimum(step, meta[0] - 1), 0))


def call(order, kernel, name, meta, in_specs, operands, out_specs, out_shape, scratch, micros, steps):
    return order.run(kernel, name, meta, in_specs, operands, out_specs, out_shape, scratch, micros=micros, steps=steps)


def shaped(rows, width, dtype):
    return jax.ShapeDtypeStruct((rows, width), dtype)


MARKS = 16


def enc_in(order, meta, patches, raw, far_raw, params, qkv):
    rows, width = patches.shape

    def marks_of(seen, padded, label):
        seen, kept, label = seen[...].astype(F32), 1.0 - padded[...].astype(F32), label[...].astype(F32) + 1.0
        row, result = iota((MARKS, rows), 0), jnp.zeros((MARKS, rows), F32)
        for index, value in enumerate((seen * kept * label, label, seen, kept * label)):
            result = jnp.where(row == index, value, result)
        return result

    def kernel(meta, patches_ref, *refs):
        raw_refs, far_refs, (params_ref, qkv_ref) = refs[:3], refs[3:6], refs[6:8]
        sel_ref, code_ref, far_code_ref, label_ref, marks_ref, far_marks_ref, columns_ref, s_ref, n_ref, q_ref, kv_ref, place_s = refs[8:]
        step = pl.program_id(0)

        @pl.when(step == 0)
        def _():
            below = (iota((rows, rows), 0) <= iota((rows, rows), 1)).astype(F32).astype(BF16)
            for index, (source, target) in enumerate(((raw_refs, marks_ref), (far_refs, far_marks_ref))):
                marks = marks_of(*source)
                target[...] = marks
                place = matmul(marks.astype(BF16), below)[2:3, :]
                place_s[index : index + 1, :] = jnp.where(marks[2:3, :] > 0, place - 1.0, -1.0)
            columns_ref[...] = marks_ref[...].T

        @pl.when(step < jnp.maximum(meta[0], meta[1]))
        def _():
            target = (step * TILE + iota((TILE, rows), 0)).astype(F32)
            sel = jnp.where(target == place_s[0:1, :], 1.0, 0.0).astype(BF16)
            far_sel = jnp.where(target == place_s[1:2, :], 1.0, 0.0).astype(BF16)
            sel_ref[...] = sel
            own_marks = marks_ref[...].astype(BF16)
            code_ref[...] = matmul_nt(own_marks, sel)
            far_code_ref[...] = matmul_nt(far_marks_ref[...].astype(BF16), far_sel)
            label_ref[...] = matmul_nt(sel, own_marks)

        @pl.when(step < meta[0])
        def _():
            stream = matmul(sel_ref[...], patches_ref[...])
            s_ref[...] = stream.astype(BF16)
            unit, _ = normed_rows(stream)
            normed = (unit * params_ref[:, :width] + params_ref[:, width : 2 * width]).astype(BF16)
            n_ref[...] = normed
            q_ref[...] = matmul(normed, qkv_ref[:, :width]).astype(BF16)
            kv_ref[...] = matmul(normed, qkv_ref[:, width:]).astype(BF16)

    def last_tile(step, meta):
        return jnp.minimum(step, jnp.maximum(meta[0], meta[1]) - 1)

    lane_tile = pl.BlockSpec((MARKS, TILE), lambda step, meta: (0, last_tile(step, meta)))

    def tile(size):
        return pl.BlockSpec((TILE, size), lambda step, meta: (last_tile(step, meta), 0))

    operands = (patches, *raw, *far_raw, params, qkv)
    return call(
        order,
        kernel,
        "enc_in",
        meta,
        [whole(value.shape) for value in operands],
        operands,
        [tile(rows), lane_tile, lane_tile, tile(MARKS), out_whole((MARKS, rows)), out_whole((MARKS, rows)), out_whole((rows, MARKS))]
        + [live_tile(w) for w in (width, width, width, 2 * width)],
        [shaped(rows, rows, BF16), shaped(MARKS, rows, F32), shaped(MARKS, rows, F32), shaped(rows, MARKS, F32)]
        + [shaped(MARKS, rows, F32), shaped(MARKS, rows, F32), shaped(rows, MARKS, F32)]
        + [shaped(rows, w, BF16) for w in (width, width, width, 2 * width)],
        [pltpu.VMEM((8, rows), F32)],
        7.0,
        rows // TILE,
    )


def spread_keys(count, tiles, kv_ref, far_ref, far_tiles, k_s, v_s):
    size = count * TILE
    width = kv_ref.shape[1] // 2
    for source, live, base in ((kv_ref, tiles, 0), (far_ref, far_tiles, size)):
        ok = iota((size, LANES), 0) < live * TILE
        for group in range(width // LANES):
            at = slice(group * LANES, (group + 1) * LANES)
            value_at = slice(width + group * LANES, width + (group + 1) * LANES)
            k_s[group, base : base + size, :] = jnp.where(ok, source[:size, at].astype(F32), 0.0).astype(BF16)
            v_s[group, base : base + size, :LANES] = jnp.where(ok, source[:size, value_at].astype(F32), 0.0).astype(BF16)
            if v_s.shape[2] > LANES:
                v_s[group, base : base + size, LANES:] = jnp.ones((size, v_s.shape[2] - LANES), BF16)


def write_mask(mask_ref, label, code, far_code, size, step):
    shape = (label.shape[0], size)
    near = (label == code) | (iota(shape, 1) == step * TILE + iota(shape, 0))
    mask_ref[:, :size] = jnp.where(near, 0.0, NEVER)
    mask_ref[:, size : 2 * size] = jnp.where(label == far_code, 0.0, NEVER)


def enc_main(order, meta, s, q, kv, far_kv, label, code, far_code, params, out, up, down, embed, heads):
    rows, width = s.shape
    wide, lifted_width = up.shape[1], embed.shape[1]
    groups, head, most = width // LANES, width // heads, rows // TILE
    part = width

    def kernel(meta, s_ref, q_ref, kv_ref, far_ref, label_ref, code_ref, far_code_ref, params_ref, out_w, up_w, down_w, embed_w,
               o_ref, tot_ref, m_ref, n_ref, g_ref, gp_ref, e_ref, hi_ref, lo_ref, q_s, k_s, v_s, mask_s, o_s):
        step = pl.program_id(0)
        tiles, far_tiles = meta[0], meta[1]
        count = jnp.maximum(tiles, far_tiles)

        def param(start, size):
            return params_ref[:, start : start + size]

        @pl.when(step < tiles)
        def _():
            fill_groups(q_s, q_ref)
            for size in range(1, most + 1):

                @pl.when(count == size)
                def _(size=size):
                    @pl.when(step == 0)
                    def _():
                        spread_keys(size, tiles, kv_ref, far_ref, far_tiles, k_s, v_s)

                    span = size * TILE
                    write_mask(mask_s, label_ref[:, 1:2], code_ref[0:1, :span], far_code_ref[0:1, :span], span, step)
                    attend_forward(2 * span, head, q_s, k_s, v_s, mask_s, o_s, totals=tot_ref)

            for group in range(groups):
                o_ref[:, group * LANES : (group + 1) * LANES] = o_s[group].astype(BF16)
            middle = s_ref[...].astype(F32) + matmul(o_ref[...], out_w[...]) + param(2 * width, width)
            m_ref[...] = middle
            unit, _ = normed_rows(middle)
            normed = (unit * param(3 * width, width) + param(4 * width, width)).astype(BF16)
            n_ref[...] = normed
            encoded = middle + param(5 * width + wide, width)
            for j in range(0, wide, part):
                u = matmul(normed, up_w[:, j : j + part]) + param(5 * width + j, part)
                g, slope = gelu_pair(u)
                g = g.astype(BF16)
                g_ref[:, j : j + part] = g
                gp_ref[:, j : j + part] = slope.astype(BF16)
                encoded = encoded + matmul(g, down_w[j : j + part, :])
            low = encoded.astype(BF16)
            e_ref[...] = low
            lifted = matmul(low, embed_w[...]) + param(6 * width + wide, lifted_width)
            high = lifted.astype(BF16)
            hi_ref[...] = high
            lo_ref[...] = (lifted - high.astype(F32)).astype(BF16)

    tall = label.shape[1]
    return call(
        order,
        kernel,
        "enc_main",
        meta,
        [live_tile(width), live_tile(width), whole(kv.shape), whole(kv.shape), live_tile(tall), whole(code.shape), whole(code.shape)]
        + [whole(value.shape) for value in (params, out, up, down, embed)],
        (s, q, kv, far_kv, label, code, far_code, params, out, up, down, embed),
        [live_tile(w) for w in (width, LANES, width, width, wide, wide, width, lifted_width, lifted_width)],
        [shaped(rows, width, BF16), shaped(rows, LANES, F32), shaped(rows, width, F32), shaped(rows, width, BF16)]
        + [shaped(rows, wide, BF16)] * 2 + [shaped(rows, width, BF16)] + [shaped(rows, lifted_width, BF16)] * 2,
        [
            pltpu.VMEM((groups, TILE, LANES), F32),
            pltpu.VMEM((groups, 2 * rows, LANES), BF16),
            pltpu.VMEM((groups, 2 * rows, 2 * LANES), BF16),
            pltpu.VMEM((TILE, 2 * rows), F32),
            pltpu.VMEM((groups, TILE, LANES), F32),
        ],
        20.0,
        most,
    )


def dec_in(order, meta, sel, high, low, columns, params, qkv):
    rows, width = high.shape
    tall = columns.shape[1]

    def kernel(meta, sel_ref, hi_ref, lo_ref, col_ref, params_ref, qkv_ref, start_ref, n_ref, q_ref, kv_ref, total):
        total[...] = jnp.zeros_like(total)

        def add(tile, carry):
            at = pl.ds(pl.multiple_of(tile * TILE, TILE), TILE)
            total[...] += matmul_tn(sel_ref[at, :], hi_ref[at, :]) + matmul_tn(sel_ref[at, :], lo_ref[at, :])
            return carry

        lax.fori_loop(0, meta[0], add, 0)
        start = jnp.where(col_ref[:, 2:3] > 0, total[...], params_ref[:, params.shape[1] - width :])
        start_ref[...] = start
        unit, _ = normed_rows(start)
        normed = (unit * params_ref[:, :width] + params_ref[:, width : 2 * width]).astype(BF16)
        n_ref[...] = normed
        q_ref[...] = matmul(normed, qkv_ref[:, :width]).astype(BF16)
        kv_ref[...] = matmul(normed, qkv_ref[:, width:]).astype(BF16)

    return call(
        order,
        kernel,
        "dec_in",
        meta,
        [pl.BlockSpec((rows, TILE), lambda step, meta: (0, step)), whole(high.shape), whole(low.shape), row_tile(tall)]
        + [whole(value.shape) for value in (params, qkv)],
        (sel, high, low, columns, params, qkv),
        [row_tile(w) for w in (width, width, width, 2 * width)],
        [shaped(rows, width, F32)] + [shaped(rows, w, BF16) for w in (width, width, 2 * width)],
        [pltpu.VMEM((TILE, width), F32)],
        7.0,
        rows // TILE,
    )


def give_key_grads(size, scale, dk_s, dv_s, near_ref, far_ref):
    groups = dk_s.shape[0]
    for index, (source, factor) in enumerate(((dk_s, scale), (dv_s, 1.0))):
        for group in range(groups):
            at = slice((index * groups + group) * LANES, (index * groups + group + 1) * LANES)
            near_ref[:size, at] = source[group, :, :size].T * factor
            far_ref[:size, at] = (source[group, :, size : 2 * size].T * factor).astype(BF16)


def dec_main(order, meta, start, q, kv, far_kv, columns, marks, far_marks, cotangent, params, out, up, down, heads):
    rows, width = start.shape
    wide = up.shape[1]
    groups, head, steps = width // LANES, width // heads, rows // TILE
    part = width
    tall = columns.shape[1]

    def kernel(meta, start_ref, q_ref, kv_ref, far_ref, col_ref, marks_ref, far_marks_ref, cot_ref, params_ref, out_w, up_w, down_w,
               dec_ref, o_ref, n_ref, g_ref, ub_ref, mb_ref, tm_ref, dq_ref, near_ref, back_ref,
               outb_ref, gainb_ref, shiftb_ref, upb_ref, downb_ref,
               q_s, k_s, v_s, mask_s, probs, o_s, inv_s, ob_s, dq_s, dk_s, dv_s, slope_s):
        step = pl.program_id(0)

        def param(begin, size):
            return params_ref[:, begin : begin + size]

        @pl.when(step == 0)
        def _():
            spread_keys(steps, steps, kv_ref, far_ref, steps, k_s, v_s)
            for ref in (dk_s, dv_s, outb_ref, gainb_ref, shiftb_ref, upb_ref, downb_ref):
                ref[...] = jnp.zeros_like(ref)

        fill_groups(q_s, q_ref)
        write_mask(mask_s, col_ref[:, 1:2], marks_ref[3:4, :], far_marks_ref[3:4, :], rows, step)
        attend_forward(2 * rows, head, q_s, k_s, v_s, mask_s, o_s, probs=probs, inverse_s=inv_s)
        for group in range(groups):
            o_ref[:, group * LANES : (group + 1) * LANES] = o_s[group].astype(BF16)
        middle = start_ref[...] + matmul(o_ref[...], out_w[...]) + param(2 * width, width)
        unit, inverse = normed_rows(middle)
        gain_b = param(3 * width, width)
        normed = (unit * gain_b + param(4 * width, width)).astype(BF16)
        n_ref[...] = normed
        decoded = middle + param(5 * width + wide, width)
        for j in range(0, wide, part):
            g, slope = gelu_pair(matmul(normed, up_w[:, j : j + part]) + param(5 * width + j, part))
            g = g.astype(BF16)
            g_ref[:, j : j + part] = g
            slope_s[:, j : j + part] = slope
            decoded = decoded + matmul(g, down_w[j : j + part, :])
        dec_ref[...] = decoded.astype(BF16)
        top = cot_ref[...]
        normed_grad = jnp.zeros((TILE, width), F32)
        for j in range(0, wide, part):
            low = (slope_s[:, j : j + part] * matmul_nt(top, down_w[j : j + part, :])).astype(BF16)
            ub_ref[:, j : j + part] = low
            upb_ref[:, j : j + part] += colsum(low)
            normed_grad = normed_grad + matmul_nt(low, up_w[:, j : j + part])
        downb_ref[...] += colsum(top)
        gainb_ref[...] += colsum(normed_grad * unit)
        shiftb_ref[...] += colsum(normed_grad)
        middle_grad = top.astype(F32) + norm_back(normed_grad, unit, inverse, gain_b)
        tm_ref[...] = middle_grad
        low = middle_grad.astype(BF16)
        mb_ref[...] = low
        outb_ref[...] += colsum(low)
        attended_grad = matmul_nt(low, out_w[...])
        for group in range(groups):
            scaled = attended_grad[:, group * LANES : (group + 1) * LANES] * inv_s[group]
            ob_s[group] = scaled.astype(BF16).astype(F32)
        attend_backward(2 * rows, head, q_s, k_s, v_s, o_s, ob_s, dq_s, dk_s, dv_s, probs=probs)
        scale = head ** (-0.5)
        for group in range(groups):
            dq_ref[:, group * LANES : (group + 1) * LANES] = (dq_s[group] * scale).astype(BF16)

        @pl.when(step == steps - 1)
        def _():
            give_key_grads(rows, scale, dk_s, dv_s, near_ref, back_ref)

    small = [width, width, width, wide, width]
    return call(
        order,
        kernel,
        "dec_main",
        meta,
        [row_tile(width), row_tile(width), whole(kv.shape), whole(kv.shape), row_tile(tall), whole(marks.shape), whole(marks.shape)]
        + [row_tile(width)] + [whole(value.shape) for value in (params, out, up, down)],
        (start, q, kv, far_kv, columns, marks, far_marks, cotangent, params, out, up, down),
        [row_tile(w) for w in (width, width, width, wide, wide, width, width, width)]
        + [out_whole((rows, 2 * width))] * 2 + [out_whole((1, w)) for w in small],
        [shaped(rows, w, BF16) for w in (width, width, width, wide, wide, width)]
        + [shaped(rows, width, F32), shaped(rows, width, BF16), shaped(rows, 2 * width, F32), shaped(rows, 2 * width, BF16)]
        + [shaped(1, w, F32) for w in small],
        [
            pltpu.VMEM((groups, TILE, LANES), F32),
            pltpu.VMEM((groups, 2 * rows, LANES), BF16),
            pltpu.VMEM((groups, 2 * rows, 2 * LANES), BF16),
            pltpu.VMEM((TILE, 2 * rows), F32),
            pltpu.VMEM((heads, TILE, 2 * rows), BF16),
        ]
        + [pltpu.VMEM((groups, TILE, LANES), F32)] * 4
        + [pltpu.VMEM((groups, LANES, 2 * rows), F32)] * 2
        + [pltpu.VMEM((TILE, wide), F32)],
        95.0,
        steps,
    )


def dec_head(order, meta, start, dq, near, back, middle_grad, columns, params, qkv):
    rows, width = start.shape
    tall = columns.shape[1]

    def kernel(meta, start_ref, dq_ref, near_ref, back_ref, tm_ref, col_ref, params_ref, qkv_ref,
               dqkv_ref, lb_ref, gain_ref, shift_ref, bias_ref, token_ref):
        step = pl.program_id(0)

        @pl.when(step == 0)
        def _():
            for ref in (gain_ref, shift_ref, bias_ref, token_ref):
                ref[...] = jnp.zeros_like(ref)

        dqkv_ref[:, :width] = dq_ref[...]
        dqkv_ref[:, width:] = (near_ref[...] + back_ref[...].astype(F32)).astype(BF16)
        grad = matmul_nt(dqkv_ref[...], qkv_ref[...])
        unit, inverse = normed_rows(start_ref[...])
        gain_ref[...] += colsum(grad * unit)
        shift_ref[...] += colsum(grad)
        start_grad = tm_ref[...] + norm_back(grad, unit, inverse, params_ref[:, :width])
        seen = col_ref[:, 2:3] > 0
        token_ref[...] += colsum(jnp.where(seen, 0.0, start_grad))
        low = jnp.where(seen, start_grad, 0.0).astype(BF16)
        lb_ref[...] = low
        bias_ref[...] += colsum(low)

    return call(
        order,
        kernel,
        "dec_head",
        meta,
        [row_tile(width), row_tile(width), row_tile(2 * width), row_tile(2 * width), row_tile(width), row_tile(tall)]
        + [whole(params.shape), whole(qkv.shape)],
        (start, dq, near, back, middle_grad, columns, params, qkv),
        [row_tile(3 * width), row_tile(width)] + [out_whole((1, width))] * 4,
        [shaped(rows, 3 * width, BF16), shaped(rows, width, BF16)] + [shaped(1, width, F32)] * 4,
        [],
        7.0,
        rows // TILE,
    )


def enc_back(order, meta, sel, lb, slope, m, q, kv, far_kv, o, totals, label, code, far_code, params, out, up, down, embed, heads):
    rows, width = m.shape
    wide, lifted_width = up.shape[1], embed.shape[1]
    groups, head, most = width // LANES, width // heads, rows // TILE
    part = width
    tall = label.shape[1]

    def kernel(meta, sel_ref, lb_ref, slope_ref, m_ref, q_ref, kv_ref, far_ref, o_ref, tot_ref, label_ref, code_ref, far_code_ref,
               params_ref, out_w, up_w, down_w, embed_w,
               lbc_ref, tb_ref, ub_ref, mb_ref, tm_ref, dq_ref, near_ref, back_ref,
               outb_ref, gainb_ref, shiftb_ref, upb_ref, downb_ref,
               q_s, k_s, v_s, mask_s, o_s, ob_s, dq_s, dk_s, dv_s):
        step = pl.program_id(0)
        tiles, far_tiles = meta[0], meta[1]
        count = jnp.maximum(tiles, far_tiles)
        scale = head ** (-0.5)

        @pl.when(step == 0)
        def _():
            for ref in (dk_s, dv_s, outb_ref, gainb_ref, shiftb_ref, upb_ref, downb_ref):
                ref[...] = jnp.zeros_like(ref)

        @pl.when(step < tiles)
        def _():
            lb_here = matmul(sel_ref[...], lb_ref[...]).astype(BF16)
            lbc_ref[...] = lb_here
            grad_top = matmul_nt(lb_here, embed_w[...])
            top = grad_top.astype(BF16)
            tb_ref[...] = top
            normed_grad = jnp.zeros((TILE, width), F32)
            for j in range(0, wide, part):
                low = (slope_ref[:, j : j + part].astype(F32) * matmul_nt(top, down_w[j : j + part, :])).astype(BF16)
                ub_ref[:, j : j + part] = low
                upb_ref[:, j : j + part] += colsum(low)
                normed_grad = normed_grad + matmul_nt(low, up_w[:, j : j + part])
            unit, inverse = normed_rows(m_ref[...])
            downb_ref[...] += colsum(top)
            gainb_ref[...] += colsum(normed_grad * unit)
            shiftb_ref[...] += colsum(normed_grad)
            middle_grad = grad_top + norm_back(normed_grad, unit, inverse, params_ref[:, 3 * width : 4 * width])
            tm_ref[...] = middle_grad
            low = middle_grad.astype(BF16)
            mb_ref[...] = low
            outb_ref[...] += colsum(low)
            attended_grad = matmul_nt(low, out_w[...]).astype(BF16)
            fill_groups(ob_s, attended_grad)
            fill_groups(o_s, o_ref)
            fill_groups(q_s, q_ref)
            for size in range(1, most + 1):

                @pl.when(count == size)
                def _(size=size):
                    @pl.when(step == 0)
                    def _():
                        spread_keys(size, tiles, kv_ref, far_ref, far_tiles, k_s, v_s)

                    span = size * TILE
                    write_mask(mask_s, label_ref[:, 1:2], code_ref[0:1, :span], far_code_ref[0:1, :span], span, step)
                    attend_backward(
                        2 * span, head, q_s, k_s, v_s, o_s, ob_s, dq_s, dk_s, dv_s, mask_ref=mask_s, totals=tot_ref[...]
                    )

                    @pl.when(step == tiles - 1)
                    def _():
                        give_key_grads(span, scale, dk_s, dv_s, near_ref, back_ref)

            for group in range(groups):
                dq_ref[:, group * LANES : (group + 1) * LANES] = (dq_s[group] * scale).astype(BF16)

    small = [width, width, width, wide, width]
    return call(
        order,
        kernel,
        "enc_back",
        meta,
        [live_tile(rows), whole(lb.shape), live_tile(wide), live_tile(width), live_tile(width), whole(kv.shape), whole(kv.shape)]
        + [live_tile(width), live_tile(LANES), live_tile(tall), whole(code.shape), whole(code.shape)]
        + [whole(value.shape) for value in (params, out, up, down, embed)],
        (sel, lb, slope, m, q, kv, far_kv, o, totals, label, code, far_code, params, out, up, down, embed),
        [live_tile(w) for w in (lifted_width, width, wide, width, width, width)]
        + [whole((rows, 2 * width))] * 2 + [out_whole((1, w)) for w in small],
        [shaped(rows, w, BF16) for w in (lifted_width, width, wide, width)]
        + [shaped(rows, width, F32), shaped(rows, width, BF16), shaped(rows, 2 * width, F32), shaped(rows, 2 * width, BF16)]
        + [shaped(1, w, F32) for w in small],
        [
            pltpu.VMEM((groups, TILE, LANES), F32),
            pltpu.VMEM((groups, 2 * rows, LANES), BF16),
            pltpu.VMEM((groups, 2 * rows, LANES), BF16),
            pltpu.VMEM((TILE, 2 * rows), F32),
        ]
        + [pltpu.VMEM((groups, TILE, LANES), F32)] * 3
        + [pltpu.VMEM((groups, LANES, 2 * rows), F32)] * 2,
        24.0,
        most,
    )


def enc_head(order, meta, sel, s, dq, near, back, middle_grad, params, qkv):
    rows, width = s.shape
    steps = rows // TILE

    def kernel(meta, sel_ref, s_ref, dq_ref, near_ref, back_ref, tm_ref, params_ref, qkv_ref,
               dqkv_ref, grad_ref, gain_ref, shift_ref, total):
        step = pl.program_id(0)

        @pl.when(step == 0)
        def _():
            for ref in (gain_ref, shift_ref, total):
                ref[...] = jnp.zeros_like(ref)

        @pl.when(step < meta[0])
        def _():
            dqkv_ref[:, :width] = dq_ref[...]
            dqkv_ref[:, width:] = (near_ref[...] + back_ref[...].astype(F32)).astype(BF16)
            grad = matmul_nt(dqkv_ref[...], qkv_ref[...])
            unit, inverse = normed_rows(s_ref[...].astype(F32))
            gain_ref[...] += colsum(grad * unit)
            shift_ref[...] += colsum(grad)
            stream_grad = tm_ref[...] + norm_back(grad, unit, inverse, params_ref[:, :width])
            total[...] += matmul_tn(sel_ref[...], stream_grad.astype(BF16))

        @pl.when(step == steps - 1)
        def _():
            grad_ref[...] = total[...].astype(BF16)

    return call(
        order,
        kernel,
        "enc_head",
        meta,
        [live_tile(w) for w in (rows, width, width, 2 * width, 2 * width, width)] + [whole(params.shape), whole(qkv.shape)],
        (sel, s, dq, near, back, middle_grad, params, qkv),
        [live_tile(3 * width), out_whole((rows, width))] + [out_whole((1, width))] * 2,
        [shaped(rows, 3 * width, BF16), shaped(rows, width, BF16)] + [shaped(1, width, F32)] * 2,
        [pltpu.VMEM((rows, width), F32)],
        8.0,
        steps,
    )


def joined(values):
    total, offset = sum(value.size for value in values), 0
    row = jnp.zeros((total,), F32)
    for value in values:
        row = row + jnp.pad(value.astype(F32), (offset, total - offset - value.size))
        offset += value.size
    return row.reshape(1, total)


class SmallSum:
    def __init__(self, order, values):
        self.order, self.sizes = order, [value.size for value in values]
        sizes = self.sizes

        def kernel(*refs):
            offset = 0
            for ref, size in zip(refs, sizes):
                refs[-1][:, offset : offset + size] = ref[...]
                offset += size

        (self.total,) = order.run_small(kernel, "pack", values, [shaped(1, sum(sizes), F32)])
        self.due = [(axis, bit) for axis in ("blk", "dp") for bit in range(bits_of(lax.axis_size(axis)))]
        self.send()

    def send(self):
        self.arrived = across(self.total, *self.due.pop(0))

    def add(self):
        def kernel(a_ref, b_ref, out_ref):
            out_ref[...] = a_ref[...] + b_ref[...]

        (self.total,) = self.order.run_small(
            kernel, "add_small", [self.total, self.arrived], [shaped(*self.total.shape, F32)]
        )
        if self.due:
            self.send()

    def parts(self):
        flat, results, offset = self.total.reshape(-1), [], 0
        for size in self.sizes:
            results.append(flat[offset : offset + size])
            offset += size
        return results


def local(
    patches,
    visible,
    padding,
    field_ids,
    enc_gain_a,
    enc_shift_a,
    enc_qkv,
    enc_out,
    enc_out_bias,
    enc_gain_b,
    enc_shift_b,
    enc_up,
    enc_up_bias,
    enc_down,
    enc_down_bias,
    embed_map,
    embed_bias,
    mask_token,
    dec_gain_a,
    dec_shift_a,
    dec_qkv,
    dec_out,
    dec_out_bias,
    dec_gain_b,
    dec_shift_b,
    dec_up,
    dec_up_bias,
    dec_down,
    dec_down_bias,
    cotangent,
):
    rows = patches.shape[0]
    tiles_most = rows // TILE
    raw = [value.reshape(1, rows) for value in (visible, padding, field_ids)]
    far_raw = [across(value, "blk", 0) for value in raw]
    counts = jnp.stack([jnp.sum(raw[0]), jnp.sum(far_raw[0])]).astype(jnp.int32)
    meta = jnp.clip((counts + TILE - 1) // TILE, 1, tiles_most)

    enc_params = joined(
        [enc_gain_a, enc_shift_a, enc_out_bias, enc_gain_b, enc_shift_b, enc_up_bias, enc_down_bias, embed_bias]
    )
    dec_params = joined(
        [dec_gain_a, dec_shift_a, dec_out_bias, dec_gain_b, dec_shift_b, dec_up_bias, dec_down_bias, mask_token]
    )

    order = Order()
    shards = min(16, lax.axis_size("dp"))
    spots = jnp.stack([lax.axis_index("dp") & (shards - 1), lax.axis_index("blk")]).astype(jnp.int32)
    de, dd = enc_qkv.shape[0], dec_qkv.shape[0]
    rd, re = dd // shards, de // shards

    sel, code, far_code, label, marks, far_marks, columns, s, n1, q, kv = enc_in(order, meta, patches, raw, far_raw, enc_params, enc_qkv)
    far_kv = across(kv, "blk", 0)
    o, totals, m, n2, g, slope, low, lift_high, lift_low = enc_main(
        order, meta, s, q, kv, far_kv, label, code, far_code, enc_params, enc_out, enc_up, enc_down, embed_map, HE
    )
    start, dn1, dq_rows, dkv = dec_in(order, meta, sel, lift_high, lift_low, columns, dec_params, dec_qkv)
    far_dkv = across(dkv, "blk", 0)
    (decoded, d_o, d_n2, d_g, d_ub, d_mb, d_tm, d_dq, d_near, d_back, d_outb, d_gainb, d_shiftb, d_upb, d_downb) = dec_main(
        order, meta, start, dq_rows, dkv, far_dkv, columns, marks, far_marks, cotangent, dec_params, dec_out, dec_up, dec_down, HD
    )
    d_back = across(d_back, "blk", 0)

    def bundle(bits, *entries):
        return Bundle(order, bits, spots, meta, [Entry(*entry) for entry in entries])

    dec = bundle(
        (1, 0, 2, 3),
        ("wide", d_n2, d_ub, rd, 4, dd // 2, dec_up.shape, False),
        ("tall", d_g, cotangent, rd, 4, dd // 2, dec_down.shape, False),
        ("wide", d_o, d_mb, rd, 1, dd // 2, dec_out.shape, False),
    )
    dec.weigh()
    d_dqkv, lb, d_gaina, d_shifta, embed_b, token_grad = dec_head(
        order, meta, start, d_dq, d_near, d_back, d_tm, columns, dec_params, dec_qkv
    )
    dec.halve()
    (lbc, tb, ub, mb, tm, dq, near, back, outb, gainb, shiftb, upb, downb) = enc_back(
        order, meta, sel, lb, slope, m, q, kv, far_kv, o, totals, label, code, far_code,
        enc_params, enc_out, enc_up, enc_down, embed_map, HE,
    )
    back = across(back, "blk", 0)
    dec.halve()
    enc_a = bundle(
        (0, 1, 2, 3),
        ("wide", n2, ub, re, 4, de // 2, enc_up.shape, True),
        ("wide", o, mb, re, 1, de // 2, enc_out.shape, True),
    )
    enc_b = bundle(
        (1, 0, 2, 3),
        ("tall", g, tb, re, 4, de // 2, enc_down.shape, True),
        ("wide", low, lbc, re, 1, dd // 2, embed_map.shape, True),
    )
    enc_a.weigh()
    enc_b.weigh()
    dec.halve()
    enc_a.halve()
    dqkv, patches_grad, gaina, shifta = enc_head(order, meta, sel, s, dq, near, back, tm, enc_params, enc_qkv)
    enc_b.halve()
    enc_c = bundle(
        (2, 3, 0, 1),
        ("wide", n1, dqkv, re, 3, de // 2, enc_qkv.shape, True),
        ("wide", dn1, d_dqkv, rd, 3 * dd // de, de // 2, dec_qkv.shape, False),
    )
    enc_c.weigh()
    for step in (dec.halve, enc_a.halve, enc_b.halve, enc_c.halve):
        step()
    small = SmallSum(
        order,
        [gaina, shifta, outb, gainb, shiftb, upb, downb, embed_b, token_grad]
        + [d_gaina, d_shifta, d_outb, d_gainb, d_shiftb, d_upb, d_downb],
    )
    for steps in (
        (dec.own, enc_a.halve, enc_b.halve, enc_c.halve, small.add),
        (dec.join, enc_a.halve, enc_b.halve, enc_c.halve, small.add),
        (dec.join, enc_a.own, enc_b.own, enc_c.halve, small.add),
        (dec.join, enc_a.join, enc_b.join, enc_c.own, small.add),
        (dec.finish, enc_a.join, enc_b.join, enc_c.join),
    ):
        for step in steps:
            step()
    g_dec_up, g_dec_down, g_dec_out = dec.place()
    for step in (enc_a.join, enc_b.join, enc_c.join, small.add, enc_a.finish, enc_b.finish, enc_c.join, enc_c.finish):
        step()
    g_enc_up, g_enc_out = enc_a.place()
    g_enc_down, g_embed = enc_b.place()
    g_enc_qkv, g_dec_qkv = enc_c.place()
    small = small.parts()
    return (
        (decoded, patches_grad)
        + (small[0], small[1], g_enc_qkv, g_enc_out, small[2], small[3], small[4])
        + (g_enc_up, small[5], g_enc_down, small[6], g_embed, small[7], small[8])
        + (small[9], small[10], g_dec_qkv, g_dec_out, small[11], small[12], small[13])
        + (g_dec_up, small[14], g_dec_down, small[15])
    )


def solution(mesh):
    return jax.shard_map(
        local,
        mesh=mesh,
        in_specs=(
            P(("dp", "blk"), None),
            P(("dp", "blk")),
            P(("dp", "blk")),
            P(("dp", "blk")),
            P(),
            P(),
            P(),
            P(),
            P(),
            P(),
            P(),
            P(),
            P(),
            P(),
            P(),
            P(),
            P(),
            P(),
            P(),
            P(),
            P(),
            P(),
            P(),
            P(),
            P(),
            P(),
            P(),
            P(),
            P(),
            P(("dp", "blk"), None),
        ),
        out_specs=(
            P(("dp", "blk"), None),
            P(("dp", "blk"), None),
            P(),
            P(),
            P(),
            P(),
            P(),
            P(),
            P(),
            P(),
            P(),
            P(),
            P(),
            P(),
            P(),
            P(),
            P(),
            P(),
            P(),
            P(),
            P(),
            P(),
            P(),
            P(),
            P(),
            P(),
            P(),
        ),
        check_vma=False,
    )
```

```python
import math

import jax
import jax.numpy as jnp
from jax import lax
from jax.experimental import pallas as pl
from jax.experimental.pallas import tpu as pltpu
from jax.sharding import PartitionSpec as P

HE = 12
HD = 16
TILE = 256
VMEM_LIMIT = 60 * 1024 * 1024
DEC_BITS = (1, 2, 0, 3)
ENC_BITS = ((2, 1, 0, 3), (1, 0, 2, 3), (0, 1, 2, 3))
STEPS = "dcdabdcdabadbcabacdbacdscbsascsbscsaabcbc"
WEIGHT_LIMIT = 40 * 1024 * 1024
SMALL_LIMIT = 24 * 1024 * 1024
FLOPS_PER_MICRO, BYTES_PER_MICRO = 1.15e9, 3.6e6


epsilon = 1e-06


def matmul(left_side, right_side):
    return jnp.dot(left_side, right_side, preferred_element_type=jnp.float32)


def matmul_tn(left_side, right_side):
    return lax.dot_general(
        left_side, right_side, (((0,), (0,)), ((), ())), preferred_element_type=jnp.float32
    )


def matmul_nt(left_side, right_side):
    return lax.dot_general(
        left_side, right_side, (((1,), (1,)), ((), ())), preferred_element_type=jnp.float32
    )


def bits_of(count):
    return count.bit_length() - 1


def across(value, axis, bit):
    count = lax.axis_size(axis)
    return lax.ppermute(value, axis, [(i, i ^ (1 << bit)) for i in range(count)])


def cost(micros):
    return pl.CostEstimate(
        flops=int(micros * FLOPS_PER_MICRO), bytes_accessed=int(micros * BYTES_PER_MICRO), transcendentals=0
    )


TOKEN = jax.ShapeDtypeStruct((8, 128), jnp.float32)


class Order:
    def __init__(self):
        self.token, self.smalls = None, 0

    def run(self, kernel, name, scalars, in_specs, operands, out_specs, out_shape, scratch=(), micros=1.0, steps=1, limit=VMEM_LIMIT):
        count = len(in_specs)
        if self.token is not None:
            in_specs = [*in_specs, pl.BlockSpec(memory_space=pl.ANY)]
            operands = [*operands, self.token]
        more = len(in_specs) - count

        outs = len(out_specs)

        def body(meta, *refs):
            rest = refs[count + more :]
            kernel(meta, *refs[:count], *rest[:outs], *rest[outs + 1 :])

        out_specs = [*out_specs, pl.BlockSpec(memory_space=pl.ANY)]
        results = pl.pallas_call(
            body,
            out_shape=[*out_shape, TOKEN],
            grid_spec=pltpu.PrefetchScalarGridSpec(
                num_scalar_prefetch=1, grid=(steps,), in_specs=in_specs, out_specs=out_specs, scratch_shapes=list(scratch)
            ),
            compiler_params=pltpu.CompilerParams(vmem_limit_bytes=limit),
            cost_estimate=cost(micros),
            name=name,
        )(scalars, *operands)
        self.token = results[-1]
        return results[:-1]

    def run_small(self, kernel, name, operands, out_shape, scalars=None, out_specs=None, scratch=()):
        micros = 40.0 if self.smalls < 8 else 4.0
        self.smalls += 1
        count, outs = len(operands), len(out_shape)
        in_specs = [pl.BlockSpec(memory_space=pltpu.VMEM)] * count
        first = []
        if scalars is not None:
            in_specs, first = [pl.BlockSpec(memory_space=pltpu.SMEM), *in_specs], [scalars]
        if self.token is not None:
            in_specs = [*in_specs, pl.BlockSpec(memory_space=pl.ANY)]
            operands = [*operands, self.token]
        used = count + len(first)

        def body(*refs):
            rest = refs[len(in_specs) :]
            kernel(*refs[:used], *rest[:outs], *rest[outs + 1 :])

        out_specs = out_specs or [pl.BlockSpec(memory_space=pltpu.VMEM)] * outs
        results = pl.pallas_call(
            body,
            out_shape=[*out_shape, TOKEN],
            in_specs=in_specs,
            out_specs=[*out_specs, pl.BlockSpec(memory_space=pl.ANY)],
            scratch_shapes=list(scratch),
            compiler_params=pltpu.CompilerParams(vmem_limit_bytes=SMALL_LIMIT),
            cost_estimate=cost(micros),
            name=name,
        )(*first, *operands)
        self.token = results[-1]
        return results[:-1]


class Entry:
    def __init__(self, kind, lhs, rhs, r, n, width, shape, counted):
        self.kind, self.lhs, self.rhs, self.r, self.n = kind, lhs, rhs, r, n
        self.width, self.shape, self.counted = width, shape, counted


class Bundle:
    def __init__(self, order, bits, spots, tiles, entries):
        self.order, self.run, self.entries = order, order.run, entries
        self.shards = min(16, lax.axis_size("dp"))
        self.bits = [bit for bit in bits if bit < bits_of(self.shards)]
        self.spots, self.tiles = spots, tiles
        self.width = max(entry.width for entry in entries)
        self.firsts, self.bases, first, base = [], [], 0, 0
        for entry in entries:
            self.firsts.append(first)
            self.bases.append(base)
            first += entry.n
            base += entry.n * entry.r
        self.steps, self.rows = first, base

    def block(self, index_map):
        return pl.BlockSpec((1, self.rows, self.width), index_map)

    def shaped(self, count):
        return jax.ShapeDtypeStruct((count, self.rows, self.width), jnp.bfloat16)

    def size(self, count):
        return 2 * count * self.rows * self.width

    def spot_of(self, index):
        spot = jnp.int32(0)
        for at, bit in enumerate(self.bits):
            spot = spot | ((lax.shift_right_logical(index, bit) & 1) << (len(self.bits) - 1 - at))
        return spot

    def weigh(self):
        entries, shards, width = self.entries, self.shards, self.width
        token_rows = entries[0].lhs.shape[0]
        tallest = max(shards * entry.r for entry in entries)

        def unit_work(entry, offset, unit, refs, kept_ref, sent_ref, scratch, meta):
            r, n, height, span = entry.r, entry.n, shards * entry.r, entry.width
            turned, total, lhs_tile, rhs_tile, sems = scratch
            spot, half, live = meta[0], meta[1], meta[2]
            count = TILE if entry.counted else token_rows

            def block(ref):
                return ref[0] if entry.counted else ref[...]

            def put(out_ref, value):
                value = value.astype(BF16)
                if entry.kind == "wide":
                    at = pl.ds(pl.multiple_of(offset + unit * r, 16), r)
                    for shard in range(shards):
                        target = self.spot_of(lax.bitwise_xor(jnp.int32(shard), spot))
                        out_ref[target, at, :span] = value[shard * r : (shard + 1) * r]
                        if span < width:
                            out_ref[target, at, span:] = jnp.zeros((r, width - span), BF16)
                else:
                    each, tall = shards // n, n * r
                    for inner in range(each):
                        target = self.spot_of(lax.bitwise_xor(unit * each + inner, spot))
                        out_ref[target, offset : offset + tall, :span] = value[inner * tall : (inner + 1) * tall]

            def turn():
                turned[:height, :count] = block(refs[0]).T

            if entry.kind == "wide":
                pl.when(unit == 0)(turn)
            else:
                turn()

            def product(rhs_ref):
                return matmul(turned[:height, :count], block(rhs_ref))

            def add_rest(flip):
                lhs_at = 0 if entry.kind == "wide" else unit * height
                rhs_at = (half ^ flip) * span if entry.kind == "tall" else ((half ^ flip) * n + unit) * span

                def add(tile, carry):
                    copies = [
                        pltpu.make_async_copy(
                            source.at[tile, :, pl.ds(pl.multiple_of(jnp.int32(at), LANES), size)], target.at[:, :size], sems.at[index]
                        )
                        for index, (source, target, at, size) in enumerate(
                            ((refs[3], lhs_tile, lhs_at, height), (refs[4], rhs_tile, rhs_at, span))
                        )
                    ]
                    for copy in copies:
                        copy.start()
                    for copy in copies:
                        copy.wait()
                    total[:height, :span] += matmul_tn(lhs_tile[:, :height], rhs_tile[:, :span])
                    return carry

                lax.fori_loop(1, live, add, 0)

            for flip, rhs_ref, out_ref in ((1, refs[1], sent_ref), (0, refs[2], kept_ref)):
                if not entry.counted:
                    put(out_ref, product(rhs_ref))
                    continue

                @pl.when(live == 1)
                def _(rhs_ref=rhs_ref, out_ref=out_ref):
                    put(out_ref, product(rhs_ref))

                @pl.when(live > 1)
                def _(flip=flip, rhs_ref=rhs_ref, out_ref=out_ref):
                    total[:height, :span] = product(rhs_ref)
                    add_rest(flip)
                    put(out_ref, total[:height, :span])

        starts, in_specs, operands = [], [], []
        for first, entry in zip(self.firsts, entries):
            n, height, span = entry.n, shards * entry.r, entry.width
            starts.append(len(operands))

            def unit_of(step, first=first, n=n):
                return jnp.clip(step - first, 0, n - 1)

            def spec(size, column, depth, entry=entry):
                mode = pl.Buffered(depth)
                if entry.counted:
                    return pl.BlockSpec((1, TILE, size), lambda step, meta: (0, 0, column(step, meta)), pipeline_mode=mode)
                return pl.BlockSpec((token_rows, size), lambda step, meta: (0, column(step, meta)), pipeline_mode=mode)

            if entry.kind == "wide":
                in_specs.append(spec(height, lambda step, meta: 0, 1))
                for flip in (1, 0):
                    in_specs.append(
                        spec(span, lambda step, meta, n=n, unit_of=unit_of, flip=flip: (meta[1] ^ flip) * n + unit_of(step), 2)
                    )
            else:
                in_specs.append(spec(height, lambda step, meta, unit_of=unit_of: unit_of(step), 2))
                for flip in (1, 0):
                    in_specs.append(spec(span, lambda step, meta, flip=flip: meta[1] ^ flip, 1))
            lhs, rhs = entry.lhs, entry.rhs
            if entry.counted:
                lhs, rhs = (value.reshape(-1, TILE, value.shape[1]) for value in (lhs, rhs))
                in_specs += [pl.BlockSpec(memory_space=pl.ANY)] * 2
                operands += [lhs, rhs, rhs, lhs, rhs]
            else:
                operands += [lhs, rhs, rhs]
        starts.append(len(operands))

        def kernel(meta, *refs):
            sent_ref, kept_ref, *scratch = refs[len(operands) :]
            step = pl.program_id(0)
            for index, entry in enumerate(entries):
                first = self.firsts[index]

                @pl.when((step >= first) & (step < first + entry.n))
                def _(index=index, entry=entry, first=first):
                    ins = refs[starts[index] : starts[index + 1]]
                    unit_work(entry, self.bases[index], step - first, ins, kept_ref, sent_ref, scratch, meta)

        shape = (shards, self.rows, width)
        sent, kept = self.run(
            kernel,
            "weight_grads",
            jnp.concatenate([self.spots, self.tiles[:1]]),
            in_specs,
            operands,
            [pl.BlockSpec(shape, lambda step, meta: (0, 0, 0))] * 2,
            [self.shaped(shards)] * 2,
            [
                pltpu.VMEM((tallest, token_rows), BF16),
                pltpu.VMEM((tallest, width), F32),
                pltpu.VMEM((TILE, tallest), BF16),
                pltpu.VMEM((TILE, width), BF16),
                pltpu.SemaphoreType.DMA((2,)),
            ],
            micros=40.0,
            steps=self.steps,
            limit=WEIGHT_LIMIT,
        )
        self.terms = (kept, across(sent, "blk", 0))
        self.due, self.stage = list(self.bits), 0

    def step(self):
        bits = len(self.bits)
        for last, step in ((bits, self.halve), (bits + 1, self.own), (2 * bits, self.join), (2 * bits + 1, self.finish)):
            if self.stage < last:
                self.stage += 1
                step()
                return
        self.placed = self.place()

    def halve(self):
        bit = self.due.pop(0)
        first, second = self.terms
        count = first.shape[0] // 2

        def kernel(a_ref, b_ref, sent_ref, stay_ref):
            for base, target in ((count, sent_ref), (0, stay_ref)):

                def add(index, carry, base=base, target=target):
                    target[index] = (a_ref[base + index].astype(F32) + b_ref[base + index].astype(F32)).astype(BF16)
                    return carry

                lax.fori_loop(0, count, add, 0)

        sent, stay = self.order.run_small(
            kernel, "halve", [first, second], [self.shaped(count)] * 2
        )
        self.terms = (stay, across(sent, "dp", bit))

    def own(self):
        def kernel(a_ref, b_ref, out_ref):
            out_ref[...] = (a_ref[...].astype(F32) + b_ref[...].astype(F32)).astype(BF16)

        def add(a, b):
            return self.order.run_small(kernel, "own", [a, b], [self.shaped(1)])[0]

        total = add(*self.terms)
        for bit in range(bits_of(self.shards), bits_of(lax.axis_size("dp"))):
            total = add(total, across(total, "dp", bit))
        self.due = list(reversed(self.bits))
        self.spread(total)

    def spread(self, held):
        bit = self.due.pop(0)
        self.held = (held, across(held, "dp", bit))

    def join(self):
        count = self.held[0].shape[0]

        def kernel(a_ref, b_ref, out_ref):
            out_ref[:count] = a_ref[...]
            out_ref[count:] = b_ref[...]

        (held,) = self.order.run_small(
            kernel, "join", list(self.held), [self.shaped(2 * count)]
        )
        self.spread(held)

    def finish(self):
        self.other = [across(held, "blk", 0) for held in self.held]

    def place(self):
        entries, shards, bits, slots = self.entries, self.shards, self.bits, 4
        half_count = shards // 2
        heights = [entry.r if entry.kind == "wide" else entry.n * entry.r for entry in entries]
        count = len(entries)

        def kernel(meta, *refs):
            sources = refs[:4]
            outs, stages, sems = refs[4 : 4 + count], refs[4 + count : 4 + 2 * count], refs[-1]
            side = meta[1]

            def copies(slot, row_block):
                return [
                    pltpu.make_async_copy(
                        stage.at[slot],
                        out_ref.at[pl.ds(pl.multiple_of(row_block * height, 8), height), :],
                        sems.at[index, slot],
                    )
                    for index, (stage, out_ref, height) in enumerate(zip(stages, outs, heights))
                ]

            for upper in range(2):
                mine, other = sources[upper], sources[2 + upper]

                def one(index, carry, upper=upper, mine=mine, other=other):
                    step = upper * half_count + index
                    slot = lax.rem(step, slots)

                    @pl.when(step >= slots)
                    def _():
                        for copy in copies(slot, 0):
                            copy.wait()

                    for entry, offset, stage in zip(entries, self.bases, stages):
                        span = entry.width
                        for which, source in ((side, mine), (1 - side, other)):
                            for unit in range(entry.n):
                                row = offset + unit * entry.r
                                value = source[index, row : row + entry.r, :span].astype(F32)
                                if entry.kind == "wide":
                                    at = pl.ds(pl.multiple_of((which * entry.n + unit) * span, LANES), span)
                                    stage[slot, :, at] = value
                                else:
                                    at = pl.ds(pl.multiple_of(which * span, LANES), span)
                                    stage[slot, unit * entry.r : (unit + 1) * entry.r, at] = value
                    shard = jnp.int32(0)
                    for at, bit in enumerate(bits):
                        shard = shard | ((lax.shift_right_logical(step, len(bits) - 1 - at) & 1) << bit)
                    for copy in copies(slot, lax.bitwise_xor(shard, meta[0])):
                        copy.start()
                    return carry

                lax.fori_loop(0, half_count, one, 0)
            for step in range(max(shards - slots, 0), shards):
                for copy in copies(step % slots, 0):
                    copy.wait()

        return self.order.run_small(
            kernel,
            "place_shards",
            [self.held[0], self.held[1], *self.other],
            [jax.ShapeDtypeStruct(entry.shape, jnp.float32) for entry in entries],
            scalars=self.spots,
            out_specs=[pl.BlockSpec(memory_space=pl.ANY)] * count,
            scratch=[pltpu.VMEM((slots, height, entry.shape[1]), F32) for height, entry in zip(heights, entries)]
            + [pltpu.SemaphoreType.DMA((count, slots))],
        )


LOG2E = math.log2(math.e)
NEVER = -1e30
LANES = 128
BF16, F32 = jnp.bfloat16, jnp.float32


def colsum(value):
    return jnp.sum(value.astype(F32), axis=0, keepdims=True)


def normed_rows(stream):
    centred = stream - jnp.mean(stream, axis=-1, keepdims=True)
    inverse = lax.rsqrt(jnp.mean(centred * centred, axis=-1, keepdims=True) + epsilon)
    return centred * inverse, inverse


def norm_back(grad, unit, inverse, gain):
    grad = grad * gain
    inner = jnp.mean(grad * unit, axis=-1, keepdims=True)
    return inverse * (grad - jnp.mean(grad, axis=-1, keepdims=True) - unit * inner)


def gelu_pair(u):
    bell = jnp.exp2(u * u * (-0.5 * LOG2E))
    t = 1.0 / (1.0 + (0.3275911 * math.sqrt(0.5)) * jnp.abs(u))
    poly = ((((1.061405429 * t - 1.453152027) * t + 1.421413741) * t - 0.284496736) * t + 0.254829592) * t
    tail = 0.5 * poly * bell
    phi = jnp.where(u < 0, tail, 1.0 - tail)
    return u * phi, phi + u * bell * (1.0 / math.sqrt(2.0 * math.pi))


def iota(shape, axis):
    return lax.broadcasted_iota(jnp.int32, shape, axis)


def fill_groups(target, source):
    for group in range(target.shape[0]):
        target[group] = source[:, group * LANES : (group + 1) * LANES].astype(target.dtype)


def attend_forward(keys, head, q_s, k_s, v_s, mask_ref, o_s, probs=None, inverse_s=None, totals=None):
    groups, rows, _ = q_s.shape
    inside = LANES // head
    lanes = iota((rows, LANES), 1)
    which = lax.div(lanes, jnp.int32(head))
    if totals is not None:
        totals[...] = jnp.zeros_like(totals)

    def one_group(group, carry):
        queries = q_s[group]
        key_rows = k_s[group, :keys, :]
        values = v_s[group, :keys, :]
        blended = jnp.zeros((rows, LANES), F32)
        inverses = jnp.zeros((rows, LANES), F32)
        for h in range(inside):
            own = which == h
            query = jnp.where(own, queries, 0.0).astype(BF16)
            scores = matmul_nt(query, key_rows) + mask_ref[:, :keys]
            top = jnp.max(scores, axis=1, keepdims=True)
            prob = jnp.exp2(scores - top).astype(BF16)
            if probs is not None:
                probs[group * inside + h, :, :keys] = prob
            both = matmul(prob, values)
            inverse = 1.0 / both[:, LANES:]
            blended = jnp.where(own, both[:, :LANES] * inverse, blended)
            if inverse_s is not None:
                inverses = jnp.where(own, inverse, inverses)
            if totals is not None:
                at = lanes == group * inside + h
                totals[...] = jnp.where(at, top + jnp.log2(both[:, LANES:]), totals[...])
        o_s[group] = blended
        if inverse_s is not None:
            inverse_s[group] = inverses
        return carry

    lax.fori_loop(0, groups, one_group, 0)


def attend_backward(keys, head, q_s, k_s, v_s, o_s, ob_s, dq_s, dk_s, dv_s, probs=None, mask_ref=None, totals=None):
    groups, rows, _ = q_s.shape
    inside = LANES // head
    lanes = iota((rows, LANES), 1)
    which = lax.div(lanes, jnp.int32(head))

    def one_group(group, carry):
        queries, grads = q_s[group], ob_s[group]
        key_rows = k_s[group, :keys, :]
        values = v_s[group, :keys, :LANES]
        product = grads * o_s[group]
        queries_t = queries.T.astype(BF16)
        grads_t = grads.T.astype(BF16)
        query_grad = jnp.zeros((rows, LANES), F32)
        for h in range(inside):
            own = which == h
            at = slice(h * head, (h + 1) * head)
            inner = jnp.sum(jnp.where(own, product, 0.0), axis=1, keepdims=True)
            if probs is not None:
                prob = probs[group * inside + h, :, :keys]
            else:
                query = jnp.where(own, queries, 0.0).astype(BF16)
                total = jnp.sum(jnp.where(lanes == group * inside + h, totals, 0.0), axis=1, keepdims=True)
                prob = jnp.exp2(matmul_nt(query, key_rows) + (mask_ref[:, :keys] - total)).astype(BF16)
            grad_probs = matmul_nt(jnp.where(own, grads, 0.0).astype(BF16), values)
            score_grad = (prob.astype(F32) * (grad_probs - inner)).astype(BF16)
            query_grad = jnp.where(own, matmul(score_grad, key_rows), query_grad)
            dk_s[group, at, :keys] += matmul(queries_t[at], score_grad)
            dv_s[group, at, :keys] += matmul(grads_t[at], prob)
        dq_s[group] = query_grad
        return carry

    lax.fori_loop(0, groups, one_group, 0)


def whole(shape):
    rank = len(shape)
    return pl.BlockSpec(shape, lambda step, meta: (0,) * rank, pipeline_mode=pl.Buffered(1))


def out_whole(shape):
    rank = len(shape)
    return pl.BlockSpec(shape, lambda step, meta: (0,) * rank)


def row_tile(width):
    return pl.BlockSpec((TILE, width), lambda step, meta: (step, 0))


def live_tile(width):
    return pl.BlockSpec((TILE, width), lambda step, meta: (jnp.minimum(step, meta[0] - 1), 0))


def call(order, kernel, name, meta, in_specs, operands, out_specs, out_shape, scratch, micros, steps):
    return order.run(kernel, name, meta, in_specs, operands, out_specs, out_shape, scratch, micros=micros, steps=steps)


def shaped(rows, width, dtype):
    return jax.ShapeDtypeStruct((rows, width), dtype)


MARKS = 16


def enc_in(order, meta, patches, raw, far_raw, params, qkv, heads):
    rows, width = patches.shape
    factor = (width // heads) ** (-0.5) * LOG2E

    def marks_of(seen, padded, label):
        seen, kept, label = seen[...].astype(F32), 1.0 - padded[...].astype(F32), label[...].astype(F32) + 1.0
        row, result = iota((MARKS, rows), 0), jnp.zeros((MARKS, rows), F32)
        for index, value in enumerate((seen * kept * label, label, seen, kept * label)):
            result = jnp.where(row == index, value, result)
        return result

    def kernel(meta, patches_ref, *refs):
        raw_refs, far_refs, (params_ref, qkv_ref) = refs[:3], refs[3:6], refs[6:8]
        sel_ref, code_ref, far_code_ref, label_ref, marks_ref, far_marks_ref, columns_ref, s_ref, n_ref, q_ref, kv_ref, place_s = refs[8:]
        step = pl.program_id(0)

        @pl.when(step == 0)
        def _():
            below = (iota((rows, rows), 0) <= iota((rows, rows), 1)).astype(F32).astype(BF16)
            for index, (source, target) in enumerate(((raw_refs, marks_ref), (far_refs, far_marks_ref))):
                marks = marks_of(*source)
                target[...] = marks
                place = matmul(marks.astype(BF16), below)[2:3, :]
                place_s[index : index + 1, :] = jnp.where(marks[2:3, :] > 0, place - 1.0, -1.0)
            columns_ref[...] = marks_ref[...].T

        @pl.when(step < jnp.maximum(meta[0], meta[1]))
        def _():
            target = (step * TILE + iota((TILE, rows), 0)).astype(F32)
            sel = jnp.where(target == place_s[0:1, :], 1.0, 0.0).astype(BF16)
            far_sel = jnp.where(target == place_s[1:2, :], 1.0, 0.0).astype(BF16)
            sel_ref[...] = sel
            own_marks = marks_ref[...].astype(BF16)
            code_ref[...] = matmul_nt(own_marks, sel)
            far_code_ref[...] = matmul_nt(far_marks_ref[...].astype(BF16), far_sel)
            label_ref[...] = matmul_nt(sel, own_marks)

        @pl.when(step < meta[0])
        def _():
            stream = matmul(sel_ref[...], patches_ref[...])
            s_ref[...] = stream.astype(BF16)
            unit, _ = normed_rows(stream)
            normed = (unit * params_ref[:, :width] + params_ref[:, width : 2 * width]).astype(BF16)
            n_ref[...] = normed
            q_ref[...] = (matmul(normed, qkv_ref[:, :width]) * factor).astype(BF16)
            kv_ref[...] = matmul(normed, qkv_ref[:, width:]).astype(BF16)

    def last_tile(step, meta):
        return jnp.minimum(step, jnp.maximum(meta[0], meta[1]) - 1)

    lane_tile = pl.BlockSpec((MARKS, TILE), lambda step, meta: (0, last_tile(step, meta)))

    def tile(size):
        return pl.BlockSpec((TILE, size), lambda step, meta: (last_tile(step, meta), 0))

    operands = (patches, *raw, *far_raw, params, qkv)
    return call(
        order,
        kernel,
        "enc_in",
        meta,
        [whole(value.shape) for value in operands],
        operands,
        [tile(rows), lane_tile, lane_tile, tile(MARKS), out_whole((MARKS, rows)), out_whole((MARKS, rows)), out_whole((rows, MARKS))]
        + [live_tile(w) for w in (width, width, width, 2 * width)],
        [shaped(rows, rows, BF16), shaped(MARKS, rows, F32), shaped(MARKS, rows, F32), shaped(rows, MARKS, F32)]
        + [shaped(MARKS, rows, F32), shaped(MARKS, rows, F32), shaped(rows, MARKS, F32)]
        + [shaped(rows, w, BF16) for w in (width, width, width, 2 * width)],
        [pltpu.VMEM((8, rows), F32)],
        7.0,
        rows // TILE,
    )


def spread_keys(count, tiles, kv_ref, far_ref, far_tiles, k_s, v_s):
    size = count * TILE
    width = kv_ref.shape[1] // 2
    for source, live, base in ((kv_ref, tiles, 0), (far_ref, far_tiles, size)):
        ok = iota((size, LANES), 0) < live * TILE
        for group in range(width // LANES):
            at = slice(group * LANES, (group + 1) * LANES)
            value_at = slice(width + group * LANES, width + (group + 1) * LANES)
            k_s[group, base : base + size, :] = jnp.where(ok, source[:size, at].astype(F32), 0.0).astype(BF16)
            v_s[group, base : base + size, :LANES] = jnp.where(ok, source[:size, value_at].astype(F32), 0.0).astype(BF16)
            if v_s.shape[2] > LANES:
                v_s[group, base : base + size, LANES:] = jnp.ones((size, v_s.shape[2] - LANES), BF16)


def write_mask(mask_ref, label, code, far_code, size, step):
    shape = (label.shape[0], size)
    near = (label == code) | (iota(shape, 1) == step * TILE + iota(shape, 0))
    mask_ref[:, :size] = jnp.where(near, 0.0, NEVER)
    mask_ref[:, size : 2 * size] = jnp.where(label == far_code, 0.0, NEVER)


def enc_main(order, meta, s, q, kv, far_kv, label, code, far_code, params, out, up, down, embed, heads):
    rows, width = s.shape
    wide, lifted_width = up.shape[1], embed.shape[1]
    groups, head, most = width // LANES, width // heads, rows // TILE
    part = width

    def kernel(meta, s_ref, q_ref, kv_ref, far_ref, label_ref, code_ref, far_code_ref, params_ref, out_w, up_w, down_w, embed_w,
               o_ref, tot_ref, m_ref, n_ref, g_ref, gp_ref, e_ref, hi_ref, lo_ref, q_s, k_s, v_s, mask_s, o_s):
        step = pl.program_id(0)
        tiles, far_tiles = meta[0], meta[1]
        count = jnp.maximum(tiles, far_tiles)

        def param(start, size):
            return params_ref[:, start : start + size]

        @pl.when(step < tiles)
        def _():
            fill_groups(q_s, q_ref)
            for size in range(1, most + 1):

                @pl.when(count == size)
                def _(size=size):
                    @pl.when(step == 0)
                    def _():
                        spread_keys(size, tiles, kv_ref, far_ref, far_tiles, k_s, v_s)

                    span = size * TILE
                    write_mask(mask_s, label_ref[:, 1:2], code_ref[0:1, :span], far_code_ref[0:1, :span], span, step)
                    attend_forward(2 * span, head, q_s, k_s, v_s, mask_s, o_s, totals=tot_ref)

            for group in range(groups):
                o_ref[:, group * LANES : (group + 1) * LANES] = o_s[group].astype(BF16)
            middle = s_ref[...].astype(F32) + matmul(o_ref[...], out_w[...]) + param(2 * width, width)
            m_ref[...] = middle
            unit, _ = normed_rows(middle)
            normed = (unit * param(3 * width, width) + param(4 * width, width)).astype(BF16)
            n_ref[...] = normed
            encoded = middle + param(5 * width + wide, width)
            for j in range(0, wide, part):
                u = matmul(normed, up_w[:, j : j + part]) + param(5 * width + j, part)
                g, slope = gelu_pair(u)
                g = g.astype(BF16)
                g_ref[:, j : j + part] = g
                gp_ref[:, j : j + part] = slope.astype(BF16)
                encoded = encoded + matmul(g, down_w[j : j + part, :])
            low = encoded.astype(BF16)
            e_ref[...] = low
            lifted = matmul(low, embed_w[...]) + param(6 * width + wide, lifted_width)
            high = lifted.astype(BF16)
            hi_ref[...] = high
            lo_ref[...] = (lifted - high.astype(F32)).astype(BF16)

    tall = label.shape[1]
    return call(
        order,
        kernel,
        "enc_main",
        meta,
        [live_tile(width), live_tile(width), whole(kv.shape), whole(kv.shape), live_tile(tall), whole(code.shape), whole(code.shape)]
        + [whole(value.shape) for value in (params, out, up, down, embed)],
        (s, q, kv, far_kv, label, code, far_code, params, out, up, down, embed),
        [live_tile(w) for w in (width, LANES, width, width, wide, wide, width, lifted_width, lifted_width)],
        [shaped(rows, width, BF16), shaped(rows, LANES, F32), shaped(rows, width, F32), shaped(rows, width, BF16)]
        + [shaped(rows, wide, BF16)] * 2 + [shaped(rows, width, BF16)] + [shaped(rows, lifted_width, BF16)] * 2,
        [
            pltpu.VMEM((groups, TILE, LANES), F32),
            pltpu.VMEM((groups, 2 * rows, LANES), BF16),
            pltpu.VMEM((groups, 2 * rows, 2 * LANES), BF16),
            pltpu.VMEM((TILE, 2 * rows), F32),
            pltpu.VMEM((groups, TILE, LANES), F32),
        ],
        20.0,
        most,
    )


def dec_in(order, meta, sel, high, low, columns, params, qkv, heads):
    rows, width = high.shape
    tall = columns.shape[1]
    factor = (width // heads) ** (-0.5) * LOG2E

    def kernel(meta, sel_ref, hi_ref, lo_ref, col_ref, params_ref, qkv_ref, start_ref, n_ref, q_ref, kv_ref, total):
        total[...] = jnp.zeros_like(total)

        def add(tile, carry):
            at = pl.ds(pl.multiple_of(tile * TILE, TILE), TILE)
            total[...] += matmul_tn(sel_ref[at, :], hi_ref[at, :]) + matmul_tn(sel_ref[at, :], lo_ref[at, :])
            return carry

        lax.fori_loop(0, meta[0], add, 0)
        start = jnp.where(col_ref[:, 2:3] > 0, total[...], params_ref[:, params.shape[1] - width :])
        start_ref[...] = start
        unit, _ = normed_rows(start)
        normed = (unit * params_ref[:, :width] + params_ref[:, width : 2 * width]).astype(BF16)
        n_ref[...] = normed
        q_ref[...] = (matmul(normed, qkv_ref[:, :width]) * factor).astype(BF16)
        kv_ref[...] = matmul(normed, qkv_ref[:, width:]).astype(BF16)

    return call(
        order,
        kernel,
        "dec_in",
        meta,
        [pl.BlockSpec((rows, TILE), lambda step, meta: (0, step)), whole(high.shape), whole(low.shape), row_tile(tall)]
        + [whole(value.shape) for value in (params, qkv)],
        (sel, high, low, columns, params, qkv),
        [row_tile(w) for w in (width, width, width, 2 * width)],
        [shaped(rows, width, F32)] + [shaped(rows, w, BF16) for w in (width, width, 2 * width)],
        [pltpu.VMEM((TILE, width), F32)],
        7.0,
        rows // TILE,
    )


def give_key_grads(size, dk_s, dv_s, near_ref, far_ref):
    groups = dk_s.shape[0]
    for index, (source, factor) in enumerate(((dk_s, 1.0 / LOG2E), (dv_s, 1.0))):
        for group in range(groups):
            at = slice((index * groups + group) * LANES, (index * groups + group + 1) * LANES)
            near_ref[:size, at] = source[group, :, :size].T * factor
            far_ref[:size, at] = (source[group, :, size : 2 * size].T * factor).astype(BF16)


def dec_main(order, meta, start, q, kv, far_kv, columns, marks, far_marks, cotangent, params, out, up, down, heads):
    rows, width = start.shape
    wide = up.shape[1]
    groups, head, steps = width // LANES, width // heads, rows // TILE
    part = width
    tall = columns.shape[1]

    def kernel(meta, start_ref, q_ref, kv_ref, far_ref, col_ref, marks_ref, far_marks_ref, cot_ref, params_ref, out_w, up_w, down_w,
               dec_ref, o_ref, n_ref, g_ref, ub_ref, mb_ref, tm_ref, dq_ref, near_ref, back_ref,
               outb_ref, gainb_ref, shiftb_ref, upb_ref, downb_ref,
               q_s, k_s, v_s, mask_s, probs, o_s, inv_s, ob_s, dq_s, dk_s, dv_s, slope_s):
        step = pl.program_id(0)

        def param(begin, size):
            return params_ref[:, begin : begin + size]

        @pl.when(step == 0)
        def _():
            spread_keys(steps, steps, kv_ref, far_ref, steps, k_s, v_s)
            for ref in (dk_s, dv_s, outb_ref, gainb_ref, shiftb_ref, upb_ref, downb_ref):
                ref[...] = jnp.zeros_like(ref)

        fill_groups(q_s, q_ref)
        write_mask(mask_s, col_ref[:, 1:2], marks_ref[3:4, :], far_marks_ref[3:4, :], rows, step)
        attend_forward(2 * rows, head, q_s, k_s, v_s, mask_s, o_s, probs=probs, inverse_s=inv_s)
        for group in range(groups):
            o_ref[:, group * LANES : (group + 1) * LANES] = o_s[group].astype(BF16)
        middle = start_ref[...] + matmul(o_ref[...], out_w[...]) + param(2 * width, width)
        unit, inverse = normed_rows(middle)
        gain_b = param(3 * width, width)
        normed = (unit * gain_b + param(4 * width, width)).astype(BF16)
        n_ref[...] = normed
        decoded = middle + param(5 * width + wide, width)
        for j in range(0, wide, part):
            g, slope = gelu_pair(matmul(normed, up_w[:, j : j + part]) + param(5 * width + j, part))
            g = g.astype(BF16)
            g_ref[:, j : j + part] = g
            slope_s[:, j : j + part] = slope
            decoded = decoded + matmul(g, down_w[j : j + part, :])
        dec_ref[...] = decoded.astype(BF16)
        top = cot_ref[...]
        normed_grad = jnp.zeros((TILE, width), F32)
        for j in range(0, wide, part):
            low = (slope_s[:, j : j + part] * matmul_nt(top, down_w[j : j + part, :])).astype(BF16)
            ub_ref[:, j : j + part] = low
            upb_ref[:, j : j + part] += colsum(low)
            normed_grad = normed_grad + matmul_nt(low, up_w[:, j : j + part])
        downb_ref[...] += colsum(top)
        gainb_ref[...] += colsum(normed_grad * unit)
        shiftb_ref[...] += colsum(normed_grad)
        middle_grad = top.astype(F32) + norm_back(normed_grad, unit, inverse, gain_b)
        tm_ref[...] = middle_grad
        low = middle_grad.astype(BF16)
        mb_ref[...] = low
        outb_ref[...] += colsum(low)
        attended_grad = matmul_nt(low, out_w[...])
        for group in range(groups):
            scaled = attended_grad[:, group * LANES : (group + 1) * LANES] * inv_s[group]
            ob_s[group] = scaled.astype(BF16).astype(F32)
        attend_backward(2 * rows, head, q_s, k_s, v_s, o_s, ob_s, dq_s, dk_s, dv_s, probs=probs)
        scale = head ** (-0.5)
        for group in range(groups):
            dq_ref[:, group * LANES : (group + 1) * LANES] = (dq_s[group] * scale).astype(BF16)

        @pl.when(step == steps - 1)
        def _():
            give_key_grads(rows, dk_s, dv_s, near_ref, back_ref)

    small = [width, width, width, wide, width]
    return call(
        order,
        kernel,
        "dec_main",
        meta,
        [row_tile(width), row_tile(width), whole(kv.shape), whole(kv.shape), row_tile(tall), whole(marks.shape), whole(marks.shape)]
        + [row_tile(width)] + [whole(value.shape) for value in (params, out, up, down)],
        (start, q, kv, far_kv, columns, marks, far_marks, cotangent, params, out, up, down),
        [row_tile(w) for w in (width, width, width, wide, wide, width, width, width)]
        + [out_whole((rows, 2 * width))] * 2 + [out_whole((1, w)) for w in small],
        [shaped(rows, w, BF16) for w in (width, width, width, wide, wide, width)]
        + [shaped(rows, width, F32), shaped(rows, width, BF16), shaped(rows, 2 * width, F32), shaped(rows, 2 * width, BF16)]
        + [shaped(1, w, F32) for w in small],
        [
            pltpu.VMEM((groups, TILE, LANES), F32),
            pltpu.VMEM((groups, 2 * rows, LANES), BF16),
            pltpu.VMEM((groups, 2 * rows, 2 * LANES), BF16),
            pltpu.VMEM((TILE, 2 * rows), F32),
            pltpu.VMEM((heads, TILE, 2 * rows), BF16),
        ]
        + [pltpu.VMEM((groups, TILE, LANES), F32)] * 4
        + [pltpu.VMEM((groups, LANES, 2 * rows), F32)] * 2
        + [pltpu.VMEM((TILE, wide), F32)],
        95.0,
        steps,
    )


def dec_head(order, meta, start, dq, near, back, middle_grad, columns, params, qkv):
    rows, width = start.shape
    tall = columns.shape[1]

    def kernel(meta, start_ref, dq_ref, near_ref, back_ref, tm_ref, col_ref, params_ref, qkv_ref,
               dqkv_ref, lb_ref, gain_ref, shift_ref, bias_ref, token_ref):
        step = pl.program_id(0)

        @pl.when(step == 0)
        def _():
            for ref in (gain_ref, shift_ref, bias_ref, token_ref):
                ref[...] = jnp.zeros_like(ref)

        dqkv_ref[:, :width] = dq_ref[...]
        dqkv_ref[:, width:] = (near_ref[...] + back_ref[...].astype(F32)).astype(BF16)
        grad = matmul_nt(dqkv_ref[...], qkv_ref[...])
        unit, inverse = normed_rows(start_ref[...])
        gain_ref[...] += colsum(grad * unit)
        shift_ref[...] += colsum(grad)
        start_grad = tm_ref[...] + norm_back(grad, unit, inverse, params_ref[:, :width])
        seen = col_ref[:, 2:3] > 0
        token_ref[...] += colsum(jnp.where(seen, 0.0, start_grad))
        low = jnp.where(seen, start_grad, 0.0).astype(BF16)
        lb_ref[...] = low
        bias_ref[...] += colsum(low)

    return call(
        order,
        kernel,
        "dec_head",
        meta,
        [row_tile(width), row_tile(width), row_tile(2 * width), row_tile(2 * width), row_tile(width), row_tile(tall)]
        + [whole(params.shape), whole(qkv.shape)],
        (start, dq, near, back, middle_grad, columns, params, qkv),
        [row_tile(3 * width), row_tile(width)] + [out_whole((1, width))] * 4,
        [shaped(rows, 3 * width, BF16), shaped(rows, width, BF16)] + [shaped(1, width, F32)] * 4,
        [],
        40.0,
        rows // TILE,
    )


def enc_back(order, meta, sel, lb, slope, m, q, kv, far_kv, o, totals, label, code, far_code, params, out, up, down, embed, heads):
    rows, width = m.shape
    wide, lifted_width = up.shape[1], embed.shape[1]
    groups, head, most = width // LANES, width // heads, rows // TILE
    part = width
    tall = label.shape[1]

    def kernel(meta, sel_ref, lb_ref, slope_ref, m_ref, q_ref, kv_ref, far_ref, o_ref, tot_ref, label_ref, code_ref, far_code_ref,
               params_ref, out_w, up_w, down_w, embed_w,
               lbc_ref, tb_ref, ub_ref, mb_ref, tm_ref, dq_ref, near_ref, back_ref,
               outb_ref, gainb_ref, shiftb_ref, upb_ref, downb_ref,
               q_s, k_s, v_s, mask_s, o_s, ob_s, dq_s, dk_s, dv_s):
        step = pl.program_id(0)
        tiles, far_tiles = meta[0], meta[1]
        count = jnp.maximum(tiles, far_tiles)
        scale = head ** (-0.5)

        @pl.when(step == 0)
        def _():
            for ref in (dk_s, dv_s, outb_ref, gainb_ref, shiftb_ref, upb_ref, downb_ref):
                ref[...] = jnp.zeros_like(ref)

        @pl.when(step < tiles)
        def _():
            lb_here = matmul(sel_ref[...], lb_ref[...]).astype(BF16)
            lbc_ref[...] = lb_here
            grad_top = matmul_nt(lb_here, embed_w[...])
            top = grad_top.astype(BF16)
            tb_ref[...] = top
            normed_grad = jnp.zeros((TILE, width), F32)
            for j in range(0, wide, part):
                low = (slope_ref[:, j : j + part].astype(F32) * matmul_nt(top, down_w[j : j + part, :])).astype(BF16)
                ub_ref[:, j : j + part] = low
                upb_ref[:, j : j + part] += colsum(low)
                normed_grad = normed_grad + matmul_nt(low, up_w[:, j : j + part])
            unit, inverse = normed_rows(m_ref[...])
            downb_ref[...] += colsum(top)
            gainb_ref[...] += colsum(normed_grad * unit)
            shiftb_ref[...] += colsum(normed_grad)
            middle_grad = grad_top + norm_back(normed_grad, unit, inverse, params_ref[:, 3 * width : 4 * width])
            tm_ref[...] = middle_grad
            low = middle_grad.astype(BF16)
            mb_ref[...] = low
            outb_ref[...] += colsum(low)
            attended_grad = matmul_nt(low, out_w[...]).astype(BF16)
            fill_groups(ob_s, attended_grad)
            fill_groups(o_s, o_ref)
            fill_groups(q_s, q_ref)
            for size in range(1, most + 1):

                @pl.when(count == size)
                def _(size=size):
                    @pl.when(step == 0)
                    def _():
                        spread_keys(size, tiles, kv_ref, far_ref, far_tiles, k_s, v_s)

                    span = size * TILE
                    write_mask(mask_s, label_ref[:, 1:2], code_ref[0:1, :span], far_code_ref[0:1, :span], span, step)
                    attend_backward(
                        2 * span, head, q_s, k_s, v_s, o_s, ob_s, dq_s, dk_s, dv_s, mask_ref=mask_s, totals=tot_ref[...]
                    )

                    @pl.when(step == tiles - 1)
                    def _():
                        give_key_grads(span, dk_s, dv_s, near_ref, back_ref)

            for group in range(groups):
                dq_ref[:, group * LANES : (group + 1) * LANES] = (dq_s[group] * scale).astype(BF16)

    small = [width, width, width, wide, width]
    return call(
        order,
        kernel,
        "enc_back",
        meta,
        [live_tile(rows), whole(lb.shape), live_tile(wide), live_tile(width), live_tile(width), whole(kv.shape), whole(kv.shape)]
        + [live_tile(width), live_tile(LANES), live_tile(tall), whole(code.shape), whole(code.shape)]
        + [whole(value.shape) for value in (params, out, up, down, embed)],
        (sel, lb, slope, m, q, kv, far_kv, o, totals, label, code, far_code, params, out, up, down, embed),
        [live_tile(w) for w in (lifted_width, width, wide, width, width, width)]
        + [whole((rows, 2 * width))] * 2 + [out_whole((1, w)) for w in small],
        [shaped(rows, w, BF16) for w in (lifted_width, width, wide, width)]
        + [shaped(rows, width, F32), shaped(rows, width, BF16), shaped(rows, 2 * width, F32), shaped(rows, 2 * width, BF16)]
        + [shaped(1, w, F32) for w in small],
        [
            pltpu.VMEM((groups, TILE, LANES), F32),
            pltpu.VMEM((groups, 2 * rows, LANES), BF16),
            pltpu.VMEM((groups, 2 * rows, LANES), BF16),
            pltpu.VMEM((TILE, 2 * rows), F32),
        ]
        + [pltpu.VMEM((groups, TILE, LANES), F32)] * 3
        + [pltpu.VMEM((groups, LANES, 2 * rows), F32)] * 2,
        24.0,
        most,
    )


def enc_head(order, meta, sel, s, dq, near, back, middle_grad, params, qkv):
    rows, width = s.shape
    steps = rows // TILE

    def kernel(meta, sel_ref, s_ref, dq_ref, near_ref, back_ref, tm_ref, params_ref, qkv_ref,
               dqkv_ref, grad_ref, gain_ref, shift_ref, total):
        step = pl.program_id(0)

        @pl.when(step == 0)
        def _():
            for ref in (gain_ref, shift_ref, total):
                ref[...] = jnp.zeros_like(ref)

        @pl.when(step < meta[0])
        def _():
            dqkv_ref[:, :width] = dq_ref[...]
            dqkv_ref[:, width:] = (near_ref[...] + back_ref[...].astype(F32)).astype(BF16)
            grad = matmul_nt(dqkv_ref[...], qkv_ref[...])
            unit, inverse = normed_rows(s_ref[...].astype(F32))
            gain_ref[...] += colsum(grad * unit)
            shift_ref[...] += colsum(grad)
            stream_grad = tm_ref[...] + norm_back(grad, unit, inverse, params_ref[:, :width])
            total[...] += matmul_tn(sel_ref[...], stream_grad.astype(BF16))

        @pl.when(step == steps - 1)
        def _():
            grad_ref[...] = total[...].astype(BF16)

    return call(
        order,
        kernel,
        "enc_head",
        meta,
        [live_tile(w) for w in (rows, width, width, 2 * width, 2 * width, width)] + [whole(params.shape), whole(qkv.shape)],
        (sel, s, dq, near, back, middle_grad, params, qkv),
        [live_tile(3 * width), out_whole((rows, width))] + [out_whole((1, width))] * 2,
        [shaped(rows, 3 * width, BF16), shaped(rows, width, BF16)] + [shaped(1, width, F32)] * 2,
        [pltpu.VMEM((rows, width), F32)],
        40.0,
        steps,
    )


def joined(values):
    total, offset = sum(value.size for value in values), 0
    row = jnp.zeros((total,), F32)
    for value in values:
        row = row + jnp.pad(value.astype(F32), (offset, total - offset - value.size))
        offset += value.size
    return row.reshape(1, total)


class SmallSum:
    def __init__(self, order, values):
        self.order, self.sizes = order, [value.size for value in values]
        sizes = self.sizes

        def kernel(*refs):
            offset = 0
            for ref, size in zip(refs, sizes):
                refs[-1][:, offset : offset + size] = ref[...]
                offset += size

        self.pack, self.values = kernel, values
        self.due = [(axis, bit) for axis in ("blk", "dp") for bit in range(bits_of(lax.axis_size(axis)))]
        self.total = None

    def step(self):
        if self.total is None:
            (self.total,) = self.order.run_small(self.pack, "pack", self.values, [shaped(1, sum(self.sizes), F32)])
            self.send()
        else:
            self.add()

    def send(self):
        self.arrived = across(self.total, *self.due.pop(0))

    def add(self):
        def kernel(a_ref, b_ref, out_ref):
            out_ref[...] = a_ref[...] + b_ref[...]

        (self.total,) = self.order.run_small(
            kernel, "add_small", [self.total, self.arrived], [shaped(*self.total.shape, F32)]
        )
        self.arrived = None
        if self.due:
            self.send()

    def parts(self):
        while self.arrived is not None:
            self.add()
        flat, results, offset = self.total.reshape(-1), [], 0
        for size in self.sizes:
            results.append(flat[offset : offset + size])
            offset += size
        return results


def local(
    patches,
    visible,
    padding,
    field_ids,
    enc_gain_a,
    enc_shift_a,
    enc_qkv,
    enc_out,
    enc_out_bias,
    enc_gain_b,
    enc_shift_b,
    enc_up,
    enc_up_bias,
    enc_down,
    enc_down_bias,
    embed_map,
    embed_bias,
    mask_token,
    dec_gain_a,
    dec_shift_a,
    dec_qkv,
    dec_out,
    dec_out_bias,
    dec_gain_b,
    dec_shift_b,
    dec_up,
    dec_up_bias,
    dec_down,
    dec_down_bias,
    cotangent,
):
    rows = patches.shape[0]
    tiles_most = rows // TILE
    raw = [value.reshape(1, rows) for value in (visible, padding, field_ids)]
    far_raw = [across(value, "blk", 0) for value in raw]
    counts = jnp.stack([jnp.sum(raw[0]), jnp.sum(far_raw[0])]).astype(jnp.int32)
    meta = jnp.clip((counts + TILE - 1) // TILE, 1, tiles_most)

    enc_params = joined(
        [enc_gain_a, enc_shift_a, enc_out_bias, enc_gain_b, enc_shift_b, enc_up_bias, enc_down_bias, embed_bias]
    )
    dec_params = joined(
        [dec_gain_a, dec_shift_a, dec_out_bias, dec_gain_b, dec_shift_b, dec_up_bias, dec_down_bias, mask_token]
    )

    order = Order()
    shards = min(16, lax.axis_size("dp"))
    spots = jnp.stack([lax.axis_index("dp") & (shards - 1), lax.axis_index("blk")]).astype(jnp.int32)
    de, dd = enc_qkv.shape[0], dec_qkv.shape[0]
    rd, re = dd // shards, de // shards

    sel, code, far_code, label, marks, far_marks, columns, s, n1, q, kv = enc_in(order, meta, patches, raw, far_raw, enc_params, enc_qkv, HE)
    far_kv = across(kv, "blk", 0)
    o, totals, m, n2, g, slope, low, lift_high, lift_low = enc_main(
        order, meta, s, q, kv, far_kv, label, code, far_code, enc_params, enc_out, enc_up, enc_down, embed_map, HE
    )
    start, dn1, dq_rows, dkv = dec_in(order, meta, sel, lift_high, lift_low, columns, dec_params, dec_qkv, HD)
    far_dkv = across(dkv, "blk", 0)
    (decoded, d_o, d_n2, d_g, d_ub, d_mb, d_tm, d_dq, d_near, d_back, d_outb, d_gainb, d_shiftb, d_upb, d_downb) = dec_main(
        order, meta, start, dq_rows, dkv, far_dkv, columns, marks, far_marks, cotangent, dec_params, dec_out, dec_up, dec_down, HD
    )
    d_back = across(d_back, "blk", 0)

    def bundle(bits, *entries):
        return Bundle(order, bits, spots, meta, [Entry(*entry) for entry in entries])

    dec = bundle(
        DEC_BITS,
        ("wide", d_n2, d_ub, rd, 4, dd // 2, dec_up.shape, False),
        ("tall", d_g, cotangent, rd, 4, dd // 2, dec_down.shape, False),
        ("wide", d_o, d_mb, rd, 1, dd // 2, dec_out.shape, False),
    )
    dec.weigh()
    d_dqkv, lb, d_gaina, d_shifta, embed_b, token_grad = dec_head(
        order, meta, start, d_dq, d_near, d_back, d_tm, columns, dec_params, dec_qkv
    )
    dec.step()
    (lbc, tb, ub, mb, tm, dq, near, back, outb, gainb, shiftb, upb, downb) = enc_back(
        order, meta, sel, lb, slope, m, q, kv, far_kv, o, totals, label, code, far_code,
        enc_params, enc_out, enc_up, enc_down, embed_map, HE,
    )
    back = across(back, "blk", 0)
    dec.step()
    enc_a = bundle(
        ENC_BITS[0],
        ("wide", n2, ub, re, 4, de // 2, enc_up.shape, True),
        ("wide", o, mb, re, 1, de // 2, enc_out.shape, True),
    )
    enc_b = bundle(
        ENC_BITS[1],
        ("tall", g, tb, re, 4, de // 2, enc_down.shape, True),
        ("wide", low, lbc, re, 1, dd // 2, embed_map.shape, True),
    )
    enc_a.weigh()
    enc_b.weigh()
    enc_a.step()
    dqkv, patches_grad, gaina, shifta = enc_head(order, meta, sel, s, dq, near, back, tm, enc_params, enc_qkv)
    enc_b.step()
    dec.step()
    enc_c = bundle(
        ENC_BITS[2],
        ("wide", n1, dqkv, re, 3, de // 2, enc_qkv.shape, True),
        ("wide", dn1, d_dqkv, rd, 3 * dd // de, de // 2, dec_qkv.shape, False),
    )
    enc_c.weigh()
    small = SmallSum(
        order,
        [gaina, shifta, outb, gainb, shiftb, upb, downb, embed_b, token_grad]
        + [d_gaina, d_shifta, d_outb, d_gainb, d_shiftb, d_upb, d_downb],
    )
    bundles = {"d": dec, "a": enc_a, "b": enc_b, "c": enc_c, "s": small}
    for name in STEPS:
        bundles[name].step()
    g_dec_up, g_dec_down, g_dec_out = dec.placed
    g_enc_up, g_enc_out = enc_a.placed
    g_enc_down, g_embed = enc_b.placed
    g_enc_qkv, g_dec_qkv = enc_c.placed
    small = small.parts()
    return (
        (decoded, patches_grad)
        + (small[0], small[1], g_enc_qkv, g_enc_out, small[2], small[3], small[4])
        + (g_enc_up, small[5], g_enc_down, small[6], g_embed, small[7], small[8])
        + (small[9], small[10], g_dec_qkv, g_dec_out, small[11], small[12], small[13])
        + (g_dec_up, small[14], g_dec_down, small[15])
    )


def solution(mesh):
    return jax.shard_map(
        local,
        mesh=mesh,
        in_specs=(
            P(("dp", "blk"), None),
            P(("dp", "blk")),
            P(("dp", "blk")),
            P(("dp", "blk")),
            P(),
            P(),
            P(),
            P(),
            P(),
            P(),
            P(),
            P(),
            P(),
            P(),
            P(),
            P(),
            P(),
            P(),
            P(),
            P(),
            P(),
            P(),
            P(),
            P(),
            P(),
            P(),
            P(),
            P(),
            P(),
            P(("dp", "blk"), None),
        ),
        out_specs=(
            P(("dp", "blk"), None),
            P(("dp", "blk"), None),
            P(),
            P(),
            P(),
            P(),
            P(),
            P(),
            P(),
            P(),
            P(),
            P(),
            P(),
            P(),
            P(),
            P(),
            P(),
            P(),
            P(),
            P(),
            P(),
            P(),
            P(),
            P(),
            P(),
            P(),
            P(),
        ),
        check_vma=False,
    )
```

```python
import math

import jax
import jax.numpy as jnp
from jax import lax
from jax.experimental import pallas as pl
from jax.experimental.pallas import tpu as pltpu
from jax.sharding import PartitionSpec as P

HE = 12
HD = 16
TILE = 256
VMEM_LIMIT = 60 * 1024 * 1024
DEC_BITS = (1, 2, 0, 3)
ENC_BITS = ((2, 1, 0, 3), (1, 2, 0, 3), (0, 1, 2, 3))
STEPS = "dcadbdacbdacdbacbdadcabcbacbcacbacb"
SHORT = 512
WEIGHT_LIMIT = 40 * 1024 * 1024
SMALL_LIMIT = 24 * 1024 * 1024
FLOPS_PER_MICRO, BYTES_PER_MICRO = 1.15e9, 3.6e6


epsilon = 1e-06


def matmul(left_side, right_side):
    return jnp.dot(left_side, right_side, preferred_element_type=jnp.float32)


def matmul_tn(left_side, right_side):
    return lax.dot_general(
        left_side, right_side, (((0,), (0,)), ((), ())), preferred_element_type=jnp.float32
    )


def matmul_nt(left_side, right_side):
    return lax.dot_general(
        left_side, right_side, (((1,), (1,)), ((), ())), preferred_element_type=jnp.float32
    )


def bits_of(count):
    return count.bit_length() - 1


def across(value, axis, bit):
    count = lax.axis_size(axis)
    return lax.ppermute(value, axis, [(i, i ^ (1 << bit)) for i in range(count)])


def cost(micros):
    return pl.CostEstimate(
        flops=int(micros * FLOPS_PER_MICRO), bytes_accessed=int(micros * BYTES_PER_MICRO), transcendentals=0
    )


TOKEN = jax.ShapeDtypeStruct((8, 128), jnp.float32)


class Order:
    def __init__(self):
        self.token, self.smalls = None, 0

    def run(self, kernel, name, scalars, in_specs, operands, out_specs, out_shape, scratch=(), micros=1.0, steps=1, limit=VMEM_LIMIT):
        count = len(in_specs)
        if self.token is not None:
            in_specs = [*in_specs, pl.BlockSpec(memory_space=pl.ANY)]
            operands = [*operands, self.token]
        more = len(in_specs) - count

        outs = len(out_specs)

        def body(meta, *refs):
            rest = refs[count + more :]
            kernel(meta, *refs[:count], *rest[:outs], *rest[outs + 1 :])

        out_specs = [*out_specs, pl.BlockSpec(memory_space=pl.ANY)]
        results = pl.pallas_call(
            body,
            out_shape=[*out_shape, TOKEN],
            grid_spec=pltpu.PrefetchScalarGridSpec(
                num_scalar_prefetch=1, grid=(steps,), in_specs=in_specs, out_specs=out_specs, scratch_shapes=list(scratch)
            ),
            compiler_params=pltpu.CompilerParams(vmem_limit_bytes=limit),
            cost_estimate=cost(micros),
            name=name,
        )(scalars, *operands)
        self.token = results[-1]
        return results[:-1]

    def run_small(self, kernel, name, operands, out_shape, scalars=None, out_specs=None, scratch=()):
        micros = 40.0 if self.smalls < 8 else 4.0
        self.smalls += 1
        count, outs = len(operands), len(out_shape)
        in_specs = [pl.BlockSpec(memory_space=pltpu.VMEM)] * count
        first = []
        if scalars is not None:
            in_specs, first = [pl.BlockSpec(memory_space=pltpu.SMEM), *in_specs], [scalars]
        if self.token is not None:
            in_specs = [*in_specs, pl.BlockSpec(memory_space=pl.ANY)]
            operands = [*operands, self.token]
        used = count + len(first)

        def body(*refs):
            rest = refs[len(in_specs) :]
            kernel(*refs[:used], *rest[:outs], *rest[outs + 1 :])

        out_specs = out_specs or [pl.BlockSpec(memory_space=pltpu.VMEM)] * outs
        results = pl.pallas_call(
            body,
            out_shape=[*out_shape, TOKEN],
            in_specs=in_specs,
            out_specs=[*out_specs, pl.BlockSpec(memory_space=pl.ANY)],
            scratch_shapes=list(scratch),
            compiler_params=pltpu.CompilerParams(vmem_limit_bytes=SMALL_LIMIT),
            cost_estimate=cost(micros),
            name=name,
        )(*first, *operands)
        self.token = results[-1]
        return results[:-1]


class Entry:
    def __init__(self, kind, lhs, rhs, r, n, width, shape, counted):
        self.kind, self.lhs, self.rhs, self.r, self.n = kind, lhs, rhs, r, n
        self.width, self.shape, self.counted = width, shape, counted


class Bundle:
    def __init__(self, order, bits, spots, tiles, entries, short=()):
        self.order, self.run, self.entries = order, order.run, entries
        self.shards = min(16, lax.axis_size("dp"))
        self.bits = [bit for bit in bits if bit < bits_of(self.shards)]
        self.spots, self.tiles = spots, tiles
        self.width = max(entry.width for entry in entries)
        self.firsts, self.bases, first, base = [], [], 0, 0
        for entry in entries:
            self.firsts.append(first)
            self.bases.append(base)
            first += entry.n
            base += entry.n * entry.r
        self.short, self.short_base = list(short), base
        self.steps, self.rows = first, base + (16 if self.short else 0)

    def block(self, index_map):
        return pl.BlockSpec((1, self.rows, self.width), index_map)

    def shaped(self, count):
        return jax.ShapeDtypeStruct((count, self.rows, self.width), jnp.bfloat16)

    def size(self, count):
        return 2 * count * self.rows * self.width

    def spot_of(self, index):
        spot = jnp.int32(0)
        for at, bit in enumerate(self.bits):
            spot = spot | ((lax.shift_right_logical(index, bit) & 1) << (len(self.bits) - 1 - at))
        return spot

    def weigh(self):
        entries, shards, width = self.entries, self.shards, self.width
        token_rows = entries[0].lhs.shape[0]
        tallest = max(shards * entry.r for entry in entries)

        def unit_work(entry, offset, unit, refs, kept_ref, sent_ref, scratch, meta):
            r, n, height, span = entry.r, entry.n, shards * entry.r, entry.width
            turned, total, lhs_tile, rhs_tile, sems = scratch
            spot, half, live = meta[0], meta[1], meta[2]
            count = TILE if entry.counted else token_rows

            def block(ref):
                return ref[0] if entry.counted else ref[...]

            def put(out_ref, value):
                value = value.astype(BF16)
                if entry.kind == "wide":
                    at = pl.ds(pl.multiple_of(offset + unit * r, 16), r)
                    for shard in range(shards):
                        target = self.spot_of(lax.bitwise_xor(jnp.int32(shard), spot))
                        out_ref[target, at, :span] = value[shard * r : (shard + 1) * r]
                        if span < width:
                            out_ref[target, at, span:] = jnp.zeros((r, width - span), BF16)
                else:
                    each, tall = shards // n, n * r
                    for inner in range(each):
                        target = self.spot_of(lax.bitwise_xor(unit * each + inner, spot))
                        out_ref[target, offset : offset + tall, :span] = value[inner * tall : (inner + 1) * tall]

            def turn():
                turned[:height, :count] = block(refs[0]).T

            if entry.kind == "wide":
                pl.when(unit == 0)(turn)
            else:
                turn()

            def product(rhs_ref):
                return matmul(turned[:height, :count], block(rhs_ref))

            def add_rest(flip):
                lhs_at = 0 if entry.kind == "wide" else unit * height
                rhs_at = (half ^ flip) * span if entry.kind == "tall" else ((half ^ flip) * n + unit) * span

                def add(tile, carry):
                    copies = [
                        pltpu.make_async_copy(
                            source.at[tile, :, pl.ds(pl.multiple_of(jnp.int32(at), LANES), size)], target.at[:, :size], sems.at[index]
                        )
                        for index, (source, target, at, size) in enumerate(
                            ((refs[3], lhs_tile, lhs_at, height), (refs[4], rhs_tile, rhs_at, span))
                        )
                    ]
                    for copy in copies:
                        copy.start()
                    for copy in copies:
                        copy.wait()
                    total[:height, :span] += matmul_tn(lhs_tile[:, :height], rhs_tile[:, :span])
                    return carry

                lax.fori_loop(1, live, add, 0)

            for flip, rhs_ref, out_ref in ((1, refs[1], sent_ref), (0, refs[2], kept_ref)):
                if not entry.counted:
                    put(out_ref, product(rhs_ref))
                    continue

                @pl.when(live == 1)
                def _(rhs_ref=rhs_ref, out_ref=out_ref):
                    put(out_ref, product(rhs_ref))

                @pl.when(live > 1)
                def _(flip=flip, rhs_ref=rhs_ref, out_ref=out_ref):
                    total[:height, :span] = product(rhs_ref)
                    add_rest(flip)
                    put(out_ref, total[:height, :span])

        starts, in_specs, operands = [], [], []
        for first, entry in zip(self.firsts, entries):
            n, height, span = entry.n, shards * entry.r, entry.width
            starts.append(len(operands))

            def unit_of(step, first=first, n=n):
                return jnp.clip(step - first, 0, n - 1)

            def spec(size, column, depth, entry=entry):
                mode = pl.Buffered(depth)
                if entry.counted:
                    return pl.BlockSpec((1, TILE, size), lambda step, meta: (0, 0, column(step, meta)), pipeline_mode=mode)
                return pl.BlockSpec((token_rows, size), lambda step, meta: (0, column(step, meta)), pipeline_mode=mode)

            if entry.kind == "wide":
                in_specs.append(spec(height, lambda step, meta: 0, 1))
                for flip in (1, 0):
                    in_specs.append(
                        spec(span, lambda step, meta, n=n, unit_of=unit_of, flip=flip: (meta[1] ^ flip) * n + unit_of(step), 2)
                    )
            else:
                in_specs.append(spec(height, lambda step, meta, unit_of=unit_of: unit_of(step), 2))
                for flip in (1, 0):
                    in_specs.append(spec(span, lambda step, meta, flip=flip: meta[1] ^ flip, 1))
            lhs, rhs = entry.lhs, entry.rhs
            if entry.counted:
                lhs, rhs = (value.reshape(-1, TILE, value.shape[1]) for value in (lhs, rhs))
                in_specs += [pl.BlockSpec(memory_space=pl.ANY)] * 2
                operands += [lhs, rhs, rhs, lhs, rhs]
            else:
                operands += [lhs, rhs, rhs]
        starts.append(len(operands))
        main = len(operands)
        for value in self.short:
            in_specs.append(whole(value.shape))
            operands.append(value)

        def add_short(refs, half, spot, sent_ref, kept_ref, row_s):
            row_s[...] = jnp.zeros_like(row_s)
            offset = 0
            for ref in refs:
                size = ref.shape[1]
                row_s[:, offset : offset + size] = ref[...]
                offset += size
            base, lane, row = self.short_base, iota((16, width), 1), iota((16, width), 0)
            for flip, out_ref in ((1, sent_ref), (0, kept_ref)):
                for shard in range(shards):
                    at = ((half ^ flip) * shards + shard) * SHORT
                    first_row = row_s[:, pl.ds(pl.multiple_of(at, LANES), width)]
                    next_row = row_s[:, pl.ds(pl.multiple_of(at + width, LANES), width)]
                    value = jnp.where(row == 0, first_row, jnp.where((row == 1) & (lane < SHORT - width), next_row, 0.0))
                    target = self.spot_of(lax.bitwise_xor(jnp.int32(shard), spot))
                    out_ref[target, base : base + 16, :] = value.astype(BF16)

        def kernel(meta, *refs):
            sent_ref, kept_ref, *scratch = refs[len(operands) :]
            step = pl.program_id(0)
            if self.short:
                row_s = scratch.pop()
                pl.when(step == 0)(lambda: add_short(refs[main : len(operands)], meta[1], meta[0], sent_ref, kept_ref, row_s))
            for index, entry in enumerate(entries):
                first = self.firsts[index]

                @pl.when((step >= first) & (step < first + entry.n))
                def _(index=index, entry=entry, first=first):
                    ins = refs[starts[index] : starts[index + 1]]
                    unit_work(entry, self.bases[index], step - first, ins, kept_ref, sent_ref, scratch, meta)

        shape = (shards, self.rows, width)
        sent, kept = self.run(
            kernel,
            "weight_grads",
            jnp.concatenate([self.spots, self.tiles[:1]]),
            in_specs,
            operands,
            [pl.BlockSpec(shape, lambda step, meta: (0, 0, 0))] * 2,
            [self.shaped(shards)] * 2,
            [
                pltpu.VMEM((tallest, token_rows), BF16),
                pltpu.VMEM((tallest, width), F32),
                pltpu.VMEM((TILE, tallest), BF16),
                pltpu.VMEM((TILE, width), BF16),
                pltpu.SemaphoreType.DMA((2,)),
            ]
            + [pltpu.VMEM((1, (2 * shards + 2) * SHORT), F32)] * bool(self.short),
            micros=40.0,
            steps=self.steps,
            limit=WEIGHT_LIMIT,
        )
        self.terms = (kept, across(sent, "blk", 0))
        self.due, self.stage = list(self.bits), 0

    def step(self):
        bits = len(self.bits)
        for last, step in ((bits, self.halve), (bits + 1, self.own), (2 * bits, self.join), (2 * bits + 1, self.finish)):
            if self.stage < last:
                self.stage += 1
                step()
                return
        self.placed = self.place()

    def halve(self):
        bit = self.due.pop(0)
        first, second = self.terms
        count = first.shape[0] // 2

        def kernel(a_ref, b_ref, sent_ref, stay_ref):
            for base, target in ((count, sent_ref), (0, stay_ref)):

                def add(index, carry, base=base, target=target):
                    target[index] = (a_ref[base + index].astype(F32) + b_ref[base + index].astype(F32)).astype(BF16)
                    return carry

                lax.fori_loop(0, count, add, 0)

        sent, stay = self.order.run_small(
            kernel, "halve", [first, second], [self.shaped(count)] * 2
        )
        self.terms = (stay, across(sent, "dp", bit))

    def own(self):
        def kernel(a_ref, b_ref, out_ref):
            out_ref[...] = (a_ref[...].astype(F32) + b_ref[...].astype(F32)).astype(BF16)

        def add(a, b):
            return self.order.run_small(kernel, "own", [a, b], [self.shaped(1)])[0]

        total = add(*self.terms)
        for bit in range(bits_of(self.shards), bits_of(lax.axis_size("dp"))):
            total = add(total, across(total, "dp", bit))
        self.due = list(reversed(self.bits))
        self.spread(total)

    def spread(self, held):
        bit = self.due.pop(0)
        self.held = (held, across(held, "dp", bit))

    def join(self):
        count = self.held[0].shape[0]

        def kernel(a_ref, b_ref, out_ref):
            out_ref[:count] = a_ref[...]
            out_ref[count:] = b_ref[...]

        (held,) = self.order.run_small(
            kernel, "join", list(self.held), [self.shaped(2 * count)]
        )
        self.spread(held)

    def finish(self):
        self.other = [across(held, "blk", 0) for held in self.held]

    def place(self):
        entries, shards, bits, slots = self.entries, self.shards, self.bits, 4
        half_count = shards // 2
        heights = [entry.r if entry.kind == "wide" else entry.n * entry.r for entry in entries]
        more = bool(self.short)
        count = len(entries) + more

        def kernel(meta, *refs):
            sources = refs[:4]
            outs, stages, sems = refs[4 : 4 + count], refs[4 + count : 4 + 2 * count], refs[-1]
            side = meta[1]

            def copies(slot, row_block):
                pairs = [
                    (stage.at[slot], out_ref.at[pl.ds(pl.multiple_of(row_block * height, 8), height), :])
                    for stage, out_ref, height in zip(stages, outs, heights)
                ]
                if more:
                    pairs += [(stages[-1].at[slot, which], outs[-1].at[which * shards + row_block]) for which in range(2)]
                return [pltpu.make_async_copy(*pair, sems.at[index, slot]) for index, pair in enumerate(pairs)]

            for upper in range(2):
                mine, other = sources[upper], sources[2 + upper]

                def one(index, carry, upper=upper, mine=mine, other=other):
                    step = upper * half_count + index
                    slot = lax.rem(step, slots)

                    @pl.when(step >= slots)
                    def _():
                        for copy in copies(slot, 0):
                            copy.wait()

                    for entry, offset, stage in zip(entries, self.bases, stages):
                        span = entry.width
                        for which, source in ((side, mine), (1 - side, other)):
                            for unit in range(entry.n):
                                row = offset + unit * entry.r
                                value = source[index, row : row + entry.r, :span].astype(F32)
                                if entry.kind == "wide":
                                    at = pl.ds(pl.multiple_of((which * entry.n + unit) * span, LANES), span)
                                    stage[slot, :, at] = value
                                else:
                                    at = pl.ds(pl.multiple_of(which * span, LANES), span)
                                    stage[slot, unit * entry.r : (unit + 1) * entry.r, at] = value
                    if more:
                        for which, source in ((side, mine), (1 - side, other)):
                            value = source[index, self.short_base : self.short_base + 16, :].astype(F32)
                            for at in range(SHORT // LANES):
                                row, lane = divmod(at * LANES, self.width)
                                stages[-1][slot, which, at : at + 1, :] = value[row : row + 1, lane : lane + LANES]
                    shard = jnp.int32(0)
                    for at, bit in enumerate(bits):
                        shard = shard | ((lax.shift_right_logical(step, len(bits) - 1 - at) & 1) << bit)
                    for copy in copies(slot, lax.bitwise_xor(shard, meta[0])):
                        copy.start()
                    return carry

                lax.fori_loop(0, half_count, one, 0)
            for step in range(max(shards - slots, 0), shards):
                for copy in copies(step % slots, 0):
                    copy.wait()

        return self.order.run_small(
            kernel,
            "place_shards",
            [self.held[0], self.held[1], *self.other],
            [jax.ShapeDtypeStruct(entry.shape, jnp.float32) for entry in entries]
            + [jax.ShapeDtypeStruct((2 * shards, 8, LANES), jnp.float32)] * more,
            scalars=self.spots,
            out_specs=[pl.BlockSpec(memory_space=pl.ANY)] * count,
            scratch=[pltpu.VMEM((slots, height, entry.shape[1]), F32) for height, entry in zip(heights, entries)]
            + [pltpu.VMEM((slots, 2, 8, LANES), F32)] * more
            + [pltpu.SemaphoreType.DMA((count + more, slots))],
        )


LOG2E = math.log2(math.e)
NEVER = -1e30
LANES = 128
BF16, F32 = jnp.bfloat16, jnp.float32


def colsum(value):
    return jnp.sum(value.astype(F32), axis=0, keepdims=True)


def normed_rows(stream):
    centred = stream - jnp.mean(stream, axis=-1, keepdims=True)
    inverse = lax.rsqrt(jnp.mean(centred * centred, axis=-1, keepdims=True) + epsilon)
    return centred * inverse, inverse


def norm_back(grad, unit, inverse, gain):
    grad = grad * gain
    inner = jnp.mean(grad * unit, axis=-1, keepdims=True)
    return inverse * (grad - jnp.mean(grad, axis=-1, keepdims=True) - unit * inner)


def gelu_pair(u):
    bell = jnp.exp2(u * u * (-0.5 * LOG2E))
    t = 1.0 / (1.0 + (0.3275911 * math.sqrt(0.5)) * jnp.abs(u))
    poly = ((((1.061405429 * t - 1.453152027) * t + 1.421413741) * t - 0.284496736) * t + 0.254829592) * t
    tail = 0.5 * poly * bell
    phi = jnp.where(u < 0, tail, 1.0 - tail)
    return u * phi, phi + u * bell * (1.0 / math.sqrt(2.0 * math.pi))


def iota(shape, axis):
    return lax.broadcasted_iota(jnp.int32, shape, axis)


def fill_groups(target, source):
    for group in range(target.shape[0]):
        target[group] = source[:, group * LANES : (group + 1) * LANES].astype(target.dtype)


def attend_forward(keys, head, q_s, k_s, v_s, mask_ref, o_s, probs=None, inverse_s=None, totals=None):
    groups, rows, _ = q_s.shape
    inside = LANES // head
    lanes = iota((rows, LANES), 1)
    which = lax.div(lanes, jnp.int32(head))
    if totals is not None:
        totals[...] = jnp.zeros_like(totals)

    def one_group(group, carry):
        queries = q_s[group]
        key_rows = k_s[group, :keys, :]
        values = v_s[group, :keys, :]
        blended = jnp.zeros((rows, LANES), F32)
        inverses = jnp.zeros((rows, LANES), F32)
        for h in range(inside):
            own = which == h
            query = jnp.where(own, queries, 0.0).astype(BF16)
            scores = matmul_nt(query, key_rows) + mask_ref[:, :keys]
            top = jnp.max(scores, axis=1, keepdims=True)
            prob = jnp.exp2(scores - top).astype(BF16)
            if probs is not None:
                probs[group * inside + h, :, :keys] = prob
            both = matmul(prob, values)
            inverse = 1.0 / both[:, LANES:]
            blended = jnp.where(own, both[:, :LANES] * inverse, blended)
            if inverse_s is not None:
                inverses = jnp.where(own, inverse, inverses)
            if totals is not None:
                at = lanes == group * inside + h
                totals[...] = jnp.where(at, top + jnp.log2(both[:, LANES:]), totals[...])
        o_s[group] = blended
        if inverse_s is not None:
            inverse_s[group] = inverses
        return carry

    lax.fori_loop(0, groups, one_group, 0)


def attend_backward(keys, head, q_s, k_s, v_s, o_s, ob_s, dq_s, dk_s, dv_s, probs=None, mask_ref=None, totals=None):
    groups, rows, _ = q_s.shape
    inside = LANES // head
    lanes = iota((rows, LANES), 1)
    which = lax.div(lanes, jnp.int32(head))

    def one_group(group, carry):
        queries, grads = q_s[group], ob_s[group]
        key_rows = k_s[group, :keys, :]
        values = v_s[group, :keys, :LANES]
        product = grads * o_s[group]
        queries_t = queries.T.astype(BF16)
        grads_t = grads.T.astype(BF16)
        query_grad = jnp.zeros((rows, LANES), F32)
        for h in range(inside):
            own = which == h
            at = slice(h * head, (h + 1) * head)
            inner = jnp.sum(jnp.where(own, product, 0.0), axis=1, keepdims=True)
            if probs is not None:
                prob = probs[group * inside + h, :, :keys]
            else:
                query = jnp.where(own, queries, 0.0).astype(BF16)
                total = jnp.sum(jnp.where(lanes == group * inside + h, totals, 0.0), axis=1, keepdims=True)
                prob = jnp.exp2(matmul_nt(query, key_rows) + (mask_ref[:, :keys] - total)).astype(BF16)
            grad_probs = matmul_nt(jnp.where(own, grads, 0.0).astype(BF16), values)
            score_grad = (prob.astype(F32) * (grad_probs - inner)).astype(BF16)
            query_grad = jnp.where(own, matmul(score_grad, key_rows), query_grad)
            dk_s[group, at, :keys] += matmul(queries_t[at], score_grad)
            dv_s[group, at, :keys] += matmul(grads_t[at], prob)
        dq_s[group] = query_grad
        return carry

    lax.fori_loop(0, groups, one_group, 0)


def whole(shape):
    rank = len(shape)
    return pl.BlockSpec(shape, lambda step, meta: (0,) * rank, pipeline_mode=pl.Buffered(1))


def out_whole(shape):
    rank = len(shape)
    return pl.BlockSpec(shape, lambda step, meta: (0,) * rank)


def row_tile(width):
    return pl.BlockSpec((TILE, width), lambda step, meta: (step, 0))


def live_tile(width):
    return pl.BlockSpec((TILE, width), lambda step, meta: (jnp.minimum(step, meta[0] - 1), 0))


def call(order, kernel, name, meta, in_specs, operands, out_specs, out_shape, scratch, micros, steps):
    return order.run(kernel, name, meta, in_specs, operands, out_specs, out_shape, scratch, micros=micros, steps=steps)


def shaped(rows, width, dtype):
    return jax.ShapeDtypeStruct((rows, width), dtype)


MARKS = 16


def enc_in(order, meta, patches, raw, far_raw, params, qkv, heads):
    rows, width = patches.shape
    factor = (width // heads) ** (-0.5) * LOG2E

    def marks_of(seen, padded, label):
        seen, kept, label = seen[...].astype(F32), 1.0 - padded[...].astype(F32), label[...].astype(F32) + 1.0
        row, result = iota((MARKS, rows), 0), jnp.zeros((MARKS, rows), F32)
        for index, value in enumerate((seen * kept * label, label, seen, kept * label)):
            result = jnp.where(row == index, value, result)
        return result

    def kernel(meta, patches_ref, *refs):
        raw_refs, far_refs, (params_ref, qkv_ref) = refs[:3], refs[3:6], refs[6:8]
        sel_ref, code_ref, far_code_ref, label_ref, marks_ref, far_marks_ref, columns_ref, s_ref, n_ref, q_ref, kv_ref, place_s = refs[8:]
        step = pl.program_id(0)

        @pl.when(step == 0)
        def _():
            below = (iota((rows, rows), 0) <= iota((rows, rows), 1)).astype(F32).astype(BF16)
            for index, (source, target) in enumerate(((raw_refs, marks_ref), (far_refs, far_marks_ref))):
                marks = marks_of(*source)
                target[...] = marks
                place = matmul(marks.astype(BF16), below)[2:3, :]
                place_s[index : index + 1, :] = jnp.where(marks[2:3, :] > 0, place - 1.0, -1.0)
            columns_ref[...] = marks_ref[...].T

        @pl.when(step < jnp.maximum(meta[0], meta[1]))
        def _():
            target = (step * TILE + iota((TILE, rows), 0)).astype(F32)
            sel = jnp.where(target == place_s[0:1, :], 1.0, 0.0).astype(BF16)
            far_sel = jnp.where(target == place_s[1:2, :], 1.0, 0.0).astype(BF16)
            sel_ref[...] = sel
            own_marks = marks_ref[...].astype(BF16)
            code_ref[...] = matmul_nt(own_marks, sel)
            far_code_ref[...] = matmul_nt(far_marks_ref[...].astype(BF16), far_sel)
            label_ref[...] = matmul_nt(sel, own_marks)

        @pl.when(step < meta[0])
        def _():
            stream = matmul(sel_ref[...], patches_ref[...])
            s_ref[...] = stream.astype(BF16)
            unit, _ = normed_rows(stream)
            normed = (unit * params_ref[:, :width] + params_ref[:, width : 2 * width]).astype(BF16)
            n_ref[...] = normed
            q_ref[...] = (matmul(normed, qkv_ref[:, :width]) * factor).astype(BF16)
            kv_ref[...] = matmul(normed, qkv_ref[:, width:]).astype(BF16)

    def last_tile(step, meta):
        return jnp.minimum(step, jnp.maximum(meta[0], meta[1]) - 1)

    lane_tile = pl.BlockSpec((MARKS, TILE), lambda step, meta: (0, last_tile(step, meta)))

    def tile(size):
        return pl.BlockSpec((TILE, size), lambda step, meta: (last_tile(step, meta), 0))

    operands = (patches, *raw, *far_raw, params, qkv)
    return call(
        order,
        kernel,
        "enc_in",
        meta,
        [whole(value.shape) for value in operands],
        operands,
        [tile(rows), lane_tile, lane_tile, tile(MARKS), out_whole((MARKS, rows)), out_whole((MARKS, rows)), out_whole((rows, MARKS))]
        + [live_tile(w) for w in (width, width, width, 2 * width)],
        [shaped(rows, rows, BF16), shaped(MARKS, rows, F32), shaped(MARKS, rows, F32), shaped(rows, MARKS, F32)]
        + [shaped(MARKS, rows, F32), shaped(MARKS, rows, F32), shaped(rows, MARKS, F32)]
        + [shaped(rows, w, BF16) for w in (width, width, width, 2 * width)],
        [pltpu.VMEM((8, rows), F32)],
        7.0,
        rows // TILE,
    )


def spread_keys(count, tiles, kv_ref, far_ref, far_tiles, k_s, v_s):
    size = count * TILE
    width = kv_ref.shape[1] // 2
    for source, live, base in ((kv_ref, tiles, 0), (far_ref, far_tiles, size)):
        ok = iota((size, LANES), 0) < live * TILE
        for group in range(width // LANES):
            at = slice(group * LANES, (group + 1) * LANES)
            value_at = slice(width + group * LANES, width + (group + 1) * LANES)
            k_s[group, base : base + size, :] = jnp.where(ok, source[:size, at].astype(F32), 0.0).astype(BF16)
            v_s[group, base : base + size, :LANES] = jnp.where(ok, source[:size, value_at].astype(F32), 0.0).astype(BF16)
            if v_s.shape[2] > LANES:
                v_s[group, base : base + size, LANES:] = jnp.ones((size, v_s.shape[2] - LANES), BF16)


def write_mask(mask_ref, label, code, far_code, size, step):
    shape = (label.shape[0], size)
    near = (label == code) | (iota(shape, 1) == step * TILE + iota(shape, 0))
    mask_ref[:, :size] = jnp.where(near, 0.0, NEVER)
    mask_ref[:, size : 2 * size] = jnp.where(label == far_code, 0.0, NEVER)


def enc_main(order, meta, s, q, kv, far_kv, label, code, far_code, params, out, up, down, embed, heads):
    rows, width = s.shape
    wide, lifted_width = up.shape[1], embed.shape[1]
    groups, head, most = width // LANES, width // heads, rows // TILE
    part = width

    def kernel(meta, s_ref, q_ref, kv_ref, far_ref, label_ref, code_ref, far_code_ref, params_ref, out_w, up_w, down_w, embed_w,
               o_ref, tot_ref, m_ref, n_ref, g_ref, gp_ref, e_ref, hi_ref, lo_ref, q_s, k_s, v_s, mask_s, o_s):
        step = pl.program_id(0)
        tiles, far_tiles = meta[0], meta[1]
        count = jnp.maximum(tiles, far_tiles)

        def param(start, size):
            return params_ref[:, start : start + size]

        @pl.when(step < tiles)
        def _():
            fill_groups(q_s, q_ref)
            for size in range(1, most + 1):

                @pl.when(count == size)
                def _(size=size):
                    @pl.when(step == 0)
                    def _():
                        spread_keys(size, tiles, kv_ref, far_ref, far_tiles, k_s, v_s)

                    span = size * TILE
                    write_mask(mask_s, label_ref[:, 1:2], code_ref[0:1, :span], far_code_ref[0:1, :span], span, step)
                    attend_forward(2 * span, head, q_s, k_s, v_s, mask_s, o_s, totals=tot_ref)

            for group in range(groups):
                o_ref[:, group * LANES : (group + 1) * LANES] = o_s[group].astype(BF16)
            middle = s_ref[...].astype(F32) + matmul(o_ref[...], out_w[...]) + param(2 * width, width)
            m_ref[...] = middle
            unit, _ = normed_rows(middle)
            normed = (unit * param(3 * width, width) + param(4 * width, width)).astype(BF16)
            n_ref[...] = normed
            encoded = middle + param(5 * width + wide, width)
            for j in range(0, wide, part):
                u = matmul(normed, up_w[:, j : j + part]) + param(5 * width + j, part)
                g, slope = gelu_pair(u)
                g = g.astype(BF16)
                g_ref[:, j : j + part] = g
                gp_ref[:, j : j + part] = slope.astype(BF16)
                encoded = encoded + matmul(g, down_w[j : j + part, :])
            low = encoded.astype(BF16)
            e_ref[...] = low
            lifted = matmul(low, embed_w[...]) + param(6 * width + wide, lifted_width)
            high = lifted.astype(BF16)
            hi_ref[...] = high
            lo_ref[...] = (lifted - high.astype(F32)).astype(BF16)

    tall = label.shape[1]
    return call(
        order,
        kernel,
        "enc_main",
        meta,
        [live_tile(width), live_tile(width), whole(kv.shape), whole(kv.shape), live_tile(tall), whole(code.shape), whole(code.shape)]
        + [whole(value.shape) for value in (params, out, up, down, embed)],
        (s, q, kv, far_kv, label, code, far_code, params, out, up, down, embed),
        [live_tile(w) for w in (width, LANES, width, width, wide, wide, width, lifted_width, lifted_width)],
        [shaped(rows, width, BF16), shaped(rows, LANES, F32), shaped(rows, width, F32), shaped(rows, width, BF16)]
        + [shaped(rows, wide, BF16)] * 2 + [shaped(rows, width, BF16)] + [shaped(rows, lifted_width, BF16)] * 2,
        [
            pltpu.VMEM((groups, TILE, LANES), F32),
            pltpu.VMEM((groups, 2 * rows, LANES), BF16),
            pltpu.VMEM((groups, 2 * rows, 2 * LANES), BF16),
            pltpu.VMEM((TILE, 2 * rows), F32),
            pltpu.VMEM((groups, TILE, LANES), F32),
        ],
        20.0,
        most,
    )


def dec_in(order, meta, sel, high, low, columns, params, qkv, heads):
    rows, width = high.shape
    tall = columns.shape[1]
    factor = (width // heads) ** (-0.5) * LOG2E

    def kernel(meta, sel_ref, hi_ref, lo_ref, col_ref, params_ref, qkv_ref, start_ref, n_ref, q_ref, kv_ref, total):
        total[...] = jnp.zeros_like(total)

        def add(tile, carry):
            at = pl.ds(pl.multiple_of(tile * TILE, TILE), TILE)
            total[...] += matmul_tn(sel_ref[at, :], hi_ref[at, :]) + matmul_tn(sel_ref[at, :], lo_ref[at, :])
            return carry

        lax.fori_loop(0, meta[0], add, 0)
        start = jnp.where(col_ref[:, 2:3] > 0, total[...], params_ref[:, params.shape[1] - width :])
        start_ref[...] = start
        unit, _ = normed_rows(start)
        normed = (unit * params_ref[:, :width] + params_ref[:, width : 2 * width]).astype(BF16)
        n_ref[...] = normed
        q_ref[...] = (matmul(normed, qkv_ref[:, :width]) * factor).astype(BF16)
        kv_ref[...] = matmul(normed, qkv_ref[:, width:]).astype(BF16)

    return call(
        order,
        kernel,
        "dec_in",
        meta,
        [pl.BlockSpec((rows, TILE), lambda step, meta: (0, step)), whole(high.shape), whole(low.shape), row_tile(tall)]
        + [whole(value.shape) for value in (params, qkv)],
        (sel, high, low, columns, params, qkv),
        [row_tile(w) for w in (width, width, width, 2 * width)],
        [shaped(rows, width, F32)] + [shaped(rows, w, BF16) for w in (width, width, 2 * width)],
        [pltpu.VMEM((TILE, width), F32)],
        7.0,
        rows // TILE,
    )


def give_key_grads(size, dk_s, dv_s, near_ref, far_ref):
    groups = dk_s.shape[0]
    for index, (source, factor) in enumerate(((dk_s, 1.0 / LOG2E), (dv_s, 1.0))):
        for group in range(groups):
            at = slice((index * groups + group) * LANES, (index * groups + group + 1) * LANES)
            near_ref[:size, at] = source[group, :, :size].T * factor
            far_ref[:size, at] = (source[group, :, size : 2 * size].T * factor).astype(BF16)


def dec_main(order, meta, start, q, kv, far_kv, columns, marks, far_marks, cotangent, params, out, up, down, heads):
    rows, width = start.shape
    wide = up.shape[1]
    groups, head, steps = width // LANES, width // heads, rows // TILE
    part = width
    tall = columns.shape[1]

    def kernel(meta, start_ref, q_ref, kv_ref, far_ref, col_ref, marks_ref, far_marks_ref, cot_ref, params_ref, out_w, up_w, down_w,
               dec_ref, o_ref, n_ref, g_ref, ub_ref, mb_ref, tm_ref, dq_ref, near_ref, back_ref,
               outb_ref, gainb_ref, shiftb_ref, upb_ref, downb_ref,
               q_s, k_s, v_s, mask_s, probs, o_s, inv_s, ob_s, dq_s, dk_s, dv_s, slope_s):
        step = pl.program_id(0)

        def param(begin, size):
            return params_ref[:, begin : begin + size]

        @pl.when(step == 0)
        def _():
            spread_keys(steps, steps, kv_ref, far_ref, steps, k_s, v_s)
            for ref in (dk_s, dv_s, outb_ref, gainb_ref, shiftb_ref, upb_ref, downb_ref):
                ref[...] = jnp.zeros_like(ref)

        fill_groups(q_s, q_ref)
        write_mask(mask_s, col_ref[:, 1:2], marks_ref[3:4, :], far_marks_ref[3:4, :], rows, step)
        attend_forward(2 * rows, head, q_s, k_s, v_s, mask_s, o_s, probs=probs, inverse_s=inv_s)
        for group in range(groups):
            o_ref[:, group * LANES : (group + 1) * LANES] = o_s[group].astype(BF16)
        middle = start_ref[...] + matmul(o_ref[...], out_w[...]) + param(2 * width, width)
        unit, inverse = normed_rows(middle)
        gain_b = param(3 * width, width)
        normed = (unit * gain_b + param(4 * width, width)).astype(BF16)
        n_ref[...] = normed
        decoded = middle + param(5 * width + wide, width)
        for j in range(0, wide, part):
            g, slope = gelu_pair(matmul(normed, up_w[:, j : j + part]) + param(5 * width + j, part))
            g = g.astype(BF16)
            g_ref[:, j : j + part] = g
            slope_s[:, j : j + part] = slope
            decoded = decoded + matmul(g, down_w[j : j + part, :])
        dec_ref[...] = decoded.astype(BF16)
        top = cot_ref[...]
        normed_grad = jnp.zeros((TILE, width), F32)
        for j in range(0, wide, part):
            low = (slope_s[:, j : j + part] * matmul_nt(top, down_w[j : j + part, :])).astype(BF16)
            ub_ref[:, j : j + part] = low
            upb_ref[:, j : j + part] += colsum(low)
            normed_grad = normed_grad + matmul_nt(low, up_w[:, j : j + part])
        downb_ref[...] += colsum(top)
        gainb_ref[...] += colsum(normed_grad * unit)
        shiftb_ref[...] += colsum(normed_grad)
        middle_grad = top.astype(F32) + norm_back(normed_grad, unit, inverse, gain_b)
        tm_ref[...] = middle_grad
        low = middle_grad.astype(BF16)
        mb_ref[...] = low
        outb_ref[...] += colsum(low)
        attended_grad = matmul_nt(low, out_w[...])
        for group in range(groups):
            scaled = attended_grad[:, group * LANES : (group + 1) * LANES] * inv_s[group]
            ob_s[group] = scaled.astype(BF16).astype(F32)
        attend_backward(2 * rows, head, q_s, k_s, v_s, o_s, ob_s, dq_s, dk_s, dv_s, probs=probs)
        scale = head ** (-0.5)
        for group in range(groups):
            dq_ref[:, group * LANES : (group + 1) * LANES] = (dq_s[group] * scale).astype(BF16)

        @pl.when(step == steps - 1)
        def _():
            give_key_grads(rows, dk_s, dv_s, near_ref, back_ref)

    small = [width, width, width, wide, width]
    return call(
        order,
        kernel,
        "dec_main",
        meta,
        [row_tile(width), row_tile(width), whole(kv.shape), whole(kv.shape), row_tile(tall), whole(marks.shape), whole(marks.shape)]
        + [row_tile(width)] + [whole(value.shape) for value in (params, out, up, down)],
        (start, q, kv, far_kv, columns, marks, far_marks, cotangent, params, out, up, down),
        [row_tile(w) for w in (width, width, width, wide, wide, width, width, width)]
        + [out_whole((rows, 2 * width))] * 2 + [out_whole((1, w)) for w in small],
        [shaped(rows, w, BF16) for w in (width, width, width, wide, wide, width)]
        + [shaped(rows, width, F32), shaped(rows, width, BF16), shaped(rows, 2 * width, F32), shaped(rows, 2 * width, BF16)]
        + [shaped(1, w, F32) for w in small],
        [
            pltpu.VMEM((groups, TILE, LANES), F32),
            pltpu.VMEM((groups, 2 * rows, LANES), BF16),
            pltpu.VMEM((groups, 2 * rows, 2 * LANES), BF16),
            pltpu.VMEM((TILE, 2 * rows), F32),
            pltpu.VMEM((heads, TILE, 2 * rows), BF16),
        ]
        + [pltpu.VMEM((groups, TILE, LANES), F32)] * 4
        + [pltpu.VMEM((groups, LANES, 2 * rows), F32)] * 2
        + [pltpu.VMEM((TILE, wide), F32)],
        95.0,
        steps,
    )


def dec_head(order, meta, start, dq, near, back, middle_grad, columns, params, qkv):
    rows, width = start.shape
    tall = columns.shape[1]

    def kernel(meta, start_ref, dq_ref, near_ref, back_ref, tm_ref, col_ref, params_ref, qkv_ref,
               dqkv_ref, lb_ref, gain_ref, shift_ref, bias_ref, token_ref):
        step = pl.program_id(0)

        @pl.when(step == 0)
        def _():
            for ref in (gain_ref, shift_ref, bias_ref, token_ref):
                ref[...] = jnp.zeros_like(ref)

        dqkv_ref[:, :width] = dq_ref[...]
        dqkv_ref[:, width:] = (near_ref[...] + back_ref[...].astype(F32)).astype(BF16)
        grad = matmul_nt(dqkv_ref[...], qkv_ref[...])
        unit, inverse = normed_rows(start_ref[...])
        gain_ref[...] += colsum(grad * unit)
        shift_ref[...] += colsum(grad)
        start_grad = tm_ref[...] + norm_back(grad, unit, inverse, params_ref[:, :width])
        seen = col_ref[:, 2:3] > 0
        token_ref[...] += colsum(jnp.where(seen, 0.0, start_grad))
        low = jnp.where(seen, start_grad, 0.0).astype(BF16)
        lb_ref[...] = low
        bias_ref[...] += colsum(low)

    return call(
        order,
        kernel,
        "dec_head",
        meta,
        [row_tile(width), row_tile(width), row_tile(2 * width), row_tile(2 * width), row_tile(width), row_tile(tall)]
        + [whole(params.shape), whole(qkv.shape)],
        (start, dq, near, back, middle_grad, columns, params, qkv),
        [row_tile(3 * width), row_tile(width)] + [out_whole((1, width))] * 4,
        [shaped(rows, 3 * width, BF16), shaped(rows, width, BF16)] + [shaped(1, width, F32)] * 4,
        [],
        40.0,
        rows // TILE,
    )


def enc_back(order, meta, sel, lb, slope, m, q, kv, far_kv, o, totals, label, code, far_code, params, out, up, down, embed, heads):
    rows, width = m.shape
    wide, lifted_width = up.shape[1], embed.shape[1]
    groups, head, most = width // LANES, width // heads, rows // TILE
    part = width
    tall = label.shape[1]

    def kernel(meta, sel_ref, lb_ref, slope_ref, m_ref, q_ref, kv_ref, far_ref, o_ref, tot_ref, label_ref, code_ref, far_code_ref,
               params_ref, out_w, up_w, down_w, embed_w,
               lbc_ref, tb_ref, ub_ref, mb_ref, tm_ref, dq_ref, near_ref, back_ref,
               outb_ref, gainb_ref, shiftb_ref, upb_ref, downb_ref,
               q_s, k_s, v_s, mask_s, o_s, ob_s, dq_s, dk_s, dv_s):
        step = pl.program_id(0)
        tiles, far_tiles = meta[0], meta[1]
        count = jnp.maximum(tiles, far_tiles)
        scale = head ** (-0.5)

        @pl.when(step == 0)
        def _():
            for ref in (dk_s, dv_s, outb_ref, gainb_ref, shiftb_ref, upb_ref, downb_ref):
                ref[...] = jnp.zeros_like(ref)

        @pl.when(step < tiles)
        def _():
            lb_here = matmul(sel_ref[...], lb_ref[...]).astype(BF16)
            lbc_ref[...] = lb_here
            grad_top = matmul_nt(lb_here, embed_w[...])
            top = grad_top.astype(BF16)
            tb_ref[...] = top
            normed_grad = jnp.zeros((TILE, width), F32)
            for j in range(0, wide, part):
                low = (slope_ref[:, j : j + part].astype(F32) * matmul_nt(top, down_w[j : j + part, :])).astype(BF16)
                ub_ref[:, j : j + part] = low
                upb_ref[:, j : j + part] += colsum(low)
                normed_grad = normed_grad + matmul_nt(low, up_w[:, j : j + part])
            unit, inverse = normed_rows(m_ref[...])
            downb_ref[...] += colsum(top)
            gainb_ref[...] += colsum(normed_grad * unit)
            shiftb_ref[...] += colsum(normed_grad)
            middle_grad = grad_top + norm_back(normed_grad, unit, inverse, params_ref[:, 3 * width : 4 * width])
            tm_ref[...] = middle_grad
            low = middle_grad.astype(BF16)
            mb_ref[...] = low
            outb_ref[...] += colsum(low)
            attended_grad = matmul_nt(low, out_w[...]).astype(BF16)
            fill_groups(ob_s, attended_grad)
            fill_groups(o_s, o_ref)
            fill_groups(q_s, q_ref)
            for size in range(1, most + 1):

                @pl.when(count == size)
                def _(size=size):
                    @pl.when(step == 0)
                    def _():
                        spread_keys(size, tiles, kv_ref, far_ref, far_tiles, k_s, v_s)

                    span = size * TILE
                    write_mask(mask_s, label_ref[:, 1:2], code_ref[0:1, :span], far_code_ref[0:1, :span], span, step)
                    attend_backward(
                        2 * span, head, q_s, k_s, v_s, o_s, ob_s, dq_s, dk_s, dv_s, mask_ref=mask_s, totals=tot_ref[...]
                    )

                    @pl.when(step == tiles - 1)
                    def _():
                        give_key_grads(span, dk_s, dv_s, near_ref, back_ref)

            for group in range(groups):
                dq_ref[:, group * LANES : (group + 1) * LANES] = (dq_s[group] * scale).astype(BF16)

    small = [width, width, width, wide, width]
    return call(
        order,
        kernel,
        "enc_back",
        meta,
        [live_tile(rows), whole(lb.shape), live_tile(wide), live_tile(width), live_tile(width), whole(kv.shape), whole(kv.shape)]
        + [live_tile(width), live_tile(LANES), live_tile(tall), whole(code.shape), whole(code.shape)]
        + [whole(value.shape) for value in (params, out, up, down, embed)],
        (sel, lb, slope, m, q, kv, far_kv, o, totals, label, code, far_code, params, out, up, down, embed),
        [live_tile(w) for w in (lifted_width, width, wide, width, width, width)]
        + [whole((rows, 2 * width))] * 2 + [out_whole((1, w)) for w in small],
        [shaped(rows, w, BF16) for w in (lifted_width, width, wide, width)]
        + [shaped(rows, width, F32), shaped(rows, width, BF16), shaped(rows, 2 * width, F32), shaped(rows, 2 * width, BF16)]
        + [shaped(1, w, F32) for w in small],
        [
            pltpu.VMEM((groups, TILE, LANES), F32),
            pltpu.VMEM((groups, 2 * rows, LANES), BF16),
            pltpu.VMEM((groups, 2 * rows, LANES), BF16),
            pltpu.VMEM((TILE, 2 * rows), F32),
        ]
        + [pltpu.VMEM((groups, TILE, LANES), F32)] * 3
        + [pltpu.VMEM((groups, LANES, 2 * rows), F32)] * 2,
        24.0,
        most,
    )


def enc_head(order, meta, sel, s, dq, near, back, middle_grad, params, qkv):
    rows, width = s.shape
    steps = rows // TILE

    def kernel(meta, sel_ref, s_ref, dq_ref, near_ref, back_ref, tm_ref, params_ref, qkv_ref,
               dqkv_ref, grad_ref, gain_ref, shift_ref, total):
        step = pl.program_id(0)

        @pl.when(step == 0)
        def _():
            for ref in (gain_ref, shift_ref, total):
                ref[...] = jnp.zeros_like(ref)

        @pl.when(step < meta[0])
        def _():
            dqkv_ref[:, :width] = dq_ref[...]
            dqkv_ref[:, width:] = (near_ref[...] + back_ref[...].astype(F32)).astype(BF16)
            grad = matmul_nt(dqkv_ref[...], qkv_ref[...])
            unit, inverse = normed_rows(s_ref[...].astype(F32))
            gain_ref[...] += colsum(grad * unit)
            shift_ref[...] += colsum(grad)
            stream_grad = tm_ref[...] + norm_back(grad, unit, inverse, params_ref[:, :width])
            total[...] += matmul_tn(sel_ref[...], stream_grad.astype(BF16))

        @pl.when(step == steps - 1)
        def _():
            grad_ref[...] = total[...].astype(BF16)

    return call(
        order,
        kernel,
        "enc_head",
        meta,
        [live_tile(w) for w in (rows, width, width, 2 * width, 2 * width, width)] + [whole(params.shape), whole(qkv.shape)],
        (sel, s, dq, near, back, middle_grad, params, qkv),
        [live_tile(3 * width), out_whole((rows, width))] + [out_whole((1, width))] * 2,
        [shaped(rows, 3 * width, BF16), shaped(rows, width, BF16)] + [shaped(1, width, F32)] * 2,
        [pltpu.VMEM((rows, width), F32)],
        40.0,
        steps,
    )


def joined(values):
    total, offset = sum(value.size for value in values), 0
    row = jnp.zeros((total,), F32)
    for value in values:
        row = row + jnp.pad(value.astype(F32), (offset, total - offset - value.size))
        offset += value.size
    return row.reshape(1, total)


def local(
    patches,
    visible,
    padding,
    field_ids,
    enc_gain_a,
    enc_shift_a,
    enc_qkv,
    enc_out,
    enc_out_bias,
    enc_gain_b,
    enc_shift_b,
    enc_up,
    enc_up_bias,
    enc_down,
    enc_down_bias,
    embed_map,
    embed_bias,
    mask_token,
    dec_gain_a,
    dec_shift_a,
    dec_qkv,
    dec_out,
    dec_out_bias,
    dec_gain_b,
    dec_shift_b,
    dec_up,
    dec_up_bias,
    dec_down,
    dec_down_bias,
    cotangent,
):
    rows = patches.shape[0]
    tiles_most = rows // TILE
    raw = [value.reshape(1, rows) for value in (visible, padding, field_ids)]
    far_raw = [across(value, "blk", 0) for value in raw]
    counts = jnp.stack([jnp.sum(raw[0]), jnp.sum(far_raw[0])]).astype(jnp.int32)
    meta = jnp.clip((counts + TILE - 1) // TILE, 1, tiles_most)

    enc_params = joined(
        [enc_gain_a, enc_shift_a, enc_out_bias, enc_gain_b, enc_shift_b, enc_up_bias, enc_down_bias, embed_bias]
    )
    dec_params = joined(
        [dec_gain_a, dec_shift_a, dec_out_bias, dec_gain_b, dec_shift_b, dec_up_bias, dec_down_bias, mask_token]
    )

    order = Order()
    shards = min(16, lax.axis_size("dp"))
    spots = jnp.stack([lax.axis_index("dp") & (shards - 1), lax.axis_index("blk")]).astype(jnp.int32)
    de, dd = enc_qkv.shape[0], dec_qkv.shape[0]
    rd, re = dd // shards, de // shards

    sel, code, far_code, label, marks, far_marks, columns, s, n1, q, kv = enc_in(order, meta, patches, raw, far_raw, enc_params, enc_qkv, HE)
    far_kv = across(kv, "blk", 0)
    o, totals, m, n2, g, slope, low, lift_high, lift_low = enc_main(
        order, meta, s, q, kv, far_kv, label, code, far_code, enc_params, enc_out, enc_up, enc_down, embed_map, HE
    )
    start, dn1, dq_rows, dkv = dec_in(order, meta, sel, lift_high, lift_low, columns, dec_params, dec_qkv, HD)
    far_dkv = across(dkv, "blk", 0)
    (decoded, d_o, d_n2, d_g, d_ub, d_mb, d_tm, d_dq, d_near, d_back, d_outb, d_gainb, d_shiftb, d_upb, d_downb) = dec_main(
        order, meta, start, dq_rows, dkv, far_dkv, columns, marks, far_marks, cotangent, dec_params, dec_out, dec_up, dec_down, HD
    )
    d_back = across(d_back, "blk", 0)

    def bundle(bits, *entries, short=()):
        return Bundle(order, bits, spots, meta, [Entry(*entry) for entry in entries], short)

    dec = bundle(
        DEC_BITS,
        ("wide", d_n2, d_ub, rd, 4, dd // 2, dec_up.shape, False),
        ("tall", d_g, cotangent, rd, 4, dd // 2, dec_down.shape, False),
        ("wide", d_o, d_mb, rd, 1, dd // 2, dec_out.shape, False),
    )
    dec.weigh()
    d_dqkv, lb, d_gaina, d_shifta, embed_b, token_grad = dec_head(
        order, meta, start, d_dq, d_near, d_back, d_tm, columns, dec_params, dec_qkv
    )
    dec.step()
    (lbc, tb, ub, mb, tm, dq, near, back, outb, gainb, shiftb, upb, downb) = enc_back(
        order, meta, sel, lb, slope, m, q, kv, far_kv, o, totals, label, code, far_code,
        enc_params, enc_out, enc_up, enc_down, embed_map, HE,
    )
    back = across(back, "blk", 0)
    dec.step()
    enc_a = bundle(
        ENC_BITS[0],
        ("wide", n2, ub, re, 4, de // 2, enc_up.shape, True),
        ("wide", o, mb, re, 1, de // 2, enc_out.shape, True),
    )
    enc_b = bundle(
        ENC_BITS[1],
        ("tall", g, tb, re, 4, de // 2, enc_down.shape, True),
        ("wide", low, lbc, re, 1, dd // 2, embed_map.shape, True),
    )
    enc_a.weigh()
    enc_b.weigh()
    enc_a.step()
    dqkv, patches_grad, gaina, shifta = enc_head(order, meta, sel, s, dq, near, back, tm, enc_params, enc_qkv)
    enc_b.step()
    dec.step()
    short = [gaina, shifta, outb, gainb, shiftb, upb, downb, embed_b, token_grad]
    short += [d_gaina, d_shifta, d_outb, d_gainb, d_shiftb, d_upb, d_downb]
    enc_c = bundle(
        ENC_BITS[2],
        ("wide", n1, dqkv, re, 3, de // 2, enc_qkv.shape, True),
        ("wide", dn1, d_dqkv, rd, 3 * dd // de, de // 2, dec_qkv.shape, False),
        short=short,
    )
    enc_c.weigh()
    bundles = {"d": dec, "a": enc_a, "b": enc_b, "c": enc_c}
    for name in STEPS:
        bundles[name].step()
    g_dec_up, g_dec_down, g_dec_out = dec.placed
    g_enc_up, g_enc_out = enc_a.placed
    g_enc_down, g_embed = enc_b.placed
    g_enc_qkv, g_dec_qkv, sums = enc_c.placed
    sums = sums[:, : SHORT // LANES, :].reshape(-1)
    small, offset = [], 0
    for value in short:
        small.append(sums[offset : offset + value.size])
        offset += value.size
    return (
        (decoded, patches_grad)
        + (small[0], small[1], g_enc_qkv, g_enc_out, small[2], small[3], small[4])
        + (g_enc_up, small[5], g_enc_down, small[6], g_embed, small[7], small[8])
        + (small[9], small[10], g_dec_qkv, g_dec_out, small[11], small[12], small[13])
        + (g_dec_up, small[14], g_dec_down, small[15])
    )


def solution(mesh):
    return jax.shard_map(
        local,
        mesh=mesh,
        in_specs=(
            P(("dp", "blk"), None),
            P(("dp", "blk")),
            P(("dp", "blk")),
            P(("dp", "blk")),
            P(),
            P(),
            P(),
            P(),
            P(),
            P(),
            P(),
            P(),
            P(),
            P(),
            P(),
            P(),
            P(),
            P(),
            P(),
            P(),
            P(),
            P(),
            P(),
            P(),
            P(),
            P(),
            P(),
            P(),
            P(),
            P(("dp", "blk"), None),
        ),
        out_specs=(
            P(("dp", "blk"), None),
            P(("dp", "blk"), None),
            P(),
            P(),
            P(),
            P(),
            P(),
            P(),
            P(),
            P(),
            P(),
            P(),
            P(),
            P(),
            P(),
            P(),
            P(),
            P(),
            P(),
            P(),
            P(),
            P(),
            P(),
            P(),
            P(),
            P(),
            P(),
        ),
        check_vma=False,
    )
```

```python
import math

import jax
import jax.numpy as jnp
from jax import lax
from jax.experimental import pallas as pl
from jax.experimental.pallas import tpu as pltpu
from jax.sharding import PartitionSpec as P

HE = 12
HD = 16
TILE = 256
VMEM_LIMIT = 60 * 1024 * 1024
DEC_BITS = ((1, 0, 2, 3), (0, 1, 2, 3))
ENC_BITS = (((2, 0, 1, 3), (1, 2, 0, 3)), ((1, 0, 2, 3), (0, 2, 1, 3)), ((0, 1, 2, 3), (1, 0, 2, 3)))
STEPS = "abdcabdcabdcabdcabdcabdcabdcabcabcc"
SHORT = 512
WEIGHT_LIMIT = 40 * 1024 * 1024
SMALL_LIMIT = 24 * 1024 * 1024
FLOPS_PER_MICRO, BYTES_PER_MICRO = 1.15e9, 3.6e6


epsilon = 1e-06


def matmul(left_side, right_side):
    return jnp.dot(left_side, right_side, preferred_element_type=jnp.float32)


def matmul_tn(left_side, right_side):
    return lax.dot_general(
        left_side, right_side, (((0,), (0,)), ((), ())), preferred_element_type=jnp.float32
    )


def matmul_nt(left_side, right_side):
    return lax.dot_general(
        left_side, right_side, (((1,), (1,)), ((), ())), preferred_element_type=jnp.float32
    )


def bits_of(count):
    return count.bit_length() - 1


def across(value, axis, bit):
    count = lax.axis_size(axis)
    return lax.ppermute(value, axis, [(i, i ^ (1 << bit)) for i in range(count)])


def cost(micros):
    return pl.CostEstimate(
        flops=int(micros * FLOPS_PER_MICRO), bytes_accessed=int(micros * BYTES_PER_MICRO), transcendentals=0
    )


TOKEN = jax.ShapeDtypeStruct((8, 128), jnp.float32)


def across_bits(value, bits):
    count, cores = lax.axis_size("dp"), lax.axis_size("blk")
    pairs = [(i * cores + b, (i ^ (1 << bits[b])) * cores + b) for i in range(count) for b in range(cores)]
    return lax.ppermute(value, ("dp", "blk"), pairs)


class Order:
    def __init__(self):
        self.token, self.smalls = None, 0

    def run(self, kernel, name, scalars, in_specs, operands, out_specs, out_shape, scratch=(), micros=1.0, steps=1, limit=VMEM_LIMIT):
        count = len(in_specs)
        if self.token is not None:
            in_specs = [*in_specs, pl.BlockSpec(memory_space=pl.ANY)]
            operands = [*operands, self.token]
        more = len(in_specs) - count

        outs = len(out_specs)

        def body(meta, *refs):
            rest = refs[count + more :]
            kernel(meta, *refs[:count], *rest[:outs], *rest[outs + 1 :])

        out_specs = [*out_specs, pl.BlockSpec(memory_space=pl.ANY)]
        results = pl.pallas_call(
            body,
            out_shape=[*out_shape, TOKEN],
            grid_spec=pltpu.PrefetchScalarGridSpec(
                num_scalar_prefetch=1, grid=(steps,), in_specs=in_specs, out_specs=out_specs, scratch_shapes=list(scratch)
            ),
            compiler_params=pltpu.CompilerParams(vmem_limit_bytes=limit),
            cost_estimate=cost(micros),
            name=name,
        )(scalars, *operands)
        self.token = results[-1]
        return results[:-1]

    def run_small(self, kernel, name, operands, out_shape, scalars=None, out_specs=None, scratch=(), earlier=()):
        micros = 12.0 if self.smalls < 8 else 4.0
        self.smalls += 1
        count, outs = len(operands), len(out_shape)
        in_specs = [pl.BlockSpec(memory_space=pltpu.VMEM)] * count
        first = []
        if scalars is not None:
            in_specs, first = [pl.BlockSpec(memory_space=pltpu.SMEM), *in_specs], [scalars]
        aliases = {len(in_specs) + index: index for index in range(len(earlier))}
        in_specs = [*in_specs, *[pl.BlockSpec(memory_space=pl.ANY)] * len(earlier)]
        operands, count = [*operands, *earlier], count + len(earlier)
        if self.token is not None:
            in_specs = [*in_specs, pl.BlockSpec(memory_space=pl.ANY)]
            operands = [*operands, self.token]
        used = count + len(first)

        def body(*refs):
            rest = refs[len(in_specs) :]
            kernel(*refs[:used], *rest[:outs], *rest[outs + 1 :])

        out_specs = out_specs or [pl.BlockSpec(memory_space=pltpu.VMEM)] * outs
        results = pl.pallas_call(
            body,
            out_shape=[*out_shape, TOKEN],
            in_specs=in_specs,
            out_specs=[*out_specs, pl.BlockSpec(memory_space=pl.ANY)],
            scratch_shapes=list(scratch),
            input_output_aliases=aliases,
            compiler_params=pltpu.CompilerParams(vmem_limit_bytes=SMALL_LIMIT),
            cost_estimate=cost(micros),
            name=name,
        )(*first, *operands)
        self.token = results[-1]
        return results[:-1]


class Entry:
    def __init__(self, kind, lhs, rhs, r, n, width, shape, counted):
        self.kind, self.lhs, self.rhs, self.r, self.n = kind, lhs, rhs, r, n
        self.width, self.shape, self.counted = width, shape, counted


class Bundle:
    def __init__(self, order, bits, spots, tiles, entries, short=()):
        self.order, self.run, self.entries = order, order.run, entries
        self.shards = min(16, lax.axis_size("dp"))
        self.bits = [[bit for bit in each if bit < bits_of(self.shards)] for each in bits]
        self.stages = len(self.bits[0])
        self.spots, self.tiles = spots, tiles
        self.width = max(entry.width for entry in entries)
        self.firsts, self.bases, first, base = [], [], 0, 0
        for entry in entries:
            self.firsts.append(first)
            self.bases.append(base)
            first += entry.n
            base += entry.n * entry.r
        self.short, self.short_base = list(short), base
        self.steps, self.rows = first, base + (16 if self.short else 0)

    def block(self, index_map):
        return pl.BlockSpec((1, self.rows, self.width), index_map)

    def shaped(self, count):
        return jax.ShapeDtypeStruct((count, self.rows, self.width), jnp.bfloat16)

    def size(self, count):
        return 2 * count * self.rows * self.width

    def spot_of(self, index, core):
        spots = []
        for bits in self.bits:
            spot = jnp.int32(0)
            for at, bit in enumerate(bits):
                spot = spot | ((lax.shift_right_logical(index, bit) & 1) << (len(bits) - 1 - at))
            spots.append(spot)
        return jnp.where(core == 0, *spots)

    def index_of(self, spot, core):
        indices = []
        for bits in self.bits:
            index = jnp.int32(0)
            for at, bit in enumerate(bits):
                index = index | ((lax.shift_right_logical(spot, len(bits) - 1 - at) & 1) << bit)
            indices.append(index)
        return jnp.where(core == 0, *indices)

    def weigh(self):
        entries, shards, width = self.entries, self.shards, self.width
        token_rows = entries[0].lhs.shape[0]
        tallest = max(shards * entry.r for entry in entries)

        def unit_work(entry, offset, unit, refs, kept_ref, sent_ref, scratch, meta):
            r, n, height, span = entry.r, entry.n, shards * entry.r, entry.width
            turned, total, lhs_tile, rhs_tile, sems = scratch
            spot, half, live = meta[0], meta[1], meta[2]
            count = TILE if entry.counted else token_rows

            def block(ref):
                return ref[0] if entry.counted else ref[...]

            def put(out_ref, value, core):
                value = value.astype(BF16)
                if entry.kind == "wide":
                    at = pl.ds(pl.multiple_of(offset + unit * r, 16), r)
                    for shard in range(shards):
                        target = self.spot_of(lax.bitwise_xor(jnp.int32(shard), spot), core)
                        out_ref[target, at, :span] = value[shard * r : (shard + 1) * r]
                        if span < width:
                            out_ref[target, at, span:] = jnp.zeros((r, width - span), BF16)
                else:
                    each, tall = shards // n, n * r
                    for inner in range(each):
                        target = self.spot_of(lax.bitwise_xor(unit * each + inner, spot), core)
                        out_ref[target, offset : offset + tall, :span] = value[inner * tall : (inner + 1) * tall]

            def turn():
                turned[:height, :count] = block(refs[0]).T

            if entry.kind == "wide":
                pl.when(unit == 0)(turn)
            else:
                turn()

            def product(rhs_ref):
                return matmul(turned[:height, :count], block(rhs_ref))

            def add_rest(flip):
                lhs_at = 0 if entry.kind == "wide" else unit * height
                rhs_at = (half ^ flip) * span if entry.kind == "tall" else ((half ^ flip) * n + unit) * span

                def add(tile, carry):
                    copies = [
                        pltpu.make_async_copy(
                            source.at[tile, :, pl.ds(pl.multiple_of(jnp.int32(at), LANES), size)], target.at[:, :size], sems.at[index]
                        )
                        for index, (source, target, at, size) in enumerate(
                            ((refs[3], lhs_tile, lhs_at, height), (refs[4], rhs_tile, rhs_at, span))
                        )
                    ]
                    for copy in copies:
                        copy.start()
                    for copy in copies:
                        copy.wait()
                    total[:height, :span] += matmul_tn(lhs_tile[:, :height], rhs_tile[:, :span])
                    return carry

                lax.fori_loop(1, live, add, 0)

            for flip, rhs_ref, out_ref in ((1, refs[1], sent_ref), (0, refs[2], kept_ref)):
                if not entry.counted:
                    put(out_ref, product(rhs_ref), half ^ flip)
                    continue

                @pl.when(live == 1)
                def _(flip=flip, rhs_ref=rhs_ref, out_ref=out_ref):
                    put(out_ref, product(rhs_ref), half ^ flip)

                @pl.when(live > 1)
                def _(flip=flip, rhs_ref=rhs_ref, out_ref=out_ref):
                    total[:height, :span] = product(rhs_ref)
                    add_rest(flip)
                    put(out_ref, total[:height, :span], half ^ flip)

        starts, in_specs, operands = [], [], []
        for first, entry in zip(self.firsts, entries):
            n, height, span = entry.n, shards * entry.r, entry.width
            starts.append(len(operands))

            def unit_of(step, first=first, n=n):
                return jnp.clip(step - first, 0, n - 1)

            def spec(size, column, depth, entry=entry):
                mode = pl.Buffered(depth)
                if entry.counted:
                    return pl.BlockSpec((1, TILE, size), lambda step, meta: (0, 0, column(step, meta)), pipeline_mode=mode)
                return pl.BlockSpec((token_rows, size), lambda step, meta: (0, column(step, meta)), pipeline_mode=mode)

            if entry.kind == "wide":
                in_specs.append(spec(height, lambda step, meta: 0, 1))
                for flip in (1, 0):
                    in_specs.append(
                        spec(span, lambda step, meta, n=n, unit_of=unit_of, flip=flip: (meta[1] ^ flip) * n + unit_of(step), 2)
                    )
            else:
                in_specs.append(spec(height, lambda step, meta, unit_of=unit_of: unit_of(step), 2))
                for flip in (1, 0):
                    in_specs.append(spec(span, lambda step, meta, flip=flip: meta[1] ^ flip, 1))
            lhs, rhs = entry.lhs, entry.rhs
            if entry.counted:
                lhs, rhs = (value.reshape(-1, TILE, value.shape[1]) for value in (lhs, rhs))
                in_specs += [pl.BlockSpec(memory_space=pl.ANY)] * 2
                operands += [lhs, rhs, rhs, lhs, rhs]
            else:
                operands += [lhs, rhs, rhs]
        starts.append(len(operands))
        main = len(operands)
        for value in self.short:
            in_specs.append(whole(value.shape))
            operands.append(value)

        def add_short(refs, half, spot, sent_ref, kept_ref, row_s):
            row_s[...] = jnp.zeros_like(row_s)
            offset = 0
            for ref in refs:
                size = ref.shape[1]
                row_s[:, offset : offset + size] = ref[...]
                offset += size
            base, lane, row = self.short_base, iota((16, width), 1), iota((16, width), 0)
            for flip, out_ref in ((1, sent_ref), (0, kept_ref)):
                for shard in range(shards):
                    at = ((half ^ flip) * shards + shard) * SHORT
                    first_row = row_s[:, pl.ds(pl.multiple_of(at, LANES), width)]
                    next_row = row_s[:, pl.ds(pl.multiple_of(at + width, LANES), width)]
                    value = jnp.where(row == 0, first_row, jnp.where((row == 1) & (lane < SHORT - width), next_row, 0.0))
                    target = self.spot_of(lax.bitwise_xor(jnp.int32(shard), spot), half ^ flip)
                    out_ref[target, base : base + 16, :] = value.astype(BF16)

        def kernel(meta, *refs):
            sent_ref, kept_ref, *scratch = refs[len(operands) :]
            step = pl.program_id(0)
            if self.short:
                row_s = scratch.pop()
                pl.when(step == 0)(lambda: add_short(refs[main : len(operands)], meta[1], meta[0], sent_ref, kept_ref, row_s))
            for index, entry in enumerate(entries):
                first = self.firsts[index]

                @pl.when((step >= first) & (step < first + entry.n))
                def _(index=index, entry=entry, first=first):
                    ins = refs[starts[index] : starts[index + 1]]
                    unit_work(entry, self.bases[index], step - first, ins, kept_ref, sent_ref, scratch, meta)

        shape = (shards, self.rows, width)
        sent, kept = self.run(
            kernel,
            "weight_grads",
            jnp.concatenate([self.spots, self.tiles[:1]]),
            in_specs,
            operands,
            [pl.BlockSpec(shape, lambda step, meta: (0, 0, 0))] * 2,
            [self.shaped(shards)] * 2,
            [
                pltpu.VMEM((tallest, token_rows), BF16),
                pltpu.VMEM((tallest, width), F32),
                pltpu.VMEM((TILE, tallest), BF16),
                pltpu.VMEM((TILE, width), BF16),
                pltpu.SemaphoreType.DMA((2,)),
            ]
            + [pltpu.VMEM((1, (2 * shards + 2) * SHORT), F32)] * bool(self.short),
            micros=6.0,
            steps=self.steps,
            limit=WEIGHT_LIMIT,
        )
        self.terms = (kept, across(sent, "blk", 0))
        self.due, self.stage = list(zip(*self.bits)), 0

    def step(self):
        bits = self.stages
        for last, step in ((bits, self.halve), (bits + 1, self.own), (2 * bits, self.join), (2 * bits + 1, self.place_first)):
            if self.stage < last:
                self.stage += 1
                step()
                return
        self.placed = self.place(1, self.half_placed)

    def halve(self):
        bit = self.due.pop(0)
        first, second = self.terms
        count = first.shape[0] // 2

        def kernel(a_ref, b_ref, sent_ref, stay_ref):
            for base, target in ((count, sent_ref), (0, stay_ref)):

                def add(index, carry, base=base, target=target):
                    target[index] = (a_ref[base + index].astype(F32) + b_ref[base + index].astype(F32)).astype(BF16)
                    return carry

                lax.fori_loop(0, count, add, 0)

        sent, stay = self.order.run_small(
            kernel, "halve", [first, second], [self.shaped(count)] * 2
        )
        self.terms = (stay, across_bits(sent, bit))

    def own(self):
        def kernel(a_ref, b_ref, out_ref):
            out_ref[...] = (a_ref[...].astype(F32) + b_ref[...].astype(F32)).astype(BF16)

        def add(a, b):
            return self.order.run_small(kernel, "own", [a, b], [self.shaped(1)])[0]

        total = add(*self.terms)
        for bit in range(bits_of(self.shards), bits_of(lax.axis_size("dp"))):
            total = add(total, across(total, "dp", bit))
        self.due = list(reversed(list(zip(*self.bits))))
        self.spread(total)

    def spread(self, held):
        bit = self.due.pop(0)
        self.held = (held, across_bits(held, bit))
        if not self.due:
            self.other = [across(held, "blk", 0)]

    def join(self):
        count = self.held[0].shape[0]

        def kernel(a_ref, b_ref, out_ref):
            out_ref[:count] = a_ref[...]
            out_ref[count:] = b_ref[...]

        (held,) = self.order.run_small(
            kernel, "join", list(self.held), [self.shaped(2 * count)]
        )
        self.spread(held)

    def place_first(self):
        self.half_placed = self.place(0, [])
        self.other.append(across(self.held[1], "blk", 0))

    def place(self, part, earlier):
        entries, shards, slots = self.entries, self.shards, 4
        half_count = shards // 2
        sizes = [
            (entry.r, entry.n * entry.width) if entry.kind == "wide" else (entry.n * entry.r, entry.width) for entry in entries
        ]
        more = bool(self.short)
        count = len(entries) + more

        def kernel(meta, *refs):
            sources, refs = refs[:2], refs[2 + len(earlier) :]
            outs, stages, sems = refs[:count], refs[count : 2 * count], refs[-1]
            side = meta[1]

            def copies(slot, shard, which):
                pairs = [
                    (
                        stage.at[slot],
                        out_ref.at[
                            pl.ds(pl.multiple_of(shard * height, 8), height), pl.ds(pl.multiple_of(which * size, LANES), size)
                        ],
                    )
                    for stage, out_ref, (height, size) in zip(stages, outs, sizes)
                ]
                if more:
                    pairs.append((stages[-1].at[slot], outs[-1].at[which * shards + shard]))
                return [pltpu.make_async_copy(*pair, sems.at[index, slot]) for index, pair in enumerate(pairs)]

            for turn, source in enumerate(sources):
                which = side ^ turn

                def one(index, carry, turn=turn, source=source, which=which):
                    step = turn * half_count + index
                    slot = lax.rem(step, slots)

                    @pl.when(step >= slots)
                    def _():
                        for copy in copies(slot, 0, 0):
                            copy.wait()

                    for entry, offset, stage in zip(entries, self.bases, stages):
                        span = entry.width
                        for unit in range(entry.n):
                            row = offset + unit * entry.r
                            value = source[index, row : row + entry.r, :span].astype(F32)
                            if entry.kind == "wide":
                                stage[slot, :, unit * span : (unit + 1) * span] = value
                            else:
                                stage[slot, unit * entry.r : (unit + 1) * entry.r, :] = value
                    if more:
                        value = source[index, self.short_base : self.short_base + 16, :].astype(F32)
                        for at in range(SHORT // LANES):
                            row, lane = divmod(at * LANES, self.width)
                            stages[-1][slot, at : at + 1, :] = value[row : row + 1, lane : lane + LANES]
                    shard = lax.bitwise_xor(self.index_of(part * half_count + index, which), meta[0])
                    for copy in copies(slot, shard, which):
                        copy.start()
                    return carry

                lax.fori_loop(0, half_count, one, 0)
            for step in range(max(shards - slots, 0), shards):
                for copy in copies(step % slots, 0, 0):
                    copy.wait()

        return self.order.run_small(
            kernel,
            "place_shards",
            [self.held[part], self.other[part]],
            [jax.ShapeDtypeStruct(entry.shape, jnp.float32) for entry in entries]
            + [jax.ShapeDtypeStruct((2 * shards, 8, LANES), jnp.float32)] * more,
            scalars=self.spots,
            out_specs=[pl.BlockSpec(memory_space=pl.ANY)] * count,
            scratch=[pltpu.VMEM((slots, *size), F32) for size in sizes]
            + [pltpu.VMEM((slots, 8, LANES), F32)] * more
            + [pltpu.SemaphoreType.DMA((count, slots))],
            earlier=earlier,
        )


LOG2E = math.log2(math.e)
NEVER = -1e30
LANES = 128
BF16, F32 = jnp.bfloat16, jnp.float32


def colsum(value):
    return jnp.sum(value.astype(F32), axis=0, keepdims=True)


def normed_rows(stream):
    centred = stream - jnp.mean(stream, axis=-1, keepdims=True)
    inverse = lax.rsqrt(jnp.mean(centred * centred, axis=-1, keepdims=True) + epsilon)
    return centred * inverse, inverse


def norm_back(grad, unit, inverse, gain):
    grad = grad * gain
    inner = jnp.mean(grad * unit, axis=-1, keepdims=True)
    return inverse * (grad - jnp.mean(grad, axis=-1, keepdims=True) - unit * inner)


def gelu_pair(u):
    bell = jnp.exp2(u * u * (-0.5 * LOG2E))
    t = 1.0 / (1.0 + (0.3275911 * math.sqrt(0.5)) * jnp.abs(u))
    poly = ((((1.061405429 * t - 1.453152027) * t + 1.421413741) * t - 0.284496736) * t + 0.254829592) * t
    tail = 0.5 * poly * bell
    phi = jnp.where(u < 0, tail, 1.0 - tail)
    return u * phi, phi + u * bell * (1.0 / math.sqrt(2.0 * math.pi))


def iota(shape, axis):
    return lax.broadcasted_iota(jnp.int32, shape, axis)


def fill_groups(target, source):
    for group in range(target.shape[0]):
        target[group] = source[:, group * LANES : (group + 1) * LANES].astype(target.dtype)


def attend_forward(keys, head, q_s, k_s, v_s, mask_ref, o_s, probs=None, inverse_s=None, totals=None):
    groups, rows, _ = q_s.shape
    inside = LANES // head
    lanes = iota((rows, LANES), 1)
    which = lax.div(lanes, jnp.int32(head))
    if totals is not None:
        totals[...] = jnp.zeros_like(totals)

    def one_group(group, carry):
        queries = q_s[group]
        key_rows = k_s[group, :keys, :]
        values = v_s[group, :keys, :]
        blended = jnp.zeros((rows, LANES), F32)
        inverses = jnp.zeros((rows, LANES), F32)
        for h in range(inside):
            own = which == h
            query = jnp.where(own, queries, 0.0).astype(BF16)
            scores = matmul_nt(query, key_rows) + mask_ref[:, :keys]
            top = jnp.max(scores, axis=1, keepdims=True)
            prob = jnp.exp2(scores - top).astype(BF16)
            if probs is not None:
                probs[group * inside + h, :, :keys] = prob
            both = matmul(prob, values)
            inverse = 1.0 / both[:, LANES:]
            blended = jnp.where(own, both[:, :LANES] * inverse, blended)
            if inverse_s is not None:
                inverses = jnp.where(own, inverse, inverses)
            if totals is not None:
                at = lanes == group * inside + h
                totals[...] = jnp.where(at, top + jnp.log2(both[:, LANES:]), totals[...])
        o_s[group] = blended
        if inverse_s is not None:
            inverse_s[group] = inverses
        return carry

    lax.fori_loop(0, groups, one_group, 0)


def attend_backward(keys, head, q_s, k_s, v_s, o_s, ob_s, dq_s, dk_s, dv_s, probs=None, mask_ref=None, totals=None):
    groups, rows, _ = q_s.shape
    inside = LANES // head
    lanes = iota((rows, LANES), 1)
    which = lax.div(lanes, jnp.int32(head))

    def one_group(group, carry):
        queries, grads = q_s[group], ob_s[group]
        key_rows = k_s[group, :keys, :]
        values = v_s[group, :keys, :LANES]
        product = grads * o_s[group]
        queries_t = queries.T.astype(BF16)
        grads_t = grads.T.astype(BF16)
        query_grad = jnp.zeros((rows, LANES), F32)
        for h in range(inside):
            own = which == h
            at = slice(h * head, (h + 1) * head)
            inner = jnp.sum(jnp.where(own, product, 0.0), axis=1, keepdims=True)
            if probs is not None:
                prob = probs[group * inside + h, :, :keys]
            else:
                query = jnp.where(own, queries, 0.0).astype(BF16)
                total = jnp.sum(jnp.where(lanes == group * inside + h, totals, 0.0), axis=1, keepdims=True)
                prob = jnp.exp2(matmul_nt(query, key_rows) + (mask_ref[:, :keys] - total)).astype(BF16)
            grad_probs = matmul_nt(jnp.where(own, grads, 0.0).astype(BF16), values)
            score_grad = (prob.astype(F32) * (grad_probs - inner)).astype(BF16)
            query_grad = jnp.where(own, matmul(score_grad, key_rows), query_grad)
            dk_s[group, at, :keys] += matmul(queries_t[at], score_grad)
            dv_s[group, at, :keys] += matmul(grads_t[at], prob)
        dq_s[group] = query_grad
        return carry

    lax.fori_loop(0, groups, one_group, 0)


def whole(shape):
    rank = len(shape)
    return pl.BlockSpec(shape, lambda step, meta: (0,) * rank, pipeline_mode=pl.Buffered(1))


def out_whole(shape):
    rank = len(shape)
    return pl.BlockSpec(shape, lambda step, meta: (0,) * rank)


def row_tile(width):
    return pl.BlockSpec((TILE, width), lambda step, meta: (step, 0))


def live_tile(width):
    return pl.BlockSpec((TILE, width), lambda step, meta: (jnp.minimum(step, meta[0] - 1), 0))


def call(order, kernel, name, meta, in_specs, operands, out_specs, out_shape, scratch, micros, steps):
    return order.run(kernel, name, meta, in_specs, operands, out_specs, out_shape, scratch, micros=micros, steps=steps)


def shaped(rows, width, dtype):
    return jax.ShapeDtypeStruct((rows, width), dtype)


MARKS = 16


def enc_in(order, meta, patches, raw, far_raw, params, qkv, heads):
    rows, width = patches.shape
    factor = (width // heads) ** (-0.5) * LOG2E

    def marks_of(seen, padded, label):
        seen, kept, label = seen[...].astype(F32), 1.0 - padded[...].astype(F32), label[...].astype(F32) + 1.0
        row, result = iota((MARKS, rows), 0), jnp.zeros((MARKS, rows), F32)
        for index, value in enumerate((seen * kept * label, label, seen, kept * label)):
            result = jnp.where(row == index, value, result)
        return result

    def kernel(meta, patches_ref, *refs):
        raw_refs, far_refs, (params_ref, qkv_ref) = refs[:3], refs[3:6], refs[6:8]
        sel_ref, code_ref, far_code_ref, label_ref, marks_ref, far_marks_ref, columns_ref, s_ref, n_ref, q_ref, kv_ref, place_s = refs[8:]
        step = pl.program_id(0)

        @pl.when(step == 0)
        def _():
            below = (iota((rows, rows), 0) <= iota((rows, rows), 1)).astype(F32).astype(BF16)
            for index, (source, target) in enumerate(((raw_refs, marks_ref), (far_refs, far_marks_ref))):
                marks = marks_of(*source)
                target[...] = marks
                place = matmul(marks.astype(BF16), below)[2:3, :]
                place_s[index : index + 1, :] = jnp.where(marks[2:3, :] > 0, place - 1.0, -1.0)
            columns_ref[...] = marks_ref[...].T

        @pl.when(step < jnp.maximum(meta[0], meta[1]))
        def _():
            target = (step * TILE + iota((TILE, rows), 0)).astype(F32)
            sel = jnp.where(target == place_s[0:1, :], 1.0, 0.0).astype(BF16)
            far_sel = jnp.where(target == place_s[1:2, :], 1.0, 0.0).astype(BF16)
            sel_ref[...] = sel
            own_marks = marks_ref[...].astype(BF16)
            code_ref[...] = matmul_nt(own_marks, sel)
            far_code_ref[...] = matmul_nt(far_marks_ref[...].astype(BF16), far_sel)
            label_ref[...] = matmul_nt(sel, own_marks)

        @pl.when(step < meta[0])
        def _():
            stream = matmul(sel_ref[...], patches_ref[...])
            s_ref[...] = stream.astype(BF16)
            unit, _ = normed_rows(stream)
            normed = (unit * params_ref[:, :width] + params_ref[:, width : 2 * width]).astype(BF16)
            n_ref[...] = normed
            q_ref[...] = (matmul(normed, qkv_ref[:, :width]) * factor).astype(BF16)
            kv_ref[...] = matmul(normed, qkv_ref[:, width:]).astype(BF16)

    def last_tile(step, meta):
        return jnp.minimum(step, jnp.maximum(meta[0], meta[1]) - 1)

    lane_tile = pl.BlockSpec((MARKS, TILE), lambda step, meta: (0, last_tile(step, meta)))

    def tile(size):
        return pl.BlockSpec((TILE, size), lambda step, meta: (last_tile(step, meta), 0))

    operands = (patches, *raw, *far_raw, params, qkv)
    return call(
        order,
        kernel,
        "enc_in",
        meta,
        [whole(value.shape) for value in operands],
        operands,
        [tile(rows), lane_tile, lane_tile, tile(MARKS), out_whole((MARKS, rows)), out_whole((MARKS, rows)), out_whole((rows, MARKS))]
        + [live_tile(w) for w in (width, width, width, 2 * width)],
        [shaped(rows, rows, BF16), shaped(MARKS, rows, F32), shaped(MARKS, rows, F32), shaped(rows, MARKS, F32)]
        + [shaped(MARKS, rows, F32), shaped(MARKS, rows, F32), shaped(rows, MARKS, F32)]
        + [shaped(rows, w, BF16) for w in (width, width, width, 2 * width)],
        [pltpu.VMEM((8, rows), F32)],
        7.0,
        rows // TILE,
    )


def spread_keys(count, tiles, kv_ref, far_ref, far_tiles, k_s, v_s):
    size = count * TILE
    width = kv_ref.shape[1] // 2
    for source, live, base in ((kv_ref, tiles, 0), (far_ref, far_tiles, size)):
        ok = iota((size, LANES), 0) < live * TILE
        for group in range(width // LANES):
            at = slice(group * LANES, (group + 1) * LANES)
            value_at = slice(width + group * LANES, width + (group + 1) * LANES)
            k_s[group, base : base + size, :] = jnp.where(ok, source[:size, at].astype(F32), 0.0).astype(BF16)
            v_s[group, base : base + size, :LANES] = jnp.where(ok, source[:size, value_at].astype(F32), 0.0).astype(BF16)
            if v_s.shape[2] > LANES:
                v_s[group, base : base + size, LANES:] = jnp.ones((size, v_s.shape[2] - LANES), BF16)


def write_mask(mask_ref, label, code, far_code, size, step):
    shape = (label.shape[0], size)
    near = (label == code) | (iota(shape, 1) == step * TILE + iota(shape, 0))
    mask_ref[:, :size] = jnp.where(near, 0.0, NEVER)
    mask_ref[:, size : 2 * size] = jnp.where(label == far_code, 0.0, NEVER)


def enc_main(order, meta, s, q, kv, far_kv, label, code, far_code, params, out, up, down, embed, heads):
    rows, width = s.shape
    wide, lifted_width = up.shape[1], embed.shape[1]
    groups, head, most = width // LANES, width // heads, rows // TILE
    part = width

    def kernel(meta, s_ref, q_ref, kv_ref, far_ref, label_ref, code_ref, far_code_ref, params_ref, out_w, up_w, down_w, embed_w,
               o_ref, tot_ref, m_ref, n_ref, g_ref, gp_ref, e_ref, hi_ref, lo_ref, q_s, k_s, v_s, mask_s, o_s):
        step = pl.program_id(0)
        tiles, far_tiles = meta[0], meta[1]
        count = jnp.maximum(tiles, far_tiles)

        def param(start, size):
            return params_ref[:, start : start + size]

        @pl.when(step < tiles)
        def _():
            fill_groups(q_s, q_ref)
            for size in range(1, most + 1):

                @pl.when(count == size)
                def _(size=size):
                    @pl.when(step == 0)
                    def _():
                        spread_keys(size, tiles, kv_ref, far_ref, far_tiles, k_s, v_s)

                    span = size * TILE
                    write_mask(mask_s, label_ref[:, 1:2], code_ref[0:1, :span], far_code_ref[0:1, :span], span, step)
                    attend_forward(2 * span, head, q_s, k_s, v_s, mask_s, o_s, totals=tot_ref)

            for group in range(groups):
                o_ref[:, group * LANES : (group + 1) * LANES] = o_s[group].astype(BF16)
            middle = s_ref[...].astype(F32) + matmul(o_ref[...], out_w[...]) + param(2 * width, width)
            m_ref[...] = middle
            unit, _ = normed_rows(middle)
            normed = (unit * param(3 * width, width) + param(4 * width, width)).astype(BF16)
            n_ref[...] = normed
            encoded = middle + param(5 * width + wide, width)
            for j in range(0, wide, part):
                u = matmul(normed, up_w[:, j : j + part]) + param(5 * width + j, part)
                g, slope = gelu_pair(u)
                g = g.astype(BF16)
                g_ref[:, j : j + part] = g
                gp_ref[:, j : j + part] = slope.astype(BF16)
                encoded = encoded + matmul(g, down_w[j : j + part, :])
            low = encoded.astype(BF16)
            e_ref[...] = low
            lifted = matmul(low, embed_w[...]) + param(6 * width + wide, lifted_width)
            high = lifted.astype(BF16)
            hi_ref[...] = high
            lo_ref[...] = (lifted - high.astype(F32)).astype(BF16)

    tall = label.shape[1]
    return call(
        order,
        kernel,
        "enc_main",
        meta,
        [live_tile(width), live_tile(width), whole(kv.shape), whole(kv.shape), live_tile(tall), whole(code.shape), whole(code.shape)]
        + [whole(value.shape) for value in (params, out, up, down, embed)],
        (s, q, kv, far_kv, label, code, far_code, params, out, up, down, embed),
        [live_tile(w) for w in (width, LANES, width, width, wide, wide, width, lifted_width, lifted_width)],
        [shaped(rows, width, BF16), shaped(rows, LANES, F32), shaped(rows, width, F32), shaped(rows, width, BF16)]
        + [shaped(rows, wide, BF16)] * 2 + [shaped(rows, width, BF16)] + [shaped(rows, lifted_width, BF16)] * 2,
        [
            pltpu.VMEM((groups, TILE, LANES), F32),
            pltpu.VMEM((groups, 2 * rows, LANES), BF16),
            pltpu.VMEM((groups, 2 * rows, 2 * LANES), BF16),
            pltpu.VMEM((TILE, 2 * rows), F32),
            pltpu.VMEM((groups, TILE, LANES), F32),
        ],
        20.0,
        most,
    )


def dec_in(order, meta, sel, high, low, columns, params, qkv, heads):
    rows, width = high.shape
    tall = columns.shape[1]
    factor = (width // heads) ** (-0.5) * LOG2E

    def kernel(meta, sel_ref, hi_ref, lo_ref, col_ref, params_ref, qkv_ref, start_ref, n_ref, q_ref, kv_ref, total):
        total[...] = jnp.zeros_like(total)

        def add(tile, carry):
            at = pl.ds(pl.multiple_of(tile * TILE, TILE), TILE)
            total[...] += matmul_tn(sel_ref[at, :], hi_ref[at, :]) + matmul_tn(sel_ref[at, :], lo_ref[at, :])
            return carry

        lax.fori_loop(0, meta[0], add, 0)
        start = jnp.where(col_ref[:, 2:3] > 0, total[...], params_ref[:, params.shape[1] - width :])
        start_ref[...] = start
        unit, _ = normed_rows(start)
        normed = (unit * params_ref[:, :width] + params_ref[:, width : 2 * width]).astype(BF16)
        n_ref[...] = normed
        q_ref[...] = (matmul(normed, qkv_ref[:, :width]) * factor).astype(BF16)
        kv_ref[...] = matmul(normed, qkv_ref[:, width:]).astype(BF16)

    return call(
        order,
        kernel,
        "dec_in",
        meta,
        [pl.BlockSpec((rows, TILE), lambda step, meta: (0, step)), whole(high.shape), whole(low.shape), row_tile(tall)]
        + [whole(value.shape) for value in (params, qkv)],
        (sel, high, low, columns, params, qkv),
        [row_tile(w) for w in (width, width, width, 2 * width)],
        [shaped(rows, width, F32)] + [shaped(rows, w, BF16) for w in (width, width, 2 * width)],
        [pltpu.VMEM((TILE, width), F32)],
        7.0,
        rows // TILE,
    )


def give_key_grads(size, dk_s, dv_s, near_ref, far_ref):
    groups = dk_s.shape[0]
    for index, (source, factor) in enumerate(((dk_s, 1.0 / LOG2E), (dv_s, 1.0))):
        for group in range(groups):
            at = slice((index * groups + group) * LANES, (index * groups + group + 1) * LANES)
            near_ref[:size, at] = source[group, :, :size].T * factor
            far_ref[:size, at] = (source[group, :, size : 2 * size].T * factor).astype(BF16)


def dec_main(order, meta, start, q, kv, far_kv, columns, marks, far_marks, cotangent, params, out, up, down, heads):
    rows, width = start.shape
    wide = up.shape[1]
    groups, head, steps = width // LANES, width // heads, rows // TILE
    part = width
    tall = columns.shape[1]

    def kernel(meta, start_ref, q_ref, kv_ref, far_ref, col_ref, marks_ref, far_marks_ref, cot_ref, params_ref, out_w, up_w, down_w,
               dec_ref, o_ref, n_ref, g_ref, ub_ref, mb_ref, tm_ref, dq_ref, near_ref, back_ref,
               outb_ref, gainb_ref, shiftb_ref, upb_ref, downb_ref,
               q_s, k_s, v_s, mask_s, probs, o_s, inv_s, ob_s, dq_s, dk_s, dv_s, slope_s):
        step = pl.program_id(0)

        def param(begin, size):
            return params_ref[:, begin : begin + size]

        @pl.when(step == 0)
        def _():
            spread_keys(steps, steps, kv_ref, far_ref, steps, k_s, v_s)
            for ref in (dk_s, dv_s, outb_ref, gainb_ref, shiftb_ref, upb_ref, downb_ref):
                ref[...] = jnp.zeros_like(ref)

        fill_groups(q_s, q_ref)
        write_mask(mask_s, col_ref[:, 1:2], marks_ref[3:4, :], far_marks_ref[3:4, :], rows, step)
        attend_forward(2 * rows, head, q_s, k_s, v_s, mask_s, o_s, probs=probs, inverse_s=inv_s)
        for group in range(groups):
            o_ref[:, group * LANES : (group + 1) * LANES] = o_s[group].astype(BF16)
        middle = start_ref[...] + matmul(o_ref[...], out_w[...]) + param(2 * width, width)
        unit, inverse = normed_rows(middle)
        gain_b = param(3 * width, width)
        normed = (unit * gain_b + param(4 * width, width)).astype(BF16)
        n_ref[...] = normed
        decoded = middle + param(5 * width + wide, width)
        for j in range(0, wide, part):
            g, slope = gelu_pair(matmul(normed, up_w[:, j : j + part]) + param(5 * width + j, part))
            g = g.astype(BF16)
            g_ref[:, j : j + part] = g
            slope_s[:, j : j + part] = slope
            decoded = decoded + matmul(g, down_w[j : j + part, :])
        dec_ref[...] = decoded.astype(BF16)
        top = cot_ref[...]
        normed_grad = jnp.zeros((TILE, width), F32)
        for j in range(0, wide, part):
            low = (slope_s[:, j : j + part] * matmul_nt(top, down_w[j : j + part, :])).astype(BF16)
            ub_ref[:, j : j + part] = low
            upb_ref[:, j : j + part] += colsum(low)
            normed_grad = normed_grad + matmul_nt(low, up_w[:, j : j + part])
        downb_ref[...] += colsum(top)
        gainb_ref[...] += colsum(normed_grad * unit)
        shiftb_ref[...] += colsum(normed_grad)
        middle_grad = top.astype(F32) + norm_back(normed_grad, unit, inverse, gain_b)
        tm_ref[...] = middle_grad
        low = middle_grad.astype(BF16)
        mb_ref[...] = low
        outb_ref[...] += colsum(low)
        attended_grad = matmul_nt(low, out_w[...])
        for group in range(groups):
            scaled = attended_grad[:, group * LANES : (group + 1) * LANES] * inv_s[group]
            ob_s[group] = scaled.astype(BF16).astype(F32)
        attend_backward(2 * rows, head, q_s, k_s, v_s, o_s, ob_s, dq_s, dk_s, dv_s, probs=probs)
        scale = head ** (-0.5)
        for group in range(groups):
            dq_ref[:, group * LANES : (group + 1) * LANES] = (dq_s[group] * scale).astype(BF16)

        @pl.when(step == steps - 1)
        def _():
            give_key_grads(rows, dk_s, dv_s, near_ref, back_ref)

    small = [width, width, width, wide, width]
    return call(
        order,
        kernel,
        "dec_main",
        meta,
        [row_tile(width), row_tile(width), whole(kv.shape), whole(kv.shape), row_tile(tall), whole(marks.shape), whole(marks.shape)]
        + [row_tile(width)] + [whole(value.shape) for value in (params, out, up, down)],
        (start, q, kv, far_kv, columns, marks, far_marks, cotangent, params, out, up, down),
        [row_tile(w) for w in (width, width, width, wide, wide, width, width, width)]
        + [out_whole((rows, 2 * width))] * 2 + [out_whole((1, w)) for w in small],
        [shaped(rows, w, BF16) for w in (width, width, width, wide, wide, width)]
        + [shaped(rows, width, F32), shaped(rows, width, BF16), shaped(rows, 2 * width, F32), shaped(rows, 2 * width, BF16)]
        + [shaped(1, w, F32) for w in small],
        [
            pltpu.VMEM((groups, TILE, LANES), F32),
            pltpu.VMEM((groups, 2 * rows, LANES), BF16),
            pltpu.VMEM((groups, 2 * rows, 2 * LANES), BF16),
            pltpu.VMEM((TILE, 2 * rows), F32),
            pltpu.VMEM((heads, TILE, 2 * rows), BF16),
        ]
        + [pltpu.VMEM((groups, TILE, LANES), F32)] * 4
        + [pltpu.VMEM((groups, LANES, 2 * rows), F32)] * 2
        + [pltpu.VMEM((TILE, wide), F32)],
        95.0,
        steps,
    )


def dec_head(order, meta, start, dq, near, back, middle_grad, columns, params, qkv):
    rows, width = start.shape
    tall = columns.shape[1]

    def kernel(meta, start_ref, dq_ref, near_ref, back_ref, tm_ref, col_ref, params_ref, qkv_ref,
               dqkv_ref, lb_ref, gain_ref, shift_ref, bias_ref, token_ref):
        step = pl.program_id(0)

        @pl.when(step == 0)
        def _():
            for ref in (gain_ref, shift_ref, bias_ref, token_ref):
                ref[...] = jnp.zeros_like(ref)

        dqkv_ref[:, :width] = dq_ref[...]
        dqkv_ref[:, width:] = (near_ref[...] + back_ref[...].astype(F32)).astype(BF16)
        grad = matmul_nt(dqkv_ref[...], qkv_ref[...])
        unit, inverse = normed_rows(start_ref[...])
        gain_ref[...] += colsum(grad * unit)
        shift_ref[...] += colsum(grad)
        start_grad = tm_ref[...] + norm_back(grad, unit, inverse, params_ref[:, :width])
        seen = col_ref[:, 2:3] > 0
        token_ref[...] += colsum(jnp.where(seen, 0.0, start_grad))
        low = jnp.where(seen, start_grad, 0.0).astype(BF16)
        lb_ref[...] = low
        bias_ref[...] += colsum(low)

    return call(
        order,
        kernel,
        "dec_head",
        meta,
        [row_tile(width), row_tile(width), row_tile(2 * width), row_tile(2 * width), row_tile(width), row_tile(tall)]
        + [whole(params.shape), whole(qkv.shape)],
        (start, dq, near, back, middle_grad, columns, params, qkv),
        [row_tile(3 * width), row_tile(width)] + [out_whole((1, width))] * 4,
        [shaped(rows, 3 * width, BF16), shaped(rows, width, BF16)] + [shaped(1, width, F32)] * 4,
        [],
        40.0,
        rows // TILE,
    )


def enc_back(order, meta, sel, lb, slope, m, q, kv, far_kv, o, totals, label, code, far_code, params, out, up, down, embed, heads):
    rows, width = m.shape
    wide, lifted_width = up.shape[1], embed.shape[1]
    groups, head, most = width // LANES, width // heads, rows // TILE
    part = width
    tall = label.shape[1]

    def kernel(meta, sel_ref, lb_ref, slope_ref, m_ref, q_ref, kv_ref, far_ref, o_ref, tot_ref, label_ref, code_ref, far_code_ref,
               params_ref, out_w, up_w, down_w, embed_w,
               lbc_ref, tb_ref, ub_ref, mb_ref, tm_ref, dq_ref, near_ref, back_ref,
               outb_ref, gainb_ref, shiftb_ref, upb_ref, downb_ref,
               q_s, k_s, v_s, mask_s, o_s, ob_s, dq_s, dk_s, dv_s):
        step = pl.program_id(0)
        tiles, far_tiles = meta[0], meta[1]
        count = jnp.maximum(tiles, far_tiles)
        scale = head ** (-0.5)

        @pl.when(step == 0)
        def _():
            for ref in (dk_s, dv_s, outb_ref, gainb_ref, shiftb_ref, upb_ref, downb_ref):
                ref[...] = jnp.zeros_like(ref)

        @pl.when(step < tiles)
        def _():
            lb_here = matmul(sel_ref[...], lb_ref[...]).astype(BF16)
            lbc_ref[...] = lb_here
            grad_top = matmul_nt(lb_here, embed_w[...])
            top = grad_top.astype(BF16)
            tb_ref[...] = top
            normed_grad = jnp.zeros((TILE, width), F32)
            for j in range(0, wide, part):
                low = (slope_ref[:, j : j + part].astype(F32) * matmul_nt(top, down_w[j : j + part, :])).astype(BF16)
                ub_ref[:, j : j + part] = low
                upb_ref[:, j : j + part] += colsum(low)
                normed_grad = normed_grad + matmul_nt(low, up_w[:, j : j + part])
            unit, inverse = normed_rows(m_ref[...])
            downb_ref[...] += colsum(top)
            gainb_ref[...] += colsum(normed_grad * unit)
            shiftb_ref[...] += colsum(normed_grad)
            middle_grad = grad_top + norm_back(normed_grad, unit, inverse, params_ref[:, 3 * width : 4 * width])
            tm_ref[...] = middle_grad
            low = middle_grad.astype(BF16)
            mb_ref[...] = low
            outb_ref[...] += colsum(low)
            attended_grad = matmul_nt(low, out_w[...]).astype(BF16)
            fill_groups(ob_s, attended_grad)
            fill_groups(o_s, o_ref)
            fill_groups(q_s, q_ref)
            for size in range(1, most + 1):

                @pl.when(count == size)
                def _(size=size):
                    @pl.when(step == 0)
                    def _():
                        spread_keys(size, tiles, kv_ref, far_ref, far_tiles, k_s, v_s)

                    span = size * TILE
                    write_mask(mask_s, label_ref[:, 1:2], code_ref[0:1, :span], far_code_ref[0:1, :span], span, step)
                    attend_backward(
                        2 * span, head, q_s, k_s, v_s, o_s, ob_s, dq_s, dk_s, dv_s, mask_ref=mask_s, totals=tot_ref[...]
                    )

                    @pl.when(step == tiles - 1)
                    def _():
                        give_key_grads(span, dk_s, dv_s, near_ref, back_ref)

            for group in range(groups):
                dq_ref[:, group * LANES : (group + 1) * LANES] = (dq_s[group] * scale).astype(BF16)

    small = [width, width, width, wide, width]
    return call(
        order,
        kernel,
        "enc_back",
        meta,
        [live_tile(rows), whole(lb.shape), live_tile(wide), live_tile(width), live_tile(width), whole(kv.shape), whole(kv.shape)]
        + [live_tile(width), live_tile(LANES), live_tile(tall), whole(code.shape), whole(code.shape)]
        + [whole(value.shape) for value in (params, out, up, down, embed)],
        (sel, lb, slope, m, q, kv, far_kv, o, totals, label, code, far_code, params, out, up, down, embed),
        [live_tile(w) for w in (lifted_width, width, wide, width, width, width)]
        + [whole((rows, 2 * width))] * 2 + [out_whole((1, w)) for w in small],
        [shaped(rows, w, BF16) for w in (lifted_width, width, wide, width)]
        + [shaped(rows, width, F32), shaped(rows, width, BF16), shaped(rows, 2 * width, F32), shaped(rows, 2 * width, BF16)]
        + [shaped(1, w, F32) for w in small],
        [
            pltpu.VMEM((groups, TILE, LANES), F32),
            pltpu.VMEM((groups, 2 * rows, LANES), BF16),
            pltpu.VMEM((groups, 2 * rows, LANES), BF16),
            pltpu.VMEM((TILE, 2 * rows), F32),
        ]
        + [pltpu.VMEM((groups, TILE, LANES), F32)] * 3
        + [pltpu.VMEM((groups, LANES, 2 * rows), F32)] * 2,
        24.0,
        most,
    )


def enc_head(order, meta, sel, s, dq, near, back, middle_grad, params, qkv):
    rows, width = s.shape
    steps = rows // TILE

    def kernel(meta, sel_ref, s_ref, dq_ref, near_ref, back_ref, tm_ref, params_ref, qkv_ref,
               dqkv_ref, grad_ref, gain_ref, shift_ref, total):
        step = pl.program_id(0)

        @pl.when(step == 0)
        def _():
            for ref in (gain_ref, shift_ref, total):
                ref[...] = jnp.zeros_like(ref)

        @pl.when(step < meta[0])
        def _():
            dqkv_ref[:, :width] = dq_ref[...]
            dqkv_ref[:, width:] = (near_ref[...] + back_ref[...].astype(F32)).astype(BF16)
            grad = matmul_nt(dqkv_ref[...], qkv_ref[...])
            unit, inverse = normed_rows(s_ref[...].astype(F32))
            gain_ref[...] += colsum(grad * unit)
            shift_ref[...] += colsum(grad)
            stream_grad = tm_ref[...] + norm_back(grad, unit, inverse, params_ref[:, :width])
            total[...] += matmul_tn(sel_ref[...], stream_grad.astype(BF16))

        @pl.when(step == steps - 1)
        def _():
            grad_ref[...] = total[...].astype(BF16)

    return call(
        order,
        kernel,
        "enc_head",
        meta,
        [live_tile(w) for w in (rows, width, width, 2 * width, 2 * width, width)] + [whole(params.shape), whole(qkv.shape)],
        (sel, s, dq, near, back, middle_grad, params, qkv),
        [live_tile(3 * width), out_whole((rows, width))] + [out_whole((1, width))] * 2,
        [shaped(rows, 3 * width, BF16), shaped(rows, width, BF16)] + [shaped(1, width, F32)] * 2,
        [pltpu.VMEM((rows, width), F32)],
        8.0,
        steps,
    )


def joined(values):
    total, offset = sum(value.size for value in values), 0
    row = jnp.zeros((total,), F32)
    for value in values:
        row = row + jnp.pad(value.astype(F32), (offset, total - offset - value.size))
        offset += value.size
    return row.reshape(1, total)


def local(
    patches,
    visible,
    padding,
    field_ids,
    enc_gain_a,
    enc_shift_a,
    enc_qkv,
    enc_out,
    enc_out_bias,
    enc_gain_b,
    enc_shift_b,
    enc_up,
    enc_up_bias,
    enc_down,
    enc_down_bias,
    embed_map,
    embed_bias,
    mask_token,
    dec_gain_a,
    dec_shift_a,
    dec_qkv,
    dec_out,
    dec_out_bias,
    dec_gain_b,
    dec_shift_b,
    dec_up,
    dec_up_bias,
    dec_down,
    dec_down_bias,
    cotangent,
):
    rows = patches.shape[0]
    tiles_most = rows // TILE
    raw = [value.reshape(1, rows) for value in (visible, padding, field_ids)]
    far_raw = [across(value, "blk", 0) for value in raw]
    counts = jnp.stack([jnp.sum(raw[0]), jnp.sum(far_raw[0])]).astype(jnp.int32)
    meta = jnp.clip((counts + TILE - 1) // TILE, 1, tiles_most)

    enc_params = joined(
        [enc_gain_a, enc_shift_a, enc_out_bias, enc_gain_b, enc_shift_b, enc_up_bias, enc_down_bias, embed_bias]
    )
    dec_params = joined(
        [dec_gain_a, dec_shift_a, dec_out_bias, dec_gain_b, dec_shift_b, dec_up_bias, dec_down_bias, mask_token]
    )

    order = Order()
    shards = min(16, lax.axis_size("dp"))
    spots = jnp.stack([lax.axis_index("dp") & (shards - 1), lax.axis_index("blk")]).astype(jnp.int32)
    de, dd = enc_qkv.shape[0], dec_qkv.shape[0]
    rd, re = dd // shards, de // shards

    sel, code, far_code, label, marks, far_marks, columns, s, n1, q, kv = enc_in(order, meta, patches, raw, far_raw, enc_params, enc_qkv, HE)
    far_kv = across(kv, "blk", 0)
    o, totals, m, n2, g, slope, low, lift_high, lift_low = enc_main(
        order, meta, s, q, kv, far_kv, label, code, far_code, enc_params, enc_out, enc_up, enc_down, embed_map, HE
    )
    start, dn1, dq_rows, dkv = dec_in(order, meta, sel, lift_high, lift_low, columns, dec_params, dec_qkv, HD)
    far_dkv = across(dkv, "blk", 0)
    (decoded, d_o, d_n2, d_g, d_ub, d_mb, d_tm, d_dq, d_near, d_back, d_outb, d_gainb, d_shiftb, d_upb, d_downb) = dec_main(
        order, meta, start, dq_rows, dkv, far_dkv, columns, marks, far_marks, cotangent, dec_params, dec_out, dec_up, dec_down, HD
    )
    d_back = across(d_back, "blk", 0)

    def bundle(bits, *entries, short=()):
        return Bundle(order, bits, spots, meta, [Entry(*entry) for entry in entries], short)

    dec = bundle(
        DEC_BITS,
        ("wide", d_n2, d_ub, rd, 4, dd // 2, dec_up.shape, False),
        ("tall", d_g, cotangent, rd, 4, dd // 2, dec_down.shape, False),
        ("wide", d_o, d_mb, rd, 1, dd // 2, dec_out.shape, False),
    )
    dec.weigh()
    d_dqkv, lb, d_gaina, d_shifta, embed_b, token_grad = dec_head(
        order, meta, start, d_dq, d_near, d_back, d_tm, columns, dec_params, dec_qkv
    )
    dec.step()
    (lbc, tb, ub, mb, tm, dq, near, back, outb, gainb, shiftb, upb, downb) = enc_back(
        order, meta, sel, lb, slope, m, q, kv, far_kv, o, totals, label, code, far_code,
        enc_params, enc_out, enc_up, enc_down, embed_map, HE,
    )
    back = across(back, "blk", 0)
    dec.step()
    enc_a = bundle(
        ENC_BITS[0],
        ("wide", n2, ub, re, 4, de // 2, enc_up.shape, True),
        ("wide", o, mb, re, 1, de // 2, enc_out.shape, True),
    )
    enc_b = bundle(
        ENC_BITS[1],
        ("tall", g, tb, re, 4, de // 2, enc_down.shape, True),
        ("wide", low, lbc, re, 1, dd // 2, embed_map.shape, True),
    )
    enc_a.weigh()
    enc_b.weigh()
    enc_a.step()
    dqkv, patches_grad, gaina, shifta = enc_head(order, meta, sel, s, dq, near, back, tm, enc_params, enc_qkv)
    enc_b.step()
    dec.step()
    short = [gaina, shifta, outb, gainb, shiftb, upb, downb, embed_b, token_grad]
    short += [d_gaina, d_shifta, d_outb, d_gainb, d_shiftb, d_upb, d_downb]
    enc_c = bundle(
        ENC_BITS[2],
        ("wide", n1, dqkv, re, 3, de // 2, enc_qkv.shape, True),
        ("wide", dn1, d_dqkv, rd, 3 * dd // de, de // 2, dec_qkv.shape, False),
        short=short,
    )
    enc_c.weigh()
    bundles = {"d": dec, "a": enc_a, "b": enc_b, "c": enc_c}
    for name in STEPS:
        bundles[name].step()
    g_dec_up, g_dec_down, g_dec_out = dec.placed
    g_enc_up, g_enc_out = enc_a.placed
    g_enc_down, g_embed = enc_b.placed
    g_enc_qkv, g_dec_qkv, sums = enc_c.placed
    sums = sums[:, : SHORT // LANES, :].reshape(-1)
    small, offset = [], 0
    for value in short:
        small.append(sums[offset : offset + value.size])
        offset += value.size
    return (
        (decoded, patches_grad)
        + (small[0], small[1], g_enc_qkv, g_enc_out, small[2], small[3], small[4])
        + (g_enc_up, small[5], g_enc_down, small[6], g_embed, small[7], small[8])
        + (small[9], small[10], g_dec_qkv, g_dec_out, small[11], small[12], small[13])
        + (g_dec_up, small[14], g_dec_down, small[15])
    )


def solution(mesh):
    return jax.shard_map(
        local,
        mesh=mesh,
        in_specs=(
            P(("dp", "blk"), None),
            P(("dp", "blk")),
            P(("dp", "blk")),
            P(("dp", "blk")),
            P(),
            P(),
            P(),
            P(),
            P(),
            P(),
            P(),
            P(),
            P(),
            P(),
            P(),
            P(),
            P(),
            P(),
            P(),
            P(),
            P(),
            P(),
            P(),
            P(),
            P(),
            P(),
            P(),
            P(),
            P(),
            P(("dp", "blk"), None),
        ),
        out_specs=(
            P(("dp", "blk"), None),
            P(("dp", "blk"), None),
            P(),
            P(),
            P(),
            P(),
            P(),
            P(),
            P(),
            P(),
            P(),
            P(),
            P(),
            P(),
            P(),
            P(),
            P(),
            P(),
            P(),
            P(),
            P(),
            P(),
            P(),
            P(),
            P(),
            P(),
            P(),
        ),
        check_vma=False,
    )
```

```python
import math

import jax
import jax.numpy as jnp
from jax import lax
from jax.experimental import pallas as pl
from jax.experimental.pallas import tpu as pltpu
from jax.sharding import PartitionSpec as P

HE = 12
HD = 16
TILE = 256
VMEM_LIMIT = 60 * 1024 * 1024
DEC_BITS = ((1, 0, 2, 3), (0, 1, 2, 3))
ENC_BITS = (((2, 0, 1, 3), (1, 2, 0, 3)), ((1, 0, 2, 3), (0, 2, 1, 3)), ((0, 1, 2, 3), (1, 0, 2, 3)))
STEPS = "abdcabdcabdcabdcabdcabcdabcdcabcabc"
SHORT = 512
WEIGHT_LIMIT = 40 * 1024 * 1024
SMALL_LIMIT = 24 * 1024 * 1024
FLOPS_PER_MICRO, BYTES_PER_MICRO = 1.15e9, 3.6e6


epsilon = 1e-06


def matmul(left_side, right_side):
    return jnp.dot(left_side, right_side, preferred_element_type=jnp.float32)


def matmul_tn(left_side, right_side):
    return lax.dot_general(
        left_side, right_side, (((0,), (0,)), ((), ())), preferred_element_type=jnp.float32
    )


def matmul_nt(left_side, right_side):
    return lax.dot_general(
        left_side, right_side, (((1,), (1,)), ((), ())), preferred_element_type=jnp.float32
    )


def bits_of(count):
    return count.bit_length() - 1


def across(value, axis, bit):
    count = lax.axis_size(axis)
    return lax.ppermute(value, axis, [(i, i ^ (1 << bit)) for i in range(count)])


def cost(micros):
    return pl.CostEstimate(
        flops=int(micros * FLOPS_PER_MICRO), bytes_accessed=int(micros * BYTES_PER_MICRO), transcendentals=0
    )


TOKEN = jax.ShapeDtypeStruct((8, 128), jnp.float32)


def across_bits(value, bits):
    count, cores = lax.axis_size("dp"), lax.axis_size("blk")
    pairs = [(i * cores + b, (i ^ (1 << bits[b])) * cores + b) for i in range(count) for b in range(cores)]
    return lax.ppermute(value, ("dp", "blk"), pairs)


class Order:
    def __init__(self):
        self.token, self.smalls = None, 0

    def run(self, kernel, name, scalars, in_specs, operands, out_specs, out_shape, scratch=(), micros=1.0, steps=1, limit=VMEM_LIMIT):
        count = len(in_specs)
        if self.token is not None:
            in_specs = [*in_specs, pl.BlockSpec(memory_space=pl.ANY)]
            operands = [*operands, self.token]
        more = len(in_specs) - count

        outs = len(out_specs)

        def body(meta, *refs):
            rest = refs[count + more :]
            kernel(meta, *refs[:count], *rest[:outs], *rest[outs + 1 :])

        out_specs = [*out_specs, pl.BlockSpec(memory_space=pl.ANY)]
        results = pl.pallas_call(
            body,
            out_shape=[*out_shape, TOKEN],
            grid_spec=pltpu.PrefetchScalarGridSpec(
                num_scalar_prefetch=1, grid=(steps,), in_specs=in_specs, out_specs=out_specs, scratch_shapes=list(scratch)
            ),
            compiler_params=pltpu.CompilerParams(vmem_limit_bytes=limit),
            cost_estimate=cost(micros),
            name=name,
        )(scalars, *operands)
        self.token = results[-1]
        return results[:-1]

    def run_small(self, kernel, name, operands, out_shape, scalars=None, out_specs=None, scratch=(), earlier=()):
        micros = 12.0 if self.smalls < 8 else 4.0
        self.smalls += 1
        count, outs = len(operands), len(out_shape)
        in_specs = [pl.BlockSpec(memory_space=pltpu.VMEM)] * count
        first = []
        if scalars is not None:
            in_specs, first = [pl.BlockSpec(memory_space=pltpu.SMEM), *in_specs], [scalars]
        aliases = {len(in_specs) + index: index for index in range(len(earlier))}
        in_specs = [*in_specs, *[pl.BlockSpec(memory_space=pl.ANY)] * len(earlier)]
        operands, count = [*operands, *earlier], count + len(earlier)
        if self.token is not None:
            in_specs = [*in_specs, pl.BlockSpec(memory_space=pl.ANY)]
            operands = [*operands, self.token]
        used = count + len(first)

        def body(*refs):
            rest = refs[len(in_specs) :]
            kernel(*refs[:used], *rest[:outs], *rest[outs + 1 :])

        out_specs = out_specs or [pl.BlockSpec(memory_space=pltpu.VMEM)] * outs
        results = pl.pallas_call(
            body,
            out_shape=[*out_shape, TOKEN],
            in_specs=in_specs,
            out_specs=[*out_specs, pl.BlockSpec(memory_space=pl.ANY)],
            scratch_shapes=list(scratch),
            input_output_aliases=aliases,
            compiler_params=pltpu.CompilerParams(vmem_limit_bytes=SMALL_LIMIT),
            cost_estimate=cost(micros),
            name=name,
        )(*first, *operands)
        self.token = results[-1]
        return results[:-1]


class Entry:
    def __init__(self, kind, lhs, rhs, r, n, width, shape, counted):
        self.kind, self.lhs, self.rhs, self.r, self.n = kind, lhs, rhs, r, n
        self.width, self.shape, self.counted = width, shape, counted


class Bundle:
    def __init__(self, order, bits, spots, tiles, entries, short=()):
        self.order, self.run, self.entries = order, order.run, entries
        self.shards = min(16, lax.axis_size("dp"))
        self.bits = [[bit for bit in each if bit < bits_of(self.shards)] for each in bits]
        self.stages = len(self.bits[0])
        self.spots, self.tiles = spots, tiles
        self.width = max(entry.width for entry in entries)
        self.firsts, self.bases, first, base = [], [], 0, 0
        for entry in entries:
            self.firsts.append(first)
            self.bases.append(base)
            first += entry.n
            base += entry.n * entry.r
        self.short, self.short_base = list(short), base
        self.steps, self.rows = first, base + (16 if self.short else 0)

    def block(self, index_map):
        return pl.BlockSpec((1, self.rows, self.width), index_map)

    def shaped(self, count):
        return jax.ShapeDtypeStruct((count, self.rows, self.width), jnp.bfloat16)

    def size(self, count):
        return 2 * count * self.rows * self.width

    def spot_of(self, index, core):
        spots = []
        for bits in self.bits:
            spot = jnp.int32(0)
            for at, bit in enumerate(bits):
                spot = spot | ((lax.shift_right_logical(index, bit) & 1) << (len(bits) - 1 - at))
            spots.append(spot)
        return jnp.where(core == 0, *spots)

    def index_of(self, spot, core):
        indices = []
        for bits in self.bits:
            index = jnp.int32(0)
            for at, bit in enumerate(bits):
                index = index | ((lax.shift_right_logical(spot, len(bits) - 1 - at) & 1) << bit)
            indices.append(index)
        return jnp.where(core == 0, *indices)

    def weigh(self):
        entries, shards, width = self.entries, self.shards, self.width
        token_rows = entries[0].lhs.shape[0]
        tallest = max(shards * entry.r for entry in entries)

        def unit_work(entry, offset, unit, refs, kept_ref, sent_ref, scratch, meta):
            r, n, height, span = entry.r, entry.n, shards * entry.r, entry.width
            turned, total, lhs_tile, rhs_tile, sems = scratch
            spot, half, live = meta[0], meta[1], meta[2]
            count = TILE if entry.counted else token_rows

            def block(ref):
                return ref[0] if entry.counted else ref[...]

            def put(out_ref, value, core):
                value = value.astype(BF16)
                if entry.kind == "wide":
                    at = pl.ds(pl.multiple_of(offset + unit * r, 16), r)
                    for shard in range(shards):
                        target = self.spot_of(lax.bitwise_xor(jnp.int32(shard), spot), core)
                        out_ref[target, at, :span] = value[shard * r : (shard + 1) * r]
                        if span < width:
                            out_ref[target, at, span:] = jnp.zeros((r, width - span), BF16)
                else:
                    each, tall = shards // n, n * r
                    for inner in range(each):
                        target = self.spot_of(lax.bitwise_xor(unit * each + inner, spot), core)
                        out_ref[target, offset : offset + tall, :span] = value[inner * tall : (inner + 1) * tall]

            def turn():
                turned[:height, :count] = block(refs[0]).T

            if entry.kind == "wide":
                pl.when(unit == 0)(turn)
            else:
                turn()

            def product(rhs_ref):
                return matmul(turned[:height, :count], block(rhs_ref))

            def add_rest(flip):
                lhs_at = 0 if entry.kind == "wide" else unit * height
                rhs_at = (half ^ flip) * span if entry.kind == "tall" else ((half ^ flip) * n + unit) * span

                def add(tile, carry):
                    copies = [
                        pltpu.make_async_copy(
                            source.at[tile, :, pl.ds(pl.multiple_of(jnp.int32(at), LANES), size)], target.at[:, :size], sems.at[index]
                        )
                        for index, (source, target, at, size) in enumerate(
                            ((refs[3], lhs_tile, lhs_at, height), (refs[4], rhs_tile, rhs_at, span))
                        )
                    ]
                    for copy in copies:
                        copy.start()
                    for copy in copies:
                        copy.wait()
                    total[:height, :span] += matmul_tn(lhs_tile[:, :height], rhs_tile[:, :span])
                    return carry

                lax.fori_loop(1, live, add, 0)

            for flip, rhs_ref, out_ref in ((1, refs[1], sent_ref), (0, refs[2], kept_ref)):
                if not entry.counted:
                    put(out_ref, product(rhs_ref), half ^ flip)
                    continue

                @pl.when(live == 1)
                def _(flip=flip, rhs_ref=rhs_ref, out_ref=out_ref):
                    put(out_ref, product(rhs_ref), half ^ flip)

                @pl.when(live > 1)
                def _(flip=flip, rhs_ref=rhs_ref, out_ref=out_ref):
                    total[:height, :span] = product(rhs_ref)
                    add_rest(flip)
                    put(out_ref, total[:height, :span], half ^ flip)

        starts, in_specs, operands = [], [], []
        for first, entry in zip(self.firsts, entries):
            n, height, span = entry.n, shards * entry.r, entry.width
            starts.append(len(operands))

            def unit_of(step, first=first, n=n):
                return jnp.clip(step - first, 0, n - 1)

            def spec(size, column, depth, entry=entry):
                mode = pl.Buffered(depth)
                if entry.counted:
                    return pl.BlockSpec((1, TILE, size), lambda step, meta: (0, 0, column(step, meta)), pipeline_mode=mode)
                return pl.BlockSpec((token_rows, size), lambda step, meta: (0, column(step, meta)), pipeline_mode=mode)

            if entry.kind == "wide":
                in_specs.append(spec(height, lambda step, meta: 0, 1))
                for flip in (1, 0):
                    in_specs.append(
                        spec(span, lambda step, meta, n=n, unit_of=unit_of, flip=flip: (meta[1] ^ flip) * n + unit_of(step), 2)
                    )
            else:
                in_specs.append(spec(height, lambda step, meta, unit_of=unit_of: unit_of(step), 2))
                for flip in (1, 0):
                    in_specs.append(spec(span, lambda step, meta, flip=flip: meta[1] ^ flip, 1))
            lhs, rhs = entry.lhs, entry.rhs
            if entry.counted:
                lhs, rhs = (value.reshape(-1, TILE, value.shape[1]) for value in (lhs, rhs))
                in_specs += [pl.BlockSpec(memory_space=pl.ANY)] * 2
                operands += [lhs, rhs, rhs, lhs, rhs]
            else:
                operands += [lhs, rhs, rhs]
        starts.append(len(operands))
        main = len(operands)
        for value in self.short:
            in_specs.append(whole(value.shape))
            operands.append(value)

        def add_short(refs, half, spot, sent_ref, kept_ref, row_s):
            row_s[...] = jnp.zeros_like(row_s)
            offset = 0
            for ref in refs:
                size = ref.shape[1]
                row_s[:, offset : offset + size] = ref[...]
                offset += size
            base, lane, row = self.short_base, iota((16, width), 1), iota((16, width), 0)
            for flip, out_ref in ((1, sent_ref), (0, kept_ref)):
                for shard in range(shards):
                    at = ((half ^ flip) * shards + shard) * SHORT
                    first_row = row_s[:, pl.ds(pl.multiple_of(at, LANES), width)]
                    next_row = row_s[:, pl.ds(pl.multiple_of(at + width, LANES), width)]
                    value = jnp.where(row == 0, first_row, jnp.where((row == 1) & (lane < SHORT - width), next_row, 0.0))
                    target = self.spot_of(lax.bitwise_xor(jnp.int32(shard), spot), half ^ flip)
                    out_ref[target, base : base + 16, :] = value.astype(BF16)

        def kernel(meta, *refs):
            sent_ref, kept_ref, *scratch = refs[len(operands) :]
            step = pl.program_id(0)
            if self.short:
                row_s = scratch.pop()
                pl.when(step == 0)(lambda: add_short(refs[main : len(operands)], meta[1], meta[0], sent_ref, kept_ref, row_s))
            for index, entry in enumerate(entries):
                first = self.firsts[index]

                @pl.when((step >= first) & (step < first + entry.n))
                def _(index=index, entry=entry, first=first):
                    ins = refs[starts[index] : starts[index + 1]]
                    unit_work(entry, self.bases[index], step - first, ins, kept_ref, sent_ref, scratch, meta)

        shape = (shards, self.rows, width)
        sent, kept = self.run(
            kernel,
            "weight_grads",
            jnp.concatenate([self.spots, self.tiles[:1]]),
            in_specs,
            operands,
            [pl.BlockSpec(shape, lambda step, meta: (0, 0, 0))] * 2,
            [self.shaped(shards)] * 2,
            [
                pltpu.VMEM((tallest, token_rows), BF16),
                pltpu.VMEM((tallest, width), F32),
                pltpu.VMEM((TILE, tallest), BF16),
                pltpu.VMEM((TILE, width), BF16),
                pltpu.SemaphoreType.DMA((2,)),
            ]
            + [pltpu.VMEM((1, (2 * shards + 2) * SHORT), F32)] * bool(self.short),
            micros=6.0,
            steps=self.steps,
            limit=WEIGHT_LIMIT,
        )
        self.terms = (kept, across(sent, "blk", 0))
        self.due, self.stage = list(zip(*self.bits)), 0

    def step(self):
        bits = self.stages
        for last, step in ((bits, self.halve), (bits + 1, self.own), (2 * bits, self.join), (2 * bits + 1, self.place_first)):
            if self.stage < last:
                self.stage += 1
                step()
                return
        self.placed = self.place(1, self.half_placed)

    def halve(self):
        bit = self.due.pop(0)
        first, second = self.terms
        count = first.shape[0] // 2

        def kernel(a_ref, b_ref, sent_ref, stay_ref):
            for base, target in ((count, sent_ref), (0, stay_ref)):

                def add(index, carry, base=base, target=target):
                    target[index] = (a_ref[base + index].astype(F32) + b_ref[base + index].astype(F32)).astype(BF16)
                    return carry

                lax.fori_loop(0, count, add, 0)

        sent, stay = self.order.run_small(
            kernel, "halve", [first, second], [self.shaped(count)] * 2
        )
        self.terms = (stay, across_bits(sent, bit))

    def own(self):
        def kernel(a_ref, b_ref, out_ref):
            out_ref[...] = (a_ref[...].astype(F32) + b_ref[...].astype(F32)).astype(BF16)

        def add(a, b):
            return self.order.run_small(kernel, "own", [a, b], [self.shaped(1)])[0]

        total = add(*self.terms)
        for bit in range(bits_of(self.shards), bits_of(lax.axis_size("dp"))):
            total = add(total, across(total, "dp", bit))
        self.due = list(reversed(list(zip(*self.bits))))
        self.spread(total)

    def spread(self, held):
        bit = self.due.pop(0)
        self.held = (held, across_bits(held, bit))
        if not self.due:
            self.other = [across(held, "blk", 0)]

    def join(self):
        count = self.held[0].shape[0]

        def kernel(a_ref, b_ref, out_ref):
            out_ref[:count] = a_ref[...]
            out_ref[count:] = b_ref[...]

        (held,) = self.order.run_small(
            kernel, "join", list(self.held), [self.shaped(2 * count)]
        )
        self.spread(held)

    def place_first(self):
        self.half_placed = self.place(0, [])
        self.other.append(across(self.held[1], "blk", 0))

    def place(self, part, earlier):
        entries, shards, slots = self.entries, self.shards, self.shards
        half_count = shards // 2
        sizes = [
            (entry.r, entry.n * entry.width) if entry.kind == "wide" else (entry.n * entry.r, entry.width) for entry in entries
        ]
        more = bool(self.short)
        count = len(entries) + more

        def kernel(meta, *refs):
            sources, refs = refs[:2], refs[2 + len(earlier) :]
            outs, stages, sems = refs[:count], refs[count : 2 * count], refs[-1]
            side = meta[1]

            def copies(slot, shard, which):
                pairs = [
                    (
                        stage.at[slot],
                        out_ref.at[
                            pl.ds(pl.multiple_of(shard * height, 8), height), pl.ds(pl.multiple_of(which * size, LANES), size)
                        ],
                    )
                    for stage, out_ref, (height, size) in zip(stages, outs, sizes)
                ]
                if more:
                    pairs.append((stages[-1].at[slot], outs[-1].at[which * shards + shard]))
                return [pltpu.make_async_copy(*pair, sems.at[index, slot]) for index, pair in enumerate(pairs)]

            for turn, source in enumerate(sources):
                which = side ^ turn

                def one(index, carry, turn=turn, source=source, which=which):
                    step = turn * half_count + index
                    slot = lax.rem(step, slots)

                    @pl.when(step >= slots)
                    def _():
                        for copy in copies(slot, 0, 0):
                            copy.wait()

                    for entry, offset, stage in zip(entries, self.bases, stages):
                        span = entry.width
                        for unit in range(entry.n):
                            row = offset + unit * entry.r
                            value = source[index, row : row + entry.r, :span].astype(F32)
                            if entry.kind == "wide":
                                stage[slot, :, unit * span : (unit + 1) * span] = value
                            else:
                                stage[slot, unit * entry.r : (unit + 1) * entry.r, :] = value
                    if more:
                        value = source[index, self.short_base : self.short_base + 16, :].astype(F32)
                        for at in range(SHORT // LANES):
                            row, lane = divmod(at * LANES, self.width)
                            stages[-1][slot, at : at + 1, :] = value[row : row + 1, lane : lane + LANES]
                    shard = lax.bitwise_xor(self.index_of(part * half_count + index, which), meta[0])
                    for copy in copies(slot, shard, which):
                        copy.start()
                    return carry

                lax.fori_loop(0, half_count, one, 0)
            for step in range(max(shards - slots, 0), shards):
                for copy in copies(step % slots, 0, 0):
                    copy.wait()

        return self.order.run_small(
            kernel,
            "place_shards",
            [self.held[part], self.other[part]],
            [jax.ShapeDtypeStruct(entry.shape, jnp.float32) for entry in entries]
            + [jax.ShapeDtypeStruct((2 * shards, 8, LANES), jnp.float32)] * more,
            scalars=self.spots,
            out_specs=[pl.BlockSpec(memory_space=pl.ANY)] * count,
            scratch=[pltpu.VMEM((slots, *size), F32) for size in sizes]
            + [pltpu.VMEM((slots, 8, LANES), F32)] * more
            + [pltpu.SemaphoreType.DMA((count, slots))],
            earlier=earlier,
        )


LOG2E = math.log2(math.e)
NEVER = -1e30
LANES = 128
BF16, F32 = jnp.bfloat16, jnp.float32


def colsum(value):
    return jnp.sum(value.astype(F32), axis=0, keepdims=True)


def normed_rows(stream):
    centred = stream - jnp.mean(stream, axis=-1, keepdims=True)
    inverse = lax.rsqrt(jnp.mean(centred * centred, axis=-1, keepdims=True) + epsilon)
    return centred * inverse, inverse


def norm_back(grad, unit, inverse, gain):
    grad = grad * gain
    inner = jnp.mean(grad * unit, axis=-1, keepdims=True)
    return inverse * (grad - jnp.mean(grad, axis=-1, keepdims=True) - unit * inner)


def gelu_pair(u):
    bell = jnp.exp2(u * u * (-0.5 * LOG2E))
    t = 1.0 / (1.0 + (0.3275911 * math.sqrt(0.5)) * jnp.abs(u))
    poly = ((((1.061405429 * t - 1.453152027) * t + 1.421413741) * t - 0.284496736) * t + 0.254829592) * t
    tail = 0.5 * poly * bell
    phi = jnp.where(u < 0, tail, 1.0 - tail)
    return u * phi, phi + u * bell * (1.0 / math.sqrt(2.0 * math.pi))


def iota(shape, axis):
    return lax.broadcasted_iota(jnp.int32, shape, axis)


def fill_groups(target, source):
    for group in range(target.shape[0]):
        target[group] = source[:, group * LANES : (group + 1) * LANES].astype(target.dtype)


def attend_forward(keys, head, q_s, k_s, v_s, mask_ref, o_s, probs=None, inverse_s=None, totals=None):
    groups, rows, _ = q_s.shape
    inside = LANES // head
    lanes = iota((rows, LANES), 1)
    which = lax.div(lanes, jnp.int32(head))
    if totals is not None:
        totals[...] = jnp.zeros_like(totals)

    def one_group(group, carry):
        queries = q_s[group]
        key_rows = k_s[group, :keys, :]
        values = v_s[group, :keys, :]
        blended = jnp.zeros((rows, LANES), F32)
        inverses = jnp.zeros((rows, LANES), F32)
        for h in range(inside):
            own = which == h
            query = jnp.where(own, queries, 0.0).astype(BF16)
            scores = matmul_nt(query, key_rows) + mask_ref[:, :keys]
            top = jnp.max(scores, axis=1, keepdims=True)
            prob = jnp.exp2(scores - top).astype(BF16)
            if probs is not None:
                probs[group * inside + h, :, :keys] = prob
            both = matmul(prob, values)
            inverse = 1.0 / both[:, LANES:]
            blended = jnp.where(own, both[:, :LANES] * inverse, blended)
            if inverse_s is not None:
                inverses = jnp.where(own, inverse, inverses)
            if totals is not None:
                at = lanes == group * inside + h
                totals[...] = jnp.where(at, top + jnp.log2(both[:, LANES:]), totals[...])
        o_s[group] = blended
        if inverse_s is not None:
            inverse_s[group] = inverses
        return carry

    lax.fori_loop(0, groups, one_group, 0)


def attend_backward(keys, head, q_s, k_s, v_s, o_s, ob_s, dq_s, dk_s, dv_s, probs=None, mask_ref=None, totals=None):
    groups, rows, _ = q_s.shape
    inside = LANES // head
    lanes = iota((rows, LANES), 1)
    which = lax.div(lanes, jnp.int32(head))

    def one_group(group, carry):
        queries, grads = q_s[group], ob_s[group]
        key_rows = k_s[group, :keys, :]
        values = v_s[group, :keys, :LANES]
        product = grads * o_s[group]
        queries_t = queries.T.astype(BF16)
        grads_t = grads.T.astype(BF16)
        query_grad = jnp.zeros((rows, LANES), F32)
        for h in range(inside):
            own = which == h
            at = slice(h * head, (h + 1) * head)
            inner = jnp.sum(jnp.where(own, product, 0.0), axis=1, keepdims=True)
            if probs is not None:
                prob = probs[group * inside + h, :, :keys]
            else:
                query = jnp.where(own, queries, 0.0).astype(BF16)
                total = jnp.sum(jnp.where(lanes == group * inside + h, totals, 0.0), axis=1, keepdims=True)
                prob = jnp.exp2(matmul_nt(query, key_rows) + (mask_ref[:, :keys] - total)).astype(BF16)
            grad_probs = matmul_nt(jnp.where(own, grads, 0.0).astype(BF16), values)
            score_grad = (prob.astype(F32) * (grad_probs - inner)).astype(BF16)
            query_grad = jnp.where(own, matmul(score_grad, key_rows), query_grad)
            dk_s[group, at, :keys] += matmul(queries_t[at], score_grad)
            dv_s[group, at, :keys] += matmul(grads_t[at], prob)
        dq_s[group] = query_grad
        return carry

    lax.fori_loop(0, groups, one_group, 0)


def whole(shape):
    rank = len(shape)
    return pl.BlockSpec(shape, lambda step, meta: (0,) * rank, pipeline_mode=pl.Buffered(1))


def out_whole(shape):
    rank = len(shape)
    return pl.BlockSpec(shape, lambda step, meta: (0,) * rank)


def row_tile(width):
    return pl.BlockSpec((TILE, width), lambda step, meta: (step, 0))


def live_tile(width):
    return pl.BlockSpec((TILE, width), lambda step, meta: (jnp.minimum(step, meta[0] - 1), 0))


def call(order, kernel, name, meta, in_specs, operands, out_specs, out_shape, scratch, micros, steps):
    return order.run(kernel, name, meta, in_specs, operands, out_specs, out_shape, scratch, micros=micros, steps=steps)


def shaped(rows, width, dtype):
    return jax.ShapeDtypeStruct((rows, width), dtype)


MARKS = 16


def enc_in(order, meta, patches, raw, far_raw, params, qkv, heads):
    rows, width = patches.shape
    factor = (width // heads) ** (-0.5) * LOG2E

    def marks_of(seen, padded, label):
        seen, kept, label = seen[...].astype(F32), 1.0 - padded[...].astype(F32), label[...].astype(F32) + 1.0
        row, result = iota((MARKS, rows), 0), jnp.zeros((MARKS, rows), F32)
        for index, value in enumerate((seen * kept * label, label, seen, kept * label)):
            result = jnp.where(row == index, value, result)
        return result

    def kernel(meta, patches_ref, *refs):
        raw_refs, far_refs, (params_ref, qkv_ref) = refs[:3], refs[3:6], refs[6:8]
        sel_ref, code_ref, far_code_ref, label_ref, marks_ref, far_marks_ref, columns_ref, s_ref, n_ref, q_ref, kv_ref, place_s = refs[8:]
        step = pl.program_id(0)

        @pl.when(step == 0)
        def _():
            below = (iota((rows, rows), 0) <= iota((rows, rows), 1)).astype(F32).astype(BF16)
            for index, (source, target) in enumerate(((raw_refs, marks_ref), (far_refs, far_marks_ref))):
                marks = marks_of(*source)
                target[...] = marks
                place = matmul(marks.astype(BF16), below)[2:3, :]
                place_s[index : index + 1, :] = jnp.where(marks[2:3, :] > 0, place - 1.0, -1.0)
            columns_ref[...] = marks_ref[...].T

        @pl.when(step < jnp.maximum(meta[0], meta[1]))
        def _():
            target = (step * TILE + iota((TILE, rows), 0)).astype(F32)
            sel = jnp.where(target == place_s[0:1, :], 1.0, 0.0).astype(BF16)
            far_sel = jnp.where(target == place_s[1:2, :], 1.0, 0.0).astype(BF16)
            sel_ref[...] = sel
            own_marks = marks_ref[...].astype(BF16)
            code_ref[...] = matmul_nt(own_marks, sel)
            far_code_ref[...] = matmul_nt(far_marks_ref[...].astype(BF16), far_sel)
            label_ref[...] = matmul_nt(sel, own_marks)

        @pl.when(step < meta[0])
        def _():
            stream = matmul(sel_ref[...], patches_ref[...])
            s_ref[...] = stream.astype(BF16)
            unit, _ = normed_rows(stream)
            normed = (unit * params_ref[:, :width] + params_ref[:, width : 2 * width]).astype(BF16)
            n_ref[...] = normed
            q_ref[...] = (matmul(normed, qkv_ref[:, :width]) * factor).astype(BF16)
            kv_ref[...] = matmul(normed, qkv_ref[:, width:]).astype(BF16)

    def last_tile(step, meta):
        return jnp.minimum(step, jnp.maximum(meta[0], meta[1]) - 1)

    lane_tile = pl.BlockSpec((MARKS, TILE), lambda step, meta: (0, last_tile(step, meta)))

    def tile(size):
        return pl.BlockSpec((TILE, size), lambda step, meta: (last_tile(step, meta), 0))

    operands = (patches, *raw, *far_raw, params, qkv)
    return call(
        order,
        kernel,
        "enc_in",
        meta,
        [whole(value.shape) for value in operands],
        operands,
        [tile(rows), lane_tile, lane_tile, tile(MARKS), out_whole((MARKS, rows)), out_whole((MARKS, rows)), out_whole((rows, MARKS))]
        + [live_tile(w) for w in (width, width, width, 2 * width)],
        [shaped(rows, rows, BF16), shaped(MARKS, rows, F32), shaped(MARKS, rows, F32), shaped(rows, MARKS, F32)]
        + [shaped(MARKS, rows, F32), shaped(MARKS, rows, F32), shaped(rows, MARKS, F32)]
        + [shaped(rows, w, BF16) for w in (width, width, width, 2 * width)],
        [pltpu.VMEM((8, rows), F32)],
        7.0,
        rows // TILE,
    )


def spread_keys(count, tiles, kv_ref, far_ref, far_tiles, k_s, v_s):
    size = count * TILE
    width = kv_ref.shape[1] // 2
    for source, live, base in ((kv_ref, tiles, 0), (far_ref, far_tiles, size)):
        ok = iota((size, LANES), 0) < live * TILE
        for group in range(width // LANES):
            at = slice(group * LANES, (group + 1) * LANES)
            value_at = slice(width + group * LANES, width + (group + 1) * LANES)
            k_s[group, base : base + size, :] = jnp.where(ok, source[:size, at].astype(F32), 0.0).astype(BF16)
            v_s[group, base : base + size, :LANES] = jnp.where(ok, source[:size, value_at].astype(F32), 0.0).astype(BF16)
            if v_s.shape[2] > LANES:
                v_s[group, base : base + size, LANES:] = jnp.ones((size, v_s.shape[2] - LANES), BF16)


def write_mask(mask_ref, label, code, far_code, size, step):
    shape = (label.shape[0], size)
    near = (label == code) | (iota(shape, 1) == step * TILE + iota(shape, 0))
    mask_ref[:, :size] = jnp.where(near, 0.0, NEVER)
    mask_ref[:, size : 2 * size] = jnp.where(label == far_code, 0.0, NEVER)


def enc_main(order, meta, s, q, kv, far_kv, label, code, far_code, params, out, up, down, embed, heads):
    rows, width = s.shape
    wide, lifted_width = up.shape[1], embed.shape[1]
    groups, head, most = width // LANES, width // heads, rows // TILE
    part = width

    def kernel(meta, s_ref, q_ref, kv_ref, far_ref, label_ref, code_ref, far_code_ref, params_ref, out_w, up_w, down_w, embed_w,
               o_ref, tot_ref, m_ref, n_ref, g_ref, gp_ref, e_ref, hi_ref, lo_ref, q_s, k_s, v_s, mask_s, o_s):
        step = pl.program_id(0)
        tiles, far_tiles = meta[0], meta[1]
        count = jnp.maximum(tiles, far_tiles)

        def param(start, size):
            return params_ref[:, start : start + size]

        @pl.when(step < tiles)
        def _():
            fill_groups(q_s, q_ref)
            for size in range(1, most + 1):

                @pl.when(count == size)
                def _(size=size):
                    @pl.when(step == 0)
                    def _():
                        spread_keys(size, tiles, kv_ref, far_ref, far_tiles, k_s, v_s)

                    span = size * TILE
                    write_mask(mask_s, label_ref[:, 1:2], code_ref[0:1, :span], far_code_ref[0:1, :span], span, step)
                    attend_forward(2 * span, head, q_s, k_s, v_s, mask_s, o_s, totals=tot_ref)

            for group in range(groups):
                o_ref[:, group * LANES : (group + 1) * LANES] = o_s[group].astype(BF16)
            middle = s_ref[...].astype(F32) + matmul(o_ref[...], out_w[...]) + param(2 * width, width)
            m_ref[...] = middle
            unit, _ = normed_rows(middle)
            normed = (unit * param(3 * width, width) + param(4 * width, width)).astype(BF16)
            n_ref[...] = normed
            encoded = middle + param(5 * width + wide, width)
            for j in range(0, wide, part):
                u = matmul(normed, up_w[:, j : j + part]) + param(5 * width + j, part)
                g, slope = gelu_pair(u)
                g = g.astype(BF16)
                g_ref[:, j : j + part] = g
                gp_ref[:, j : j + part] = slope.astype(BF16)
                encoded = encoded + matmul(g, down_w[j : j + part, :])
            low = encoded.astype(BF16)
            e_ref[...] = low
            lifted = matmul(low, embed_w[...]) + param(6 * width + wide, lifted_width)
            high = lifted.astype(BF16)
            hi_ref[...] = high
            lo_ref[...] = (lifted - high.astype(F32)).astype(BF16)

    tall = label.shape[1]
    return call(
        order,
        kernel,
        "enc_main",
        meta,
        [live_tile(width), live_tile(width), whole(kv.shape), whole(kv.shape), live_tile(tall), whole(code.shape), whole(code.shape)]
        + [whole(value.shape) for value in (params, out, up, down, embed)],
        (s, q, kv, far_kv, label, code, far_code, params, out, up, down, embed),
        [live_tile(w) for w in (width, LANES, width, width, wide, wide, width, lifted_width, lifted_width)],
        [shaped(rows, width, BF16), shaped(rows, LANES, F32), shaped(rows, width, F32), shaped(rows, width, BF16)]
        + [shaped(rows, wide, BF16)] * 2 + [shaped(rows, width, BF16)] + [shaped(rows, lifted_width, BF16)] * 2,
        [
            pltpu.VMEM((groups, TILE, LANES), F32),
            pltpu.VMEM((groups, 2 * rows, LANES), BF16),
            pltpu.VMEM((groups, 2 * rows, 2 * LANES), BF16),
            pltpu.VMEM((TILE, 2 * rows), F32),
            pltpu.VMEM((groups, TILE, LANES), F32),
        ],
        20.0,
        most,
    )


def dec_in(order, meta, sel, high, low, columns, params, qkv, heads):
    rows, width = high.shape
    tall = columns.shape[1]
    factor = (width // heads) ** (-0.5) * LOG2E

    def kernel(meta, sel_ref, hi_ref, lo_ref, col_ref, params_ref, qkv_ref, start_ref, n_ref, q_ref, kv_ref, total):
        total[...] = jnp.zeros_like(total)

        def add(tile, carry):
            at = pl.ds(pl.multiple_of(tile * TILE, TILE), TILE)
            total[...] += matmul_tn(sel_ref[at, :], hi_ref[at, :]) + matmul_tn(sel_ref[at, :], lo_ref[at, :])
            return carry

        lax.fori_loop(0, meta[0], add, 0)
        start = jnp.where(col_ref[:, 2:3] > 0, total[...], params_ref[:, params.shape[1] - width :])
        start_ref[...] = start
        unit, _ = normed_rows(start)
        normed = (unit * params_ref[:, :width] + params_ref[:, width : 2 * width]).astype(BF16)
        n_ref[...] = normed
        q_ref[...] = (matmul(normed, qkv_ref[:, :width]) * factor).astype(BF16)
        kv_ref[...] = matmul(normed, qkv_ref[:, width:]).astype(BF16)

    return call(
        order,
        kernel,
        "dec_in",
        meta,
        [pl.BlockSpec((rows, TILE), lambda step, meta: (0, step)), whole(high.shape), whole(low.shape), row_tile(tall)]
        + [whole(value.shape) for value in (params, qkv)],
        (sel, high, low, columns, params, qkv),
        [row_tile(w) for w in (width, width, width, 2 * width)],
        [shaped(rows, width, F32)] + [shaped(rows, w, BF16) for w in (width, width, 2 * width)],
        [pltpu.VMEM((TILE, width), F32)],
        7.0,
        rows // TILE,
    )


def give_key_grads(size, dk_s, dv_s, near_ref, far_ref):
    groups = dk_s.shape[0]
    for index, (source, factor) in enumerate(((dk_s, 1.0 / LOG2E), (dv_s, 1.0))):
        for group in range(groups):
            at = slice((index * groups + group) * LANES, (index * groups + group + 1) * LANES)
            near_ref[:size, at] = source[group, :, :size].T * factor
            far_ref[:size, at] = (source[group, :, size : 2 * size].T * factor).astype(BF16)


def dec_main(order, meta, start, q, kv, far_kv, columns, marks, far_marks, cotangent, params, out, up, down, heads):
    rows, width = start.shape
    wide = up.shape[1]
    groups, head, steps = width // LANES, width // heads, rows // TILE
    part = width
    tall = columns.shape[1]

    def kernel(meta, start_ref, q_ref, kv_ref, far_ref, col_ref, marks_ref, far_marks_ref, cot_ref, params_ref, out_w, up_w, down_w,
               dec_ref, o_ref, n_ref, g_ref, ub_ref, mb_ref, tm_ref, dq_ref, near_ref, back_ref,
               outb_ref, gainb_ref, shiftb_ref, upb_ref, downb_ref,
               q_s, k_s, v_s, mask_s, probs, o_s, inv_s, ob_s, dq_s, dk_s, dv_s, slope_s):
        step = pl.program_id(0)

        def param(begin, size):
            return params_ref[:, begin : begin + size]

        @pl.when(step == 0)
        def _():
            spread_keys(steps, steps, kv_ref, far_ref, steps, k_s, v_s)
            for ref in (dk_s, dv_s, outb_ref, gainb_ref, shiftb_ref, upb_ref, downb_ref):
                ref[...] = jnp.zeros_like(ref)

        fill_groups(q_s, q_ref)
        write_mask(mask_s, col_ref[:, 1:2], marks_ref[3:4, :], far_marks_ref[3:4, :], rows, step)
        attend_forward(2 * rows, head, q_s, k_s, v_s, mask_s, o_s, probs=probs, inverse_s=inv_s)
        for group in range(groups):
            o_ref[:, group * LANES : (group + 1) * LANES] = o_s[group].astype(BF16)
        middle = start_ref[...] + matmul(o_ref[...], out_w[...]) + param(2 * width, width)
        unit, inverse = normed_rows(middle)
        gain_b = param(3 * width, width)
        normed = (unit * gain_b + param(4 * width, width)).astype(BF16)
        n_ref[...] = normed
        decoded = middle + param(5 * width + wide, width)
        for j in range(0, wide, part):
            g, slope = gelu_pair(matmul(normed, up_w[:, j : j + part]) + param(5 * width + j, part))
            g = g.astype(BF16)
            g_ref[:, j : j + part] = g
            slope_s[:, j : j + part] = slope
            decoded = decoded + matmul(g, down_w[j : j + part, :])
        dec_ref[...] = decoded.astype(BF16)
        top = cot_ref[...]
        normed_grad = jnp.zeros((TILE, width), F32)
        for j in range(0, wide, part):
            low = (slope_s[:, j : j + part] * matmul_nt(top, down_w[j : j + part, :])).astype(BF16)
            ub_ref[:, j : j + part] = low
            upb_ref[:, j : j + part] += colsum(low)
            normed_grad = normed_grad + matmul_nt(low, up_w[:, j : j + part])
        downb_ref[...] += colsum(top)
        gainb_ref[...] += colsum(normed_grad * unit)
        shiftb_ref[...] += colsum(normed_grad)
        middle_grad = top.astype(F32) + norm_back(normed_grad, unit, inverse, gain_b)
        tm_ref[...] = middle_grad
        low = middle_grad.astype(BF16)
        mb_ref[...] = low
        outb_ref[...] += colsum(low)
        attended_grad = matmul_nt(low, out_w[...])
        for group in range(groups):
            scaled = attended_grad[:, group * LANES : (group + 1) * LANES] * inv_s[group]
            ob_s[group] = scaled.astype(BF16).astype(F32)
        attend_backward(2 * rows, head, q_s, k_s, v_s, o_s, ob_s, dq_s, dk_s, dv_s, probs=probs)
        scale = head ** (-0.5)
        for group in range(groups):
            dq_ref[:, group * LANES : (group + 1) * LANES] = (dq_s[group] * scale).astype(BF16)

        @pl.when(step == steps - 1)
        def _():
            give_key_grads(rows, dk_s, dv_s, near_ref, back_ref)

    small = [width, width, width, wide, width]
    return call(
        order,
        kernel,
        "dec_main",
        meta,
        [row_tile(width), row_tile(width), whole(kv.shape), whole(kv.shape), row_tile(tall), whole(marks.shape), whole(marks.shape)]
        + [row_tile(width)] + [whole(value.shape) for value in (params, out, up, down)],
        (start, q, kv, far_kv, columns, marks, far_marks, cotangent, params, out, up, down),
        [row_tile(w) for w in (width, width, width, wide, wide, width, width, width)]
        + [out_whole((rows, 2 * width))] * 2 + [out_whole((1, w)) for w in small],
        [shaped(rows, w, BF16) for w in (width, width, width, wide, wide, width)]
        + [shaped(rows, width, F32), shaped(rows, width, BF16), shaped(rows, 2 * width, F32), shaped(rows, 2 * width, BF16)]
        + [shaped(1, w, F32) for w in small],
        [
            pltpu.VMEM((groups, TILE, LANES), F32),
            pltpu.VMEM((groups, 2 * rows, LANES), BF16),
            pltpu.VMEM((groups, 2 * rows, 2 * LANES), BF16),
            pltpu.VMEM((TILE, 2 * rows), F32),
            pltpu.VMEM((heads, TILE, 2 * rows), BF16),
        ]
        + [pltpu.VMEM((groups, TILE, LANES), F32)] * 4
        + [pltpu.VMEM((groups, LANES, 2 * rows), F32)] * 2
        + [pltpu.VMEM((TILE, wide), F32)],
        95.0,
        steps,
    )


def dec_head(order, meta, start, dq, near, back, middle_grad, columns, params, qkv):
    rows, width = start.shape
    tall = columns.shape[1]

    def kernel(meta, start_ref, dq_ref, near_ref, back_ref, tm_ref, col_ref, params_ref, qkv_ref,
               dqkv_ref, lb_ref, gain_ref, shift_ref, bias_ref, token_ref):
        step = pl.program_id(0)

        @pl.when(step == 0)
        def _():
            for ref in (gain_ref, shift_ref, bias_ref, token_ref):
                ref[...] = jnp.zeros_like(ref)

        dqkv_ref[:, :width] = dq_ref[...]
        dqkv_ref[:, width:] = (near_ref[...] + back_ref[...].astype(F32)).astype(BF16)
        grad = matmul_nt(dqkv_ref[...], qkv_ref[...])
        unit, inverse = normed_rows(start_ref[...])
        gain_ref[...] += colsum(grad * unit)
        shift_ref[...] += colsum(grad)
        start_grad = tm_ref[...] + norm_back(grad, unit, inverse, params_ref[:, :width])
        seen = col_ref[:, 2:3] > 0
        token_ref[...] += colsum(jnp.where(seen, 0.0, start_grad))
        low = jnp.where(seen, start_grad, 0.0).astype(BF16)
        lb_ref[...] = low
        bias_ref[...] += colsum(low)

    return call(
        order,
        kernel,
        "dec_head",
        meta,
        [row_tile(width), row_tile(width), row_tile(2 * width), row_tile(2 * width), row_tile(width), row_tile(tall)]
        + [whole(params.shape), whole(qkv.shape)],
        (start, dq, near, back, middle_grad, columns, params, qkv),
        [row_tile(3 * width), row_tile(width)] + [out_whole((1, width))] * 4,
        [shaped(rows, 3 * width, BF16), shaped(rows, width, BF16)] + [shaped(1, width, F32)] * 4,
        [],
        40.0,
        rows // TILE,
    )


def enc_back(order, meta, sel, lb, slope, m, q, kv, far_kv, o, totals, label, code, far_code, params, out, up, down, embed, heads):
    rows, width = m.shape
    wide, lifted_width = up.shape[1], embed.shape[1]
    groups, head, most = width // LANES, width // heads, rows // TILE
    part = width
    tall = label.shape[1]

    def kernel(meta, sel_ref, lb_ref, slope_ref, m_ref, q_ref, kv_ref, far_ref, o_ref, tot_ref, label_ref, code_ref, far_code_ref,
               params_ref, out_w, up_w, down_w, embed_w,
               lbc_ref, tb_ref, ub_ref, mb_ref, tm_ref, dq_ref, near_ref, back_ref,
               outb_ref, gainb_ref, shiftb_ref, upb_ref, downb_ref,
               q_s, k_s, v_s, mask_s, o_s, ob_s, dq_s, dk_s, dv_s):
        step = pl.program_id(0)
        tiles, far_tiles = meta[0], meta[1]
        count = jnp.maximum(tiles, far_tiles)
        scale = head ** (-0.5)

        @pl.when(step == 0)
        def _():
            for ref in (dk_s, dv_s, outb_ref, gainb_ref, shiftb_ref, upb_ref, downb_ref):
                ref[...] = jnp.zeros_like(ref)

        @pl.when(step < tiles)
        def _():
            lb_here = matmul(sel_ref[...], lb_ref[...]).astype(BF16)
            lbc_ref[...] = lb_here
            grad_top = matmul_nt(lb_here, embed_w[...])
            top = grad_top.astype(BF16)
            tb_ref[...] = top
            normed_grad = jnp.zeros((TILE, width), F32)
            for j in range(0, wide, part):
                low = (slope_ref[:, j : j + part].astype(F32) * matmul_nt(top, down_w[j : j + part, :])).astype(BF16)
                ub_ref[:, j : j + part] = low
                upb_ref[:, j : j + part] += colsum(low)
                normed_grad = normed_grad + matmul_nt(low, up_w[:, j : j + part])
            unit, inverse = normed_rows(m_ref[...])
            downb_ref[...] += colsum(top)
            gainb_ref[...] += colsum(normed_grad * unit)
            shiftb_ref[...] += colsum(normed_grad)
            middle_grad = grad_top + norm_back(normed_grad, unit, inverse, params_ref[:, 3 * width : 4 * width])
            tm_ref[...] = middle_grad
            low = middle_grad.astype(BF16)
            mb_ref[...] = low
            outb_ref[...] += colsum(low)
            attended_grad = matmul_nt(low, out_w[...]).astype(BF16)
            fill_groups(ob_s, attended_grad)
            fill_groups(o_s, o_ref)
            fill_groups(q_s, q_ref)
            for size in range(1, most + 1):

                @pl.when(count == size)
                def _(size=size):
                    @pl.when(step == 0)
                    def _():
                        spread_keys(size, tiles, kv_ref, far_ref, far_tiles, k_s, v_s)

                    span = size * TILE
                    write_mask(mask_s, label_ref[:, 1:2], code_ref[0:1, :span], far_code_ref[0:1, :span], span, step)
                    attend_backward(
                        2 * span, head, q_s, k_s, v_s, o_s, ob_s, dq_s, dk_s, dv_s, mask_ref=mask_s, totals=tot_ref[...]
                    )

                    @pl.when(step == tiles - 1)
                    def _():
                        give_key_grads(span, dk_s, dv_s, near_ref, back_ref)

            for group in range(groups):
                dq_ref[:, group * LANES : (group + 1) * LANES] = (dq_s[group] * scale).astype(BF16)

    small = [width, width, width, wide, width]
    return call(
        order,
        kernel,
        "enc_back",
        meta,
        [live_tile(rows), whole(lb.shape), live_tile(wide), live_tile(width), live_tile(width), whole(kv.shape), whole(kv.shape)]
        + [live_tile(width), live_tile(LANES), live_tile(tall), whole(code.shape), whole(code.shape)]
        + [whole(value.shape) for value in (params, out, up, down, embed)],
        (sel, lb, slope, m, q, kv, far_kv, o, totals, label, code, far_code, params, out, up, down, embed),
        [live_tile(w) for w in (lifted_width, width, wide, width, width, width)]
        + [whole((rows, 2 * width))] * 2 + [out_whole((1, w)) for w in small],
        [shaped(rows, w, BF16) for w in (lifted_width, width, wide, width)]
        + [shaped(rows, width, F32), shaped(rows, width, BF16), shaped(rows, 2 * width, F32), shaped(rows, 2 * width, BF16)]
        + [shaped(1, w, F32) for w in small],
        [
            pltpu.VMEM((groups, TILE, LANES), F32),
            pltpu.VMEM((groups, 2 * rows, LANES), BF16),
            pltpu.VMEM((groups, 2 * rows, LANES), BF16),
            pltpu.VMEM((TILE, 2 * rows), F32),
        ]
        + [pltpu.VMEM((groups, TILE, LANES), F32)] * 3
        + [pltpu.VMEM((groups, LANES, 2 * rows), F32)] * 2,
        24.0,
        most,
    )


def enc_head(order, meta, sel, s, dq, near, back, middle_grad, params, qkv):
    rows, width = s.shape
    steps = rows // TILE

    def kernel(meta, sel_ref, s_ref, dq_ref, near_ref, back_ref, tm_ref, params_ref, qkv_ref,
               dqkv_ref, grad_ref, gain_ref, shift_ref, total):
        step = pl.program_id(0)

        @pl.when(step == 0)
        def _():
            for ref in (gain_ref, shift_ref, total):
                ref[...] = jnp.zeros_like(ref)

        @pl.when(step < meta[0])
        def _():
            dqkv_ref[:, :width] = dq_ref[...]
            dqkv_ref[:, width:] = (near_ref[...] + back_ref[...].astype(F32)).astype(BF16)
            grad = matmul_nt(dqkv_ref[...], qkv_ref[...])
            unit, inverse = normed_rows(s_ref[...].astype(F32))
            gain_ref[...] += colsum(grad * unit)
            shift_ref[...] += colsum(grad)
            stream_grad = tm_ref[...] + norm_back(grad, unit, inverse, params_ref[:, :width])
            total[...] += matmul_tn(sel_ref[...], stream_grad.astype(BF16))

        @pl.when(step == steps - 1)
        def _():
            grad_ref[...] = total[...].astype(BF16)

    return call(
        order,
        kernel,
        "enc_head",
        meta,
        [live_tile(w) for w in (rows, width, width, 2 * width, 2 * width, width)] + [whole(params.shape), whole(qkv.shape)],
        (sel, s, dq, near, back, middle_grad, params, qkv),
        [live_tile(3 * width), out_whole((rows, width))] + [out_whole((1, width))] * 2,
        [shaped(rows, 3 * width, BF16), shaped(rows, width, BF16)] + [shaped(1, width, F32)] * 2,
        [pltpu.VMEM((rows, width), F32)],
        8.0,
        steps,
    )


def joined(values):
    total, offset = sum(value.size for value in values), 0
    row = jnp.zeros((total,), F32)
    for value in values:
        row = row + jnp.pad(value.astype(F32), (offset, total - offset - value.size))
        offset += value.size
    return row.reshape(1, total)


def local(
    patches,
    visible,
    padding,
    field_ids,
    enc_gain_a,
    enc_shift_a,
    enc_qkv,
    enc_out,
    enc_out_bias,
    enc_gain_b,
    enc_shift_b,
    enc_up,
    enc_up_bias,
    enc_down,
    enc_down_bias,
    embed_map,
    embed_bias,
    mask_token,
    dec_gain_a,
    dec_shift_a,
    dec_qkv,
    dec_out,
    dec_out_bias,
    dec_gain_b,
    dec_shift_b,
    dec_up,
    dec_up_bias,
    dec_down,
    dec_down_bias,
    cotangent,
):
    rows = patches.shape[0]
    tiles_most = rows // TILE
    raw = [value.reshape(1, rows) for value in (visible, padding, field_ids)]
    far_raw = [across(value, "blk", 0) for value in raw]
    counts = jnp.stack([jnp.sum(raw[0]), jnp.sum(far_raw[0])]).astype(jnp.int32)
    meta = jnp.clip((counts + TILE - 1) // TILE, 1, tiles_most)

    enc_params = joined(
        [enc_gain_a, enc_shift_a, enc_out_bias, enc_gain_b, enc_shift_b, enc_up_bias, enc_down_bias, embed_bias]
    )
    dec_params = joined(
        [dec_gain_a, dec_shift_a, dec_out_bias, dec_gain_b, dec_shift_b, dec_up_bias, dec_down_bias, mask_token]
    )

    order = Order()
    shards = min(16, lax.axis_size("dp"))
    spots = jnp.stack([lax.axis_index("dp") & (shards - 1), lax.axis_index("blk")]).astype(jnp.int32)
    de, dd = enc_qkv.shape[0], dec_qkv.shape[0]
    rd, re = dd // shards, de // shards

    sel, code, far_code, label, marks, far_marks, columns, s, n1, q, kv = enc_in(order, meta, patches, raw, far_raw, enc_params, enc_qkv, HE)
    far_kv = across(kv, "blk", 0)
    o, totals, m, n2, g, slope, low, lift_high, lift_low = enc_main(
        order, meta, s, q, kv, far_kv, label, code, far_code, enc_params, enc_out, enc_up, enc_down, embed_map, HE
    )
    start, dn1, dq_rows, dkv = dec_in(order, meta, sel, lift_high, lift_low, columns, dec_params, dec_qkv, HD)
    far_dkv = across(dkv, "blk", 0)
    (decoded, d_o, d_n2, d_g, d_ub, d_mb, d_tm, d_dq, d_near, d_back, d_outb, d_gainb, d_shiftb, d_upb, d_downb) = dec_main(
        order, meta, start, dq_rows, dkv, far_dkv, columns, marks, far_marks, cotangent, dec_params, dec_out, dec_up, dec_down, HD
    )
    d_back = across(d_back, "blk", 0)

    def bundle(bits, *entries, short=()):
        return Bundle(order, bits, spots, meta, [Entry(*entry) for entry in entries], short)

    dec = bundle(
        DEC_BITS,
        ("wide", d_n2, d_ub, rd, 4, dd // 2, dec_up.shape, False),
        ("tall", d_g, cotangent, rd, 4, dd // 2, dec_down.shape, False),
        ("wide", d_o, d_mb, rd, 1, dd // 2, dec_out.shape, False),
    )
    dec.weigh()
    d_dqkv, lb, d_gaina, d_shifta, embed_b, token_grad = dec_head(
        order, meta, start, d_dq, d_near, d_back, d_tm, columns, dec_params, dec_qkv
    )
    dec.step()
    (lbc, tb, ub, mb, tm, dq, near, back, outb, gainb, shiftb, upb, downb) = enc_back(
        order, meta, sel, lb, slope, m, q, kv, far_kv, o, totals, label, code, far_code,
        enc_params, enc_out, enc_up, enc_down, embed_map, HE,
    )
    back = across(back, "blk", 0)
    dec.step()
    enc_a = bundle(
        ENC_BITS[0],
        ("wide", n2, ub, re, 4, de // 2, enc_up.shape, True),
        ("wide", o, mb, re, 1, de // 2, enc_out.shape, True),
    )
    enc_b = bundle(
        ENC_BITS[1],
        ("tall", g, tb, re, 4, de // 2, enc_down.shape, True),
        ("wide", low, lbc, re, 1, dd // 2, embed_map.shape, True),
    )
    enc_a.weigh()
    enc_b.weigh()
    enc_a.step()
    dqkv, patches_grad, gaina, shifta = enc_head(order, meta, sel, s, dq, near, back, tm, enc_params, enc_qkv)
    enc_b.step()
    dec.step()
    short = [gaina, shifta, outb, gainb, shiftb, upb, downb, embed_b, token_grad]
    short += [d_gaina, d_shifta, d_outb, d_gainb, d_shiftb, d_upb, d_downb]
    enc_c = bundle(
        ENC_BITS[2],
        ("wide", n1, dqkv, re, 3, de // 2, enc_qkv.shape, True),
        ("wide", dn1, d_dqkv, rd, 3 * dd // de, de // 2, dec_qkv.shape, False),
        short=short,
    )
    enc_c.weigh()
    bundles = {"d": dec, "a": enc_a, "b": enc_b, "c": enc_c}
    for name in STEPS:
        bundles[name].step()
    g_dec_up, g_dec_down, g_dec_out = dec.placed
    g_enc_up, g_enc_out = enc_a.placed
    g_enc_down, g_embed = enc_b.placed
    g_enc_qkv, g_dec_qkv, sums = enc_c.placed
    sums = sums[:, : SHORT // LANES, :].reshape(-1)
    small, offset = [], 0
    for value in short:
        small.append(sums[offset : offset + value.size])
        offset += value.size
    return (
        (decoded, patches_grad)
        + (small[0], small[1], g_enc_qkv, g_enc_out, small[2], small[3], small[4])
        + (g_enc_up, small[5], g_enc_down, small[6], g_embed, small[7], small[8])
        + (small[9], small[10], g_dec_qkv, g_dec_out, small[11], small[12], small[13])
        + (g_dec_up, small[14], g_dec_down, small[15])
    )


def solution(mesh):
    return jax.shard_map(
        local,
        mesh=mesh,
        in_specs=(
            P(("dp", "blk"), None),
            P(("dp", "blk")),
            P(("dp", "blk")),
            P(("dp", "blk")),
            P(),
            P(),
            P(),
            P(),
            P(),
            P(),
            P(),
            P(),
            P(),
            P(),
            P(),
            P(),
            P(),
            P(),
            P(),
            P(),
            P(),
            P(),
            P(),
            P(),
            P(),
            P(),
            P(),
            P(),
            P(),
            P(("dp", "blk"), None),
        ),
        out_specs=(
            P(("dp", "blk"), None),
            P(("dp", "blk"), None),
            P(),
            P(),
            P(),
            P(),
            P(),
            P(),
            P(),
            P(),
            P(),
            P(),
            P(),
            P(),
            P(),
            P(),
            P(),
            P(),
            P(),
            P(),
            P(),
            P(),
            P(),
            P(),
            P(),
            P(),
            P(),
        ),
        check_vma=False,
    )
```

```python
import math

import jax
import jax.numpy as jnp
from jax import lax
from jax.experimental import pallas as pl
from jax.experimental.pallas import tpu as pltpu
from jax.sharding import PartitionSpec as P

HE = 12
HD = 16
TILE = 256
VMEM_LIMIT = 60 * 1024 * 1024
DEC_BITS = ((1, 0, 2, 3), (0, 1, 2, 3))
ENC_BITS = (((2, 0, 1, 3), (1, 2, 0, 3)), ((1, 0, 2, 3), (0, 2, 1, 3)), ((0, 1, 2, 3), (1, 0, 2, 3)))
STEPS = "abdcabdcabdcabdcabdcabcdabcdcabcabcabc"
SHORT = 512
WEIGHT_LIMIT = 40 * 1024 * 1024
SMALL_LIMIT = 24 * 1024 * 1024
FLOPS_PER_MICRO, BYTES_PER_MICRO = 1.15e9, 3.6e6


epsilon = 1e-06


def matmul(left_side, right_side):
    return jnp.dot(left_side, right_side, preferred_element_type=jnp.float32)


def matmul_tn(left_side, right_side):
    return lax.dot_general(
        left_side, right_side, (((0,), (0,)), ((), ())), preferred_element_type=jnp.float32
    )


def matmul_nt(left_side, right_side):
    return lax.dot_general(
        left_side, right_side, (((1,), (1,)), ((), ())), preferred_element_type=jnp.float32
    )


def bits_of(count):
    return count.bit_length() - 1


def across(value, axis, bit):
    count = lax.axis_size(axis)
    return lax.ppermute(value, axis, [(i, i ^ (1 << bit)) for i in range(count)])


def cost(micros):
    return pl.CostEstimate(
        flops=int(micros * FLOPS_PER_MICRO), bytes_accessed=int(micros * BYTES_PER_MICRO), transcendentals=0
    )


TOKEN = jax.ShapeDtypeStruct((8, 128), jnp.float32)


def across_bits(value, bits):
    count, cores = lax.axis_size("dp"), lax.axis_size("blk")
    pairs = [(i * cores + b, (i ^ (1 << bits[b])) * cores + b) for i in range(count) for b in range(cores)]
    return lax.ppermute(value, ("dp", "blk"), pairs)


class Order:
    def __init__(self):
        self.token, self.smalls = None, 0

    def run(self, kernel, name, scalars, in_specs, operands, out_specs, out_shape, scratch=(), micros=1.0, steps=1, limit=VMEM_LIMIT):
        count = len(in_specs)
        if self.token is not None:
            in_specs = [*in_specs, pl.BlockSpec(memory_space=pl.ANY)]
            operands = [*operands, self.token]
        more = len(in_specs) - count

        outs = len(out_specs)

        def body(meta, *refs):
            rest = refs[count + more :]
            kernel(meta, *refs[:count], *rest[:outs], *rest[outs + 1 :])

        out_specs = [*out_specs, pl.BlockSpec(memory_space=pl.ANY)]
        results = pl.pallas_call(
            body,
            out_shape=[*out_shape, TOKEN],
            grid_spec=pltpu.PrefetchScalarGridSpec(
                num_scalar_prefetch=1, grid=(steps,), in_specs=in_specs, out_specs=out_specs, scratch_shapes=list(scratch)
            ),
            compiler_params=pltpu.CompilerParams(vmem_limit_bytes=limit),
            cost_estimate=cost(micros),
            name=name,
        )(scalars, *operands)
        self.token = results[-1]
        return results[:-1]

    def run_small(self, kernel, name, operands, out_shape, scalars=None, out_specs=None, scratch=(), earlier=()):
        micros = 12.0 if self.smalls < 8 else 4.0
        self.smalls += 1
        count, outs = len(operands), len(out_shape)
        in_specs = [pl.BlockSpec(memory_space=pltpu.VMEM)] * count
        first = []
        if scalars is not None:
            in_specs, first = [pl.BlockSpec(memory_space=pltpu.SMEM), *in_specs], [scalars]
        aliases = {len(in_specs) + index: index for index in range(len(earlier))}
        in_specs = [*in_specs, *[pl.BlockSpec(memory_space=pl.ANY)] * len(earlier)]
        operands, count = [*operands, *earlier], count + len(earlier)
        if self.token is not None:
            in_specs = [*in_specs, pl.BlockSpec(memory_space=pl.ANY)]
            operands = [*operands, self.token]
        used = count + len(first)

        def body(*refs):
            rest = refs[len(in_specs) :]
            kernel(*refs[:used], *rest[:outs], *rest[outs + 1 :])

        out_specs = out_specs or [pl.BlockSpec(memory_space=pltpu.VMEM)] * outs
        results = pl.pallas_call(
            body,
            out_shape=[*out_shape, TOKEN],
            in_specs=in_specs,
            out_specs=[*out_specs, pl.BlockSpec(memory_space=pl.ANY)],
            scratch_shapes=list(scratch),
            input_output_aliases=aliases,
            compiler_params=pltpu.CompilerParams(vmem_limit_bytes=SMALL_LIMIT),
            cost_estimate=cost(micros),
            name=name,
        )(*first, *operands)
        self.token = results[-1]
        return results[:-1]


class Entry:
    def __init__(self, kind, lhs, rhs, r, n, width, shape, counted):
        self.kind, self.lhs, self.rhs, self.r, self.n = kind, lhs, rhs, r, n
        self.width, self.shape, self.counted = width, shape, counted


class Bundle:
    def __init__(self, order, bits, spots, tiles, entries, short=(), late=True):
        self.late = late
        self.order, self.run, self.entries = order, order.run, entries
        self.shards = min(16, lax.axis_size("dp"))
        self.bits = [[bit for bit in each if bit < bits_of(self.shards)] for each in bits]
        self.stages = len(self.bits[0])
        self.spots, self.tiles = spots, tiles
        self.width = max(entry.width for entry in entries)
        self.firsts, self.bases, first, base = [], [], 0, 0
        for entry in entries:
            self.firsts.append(first)
            self.bases.append(base)
            first += entry.n
            base += entry.n * entry.r
        self.short, self.short_base = list(short), base
        self.steps, self.rows = first, base + (16 if self.short else 0)

    def block(self, index_map):
        return pl.BlockSpec((1, self.rows, self.width), index_map)

    def shaped(self, count):
        return jax.ShapeDtypeStruct((count, self.rows, self.width), jnp.bfloat16)

    def size(self, count):
        return 2 * count * self.rows * self.width

    def spot_of(self, index, core):
        spots = []
        for bits in self.bits:
            spot = jnp.int32(0)
            for at, bit in enumerate(bits):
                spot = spot | ((lax.shift_right_logical(index, bit) & 1) << (len(bits) - 1 - at))
            spots.append(spot)
        return jnp.where(core == 0, *spots)

    def index_of(self, spot, core):
        indices = []
        for bits in self.bits:
            index = jnp.int32(0)
            for at, bit in enumerate(bits):
                index = index | ((lax.shift_right_logical(spot, len(bits) - 1 - at) & 1) << bit)
            indices.append(index)
        return jnp.where(core == 0, *indices)

    def weigh(self):
        entries, shards, width = self.entries, self.shards, self.width
        token_rows = entries[0].lhs.shape[0]
        tallest = max(shards * entry.r for entry in entries)

        def unit_work(entry, offset, unit, refs, kept_ref, sent_ref, scratch, meta):
            r, n, height, span = entry.r, entry.n, shards * entry.r, entry.width
            turned, total, lhs_tile, rhs_tile, sems = scratch
            spot, half, live = meta[0], meta[1], meta[2]
            count = TILE if entry.counted else token_rows

            def block(ref):
                return ref[0] if entry.counted else ref[...]

            def put(out_ref, value, core):
                value = value.astype(BF16)
                if entry.kind == "wide":
                    at = pl.ds(pl.multiple_of(offset + unit * r, 16), r)
                    for shard in range(shards):
                        target = self.spot_of(lax.bitwise_xor(jnp.int32(shard), spot), core)
                        out_ref[target, at, :span] = value[shard * r : (shard + 1) * r]
                        if span < width:
                            out_ref[target, at, span:] = jnp.zeros((r, width - span), BF16)
                else:
                    each, tall = shards // n, n * r
                    for inner in range(each):
                        target = self.spot_of(lax.bitwise_xor(unit * each + inner, spot), core)
                        out_ref[target, offset : offset + tall, :span] = value[inner * tall : (inner + 1) * tall]

            def turn():
                turned[:height, :count] = block(refs[0]).T

            if entry.kind == "wide":
                pl.when(unit == 0)(turn)
            else:
                turn()

            def product(rhs_ref):
                return matmul(turned[:height, :count], block(rhs_ref))

            def add_rest(flip):
                lhs_at = 0 if entry.kind == "wide" else unit * height
                rhs_at = (half ^ flip) * span if entry.kind == "tall" else ((half ^ flip) * n + unit) * span

                def add(tile, carry):
                    copies = [
                        pltpu.make_async_copy(
                            source.at[tile, :, pl.ds(pl.multiple_of(jnp.int32(at), LANES), size)], target.at[:, :size], sems.at[index]
                        )
                        for index, (source, target, at, size) in enumerate(
                            ((refs[3], lhs_tile, lhs_at, height), (refs[4], rhs_tile, rhs_at, span))
                        )
                    ]
                    for copy in copies:
                        copy.start()
                    for copy in copies:
                        copy.wait()
                    total[:height, :span] += matmul_tn(lhs_tile[:, :height], rhs_tile[:, :span])
                    return carry

                lax.fori_loop(1, live, add, 0)

            for flip, rhs_ref, out_ref in ((1, refs[1], sent_ref), (0, refs[2], kept_ref)):
                if not entry.counted:
                    put(out_ref, product(rhs_ref), half ^ flip)
                    continue

                @pl.when(live == 1)
                def _(flip=flip, rhs_ref=rhs_ref, out_ref=out_ref):
                    put(out_ref, product(rhs_ref), half ^ flip)

                @pl.when(live > 1)
                def _(flip=flip, rhs_ref=rhs_ref, out_ref=out_ref):
                    total[:height, :span] = product(rhs_ref)
                    add_rest(flip)
                    put(out_ref, total[:height, :span], half ^ flip)

        starts, in_specs, operands = [], [], []
        for first, entry in zip(self.firsts, entries):
            n, height, span = entry.n, shards * entry.r, entry.width
            starts.append(len(operands))

            def unit_of(step, first=first, n=n):
                return jnp.clip(step - first, 0, n - 1)

            def spec(size, column, depth, entry=entry):
                mode = pl.Buffered(depth)
                if entry.counted:
                    return pl.BlockSpec((1, TILE, size), lambda step, meta: (0, 0, column(step, meta)), pipeline_mode=mode)
                return pl.BlockSpec((token_rows, size), lambda step, meta: (0, column(step, meta)), pipeline_mode=mode)

            if entry.kind == "wide":
                in_specs.append(spec(height, lambda step, meta: 0, 1))
                for flip in (1, 0):
                    in_specs.append(
                        spec(span, lambda step, meta, n=n, unit_of=unit_of, flip=flip: (meta[1] ^ flip) * n + unit_of(step), 2)
                    )
            else:
                in_specs.append(spec(height, lambda step, meta, unit_of=unit_of: unit_of(step), 2))
                for flip in (1, 0):
                    in_specs.append(spec(span, lambda step, meta, flip=flip: meta[1] ^ flip, 1))
            lhs, rhs = entry.lhs, entry.rhs
            if entry.counted:
                lhs, rhs = (value.reshape(-1, TILE, value.shape[1]) for value in (lhs, rhs))
                in_specs += [pl.BlockSpec(memory_space=pl.ANY)] * 2
                operands += [lhs, rhs, rhs, lhs, rhs]
            else:
                operands += [lhs, rhs, rhs]
        starts.append(len(operands))
        main = len(operands)
        for value in self.short:
            in_specs.append(whole(value.shape))
            operands.append(value)

        def add_short(refs, half, spot, sent_ref, kept_ref, row_s):
            row_s[...] = jnp.zeros_like(row_s)
            offset = 0
            for ref in refs:
                size = ref.shape[1]
                row_s[:, offset : offset + size] = ref[...]
                offset += size
            base, lane, row = self.short_base, iota((16, width), 1), iota((16, width), 0)
            for flip, out_ref in ((1, sent_ref), (0, kept_ref)):
                for shard in range(shards):
                    at = ((half ^ flip) * shards + shard) * SHORT
                    first_row = row_s[:, pl.ds(pl.multiple_of(at, LANES), width)]
                    next_row = row_s[:, pl.ds(pl.multiple_of(at + width, LANES), width)]
                    value = jnp.where(row == 0, first_row, jnp.where((row == 1) & (lane < SHORT - width), next_row, 0.0))
                    target = self.spot_of(lax.bitwise_xor(jnp.int32(shard), spot), half ^ flip)
                    out_ref[target, base : base + 16, :] = value.astype(BF16)

        def kernel(meta, *refs):
            sent_ref, kept_ref, *scratch = refs[len(operands) :]
            step = pl.program_id(0)
            if self.short:
                row_s = scratch.pop()
                pl.when(step == 0)(lambda: add_short(refs[main : len(operands)], meta[1], meta[0], sent_ref, kept_ref, row_s))
            for index, entry in enumerate(entries):
                first = self.firsts[index]

                @pl.when((step >= first) & (step < first + entry.n))
                def _(index=index, entry=entry, first=first):
                    ins = refs[starts[index] : starts[index + 1]]
                    unit_work(entry, self.bases[index], step - first, ins, kept_ref, sent_ref, scratch, meta)

        shape = (shards, self.rows, width)
        sent, kept = self.run(
            kernel,
            "weight_grads",
            jnp.concatenate([self.spots, self.tiles[:1]]),
            in_specs,
            operands,
            [pl.BlockSpec(shape, lambda step, meta: (0, 0, 0))] * 2,
            [self.shaped(shards)] * 2,
            [
                pltpu.VMEM((tallest, token_rows), BF16),
                pltpu.VMEM((tallest, width), F32),
                pltpu.VMEM((TILE, tallest), BF16),
                pltpu.VMEM((TILE, width), BF16),
                pltpu.SemaphoreType.DMA((2,)),
            ]
            + [pltpu.VMEM((1, (2 * shards + 2) * SHORT), F32)] * bool(self.short),
            micros=6.0,
            steps=self.steps,
            limit=WEIGHT_LIMIT,
        )
        self.terms = (kept, across(sent, "blk", 0))
        self.due, self.stage = list(zip(*self.bits)), 0

    def step(self):
        bits = self.stages
        for last, step in ((bits, self.halve), (bits + 1, self.own), (2 * bits, self.join), (2 * bits + 1, self.place_first), (2 * bits + 1 + self.late, self.take)):
            if self.stage < last:
                self.stage += 1
                step()
                return
        self.placed = self.place(1, self.half_placed)

    def halve(self):
        bit = self.due.pop(0)
        first, second = self.terms
        count = first.shape[0] // 2

        def kernel(a_ref, b_ref, sent_ref, stay_ref):
            for base, target in ((count, sent_ref), (0, stay_ref)):

                def add(index, carry, base=base, target=target):
                    target[index] = (a_ref[base + index].astype(F32) + b_ref[base + index].astype(F32)).astype(BF16)
                    return carry

                lax.fori_loop(0, count, add, 0)

        sent, stay = self.order.run_small(
            kernel, "halve", [first, second], [self.shaped(count)] * 2
        )
        self.terms = (stay, across_bits(sent, bit))

    def own(self):
        def kernel(a_ref, b_ref, out_ref):
            out_ref[...] = (a_ref[...].astype(F32) + b_ref[...].astype(F32)).astype(BF16)

        def add(a, b):
            return self.order.run_small(kernel, "own", [a, b], [self.shaped(1)])[0]

        total = add(*self.terms)
        for bit in range(bits_of(self.shards), bits_of(lax.axis_size("dp"))):
            total = add(total, across(total, "dp", bit))
        self.due = list(reversed(list(zip(*self.bits))))
        self.spread(total)

    def spread(self, held):
        bit = self.due.pop(0)
        self.held = (held, across_bits(held, bit))
        if not self.due:
            self.other = [across(held, "blk", 0)]

    def join(self):
        count = self.held[0].shape[0]

        def kernel(a_ref, b_ref, out_ref):
            out_ref[:count] = a_ref[...]
            out_ref[count:] = b_ref[...]

        (held,) = self.order.run_small(
            kernel, "join", list(self.held), [self.shaped(2 * count)]
        )
        self.spread(held)

    def place_first(self):
        self.half_placed = self.place(0, [])
        if not self.late:
            self.other.append(across(self.held[1], "blk", 0))

    def take(self):
        def kernel(in_ref, out_ref):
            out_ref[...] = in_ref[...]

        (late,) = self.order.run_small(kernel, "take", [self.held[1]], [self.shaped(self.held[1].shape[0])])
        self.held = (self.held[0], late)
        self.other.append(across(late, "blk", 0))

    def place(self, part, earlier):
        entries, shards, slots = self.entries, self.shards, self.shards
        half_count = shards // 2
        sizes = [
            (entry.r, entry.n * entry.width) if entry.kind == "wide" else (entry.n * entry.r, entry.width) for entry in entries
        ]
        more = bool(self.short)
        count = len(entries) + more

        def kernel(meta, *refs):
            sources, refs = refs[:2], refs[2 + len(earlier) :]
            outs, stages, sems = refs[:count], refs[count : 2 * count], refs[-1]
            side = meta[1]

            def copies(slot, shard, which):
                pairs = [
                    (
                        stage.at[slot],
                        out_ref.at[
                            pl.ds(pl.multiple_of(shard * height, 8), height), pl.ds(pl.multiple_of(which * size, LANES), size)
                        ],
                    )
                    for stage, out_ref, (height, size) in zip(stages, outs, sizes)
                ]
                if more:
                    pairs.append((stages[-1].at[slot], outs[-1].at[which * shards + shard]))
                return [pltpu.make_async_copy(*pair, sems.at[index, slot]) for index, pair in enumerate(pairs)]

            for turn, source in enumerate(sources):
                which = side ^ turn

                def one(index, carry, turn=turn, source=source, which=which):
                    step = turn * half_count + index
                    slot = lax.rem(step, slots)

                    @pl.when(step >= slots)
                    def _():
                        for copy in copies(slot, 0, 0):
                            copy.wait()

                    for entry, offset, stage in zip(entries, self.bases, stages):
                        span = entry.width
                        for unit in range(entry.n):
                            row = offset + unit * entry.r
                            value = source[index, row : row + entry.r, :span].astype(F32)
                            if entry.kind == "wide":
                                stage[slot, :, unit * span : (unit + 1) * span] = value
                            else:
                                stage[slot, unit * entry.r : (unit + 1) * entry.r, :] = value
                    if more:
                        value = source[index, self.short_base : self.short_base + 16, :].astype(F32)
                        for at in range(SHORT // LANES):
                            row, lane = divmod(at * LANES, self.width)
                            stages[-1][slot, at : at + 1, :] = value[row : row + 1, lane : lane + LANES]
                    shard = lax.bitwise_xor(self.index_of(part * half_count + index, which), meta[0])
                    for copy in copies(slot, shard, which):
                        copy.start()
                    return carry

                lax.fori_loop(0, half_count, one, 0)
            for step in range(max(shards - slots, 0), shards):
                for copy in copies(step % slots, 0, 0):
                    copy.wait()

        return self.order.run_small(
            kernel,
            "place_shards",
            [self.held[part], self.other[part]],
            [jax.ShapeDtypeStruct(entry.shape, jnp.float32) for entry in entries]
            + [jax.ShapeDtypeStruct((2 * shards, 8, LANES), jnp.float32)] * more,
            scalars=self.spots,
            out_specs=[pl.BlockSpec(memory_space=pl.ANY)] * count,
            scratch=[pltpu.VMEM((slots, *size), F32) for size in sizes]
            + [pltpu.VMEM((slots, 8, LANES), F32)] * more
            + [pltpu.SemaphoreType.DMA((count, slots))],
            earlier=earlier,
        )


LOG2E = math.log2(math.e)
NEVER = -1e30
LANES = 128
BF16, F32 = jnp.bfloat16, jnp.float32


def colsum(value):
    return jnp.sum(value.astype(F32), axis=0, keepdims=True)


def normed_rows(stream):
    centred = stream - jnp.mean(stream, axis=-1, keepdims=True)
    inverse = lax.rsqrt(jnp.mean(centred * centred, axis=-1, keepdims=True) + epsilon)
    return centred * inverse, inverse


def norm_back(grad, unit, inverse, gain):
    grad = grad * gain
    inner = jnp.mean(grad * unit, axis=-1, keepdims=True)
    return inverse * (grad - jnp.mean(grad, axis=-1, keepdims=True) - unit * inner)


def gelu_pair(u):
    bell = jnp.exp2(u * u * (-0.5 * LOG2E))
    t = 1.0 / (1.0 + (0.3275911 * math.sqrt(0.5)) * jnp.abs(u))
    poly = ((((1.061405429 * t - 1.453152027) * t + 1.421413741) * t - 0.284496736) * t + 0.254829592) * t
    tail = 0.5 * poly * bell
    phi = jnp.where(u < 0, tail, 1.0 - tail)
    return u * phi, phi + u * bell * (1.0 / math.sqrt(2.0 * math.pi))


def iota(shape, axis):
    return lax.broadcasted_iota(jnp.int32, shape, axis)


def fill_groups(target, source):
    for group in range(target.shape[0]):
        target[group] = source[:, group * LANES : (group + 1) * LANES].astype(target.dtype)


def attend_forward(keys, head, q_s, k_s, v_s, mask_ref, o_s, probs=None, inverse_s=None, totals=None):
    groups, rows, _ = q_s.shape
    inside = LANES // head
    lanes = iota((rows, LANES), 1)
    which = lax.div(lanes, jnp.int32(head))
    if totals is not None:
        totals[...] = jnp.zeros_like(totals)

    def one_group(group, carry):
        queries = q_s[group]
        key_rows = k_s[group, :keys, :]
        values = v_s[group, :keys, :]
        blended = jnp.zeros((rows, LANES), F32)
        inverses = jnp.zeros((rows, LANES), F32)
        for h in range(inside):
            own = which == h
            query = jnp.where(own, queries, 0.0).astype(BF16)
            scores = matmul_nt(query, key_rows) + mask_ref[:, :keys]
            top = jnp.max(scores, axis=1, keepdims=True)
            prob = jnp.exp2(scores - top).astype(BF16)
            if probs is not None:
                probs[group * inside + h, :, :keys] = prob
            both = matmul(prob, values)
            inverse = 1.0 / both[:, LANES:]
            blended = jnp.where(own, both[:, :LANES] * inverse, blended)
            if inverse_s is not None:
                inverses = jnp.where(own, inverse, inverses)
            if totals is not None:
                at = lanes == group * inside + h
                totals[...] = jnp.where(at, top + jnp.log2(both[:, LANES:]), totals[...])
        o_s[group] = blended
        if inverse_s is not None:
            inverse_s[group] = inverses
        return carry

    lax.fori_loop(0, groups, one_group, 0)


def attend_backward(keys, head, q_s, k_s, v_s, o_s, ob_s, dq_s, dk_s, dv_s, probs=None, mask_ref=None, totals=None):
    groups, rows, _ = q_s.shape
    inside = LANES // head
    lanes = iota((rows, LANES), 1)
    which = lax.div(lanes, jnp.int32(head))

    def one_group(group, carry):
        queries, grads = q_s[group], ob_s[group]
        key_rows = k_s[group, :keys, :]
        values = v_s[group, :keys, :LANES]
        product = grads * o_s[group]
        queries_t = queries.T.astype(BF16)
        grads_t = grads.T.astype(BF16)
        query_grad = jnp.zeros((rows, LANES), F32)
        for h in range(inside):
            own = which == h
            at = slice(h * head, (h + 1) * head)
            inner = jnp.sum(jnp.where(own, product, 0.0), axis=1, keepdims=True)
            if probs is not None:
                prob = probs[group * inside + h, :, :keys]
            else:
                query = jnp.where(own, queries, 0.0).astype(BF16)
                total = jnp.sum(jnp.where(lanes == group * inside + h, totals, 0.0), axis=1, keepdims=True)
                prob = jnp.exp2(matmul_nt(query, key_rows) + (mask_ref[:, :keys] - total)).astype(BF16)
            grad_probs = matmul_nt(jnp.where(own, grads, 0.0).astype(BF16), values)
            score_grad = (prob.astype(F32) * (grad_probs - inner)).astype(BF16)
            query_grad = jnp.where(own, matmul(score_grad, key_rows), query_grad)
            dk_s[group, at, :keys] += matmul(queries_t[at], score_grad)
            dv_s[group, at, :keys] += matmul(grads_t[at], prob)
        dq_s[group] = query_grad
        return carry

    lax.fori_loop(0, groups, one_group, 0)


def whole(shape):
    rank = len(shape)
    return pl.BlockSpec(shape, lambda step, meta: (0,) * rank, pipeline_mode=pl.Buffered(1))


def out_whole(shape):
    rank = len(shape)
    return pl.BlockSpec(shape, lambda step, meta: (0,) * rank)


def row_tile(width):
    return pl.BlockSpec((TILE, width), lambda step, meta: (step, 0))


def live_tile(width):
    return pl.BlockSpec((TILE, width), lambda step, meta: (jnp.minimum(step, meta[0] - 1), 0))


def call(order, kernel, name, meta, in_specs, operands, out_specs, out_shape, scratch, micros, steps):
    return order.run(kernel, name, meta, in_specs, operands, out_specs, out_shape, scratch, micros=micros, steps=steps)


def shaped(rows, width, dtype):
    return jax.ShapeDtypeStruct((rows, width), dtype)


MARKS = 16


def enc_in(order, meta, patches, raw, far_raw, params, qkv, heads):
    rows, width = patches.shape
    factor = (width // heads) ** (-0.5) * LOG2E

    def marks_of(seen, padded, label):
        seen, kept, label = seen[...].astype(F32), 1.0 - padded[...].astype(F32), label[...].astype(F32) + 1.0
        row, result = iota((MARKS, rows), 0), jnp.zeros((MARKS, rows), F32)
        for index, value in enumerate((seen * kept * label, label, seen, kept * label)):
            result = jnp.where(row == index, value, result)
        return result

    def kernel(meta, patches_ref, *refs):
        raw_refs, far_refs, (params_ref, qkv_ref) = refs[:3], refs[3:6], refs[6:8]
        sel_ref, code_ref, far_code_ref, label_ref, marks_ref, far_marks_ref, columns_ref, s_ref, n_ref, q_ref, kv_ref, place_s = refs[8:]
        step = pl.program_id(0)

        @pl.when(step == 0)
        def _():
            below = (iota((rows, rows), 0) <= iota((rows, rows), 1)).astype(F32).astype(BF16)
            for index, (source, target) in enumerate(((raw_refs, marks_ref), (far_refs, far_marks_ref))):
                marks = marks_of(*source)
                target[...] = marks
                place = matmul(marks.astype(BF16), below)[2:3, :]
                place_s[index : index + 1, :] = jnp.where(marks[2:3, :] > 0, place - 1.0, -1.0)
            columns_ref[...] = marks_ref[...].T

        @pl.when(step < jnp.maximum(meta[0], meta[1]))
        def _():
            target = (step * TILE + iota((TILE, rows), 0)).astype(F32)
            sel = jnp.where(target == place_s[0:1, :], 1.0, 0.0).astype(BF16)
            far_sel = jnp.where(target == place_s[1:2, :], 1.0, 0.0).astype(BF16)
            sel_ref[...] = sel
            own_marks = marks_ref[...].astype(BF16)
            code_ref[...] = matmul_nt(own_marks, sel)
            far_code_ref[...] = matmul_nt(far_marks_ref[...].astype(BF16), far_sel)
            label_ref[...] = matmul_nt(sel, own_marks)

        @pl.when(step < meta[0])
        def _():
            stream = matmul(sel_ref[...], patches_ref[...])
            s_ref[...] = stream.astype(BF16)
            unit, _ = normed_rows(stream)
            normed = (unit * params_ref[:, :width] + params_ref[:, width : 2 * width]).astype(BF16)
            n_ref[...] = normed
            q_ref[...] = (matmul(normed, qkv_ref[:, :width]) * factor).astype(BF16)
            kv_ref[...] = matmul(normed, qkv_ref[:, width:]).astype(BF16)

    def last_tile(step, meta):
        return jnp.minimum(step, jnp.maximum(meta[0], meta[1]) - 1)

    lane_tile = pl.BlockSpec((MARKS, TILE), lambda step, meta: (0, last_tile(step, meta)))

    def tile(size):
        return pl.BlockSpec((TILE, size), lambda step, meta: (last_tile(step, meta), 0))

    operands = (patches, *raw, *far_raw, params, qkv)
    return call(
        order,
        kernel,
        "enc_in",
        meta,
        [whole(value.shape) for value in operands],
        operands,
        [tile(rows), lane_tile, lane_tile, tile(MARKS), out_whole((MARKS, rows)), out_whole((MARKS, rows)), out_whole((rows, MARKS))]
        + [live_tile(w) for w in (width, width, width, 2 * width)],
        [shaped(rows, rows, BF16), shaped(MARKS, rows, F32), shaped(MARKS, rows, F32), shaped(rows, MARKS, F32)]
        + [shaped(MARKS, rows, F32), shaped(MARKS, rows, F32), shaped(rows, MARKS, F32)]
        + [shaped(rows, w, BF16) for w in (width, width, width, 2 * width)],
        [pltpu.VMEM((8, rows), F32)],
        7.0,
        rows // TILE,
    )


def spread_keys(count, tiles, kv_ref, far_ref, far_tiles, k_s, v_s):
    size = count * TILE
    width = kv_ref.shape[1] // 2
    for source, live, base in ((kv_ref, tiles, 0), (far_ref, far_tiles, size)):
        ok = iota((size, LANES), 0) < live * TILE
        for group in range(width // LANES):
            at = slice(group * LANES, (group + 1) * LANES)
            value_at = slice(width + group * LANES, width + (group + 1) * LANES)
            k_s[group, base : base + size, :] = jnp.where(ok, source[:size, at].astype(F32), 0.0).astype(BF16)
            v_s[group, base : base + size, :LANES] = jnp.where(ok, source[:size, value_at].astype(F32), 0.0).astype(BF16)
            if v_s.shape[2] > LANES:
                v_s[group, base : base + size, LANES:] = jnp.ones((size, v_s.shape[2] - LANES), BF16)


def write_mask(mask_ref, label, code, far_code, size, step):
    shape = (label.shape[0], size)
    near = (label == code) | (iota(shape, 1) == step * TILE + iota(shape, 0))
    mask_ref[:, :size] = jnp.where(near, 0.0, NEVER)
    mask_ref[:, size : 2 * size] = jnp.where(label == far_code, 0.0, NEVER)


def enc_main(order, meta, s, q, kv, far_kv, label, code, far_code, params, out, up, down, embed, heads):
    rows, width = s.shape
    wide, lifted_width = up.shape[1], embed.shape[1]
    groups, head, most = width // LANES, width // heads, rows // TILE
    part = width

    def kernel(meta, s_ref, q_ref, kv_ref, far_ref, label_ref, code_ref, far_code_ref, params_ref, out_w, up_w, down_w, embed_w,
               o_ref, tot_ref, m_ref, n_ref, g_ref, gp_ref, e_ref, hi_ref, lo_ref, q_s, k_s, v_s, mask_s, o_s):
        step = pl.program_id(0)
        tiles, far_tiles = meta[0], meta[1]
        count = jnp.maximum(tiles, far_tiles)

        def param(start, size):
            return params_ref[:, start : start + size]

        @pl.when(step < tiles)
        def _():
            fill_groups(q_s, q_ref)
            for size in range(1, most + 1):

                @pl.when(count == size)
                def _(size=size):
                    @pl.when(step == 0)
                    def _():
                        spread_keys(size, tiles, kv_ref, far_ref, far_tiles, k_s, v_s)

                    span = size * TILE
                    write_mask(mask_s, label_ref[:, 1:2], code_ref[0:1, :span], far_code_ref[0:1, :span], span, step)
                    attend_forward(2 * span, head, q_s, k_s, v_s, mask_s, o_s, totals=tot_ref)

            for group in range(groups):
                o_ref[:, group * LANES : (group + 1) * LANES] = o_s[group].astype(BF16)
            middle = s_ref[...].astype(F32) + matmul(o_ref[...], out_w[...]) + param(2 * width, width)
            m_ref[...] = middle
            unit, _ = normed_rows(middle)
            normed = (unit * param(3 * width, width) + param(4 * width, width)).astype(BF16)
            n_ref[...] = normed
            encoded = middle + param(5 * width + wide, width)
            for j in range(0, wide, part):
                u = matmul(normed, up_w[:, j : j + part]) + param(5 * width + j, part)
                g, slope = gelu_pair(u)
                g = g.astype(BF16)
                g_ref[:, j : j + part] = g
                gp_ref[:, j : j + part] = slope.astype(BF16)
                encoded = encoded + matmul(g, down_w[j : j + part, :])
            low = encoded.astype(BF16)
            e_ref[...] = low
            lifted = matmul(low, embed_w[...]) + param(6 * width + wide, lifted_width)
            high = lifted.astype(BF16)
            hi_ref[...] = high
            lo_ref[...] = (lifted - high.astype(F32)).astype(BF16)

    tall = label.shape[1]
    return call(
        order,
        kernel,
        "enc_main",
        meta,
        [live_tile(width), live_tile(width), whole(kv.shape), whole(kv.shape), live_tile(tall), whole(code.shape), whole(code.shape)]
        + [whole(value.shape) for value in (params, out, up, down, embed)],
        (s, q, kv, far_kv, label, code, far_code, params, out, up, down, embed),
        [live_tile(w) for w in (width, LANES, width, width, wide, wide, width, lifted_width, lifted_width)],
        [shaped(rows, width, BF16), shaped(rows, LANES, F32), shaped(rows, width, F32), shaped(rows, width, BF16)]
        + [shaped(rows, wide, BF16)] * 2 + [shaped(rows, width, BF16)] + [shaped(rows, lifted_width, BF16)] * 2,
        [
            pltpu.VMEM((groups, TILE, LANES), F32),
            pltpu.VMEM((groups, 2 * rows, LANES), BF16),
            pltpu.VMEM((groups, 2 * rows, 2 * LANES), BF16),
            pltpu.VMEM((TILE, 2 * rows), F32),
            pltpu.VMEM((groups, TILE, LANES), F32),
        ],
        20.0,
        most,
    )


def dec_in(order, meta, sel, high, low, columns, params, qkv, heads):
    rows, width = high.shape
    tall = columns.shape[1]
    factor = (width // heads) ** (-0.5) * LOG2E

    def kernel(meta, sel_ref, hi_ref, lo_ref, col_ref, params_ref, qkv_ref, start_ref, n_ref, q_ref, kv_ref, total):
        total[...] = jnp.zeros_like(total)

        def add(tile, carry):
            at = pl.ds(pl.multiple_of(tile * TILE, TILE), TILE)
            total[...] += matmul_tn(sel_ref[at, :], hi_ref[at, :]) + matmul_tn(sel_ref[at, :], lo_ref[at, :])
            return carry

        lax.fori_loop(0, meta[0], add, 0)
        start = jnp.where(col_ref[:, 2:3] > 0, total[...], params_ref[:, params.shape[1] - width :])
        start_ref[...] = start
        unit, _ = normed_rows(start)
        normed = (unit * params_ref[:, :width] + params_ref[:, width : 2 * width]).astype(BF16)
        n_ref[...] = normed
        q_ref[...] = (matmul(normed, qkv_ref[:, :width]) * factor).astype(BF16)
        kv_ref[...] = matmul(normed, qkv_ref[:, width:]).astype(BF16)

    return call(
        order,
        kernel,
        "dec_in",
        meta,
        [pl.BlockSpec((rows, TILE), lambda step, meta: (0, step)), whole(high.shape), whole(low.shape), row_tile(tall)]
        + [whole(value.shape) for value in (params, qkv)],
        (sel, high, low, columns, params, qkv),
        [row_tile(w) for w in (width, width, width, 2 * width)],
        [shaped(rows, width, F32)] + [shaped(rows, w, BF16) for w in (width, width, 2 * width)],
        [pltpu.VMEM((TILE, width), F32)],
        7.0,
        rows // TILE,
    )


def give_key_grads(size, dk_s, dv_s, near_ref, far_ref):
    groups = dk_s.shape[0]
    for index, (source, factor) in enumerate(((dk_s, 1.0 / LOG2E), (dv_s, 1.0))):
        for group in range(groups):
            at = slice((index * groups + group) * LANES, (index * groups + group + 1) * LANES)
            near_ref[:size, at] = source[group, :, :size].T * factor
            far_ref[:size, at] = (source[group, :, size : 2 * size].T * factor).astype(BF16)


def dec_main(order, meta, start, q, kv, far_kv, columns, marks, far_marks, cotangent, params, out, up, down, heads):
    rows, width = start.shape
    wide = up.shape[1]
    groups, head, steps = width // LANES, width // heads, rows // TILE
    part = width
    tall = columns.shape[1]

    def kernel(meta, start_ref, q_ref, kv_ref, far_ref, col_ref, marks_ref, far_marks_ref, cot_ref, params_ref, out_w, up_w, down_w,
               dec_ref, o_ref, n_ref, g_ref, ub_ref, mb_ref, tm_ref, dq_ref, near_ref, back_ref,
               outb_ref, gainb_ref, shiftb_ref, upb_ref, downb_ref,
               q_s, k_s, v_s, mask_s, probs, o_s, inv_s, ob_s, dq_s, dk_s, dv_s, slope_s):
        step = pl.program_id(0)

        def param(begin, size):
            return params_ref[:, begin : begin + size]

        @pl.when(step == 0)
        def _():
            spread_keys(steps, steps, kv_ref, far_ref, steps, k_s, v_s)
            for ref in (dk_s, dv_s, outb_ref, gainb_ref, shiftb_ref, upb_ref, downb_ref):
                ref[...] = jnp.zeros_like(ref)

        fill_groups(q_s, q_ref)
        write_mask(mask_s, col_ref[:, 1:2], marks_ref[3:4, :], far_marks_ref[3:4, :], rows, step)
        attend_forward(2 * rows, head, q_s, k_s, v_s, mask_s, o_s, probs=probs, inverse_s=inv_s)
        for group in range(groups):
            o_ref[:, group * LANES : (group + 1) * LANES] = o_s[group].astype(BF16)
        middle = start_ref[...] + matmul(o_ref[...], out_w[...]) + param(2 * width, width)
        unit, inverse = normed_rows(middle)
        gain_b = param(3 * width, width)
        normed = (unit * gain_b + param(4 * width, width)).astype(BF16)
        n_ref[...] = normed
        decoded = middle + param(5 * width + wide, width)
        for j in range(0, wide, part):
            g, slope = gelu_pair(matmul(normed, up_w[:, j : j + part]) + param(5 * width + j, part))
            g = g.astype(BF16)
            g_ref[:, j : j + part] = g
            slope_s[:, j : j + part] = slope
            decoded = decoded + matmul(g, down_w[j : j + part, :])
        dec_ref[...] = decoded.astype(BF16)
        top = cot_ref[...]
        normed_grad = jnp.zeros((TILE, width), F32)
        for j in range(0, wide, part):
            low = (slope_s[:, j : j + part] * matmul_nt(top, down_w[j : j + part, :])).astype(BF16)
            ub_ref[:, j : j + part] = low
            upb_ref[:, j : j + part] += colsum(low)
            normed_grad = normed_grad + matmul_nt(low, up_w[:, j : j + part])
        downb_ref[...] += colsum(top)
        gainb_ref[...] += colsum(normed_grad * unit)
        shiftb_ref[...] += colsum(normed_grad)
        middle_grad = top.astype(F32) + norm_back(normed_grad, unit, inverse, gain_b)
        tm_ref[...] = middle_grad
        low = middle_grad.astype(BF16)
        mb_ref[...] = low
        outb_ref[...] += colsum(low)
        attended_grad = matmul_nt(low, out_w[...])
        for group in range(groups):
            scaled = attended_grad[:, group * LANES : (group + 1) * LANES] * inv_s[group]
            ob_s[group] = scaled.astype(BF16).astype(F32)
        attend_backward(2 * rows, head, q_s, k_s, v_s, o_s, ob_s, dq_s, dk_s, dv_s, probs=probs)
        scale = head ** (-0.5)
        for group in range(groups):
            dq_ref[:, group * LANES : (group + 1) * LANES] = (dq_s[group] * scale).astype(BF16)

        @pl.when(step == steps - 1)
        def _():
            give_key_grads(rows, dk_s, dv_s, near_ref, back_ref)

    small = [width, width, width, wide, width]
    return call(
        order,
        kernel,
        "dec_main",
        meta,
        [row_tile(width), row_tile(width), whole(kv.shape), whole(kv.shape), row_tile(tall), whole(marks.shape), whole(marks.shape)]
        + [row_tile(width)] + [whole(value.shape) for value in (params, out, up, down)],
        (start, q, kv, far_kv, columns, marks, far_marks, cotangent, params, out, up, down),
        [row_tile(w) for w in (width, width, width, wide, wide, width, width, width)]
        + [out_whole((rows, 2 * width))] * 2 + [out_whole((1, w)) for w in small],
        [shaped(rows, w, BF16) for w in (width, width, width, wide, wide, width)]
        + [shaped(rows, width, F32), shaped(rows, width, BF16), shaped(rows, 2 * width, F32), shaped(rows, 2 * width, BF16)]
        + [shaped(1, w, F32) for w in small],
        [
            pltpu.VMEM((groups, TILE, LANES), F32),
            pltpu.VMEM((groups, 2 * rows, LANES), BF16),
            pltpu.VMEM((groups, 2 * rows, 2 * LANES), BF16),
            pltpu.VMEM((TILE, 2 * rows), F32),
            pltpu.VMEM((heads, TILE, 2 * rows), BF16),
        ]
        + [pltpu.VMEM((groups, TILE, LANES), F32)] * 4
        + [pltpu.VMEM((groups, LANES, 2 * rows), F32)] * 2
        + [pltpu.VMEM((TILE, wide), F32)],
        95.0,
        steps,
    )


def dec_head(order, meta, start, dq, near, back, middle_grad, columns, params, qkv):
    rows, width = start.shape
    tall = columns.shape[1]

    def kernel(meta, start_ref, dq_ref, near_ref, back_ref, tm_ref, col_ref, params_ref, qkv_ref,
               dqkv_ref, lb_ref, gain_ref, shift_ref, bias_ref, token_ref):
        step = pl.program_id(0)

        @pl.when(step == 0)
        def _():
            for ref in (gain_ref, shift_ref, bias_ref, token_ref):
                ref[...] = jnp.zeros_like(ref)

        dqkv_ref[:, :width] = dq_ref[...]
        dqkv_ref[:, width:] = (near_ref[...] + back_ref[...].astype(F32)).astype(BF16)
        grad = matmul_nt(dqkv_ref[...], qkv_ref[...])
        unit, inverse = normed_rows(start_ref[...])
        gain_ref[...] += colsum(grad * unit)
        shift_ref[...] += colsum(grad)
        start_grad = tm_ref[...] + norm_back(grad, unit, inverse, params_ref[:, :width])
        seen = col_ref[:, 2:3] > 0
        token_ref[...] += colsum(jnp.where(seen, 0.0, start_grad))
        low = jnp.where(seen, start_grad, 0.0).astype(BF16)
        lb_ref[...] = low
        bias_ref[...] += colsum(low)

    return call(
        order,
        kernel,
        "dec_head",
        meta,
        [row_tile(width), row_tile(width), row_tile(2 * width), row_tile(2 * width), row_tile(width), row_tile(tall)]
        + [whole(params.shape), whole(qkv.shape)],
        (start, dq, near, back, middle_grad, columns, params, qkv),
        [row_tile(3 * width), row_tile(width)] + [out_whole((1, width))] * 4,
        [shaped(rows, 3 * width, BF16), shaped(rows, width, BF16)] + [shaped(1, width, F32)] * 4,
        [],
        40.0,
        rows // TILE,
    )


def enc_back(order, meta, sel, lb, slope, m, q, kv, far_kv, o, totals, label, code, far_code, params, out, up, down, embed, heads):
    rows, width = m.shape
    wide, lifted_width = up.shape[1], embed.shape[1]
    groups, head, most = width // LANES, width // heads, rows // TILE
    part = width
    tall = label.shape[1]

    def kernel(meta, sel_ref, lb_ref, slope_ref, m_ref, q_ref, kv_ref, far_ref, o_ref, tot_ref, label_ref, code_ref, far_code_ref,
               params_ref, out_w, up_w, down_w, embed_w,
               lbc_ref, tb_ref, ub_ref, mb_ref, tm_ref, dq_ref, near_ref, back_ref,
               outb_ref, gainb_ref, shiftb_ref, upb_ref, downb_ref,
               q_s, k_s, v_s, mask_s, o_s, ob_s, dq_s, dk_s, dv_s):
        step = pl.program_id(0)
        tiles, far_tiles = meta[0], meta[1]
        count = jnp.maximum(tiles, far_tiles)
        scale = head ** (-0.5)

        @pl.when(step == 0)
        def _():
            for ref in (dk_s, dv_s, outb_ref, gainb_ref, shiftb_ref, upb_ref, downb_ref):
                ref[...] = jnp.zeros_like(ref)

        @pl.when(step < tiles)
        def _():
            lb_here = matmul(sel_ref[...], lb_ref[...]).astype(BF16)
            lbc_ref[...] = lb_here
            grad_top = matmul_nt(lb_here, embed_w[...])
            top = grad_top.astype(BF16)
            tb_ref[...] = top
            normed_grad = jnp.zeros((TILE, width), F32)
            for j in range(0, wide, part):
                low = (slope_ref[:, j : j + part].astype(F32) * matmul_nt(top, down_w[j : j + part, :])).astype(BF16)
                ub_ref[:, j : j + part] = low
                upb_ref[:, j : j + part] += colsum(low)
                normed_grad = normed_grad + matmul_nt(low, up_w[:, j : j + part])
            unit, inverse = normed_rows(m_ref[...])
            downb_ref[...] += colsum(top)
            gainb_ref[...] += colsum(normed_grad * unit)
            shiftb_ref[...] += colsum(normed_grad)
            middle_grad = grad_top + norm_back(normed_grad, unit, inverse, params_ref[:, 3 * width : 4 * width])
            tm_ref[...] = middle_grad
            low = middle_grad.astype(BF16)
            mb_ref[...] = low
            outb_ref[...] += colsum(low)
            attended_grad = matmul_nt(low, out_w[...]).astype(BF16)
            fill_groups(ob_s, attended_grad)
            fill_groups(o_s, o_ref)
            fill_groups(q_s, q_ref)
            for size in range(1, most + 1):

                @pl.when(count == size)
                def _(size=size):
                    @pl.when(step == 0)
                    def _():
                        spread_keys(size, tiles, kv_ref, far_ref, far_tiles, k_s, v_s)

                    span = size * TILE
                    write_mask(mask_s, label_ref[:, 1:2], code_ref[0:1, :span], far_code_ref[0:1, :span], span, step)
                    attend_backward(
                        2 * span, head, q_s, k_s, v_s, o_s, ob_s, dq_s, dk_s, dv_s, mask_ref=mask_s, totals=tot_ref[...]
                    )

                    @pl.when(step == tiles - 1)
                    def _():
                        give_key_grads(span, dk_s, dv_s, near_ref, back_ref)

            for group in range(groups):
                dq_ref[:, group * LANES : (group + 1) * LANES] = (dq_s[group] * scale).astype(BF16)

    small = [width, width, width, wide, width]
    return call(
        order,
        kernel,
        "enc_back",
        meta,
        [live_tile(rows), whole(lb.shape), live_tile(wide), live_tile(width), live_tile(width), whole(kv.shape), whole(kv.shape)]
        + [live_tile(width), live_tile(LANES), live_tile(tall), whole(code.shape), whole(code.shape)]
        + [whole(value.shape) for value in (params, out, up, down, embed)],
        (sel, lb, slope, m, q, kv, far_kv, o, totals, label, code, far_code, params, out, up, down, embed),
        [live_tile(w) for w in (lifted_width, width, wide, width, width, width)]
        + [whole((rows, 2 * width))] * 2 + [out_whole((1, w)) for w in small],
        [shaped(rows, w, BF16) for w in (lifted_width, width, wide, width)]
        + [shaped(rows, width, F32), shaped(rows, width, BF16), shaped(rows, 2 * width, F32), shaped(rows, 2 * width, BF16)]
        + [shaped(1, w, F32) for w in small],
        [
            pltpu.VMEM((groups, TILE, LANES), F32),
            pltpu.VMEM((groups, 2 * rows, LANES), BF16),
            pltpu.VMEM((groups, 2 * rows, LANES), BF16),
            pltpu.VMEM((TILE, 2 * rows), F32),
        ]
        + [pltpu.VMEM((groups, TILE, LANES), F32)] * 3
        + [pltpu.VMEM((groups, LANES, 2 * rows), F32)] * 2,
        24.0,
        most,
    )


def enc_head(order, meta, sel, s, dq, near, back, middle_grad, params, qkv):
    rows, width = s.shape
    steps = rows // TILE

    def kernel(meta, sel_ref, s_ref, dq_ref, near_ref, back_ref, tm_ref, params_ref, qkv_ref,
               dqkv_ref, grad_ref, gain_ref, shift_ref, total):
        step = pl.program_id(0)

        @pl.when(step == 0)
        def _():
            for ref in (gain_ref, shift_ref, total):
                ref[...] = jnp.zeros_like(ref)

        @pl.when(step < meta[0])
        def _():
            dqkv_ref[:, :width] = dq_ref[...]
            dqkv_ref[:, width:] = (near_ref[...] + back_ref[...].astype(F32)).astype(BF16)
            grad = matmul_nt(dqkv_ref[...], qkv_ref[...])
            unit, inverse = normed_rows(s_ref[...].astype(F32))
            gain_ref[...] += colsum(grad * unit)
            shift_ref[...] += colsum(grad)
            stream_grad = tm_ref[...] + norm_back(grad, unit, inverse, params_ref[:, :width])
            total[...] += matmul_tn(sel_ref[...], stream_grad.astype(BF16))

        @pl.when(step == steps - 1)
        def _():
            grad_ref[...] = total[...].astype(BF16)

    return call(
        order,
        kernel,
        "enc_head",
        meta,
        [live_tile(w) for w in (rows, width, width, 2 * width, 2 * width, width)] + [whole(params.shape), whole(qkv.shape)],
        (sel, s, dq, near, back, middle_grad, params, qkv),
        [live_tile(3 * width), out_whole((rows, width))] + [out_whole((1, width))] * 2,
        [shaped(rows, 3 * width, BF16), shaped(rows, width, BF16)] + [shaped(1, width, F32)] * 2,
        [pltpu.VMEM((rows, width), F32)],
        8.0,
        steps,
    )


def joined(values):
    total, offset = sum(value.size for value in values), 0
    row = jnp.zeros((total,), F32)
    for value in values:
        row = row + jnp.pad(value.astype(F32), (offset, total - offset - value.size))
        offset += value.size
    return row.reshape(1, total)


def local(
    patches,
    visible,
    padding,
    field_ids,
    enc_gain_a,
    enc_shift_a,
    enc_qkv,
    enc_out,
    enc_out_bias,
    enc_gain_b,
    enc_shift_b,
    enc_up,
    enc_up_bias,
    enc_down,
    enc_down_bias,
    embed_map,
    embed_bias,
    mask_token,
    dec_gain_a,
    dec_shift_a,
    dec_qkv,
    dec_out,
    dec_out_bias,
    dec_gain_b,
    dec_shift_b,
    dec_up,
    dec_up_bias,
    dec_down,
    dec_down_bias,
    cotangent,
):
    rows = patches.shape[0]
    tiles_most = rows // TILE
    raw = [value.reshape(1, rows) for value in (visible, padding, field_ids)]
    far_raw = [across(value, "blk", 0) for value in raw]
    counts = jnp.stack([jnp.sum(raw[0]), jnp.sum(far_raw[0])]).astype(jnp.int32)
    meta = jnp.clip((counts + TILE - 1) // TILE, 1, tiles_most)

    enc_params = joined(
        [enc_gain_a, enc_shift_a, enc_out_bias, enc_gain_b, enc_shift_b, enc_up_bias, enc_down_bias, embed_bias]
    )
    dec_params = joined(
        [dec_gain_a, dec_shift_a, dec_out_bias, dec_gain_b, dec_shift_b, dec_up_bias, dec_down_bias, mask_token]
    )

    order = Order()
    shards = min(16, lax.axis_size("dp"))
    spots = jnp.stack([lax.axis_index("dp") & (shards - 1), lax.axis_index("blk")]).astype(jnp.int32)
    de, dd = enc_qkv.shape[0], dec_qkv.shape[0]
    rd, re = dd // shards, de // shards

    sel, code, far_code, label, marks, far_marks, columns, s, n1, q, kv = enc_in(order, meta, patches, raw, far_raw, enc_params, enc_qkv, HE)
    far_kv = across(kv, "blk", 0)
    o, totals, m, n2, g, slope, low, lift_high, lift_low = enc_main(
        order, meta, s, q, kv, far_kv, label, code, far_code, enc_params, enc_out, enc_up, enc_down, embed_map, HE
    )
    start, dn1, dq_rows, dkv = dec_in(order, meta, sel, lift_high, lift_low, columns, dec_params, dec_qkv, HD)
    far_dkv = across(dkv, "blk", 0)
    (decoded, d_o, d_n2, d_g, d_ub, d_mb, d_tm, d_dq, d_near, d_back, d_outb, d_gainb, d_shiftb, d_upb, d_downb) = dec_main(
        order, meta, start, dq_rows, dkv, far_dkv, columns, marks, far_marks, cotangent, dec_params, dec_out, dec_up, dec_down, HD
    )
    d_back = across(d_back, "blk", 0)

    def bundle(bits, *entries, short=(), late=True):
        return Bundle(order, bits, spots, meta, [Entry(*entry) for entry in entries], short, late)

    dec = bundle(
        DEC_BITS,
        ("wide", d_n2, d_ub, rd, 4, dd // 2, dec_up.shape, False),
        ("tall", d_g, cotangent, rd, 4, dd // 2, dec_down.shape, False),
        ("wide", d_o, d_mb, rd, 1, dd // 2, dec_out.shape, False),
        late=False,
    )
    dec.weigh()
    d_dqkv, lb, d_gaina, d_shifta, embed_b, token_grad = dec_head(
        order, meta, start, d_dq, d_near, d_back, d_tm, columns, dec_params, dec_qkv
    )
    dec.step()
    (lbc, tb, ub, mb, tm, dq, near, back, outb, gainb, shiftb, upb, downb) = enc_back(
        order, meta, sel, lb, slope, m, q, kv, far_kv, o, totals, label, code, far_code,
        enc_params, enc_out, enc_up, enc_down, embed_map, HE,
    )
    back = across(back, "blk", 0)
    dec.step()
    enc_a = bundle(
        ENC_BITS[0],
        ("wide", n2, ub, re, 4, de // 2, enc_up.shape, True),
        ("wide", o, mb, re, 1, de // 2, enc_out.shape, True),
    )
    enc_b = bundle(
        ENC_BITS[1],
        ("tall", g, tb, re, 4, de // 2, enc_down.shape, True),
        ("wide", low, lbc, re, 1, dd // 2, embed_map.shape, True),
    )
    enc_a.weigh()
    enc_b.weigh()
    enc_a.step()
    dqkv, patches_grad, gaina, shifta = enc_head(order, meta, sel, s, dq, near, back, tm, enc_params, enc_qkv)
    enc_b.step()
    dec.step()
    short = [gaina, shifta, outb, gainb, shiftb, upb, downb, embed_b, token_grad]
    short += [d_gaina, d_shifta, d_outb, d_gainb, d_shiftb, d_upb, d_downb]
    enc_c = bundle(
        ENC_BITS[2],
        ("wide", n1, dqkv, re, 3, de // 2, enc_qkv.shape, True),
        ("wide", dn1, d_dqkv, rd, 3 * dd // de, de // 2, dec_qkv.shape, False),
        short=short,
    )
    enc_c.weigh()
    bundles = {"d": dec, "a": enc_a, "b": enc_b, "c": enc_c}
    for name in STEPS:
        bundles[name].step()
    g_dec_up, g_dec_down, g_dec_out = dec.placed
    g_enc_up, g_enc_out = enc_a.placed
    g_enc_down, g_embed = enc_b.placed
    g_enc_qkv, g_dec_qkv, sums = enc_c.placed
    sums = sums[:, : SHORT // LANES, :].reshape(-1)
    small, offset = [], 0
    for value in short:
        small.append(sums[offset : offset + value.size])
        offset += value.size
    return (
        (decoded, patches_grad)
        + (small[0], small[1], g_enc_qkv, g_enc_out, small[2], small[3], small[4])
        + (g_enc_up, small[5], g_enc_down, small[6], g_embed, small[7], small[8])
        + (small[9], small[10], g_dec_qkv, g_dec_out, small[11], small[12], small[13])
        + (g_dec_up, small[14], g_dec_down, small[15])
    )


def solution(mesh):
    return jax.shard_map(
        local,
        mesh=mesh,
        in_specs=(
            P(("dp", "blk"), None),
            P(("dp", "blk")),
            P(("dp", "blk")),
            P(("dp", "blk")),
            P(),
            P(),
            P(),
            P(),
            P(),
            P(),
            P(),
            P(),
            P(),
            P(),
            P(),
            P(),
            P(),
            P(),
            P(),
            P(),
            P(),
            P(),
            P(),
            P(),
            P(),
            P(),
            P(),
            P(),
            P(),
            P(("dp", "blk"), None),
        ),
        out_specs=(
            P(("dp", "blk"), None),
            P(("dp", "blk"), None),
            P(),
            P(),
            P(),
            P(),
            P(),
            P(),
            P(),
            P(),
            P(),
            P(),
            P(),
            P(),
            P(),
            P(),
            P(),
            P(),
            P(),
            P(),
            P(),
            P(),
            P(),
            P(),
            P(),
            P(),
            P(),
        ),
        check_vma=False,
    )
```
